32 devices in a mesh: dp: 8 (over z, y), section: 4 (over x, core).
Axes of the slice: x: 2, y: 2, z: 4, core: 2. Of those that a mesh axis runs over, the one named last changes fastest.
Arguments:
- word_embed: bfloat16 [8192, 768], P(('dp', 'section')), may hold values from -6 to 6
- boxes: int32 [4, 8192], P(None, 'dp'), may hold values from 0 to 1023
- mask_pos: int32 [16, 96], P('dp'), may hold values from -1 to 511, as said below
- replace_ids: int32 [16, 96], P('dp'), may hold values from -1 to 16383, as said below
- cotangent: bfloat16 [8192, 768], P(('dp', 'section')), may hold values from -14 to 14
- layout_table: bfloat16 [2, 1024, 768], replicated, may hold values from -3 to 3
- vocab_table: bfloat16 [16384, 768], P('dp'), may hold values from -6 to 6
- embed_gain: float32 [768], replicated, may hold values from 0.5 to 1.5
- embed_shift: float32 [768], replicated, may hold values from -4 to 4
- qkv_weight: bfloat16 [4, 768, 1152], P('section'), may hold values from -0.21875 to 0.21875
- qv_bias: float32 [4, 2, 384], P('section'), may hold values from -3 to 3
- out_weight: bfloat16 [4, 384, 768], P('section'), may hold values from -1.75 to 1.75
- up_weight: bfloat16 [4, 768, 1536], P('section'), may hold values from -0.21875 to 0.21875
- up_bias: float32 [4, 1536], P('section'), may hold values from -3 to 3
- down_weight: bfloat16 [4, 1536, 768], P('section'), may hold values from -0.109375 to 0.109375
- layer_gains: float32 [2, 2, 768], replicated, may hold values from 0.5 to 1.5
- layer_biases: float32 [2, 4, 768], replicated, may hold values from -3 to 3
Outputs:
- activations: float32 [8192, 768], P(('dp', 'section'))
- input_grad: float32 [8192, 768], P(('dp', 'section'))
- layout_table_grad: float32 [2, 1024, 768], P(None, ('dp', 'section'))
- vocab_table_grad: float32 [16384, 768], P(('dp', 'section'))
- embed_gain_grad: float32 [768], replicated
- embed_shift_grad: float32 [768], replicated
- qkv_weight_grad: float32 [4, 768, 1152], P('section')
- qv_bias_grad: float32 [4, 2, 384], P('section')
- out_weight_grad: float32 [4, 384, 768], P('section')
- up_weight_grad: float32 [4, 768, 1536], P('section')
- up_bias_grad: float32 [4, 1536], P('section')
- down_weight_grad: float32 [4, 1536, 768], P('section')
- layer_gains_grad: float32 [2, 2, 768], replicated
- layer_biases_grad: float32 [2, 4, 768], replicated
The draws below stay inside these ranges and needn't reach their ends.
Inputs may be any that keep to these rules, and one draw needn't show every extreme that they name: `mask_pos`: each row lists distinct positions of its page first and -1 after them; a row uses between half of 96 and 96 entries, and the first row uses all. `replace_ids`: an entry is -1 exactly where mask_pos is -1, else an id of the table.
All inputs are finite; a program needn't handle non-finite values.
Results may differ from the reference program's by a relative error of at most 0.017.
Values may be sent and summed in bfloat16 or wider, within the bound.
A program may use at most 192 MiB of HBM per device.

```python
import jax
import jax.numpy as jnp
from jax import lax

D = 768
HEADS = 12
HEAD_DIM = 64
FF = 3072
COORDS = 1024
VOCAB = 16384
PAGE = 512
SLOTS = 96
PAGES = 16
TOKENS = 8192
N_SECTION = 4


def page_counts(key):
    count_key = jax.random.fold_in(key, 5)
    counts = jax.random.randint(count_key, (PAGES,), (SLOTS + 1) // 2, SLOTS + 1)
    return counts.at[0].set(SLOTS)


def draw_mask_pos(key, part):
    counts = page_counts(key)
    key = jax.random.fold_in(key, 7)
    page_keys = jax.random.split(key, PAGES)

    def page_order(page_key):
        return jax.random.permutation(page_key, PAGE)
    orders = jax.vmap(page_order)(page_keys)[:, :SLOTS].astype(jnp.int32)
    slot_index = jnp.arange(SLOTS, dtype=jnp.int32)
    return jnp.where(slot_index[None, :] < counts[:, None], orders, -1).astype(jnp.int32)


def draw_replace_ids(key, part):
    counts = page_counts(key)
    key = jax.random.fold_in(key, 11)
    ids = jax.random.randint(key, (PAGES, SLOTS), 0, VOCAB).astype(jnp.int32)
    ids = ids.at[0, 0].set(VOCAB - 1)
    slot_index = jnp.arange(SLOTS, dtype=jnp.int32)
    return jnp.where(slot_index[None, :] < counts[:, None], ids, -1).astype(jnp.int32)


def rising_scale(first_scale, ratio):
    place = jnp.arange(TOKENS, dtype=jnp.float32) / TOKENS
    return first_scale * jnp.exp(jnp.log(ratio) * place)


def draw_cotangent(key, part):
    key = jax.random.fold_in(key, 13)
    noise_key = jax.random.fold_in(key, 19)
    noise = jnp.clip(jax.random.normal(noise_key, (TOKENS, D), jnp.float32), -4.0, 4.0)
    rows = noise * rising_scale(0.6, 3.0)[:, None]
    return rows.astype(jnp.bfloat16)


def place_ends(drawn, rng, low, largest):
    longest = drawn.shape.index(max(drawn.shape))
    spots = []
    for shift in (0, 1):
        where = [jax.random.randint(jax.random.fold_in(rng, axis), (), 0, length) for axis, length in enumerate(drawn.shape)]
        where[longest] = (where[longest] + shift) % drawn.shape[longest]
        spots.append(tuple(where))
    return drawn.at[spots[0]].set(low).at[spots[1]].set(largest)


def block_levels(own_key, extent, cuts, smallest, high):
    def one(position, parts):
        heights = jax.random.uniform(jax.random.fold_in(jax.random.fold_in(own_key, 6), position), (parts,), jnp.float32, smallest / len(cuts), high / len(cuts))
        return jnp.repeat(jnp.exp(heights), extent[position] // parts).reshape((-1,) + (1,) * (len(extent) - position - 1))

    level = one(*cuts[0])
    for cut in cuts[1:]:
        level = level * one(*cut)
    return level


def normal_values(own_key, dims, scale, limit, cuts=(), held_as=jnp.bfloat16):
    result = scale * jax.random.normal(own_key, dims, jnp.float32)
    if cuts:
        result = result * block_levels(own_key, dims, cuts, -0.22, 0.18)
    return jnp.clip(result, -limit, limit).astype(held_as)


def setup_inputs(seed: int = 0) -> dict:
    seeds = jax.random.split(jax.random.key(seed), 18)
    word_embed = normal_values(seeds[0], (TOKENS, D), 1.0, 6.0, ((0, 32),))
    boxes = place_ends(jax.random.randint(seeds[1], (4, TOKENS), 0, COORDS), jax.random.fold_in(seeds[1], 1), 0, COORDS - 1).astype(jnp.int32)
    mask_pos = draw_mask_pos(jax.random.fold_in(seeds[17], 71), 0)
    replace_ids = draw_replace_ids(jax.random.fold_in(seeds[17], 71), 0)
    cotangent = draw_cotangent(jax.random.fold_in(seeds[17], 71), 0)
    layout_table = normal_values(seeds[5], (2, COORDS, D), 0.5, 3.0)
    vocab_table = normal_values(seeds[6], (VOCAB, D), 1.0, 6.0, ((0, 8),))
    embed_gain = jnp.clip(1.0 + 0.1 * jax.random.normal(seeds[7], (D,), jnp.float32), 0.5, 1.5)
    embed_shift = normal_values(seeds[8], (D,), 0.7, 4.0, (), jnp.float32)
    qkv_weight = normal_values(seeds[9], (N_SECTION, D, 3 * (D // 2)), D ** -0.5, 0.21875, ((0, 4),))
    qv_bias = normal_values(seeds[10], (N_SECTION, 2, D // 2), 0.5, 3.0, ((0, 4),), jnp.float32)
    out_weight = normal_values(seeds[11], (N_SECTION, D // 2, D), (max(D // 64, 1)) ** -0.5, 1.75, ((0, 4),))
    up_weight = normal_values(seeds[12], (N_SECTION, D, FF // 2), D ** -0.5, 0.21875, ((0, 4),))
    up_bias = normal_values(seeds[13], (N_SECTION, FF // 2), 0.5, 3.0, ((0, 4),), jnp.float32)
    down_weight = normal_values(seeds[14], (N_SECTION, FF // 2, D), FF ** -0.5, 0.109375, ((0, 4),))
    layer_gains = jnp.clip(1.0 + 0.1 * jax.random.normal(seeds[15], (2, 2, D), jnp.float32), 0.5, 1.5)
    layer_biases = normal_values(seeds[16], (2, 4, D), 0.5, 3.0, (), jnp.float32)
    return {"word_embed": word_embed, "boxes": boxes, "mask_pos": mask_pos, "replace_ids": replace_ids, "cotangent": cotangent, "layout_table": layout_table, "vocab_table": vocab_table, "embed_gain": embed_gain, "embed_shift": embed_shift, "qkv_weight": qkv_weight, "qv_bias": qv_bias, "out_weight": out_weight, "up_weight": up_weight, "up_bias": up_bias, "down_weight": down_weight, "layer_gains": layer_gains, "layer_biases": layer_biases}


@jax.custom_vjp
def low(v):
    return lax.optimization_barrier(v.astype(jnp.bfloat16)).astype(jnp.float32)

@jax.custom_vjp
def low_back(v):
    return v

def low_keep(v):
    return (low(v), None)

def low_pass(kept, grad):
    return (grad,)

def back_keep(v):
    return (v, None)

def back_low(kept, grad):
    return (low(grad),)
low.defvjp(low_keep, low_pass)
low_back.defvjp(back_keep, back_low)
EPS = 1e-12
HIGH = lax.Precision.HIGHEST
ROOT_HALF = 0.7071067811865476

def matmul(left, right):
    return jnp.dot(left, right, precision=HIGH, preferred_element_type=jnp.float32)

def normalize(values, gain, shift):
    center = values - lax.optimization_barrier(jnp.mean(values, -1, keepdims=True))
    spread = lax.optimization_barrier(jnp.mean(center * center, -1, keepdims=True))
    return center * lax.rsqrt(spread + EPS) * gain + shift

def gelu_exact(values):
    return 0.5 * values * (1.0 + jax.scipy.special.erf(values * ROOT_HALF))

def attend_page(blocks):
    queries, key_rows, value_rows = blocks
    scores = low_back(jnp.einsum('qhd,khd->hqk', queries, key_rows, precision=HIGH) * HEAD_DIM ** (-0.5))
    probs = low(jax.nn.softmax(scores, axis=-1))
    context = jnp.einsum('hqk,khd->qhd', probs, value_rows, precision=HIGH)
    return context.reshape(queries.shape[0], -1)

def layer_apply(rows, layer_params, index):
    qkv_full, qv_full, out_full, up_full, upb_full, down_full, gains, shifts = layer_params
    first_slot = 2 * index
    second_slot = 2 * index + 1
    half_width = D // 2

    def joined_cols(start):
        return jnp.concatenate([qkv_full[first_slot][:, start:start + half_width], qkv_full[second_slot][:, start:start + half_width]], 1)
    w_query = joined_cols(0)
    w_key = joined_cols(half_width)
    w_value = joined_cols(2 * half_width)
    b_query = jnp.concatenate([qv_full[first_slot][0], qv_full[second_slot][0]])
    b_value = jnp.concatenate([qv_full[first_slot][1], qv_full[second_slot][1]])
    w_out = jnp.concatenate([out_full[first_slot], out_full[second_slot]], 0)
    w_up = jnp.concatenate([up_full[first_slot], up_full[second_slot]], 1)
    b_up = jnp.concatenate([upb_full[first_slot], upb_full[second_slot]])
    w_down = jnp.concatenate([down_full[first_slot], down_full[second_slot]], 0)
    rows_low = low(rows)
    queries = low(low_back(matmul(rows_low, w_query) + b_query))
    key_rows = low(low_back(matmul(rows_low, w_key)))
    value_rows = low(low_back(matmul(rows_low, w_value) + b_value))
    page_shape = (-1, PAGE, HEADS, HEAD_DIM)
    context = lax.map(jax.checkpoint(attend_page), (queries.reshape(page_shape), key_rows.reshape(page_shape), value_rows.reshape(page_shape)))
    context = low(low_back(context.reshape(-1, D)))
    attended = low_back(matmul(context, w_out) + shifts[index, 0])
    hidden = normalize(rows + attended, gains[index, 0], shifts[index, 1])
    upper = low_back(matmul(low(hidden), w_up) + b_up)
    mixed = low_back(matmul(low(gelu_exact(upper)), w_down) + shifts[index, 2])
    return normalize(hidden + mixed, gains[index, 1], shifts[index, 3])

def forward_group(params, words_in, box_rows, mask_rows, id_rows):
    table = params[0]
    vocab = params[1]
    gain_vec = params[2]
    shift_vec = params[3]
    layer_params = params[4:]
    places = jnp.arange(PAGE, dtype=jnp.int32)
    chosen = (mask_rows[:, :, None] == places[None, None, :]).astype(jnp.float32)
    marked = jnp.any(mask_rows[:, :, None] == places[None, None, :], axis=1).reshape(-1)
    vocab_ids = jnp.arange(VOCAB, dtype=jnp.int32)
    picked = (id_rows[:, :, None] == vocab_ids[None, None, :]).astype(jnp.float32)
    slot_rows = jnp.einsum('gsv,vd->gsd', picked, vocab, precision=HIGH)
    replaced = jnp.einsum('gsp,gsd->gpd', chosen, slot_rows, precision=HIGH).reshape(-1, D)
    coords = jnp.arange(COORDS, dtype=jnp.int32)
    one_x = (box_rows[0][:, None] == coords[None, :]).astype(jnp.float32) + (box_rows[2][:, None] == coords[None, :]).astype(jnp.float32)
    one_y = (box_rows[1][:, None] == coords[None, :]).astype(jnp.float32) + (box_rows[3][:, None] == coords[None, :]).astype(jnp.float32)
    summed = jnp.where(marked[:, None], replaced, words_in) + matmul(one_x, table[0]) + matmul(one_y, table[1])
    hidden_in = normalize(low_back(summed), gain_vec, shift_vec)
    first_out = layer_apply(hidden_in, layer_params, 0)
    second_in = low(low_back(first_out))
    return layer_apply(second_in, layer_params, 1)

def reference(word_embed, boxes, mask_pos, replace_ids, cotangent, layout_table, vocab_table, embed_gain, embed_shift, qkv_weight, qv_bias, out_weight, up_weight, up_bias, down_weight, layer_gains, layer_biases):
    params = tuple((array.astype(jnp.float32) for array in (layout_table, vocab_table, embed_gain, embed_shift, qkv_weight, qv_bias, out_weight, up_weight, up_bias, down_weight, layer_gains, layer_biases)))
    group = 8
    while PAGES % group:
        group = group // 2
    groups = PAGES // group
    words = word_embed.astype(jnp.float32).reshape(groups, group * PAGE, D)
    grads_in = cotangent.astype(jnp.float32).reshape(groups, group * PAGE, D)
    box_groups = boxes.reshape(4, groups, group * PAGE).transpose(1, 0, 2)
    mask_groups = mask_pos.reshape(groups, group, SLOTS)
    id_groups = replace_ids.reshape(groups, group, SLOTS)

    def one_group(totals, pieces):
        words_in, grad_rows, box_rows, mask_rows, id_rows = pieces

        def apply_group(param_set, word_rows):
            return forward_group(param_set, word_rows, box_rows, mask_rows, id_rows)
        outputs, pullback = jax.vjp(apply_group, params, words_in)
        param_grads, word_grads = pullback(grad_rows)
        totals = jax.tree.map(jnp.add, totals, param_grads)
        return (totals, (outputs, word_grads))
    zero_grads = jax.tree.map(jnp.zeros_like, params)
    totals, (outputs, word_grads) = lax.scan(one_group, zero_grads, (words, grads_in, box_groups, mask_groups, id_groups))
    return (outputs.reshape(TOKENS, D), word_grads.reshape(TOKENS, D), totals[0], totals[1], totals[2], totals[3], totals[4], totals[5], totals[6], totals[7], totals[8], totals[9], totals[10], totals[11])
```

```python
import functools

import jax
import jax.numpy as jnp
from jax import lax
from jax.experimental import pallas as pl
from jax.experimental.pallas import tpu as pltpu
from jax.sharding import PartitionSpec as P

HEAD_DIM = 64
EPS = 1e-12
ROOT_HALF = 0.7071067811865476
INV_ROOT_TWO_PI = 0.3989422804014327
BF = jnp.bfloat16
F32 = jnp.float32


def routed(block, route):
    return lax.ppermute(block, "section", route)


SWAP = [(0, 1), (1, 0), (2, 3), (3, 2)]


def swapped(block):
    return routed(block, SWAP)


def normalize(values, gain, shift):
    center = values - jnp.mean(values, -1, keepdims=True)
    spread = jnp.mean(center * center, -1, keepdims=True)
    inverse = lax.rsqrt(spread + EPS)
    normed = center * inverse
    return (normed * gain + shift, normed, inverse)


def normalize_back(grad, normed, inverse, gain):
    scaled = grad * gain
    centered = (
        scaled
        - jnp.mean(scaled, -1, keepdims=True)
        - normed * jnp.mean(scaled * normed, -1, keepdims=True)
    )
    return (inverse * centered, jnp.sum(grad * normed, 0), jnp.sum(grad, 0))


def gelu_exact(values):
    return 0.5 * values * (1.0 + lax.erf(values * ROOT_HALF))


def gelu_slope(values):
    return (
        0.5 * (1.0 + lax.erf(values * ROOT_HALF))
        + values * jnp.exp(-0.5 * values * values) * INV_ROOT_TWO_PI
    )


def matmul(left, right):
    return jnp.dot(left, right, preferred_element_type=F32)


def matmul_left_t(left, right):
    return jnp.einsum("pa,pb->ab", left, right, preferred_element_type=F32)


def matmul_right_t(left, right):
    return jnp.einsum("pa,ba->pb", left, right, preferred_element_type=F32)


def layer_forward(rows, weights):
    w_q, w_k, w_v, b_q, b_v, w_out, w_up, b_up, w_down, gains, shifts = weights
    width = w_out.shape[0]
    heads = width // HEAD_DIM
    length = rows.shape[0]
    scale = HEAD_DIM ** (-0.5)
    rows_low = rows.astype(BF)
    queries = (matmul(rows_low, w_q) + b_q).astype(BF).reshape(length, heads, HEAD_DIM)
    key_rows = matmul(rows_low, w_k).astype(BF).reshape(length, heads, HEAD_DIM)
    value_rows = (matmul(rows_low, w_v) + b_v).astype(BF).reshape(length, heads, HEAD_DIM)
    scores = jnp.einsum("qhd,khd->hqk", queries, key_rows, preferred_element_type=F32) * scale
    highest = jnp.max(scores, -1, keepdims=True)
    expo = jnp.exp(scores - highest)
    probs = expo / jnp.sum(expo, -1, keepdims=True)
    probs_low = probs.astype(BF)
    context = jnp.einsum("hqk,khd->qhd", probs_low, value_rows, preferred_element_type=F32)
    context = context.reshape(length, width).astype(BF)
    attended = matmul(context, w_out) + shifts[0]
    hidden, normed_one, inverse_one = normalize(rows + attended, gains[0], shifts[1])
    hidden_low = hidden.astype(BF)
    upper = matmul(hidden_low, w_up) + b_up
    active = gelu_exact(upper).astype(BF)
    mixed = matmul(active, w_down) + shifts[2]
    output, normed_two, inverse_two = normalize(hidden + mixed, gains[1], shifts[3])
    kept = (
        rows_low, queries, key_rows, value_rows, probs, probs_low, context, normed_one,
        inverse_one, hidden_low, upper, active, normed_two, inverse_two,
    )
    return (output, kept)


def layer_backward(kept, grad_out, weights):
    w_q, w_k, w_v, b_q, b_v, w_out, w_up, b_up, w_down, gains, shifts = weights
    (
        rows_low, queries, key_rows, value_rows, probs, probs_low, context, normed_one,
        inverse_one, hidden_low, upper, active, normed_two, inverse_two,
    ) = kept
    width = w_out.shape[0]
    heads = width // HEAD_DIM
    length = rows_low.shape[0]
    scale = HEAD_DIM ** (-0.5)
    grad_two, gain_two, shift_two = normalize_back(grad_out, normed_two, inverse_two, gains[1])
    grad_mixed = grad_two.astype(BF)
    shift_down = jnp.sum(grad_mixed.astype(F32), 0)
    grad_active = matmul_right_t(grad_mixed, w_down)
    grad_upper = (grad_active * gelu_slope(upper)).astype(BF)
    grad_hidden = grad_two + matmul_right_t(grad_upper, w_up)
    grad_one, gain_one, shift_one = normalize_back(grad_hidden, normed_one, inverse_one, gains[0])
    grad_attended = grad_one.astype(BF)
    shift_out = jnp.sum(grad_attended.astype(F32), 0)
    grad_context = matmul_right_t(grad_attended, w_out).astype(BF).reshape(length, heads, HEAD_DIM)
    grad_probs = jnp.einsum("qhd,khd->hqk", grad_context, value_rows, preferred_element_type=F32)
    grad_scores = (probs * (grad_probs - jnp.sum(probs * grad_probs, -1, keepdims=True))).astype(BF)
    grad_q = (
        jnp.einsum("hqk,khd->qhd", grad_scores, key_rows, preferred_element_type=F32) * scale
    ).astype(BF).reshape(length, width)
    grad_k = (
        jnp.einsum("hqk,qhd->khd", grad_scores, queries, preferred_element_type=F32) * scale
    ).astype(BF).reshape(length, width)
    grad_v = jnp.einsum(
        "hqk,qhd->khd", probs_low, grad_context, preferred_element_type=F32
    ).astype(BF).reshape(length, width)
    grad_rows = (
        grad_one
        + matmul_right_t(grad_q, w_q)
        + matmul_right_t(grad_k, w_k)
        + matmul_right_t(grad_v, w_v)
    )
    gains_grad = jnp.stack([gain_one, gain_two])
    shifts_grad = jnp.stack([shift_out, shift_one, shift_down, shift_two])
    whole = (rows_low, grad_attended, hidden_low, grad_mixed)
    split = (grad_q, grad_k, grad_v, context, grad_upper, active)
    return (grad_rows, whole, split, gains_grad, shifts_grad)


GROUP = 8
BLOCK = 128
HOP = 4
DEPTH = 3


def tree_of(k):
    turn = k % 8
    return turn < 4, 1 + turn % 2, (turn // 2) % 2


def reduce_kernel(
    counts, a_ref, b_ref, small_ref, out_ref, gathered_ref, buf, total, gathered, send, recv,
    out_sem, g_send, g_recv, g_out,
):
    me = lax.axis_index("dp")
    section = lax.axis_index("section")
    z = (me % GROUP) // 2
    y = me % 2
    chunks = buf.shape[1]
    side = buf.shape[3]
    n_q, n_o, n_u, n_d = counts
    mesh_id = pl.DeviceIdType.MESH
    deltas = (-2, 2, 1 - 2 * y)
    exists = (z > 0, z < GROUP // 2 - 1, y >= 0)
    n_sections = lax.axis_size("section")

    barrier = pltpu.get_barrier_semaphore()
    for d in range(3):

        @pl.when(exists[d])
        def _():
            pl.semaphore_signal(
                barrier, inc=1, device_id=(me + deltas[d], section), device_id_type=mesh_id
            )

    for step in range(1, n_sections):
        pl.semaphore_signal(
            barrier, inc=1, device_id=(me, (section + step) % n_sections), device_id_type=mesh_id
        )
    pl.semaphore_wait(
        barrier,
        n_sections + jnp.where(exists[0], 1, 0) + jnp.where(exists[1], 1, 0),
    )

    def roles(k):
        comb, root_z, root_y = tree_of(k)
        along = jnp.logical_or(jnp.logical_not(comb), y == root_y)
        across = jnp.logical_or(comb, z == root_z)
        child = (
            exists[0] & along & (z <= root_z),
            exists[1] & along & (z >= root_z),
            across & (y == root_y),
        )
        up_z = along & (z != root_z)
        up_y = across & (y != root_y)
        parent = jnp.where(up_z, jnp.where(z < root_z, 1, 0), jnp.where(up_y, 2, 3))
        depth = jnp.abs(z - root_z) + jnp.abs(y - root_y)
        return child, parent, depth

    def transfer(k, d, source):
        delta = jnp.where(d == 0, deltas[0], jnp.where(d == 1, deltas[1], deltas[2]))
        there = jnp.where(d == 2, 2, 1 - d)
        return pltpu.make_async_remote_copy(
            src_ref=buf.at[source, k],
            dst_ref=buf.at[there, k],
            send_sem=send.at[d, k],
            recv_sem=recv.at[there, k],
            device_id=(me + delta, section),
            device_id_type=mesh_id,
        )

    def arrived(k, d):
        pltpu.make_async_remote_copy(
            src_ref=buf.at[3, k],
            dst_ref=buf.at[d, k],
            send_sem=send.at[0, k],
            recv_sem=recv.at[d, k],
            device_id=(me, section),
            device_id_type=mesh_id,
        ).wait_recv()

    def result(k, source):
        return pltpu.make_async_copy(buf.at[source, k], out_ref.at[k], out_sem.at[k])

    def product(k):
        kk = k - 1
        in_d = kk < n_d[0] * n_d[1]
        ku = kk - n_d[0] * n_d[1]
        in_u = ku < n_u[0] * n_u[1]
        ko = ku - n_u[0] * n_u[1]
        in_o = ko < n_o[0] * n_o[1]
        kq = ko - n_o[0] * n_o[1]
        a_at = jnp.where(
            in_d,
            n_q[0] + n_o[0] + n_u[0] + kk // n_d[1],
            jnp.where(
                in_u,
                n_q[0] + n_o[0] + ku // n_u[1],
                jnp.where(in_o, n_q[0] + ko // n_o[1], kq // n_q[1]),
            ),
        )
        b_at = jnp.where(
            in_d,
            n_q[1] + n_o[1] + n_u[1] + kk % n_d[1],
            jnp.where(
                in_u,
                n_q[1] + n_o[1] + ku % n_u[1],
                jnp.where(in_o, n_q[1] + ko % n_o[1], kq % n_q[1]),
            ),
        )
        left = a_ref[:, pl.ds(pl.multiple_of(a_at * BLOCK, BLOCK), BLOCK)]
        right = b_ref[:, pl.ds(pl.multiple_of(b_at * side, BLOCK), side)]
        total[...] = lax.dot_general(
            left, right, (((0,), (0,)), ((), ())), preferred_element_type=F32
        )

    def climb(k, level):
        child, parent, depth = roles(k)

        @pl.when((k >= 0) & (k < chunks) & (depth == DEPTH - level))
        def _():
            @pl.when(k == 0)
            def _():
                total[...] = small_ref[...]

            @pl.when(k > 0)
            def _():
                product(k)

            if level > 0:
                for d in range(3):

                    @pl.when(child[d])
                    def _():
                        arrived(k, d)
                        total[...] += buf[d, k].astype(F32)

            buf[3, k] = total[...].astype(BF)
            if level < DEPTH:
                transfer(k, parent, 3).start()
            else:
                for d in range(3):

                    @pl.when(child[d])
                    def _():
                        transfer(k, d, 3).start()

                result(k, 3).start()

    def descend(k, level):
        child, parent, depth = roles(k)

        @pl.when((k >= 0) & (k < chunks) & (depth == level))
        def _():
            arrived(k, parent)
            for d in range(3):

                @pl.when(child[d])
                def _():
                    transfer(k, d, parent).start()

            result(k, parent).start()

    def settle(k):
        child, parent, depth = roles(k)
        for d in range(3):

            @pl.when(child[d] | (parent == d))
            def _():
                transfer(k, d, 3).wait_send()

        result(k, 3).wait()

    def loop(low, high, body):
        def step(k, carry):
            body(k)
            return carry

        lax.fori_loop(low, high, step, 0)

    def advance(t):
        for level in range(DEPTH + 1):
            climb(t - level * HOP, level)
        for level in range(1, DEPTH + 1):
            descend(t - (DEPTH + level) * HOP, level)

    def handed(step):
        return pltpu.make_async_remote_copy(
            src_ref=gathered.at[0],
            dst_ref=gathered.at[step],
            send_sem=g_send.at[step],
            recv_sem=g_recv.at[step],
            device_id=(me, (section + n_sections - step) % n_sections),
            device_id_type=mesh_id,
        )

    last = 2 * DEPTH * HOP
    loop(0, last + HOP, advance)
    mine = roles(0)[1]
    rows = gathered.shape[1]
    gathered[0] = buf[mine, 0, :rows]
    for step in range(1, n_sections):
        handed(step).start()
    loop(last + HOP, chunks + last, advance)
    for step in range(1, n_sections):
        handed(step).wait()
    to_out = pltpu.make_async_copy(gathered, gathered_ref, g_out)
    to_out.start()
    loop(0, chunks, settle)
    to_out.wait()


def reduced(a, b, small, counts, side):
    chunks = 1 + sum(rows * columns for rows, columns in counts)
    n_sections = lax.axis_size("section")
    kept = 32
    any_space = pl.BlockSpec(memory_space=pl.ANY)
    in_vmem = pl.BlockSpec(memory_space=pltpu.VMEM)
    flops = 2 * a.shape[0] * BLOCK * side * chunks
    return pl.pallas_call(
        functools.partial(reduce_kernel, counts),
        out_shape=(
            jax.ShapeDtypeStruct((chunks, BLOCK, side), BF),
            jax.ShapeDtypeStruct((n_sections, kept, side), BF),
        ),
        in_specs=[in_vmem] * 3,
        out_specs=(any_space, any_space),
        scratch_shapes=[
            pltpu.VMEM((4, chunks, BLOCK, side), BF),
            pltpu.VMEM((BLOCK, side), F32),
            pltpu.VMEM((n_sections, kept, side), BF),
            pltpu.SemaphoreType.DMA((3, chunks)),
            pltpu.SemaphoreType.DMA((3, chunks)),
            pltpu.SemaphoreType.DMA((chunks,)),
            pltpu.SemaphoreType.DMA((n_sections,)),
            pltpu.SemaphoreType.DMA((n_sections,)),
            pltpu.SemaphoreType.DMA,
        ],
        compiler_params=pltpu.CompilerParams(
            collective_id=0, has_side_effects=True, vmem_limit_bytes=60 << 20
        ),
        cost_estimate=pl.CostEstimate(
            flops=flops, bytes_accessed=400 << 20, transcendentals=0
        ),
        name="gradient_sums",
    )(a, b, small)


def on_device(
    word_embed, boxes, mask_pos, replace_ids, cotangent, layout_table, vocab_table, embed_gain,
    embed_shift, qkv_weight, qv_bias, out_weight, up_weight, up_bias, down_weight, layer_gains,
    layer_biases,
):
    section = lax.axis_index("section")
    layer = section // 2
    half = section % 2
    is_first = layer == 0
    quarter, width = word_embed.shape
    page = 2 * quarter
    side = qkv_weight.shape[2] // 3

    words_a = routed(word_embed, [(1, 0), (2, 1)])
    words_b = routed(word_embed, [(3, 1)])
    given_a = routed(cotangent, [(0, 2), (2, 3)])
    given_b = routed(cotangent, [(1, 2)])
    words = jnp.concatenate(
        [jnp.where(half == 0, word_embed, words_a), jnp.where(half == 0, words_a, words_b)], 0
    )
    given = jnp.concatenate(
        [given_a, jnp.where(half == 0, given_b, cotangent)], 0
    ).astype(F32)

    qkv_other, out_other, up_other, down_other, qvb_other, upb_other = (
        swapped(array[0])
        for array in (qkv_weight, out_weight, up_weight, down_weight, qv_bias, up_bias)
    )
    qkv_own = qkv_weight[0]
    weights = (
        jnp.concatenate([qkv_own[:, :side], qkv_other[:, :side]], 1),
        jnp.concatenate([qkv_own[:, side : 2 * side], qkv_other[:, side : 2 * side]], 1),
        jnp.concatenate([qkv_own[:, 2 * side :], qkv_other[:, 2 * side :]], 1),
        jnp.concatenate([qv_bias[0, 0], qvb_other[0]]),
        jnp.concatenate([qv_bias[0, 1], qvb_other[1]]),
        jnp.concatenate([out_weight[0], out_other], 0),
        jnp.concatenate([up_weight[0], up_other], 1),
        jnp.concatenate([up_bias[0], upb_other]),
        jnp.concatenate([down_weight[0], down_other], 0),
        lax.dynamic_index_in_dim(layer_gains, layer, 0, keepdims=False),
        lax.dynamic_index_in_dim(layer_biases, layer, 0, keepdims=False),
    )

    listed = lax.dynamic_index_in_dim(mask_pos, half, 0, keepdims=False)
    ids = lax.dynamic_index_in_dim(replace_ids, half, 0, keepdims=False)
    slots = ids.shape[0]
    rows_held = vocab_table.shape[0]
    asked = lax.all_gather(ids, "dp", axis=0, tiled=True)
    held = jnp.arange(rows_held, dtype=jnp.int32) + lax.axis_index("dp") * rows_held
    picked = (asked[:, None] == held[None, :]).astype(BF)
    slot_rows = lax.psum_scatter(
        matmul(picked, vocab_table).astype(BF), "dp", scatter_dimension=0, tiled=True
    )

    places = jnp.arange(page, dtype=jnp.int32)
    chosen = (listed[:, None] == places[None, :]).astype(BF)
    marked = jnp.any(listed[:, None] == places[None, :], axis=0)
    replaced = matmul_left_t(chosen, slot_rows)
    box_rows = lax.dynamic_slice_in_dim(boxes, half * page, page, 1)
    coords = jnp.arange(layout_table.shape[1], dtype=jnp.int32)
    one_x, one_y = (
        (box_rows[a][:, None] == coords[None, :]).astype(BF)
        + (box_rows[a + 2][:, None] == coords[None, :]).astype(BF)
        for a in (0, 1)
    )
    summed = (
        jnp.where(marked[:, None], replaced, words.astype(F32))
        + matmul(one_x, layout_table[0])
        + matmul(one_y, layout_table[1])
    )
    hidden_in, normed_in, inverse_in = normalize(summed, embed_gain, embed_shift)

    first_out, unused_kept = layer_forward(hidden_in, weights)
    second_in = routed(first_out.astype(BF), [(0, 2), (1, 3)])
    rows = jnp.where(is_first, hidden_in, second_in.astype(F32))
    output, kept = layer_forward(rows, weights)
    second_grad = layer_backward(kept, given, weights)[0]
    first_grad = routed(second_grad.astype(BF), [(2, 0), (3, 1)])
    grad_out = jnp.where(is_first, first_grad.astype(F32), given)
    grad_rows, whole, split, gains_grad, shifts_grad = layer_backward(kept, grad_out, weights)

    grad_summed, eg_grad, es_grad = normalize_back(grad_rows, normed_in, inverse_in, embed_gain)
    grad_low = jnp.where(is_first, grad_summed, 0.0).astype(BF)
    word_grad = jnp.where(marked[:, None], 0.0, grad_low.astype(F32))
    slot_grad = matmul(chosen, grad_low).astype(BF)
    table_grad = jnp.stack([matmul_left_t(one_x, grad_low), matmul_left_t(one_y, grad_low)])
    table_part = lax.psum_scatter(
        table_grad.astype(BF), ("dp", "section"), scatter_dimension=1, tiled=True
    ).astype(F32)

    mine = jnp.where(
        is_first,
        slot_grad[: slots // 2],
        routed(slot_grad[slots // 2 :], [(0, 2), (1, 3)]),
    )
    my_ids = jnp.where(is_first, ids[: slots // 2], ids[slots // 2 :])
    all_rows = lax.all_gather(mine, ("dp", "section"), axis=0, tiled=True)
    all_ids = lax.all_gather(my_ids, ("dp", "section"), axis=0, tiled=True)
    count = rows_held // lax.axis_size("section")
    base = (lax.axis_index("dp") * lax.axis_size("section") + section) * count
    rows_here = jnp.arange(count, dtype=jnp.int32) + base
    vocab_part = matmul((rows_here[:, None] == all_ids[None, :]).astype(BF), all_rows)

    def both(array, columns):
        return jnp.concatenate([array[:, :columns], swapped(array[:, columns:])], 0)

    rows_low, grad_attended, hidden_low, grad_mixed = (
        jnp.concatenate([array, swapped(array)], 0) for array in whole
    )
    grad_q, grad_k, grad_v, context, grad_upper, active = (
        both(array, array.shape[1] // 2) for array in split
    )
    left = jnp.concatenate([rows_low, context, hidden_low, active], 1)
    right = jnp.concatenate([grad_q, grad_k, grad_v, grad_attended, grad_upper, grad_mixed], 1)
    hidden_units = grad_upper.shape[1]
    counts = (
        (width // BLOCK, 3),
        (side // BLOCK, width // side),
        (width // BLOCK, hidden_units // side),
        (hidden_units // BLOCK, width // side),
    )
    flat = jnp.concatenate(
        [
            jnp.sum(grad_q.astype(F32), 0), jnp.sum(grad_v.astype(F32), 0),
            jnp.sum(grad_upper.astype(F32), 0), gains_grad.reshape(-1), shifts_grad.reshape(-1),
            eg_grad, es_grad,
        ]
    ).reshape(-1, side)
    small_in = jnp.pad(flat, ((0, BLOCK - flat.shape[0]), (0, 0)))
    chunked, gathered = reduced(left, right, small_in, counts, side)
    outer = lax.axis_size("dp") // GROUP
    if outer > 1:
        groups = [[i + GROUP * g for g in range(outer)] for i in range(GROUP)]
        chunked, gathered = lax.psum((chunked, gathered), "dp", axis_index_groups=groups)
    chunked = chunked[1:]

    def laid(start, count):
        rows_of, columns_of = count
        part = chunked[start : start + rows_of * columns_of].astype(F32)
        part = part.reshape(rows_of, columns_of, BLOCK, side).transpose(0, 2, 1, 3)
        return part.reshape(1, rows_of * BLOCK, columns_of * side)

    n_q, n_o, n_u, n_d = (rows_of * columns_of for rows_of, columns_of in counts)
    sums = (
        laid(n_d + n_u + n_o, counts[0]), laid(n_d + n_u, counts[1]), laid(n_d, counts[2]),
        laid(0, counts[3]),
    )
    parts = gathered.astype(F32)[:, : flat.shape[0]].reshape(4, -1)
    own = parts[0]
    in_order = jnp.stack(
        [parts[0] + parts[jnp.where(half == 0, 1, 3)], parts[2] + parts[jnp.where(half == 0, 3, 1)]]
    )
    low_edge = 2 * side + hidden_units
    by_layer = jnp.where(layer == 0, in_order, in_order[::-1])[:, low_edge:]
    small = (
        by_layer[:, : 2 * width].reshape(2, 2, width),
        by_layer[:, 2 * width : 6 * width].reshape(2, 4, width),
        by_layer[0, 6 * width : 7 * width],
        by_layer[0, 7 * width :],
        own[: 2 * side].reshape(1, 2, side),
        own[2 * side : low_edge].reshape(1, hidden_units),
    )

    out_first = output[:quarter].astype(BF)
    out_second = output[quarter:].astype(BF)
    act_a = routed(out_first, [(2, 0), (3, 2)])
    act_b = routed(out_second, [(2, 1)])
    grad_first = word_grad[:quarter].astype(BF)
    grad_second = word_grad[quarter:].astype(BF)
    ing_a = routed(grad_second, [(0, 1), (1, 3)])
    ing_b = routed(grad_first, [(1, 2)])
    activations = jnp.where(
        section == 3,
        output[quarter:],
        jnp.where(section == 1, act_b, act_a).astype(F32),
    )
    input_grad = jnp.where(
        section == 0,
        word_grad[:quarter],
        jnp.where(section == 2, ing_b, ing_a).astype(F32),
    )
    return (
        activations, input_grad, table_part, vocab_part, small[2], small[3],
        sums[0],
        small[4],
        sums[1], sums[2],
        small[5],
        sums[3], small[0], small[1],
    )


def solution(mesh):
    both = ("dp", "section")
    by_section = P("section", None, None)
    return jax.shard_map(
        on_device,
        mesh=mesh,
        in_specs=(
            P(both, None), P(None, "dp"), P("dp", None), P("dp", None), P(both, None), P(),
            P("dp", None), P(), P(), by_section, by_section, by_section, by_section,
            P("section", None), by_section, P(), P(),
        ),
        out_specs=(
            P(both, None), P(both, None), P(None, both, None), P(both, None), P(), P(),
            by_section, by_section, by_section, by_section, P("section", None), by_section,
            P(), P(),
        ),
        check_vma=False,
    )
```

```python
import functools

import jax
import jax.numpy as jnp
from jax import lax
from jax.experimental import pallas as pl
from jax.experimental.pallas import tpu as pltpu
from jax.sharding import PartitionSpec as P

HEAD_DIM = 64
EPS = 1e-12
ROOT_HALF = 0.7071067811865476
INV_ROOT_TWO_PI = 0.3989422804014327
BF = jnp.bfloat16
F32 = jnp.float32


def routed(block, route):
    return lax.ppermute(block, "section", route)


SWAP = [(0, 1), (1, 0), (2, 3), (3, 2)]


def swapped(block):
    return routed(block, SWAP)


def normalize(values, gain, shift):
    center = values - jnp.mean(values, -1, keepdims=True)
    spread = jnp.mean(center * center, -1, keepdims=True)
    inverse = lax.rsqrt(spread + EPS)
    normed = center * inverse
    return (normed * gain + shift, normed, inverse)


def normalize_back(grad, normed, inverse, gain):
    scaled = grad * gain
    centered = (
        scaled
        - jnp.mean(scaled, -1, keepdims=True)
        - normed * jnp.mean(scaled * normed, -1, keepdims=True)
    )
    return (inverse * centered, jnp.sum(grad * normed, 0), jnp.sum(grad, 0))


def matmul(left, right):
    return jnp.dot(left, right, preferred_element_type=F32)


def matmul_left_t(left, right):
    return jnp.einsum("pa,pb->ab", left, right, preferred_element_type=F32)


GROUP = 8
BLOCK = 128
HOP = 4
DEPTH = 3
EXTRA = 20


def tree_of(k):
    turn = k % 8
    return turn < 4, 1 + turn % 2, (turn // 2) % 2


def rooted_at(c):
    return (c // 2) % 2 == 0, c // 2, c % 2


def loop(low, high, body):
    def step(k, carry):
        body(k)
        return carry

    lax.fori_loop(low, high, step, 0)


def reduce_kernel(
    counts, a_ref, b_ref, small_ref, edge_ref, box_ref, listed_ref,
    q_ref, o_ref, u_ref, d_ref, gathered_ref, rows_ref, table_ref,
    buf, total, gathered, edge, rows, table, piece,
    send, recv, out_sem, g_send, g_recv, e_send, e_recv, r_send, r_recv, t_send, t_recv,
    f_send, f_recv, last_sem,
):
    me = lax.axis_index("dp")
    section = lax.axis_index("section")
    n_sections = lax.axis_size("section")
    layer = section // 2
    half = section % 2
    other_core = section + 1 - 2 * half
    other_layer = (section + 2) % n_sections
    place = me % GROUP
    z = place // 2
    y = place % 2
    chunks = buf.shape[1]
    side = buf.shape[3]
    slots = rows.shape[2]
    n_q, n_o, n_u, n_d = counts
    ends = (n_d[0] * n_d[1],)
    ends += (ends[0] + n_u[0] * n_u[1],)
    ends += (ends[1] + n_o[0] * n_o[1],)
    mesh_id = pl.DeviceIdType.MESH
    deltas = (-2, 2, 1 - 2 * y)
    exists = (z > 0, z < GROUP // 2 - 1, y >= 0)

    barrier = pltpu.get_barrier_semaphore()
    for d in range(3):

        @pl.when(exists[d])
        def _():
            pl.semaphore_signal(
                barrier, inc=1, device_id=(me + deltas[d], section), device_id_type=mesh_id
            )

    for step in range(1, n_sections):
        pl.semaphore_signal(
            barrier, inc=1, device_id=(me, (section + step) % n_sections), device_id_type=mesh_id
        )
    pl.semaphore_wait(
        barrier,
        n_sections + jnp.where(exists[0], 1, 0) + jnp.where(exists[1], 1, 0),
    )

    def remote(source, target, sent, got, device):
        return pltpu.make_async_remote_copy(
            src_ref=source, dst_ref=target, send_sem=sent, recv_sem=got, device_id=device,
            device_id_type=mesh_id,
        )

    def edge_across():
        return remote(
            edge_ref.at[1], edge.at[0], e_send.at[0], e_recv.at[0], (me, other_layer)
        )

    def edge_beside(source):
        return remote(source, edge.at[1], e_send.at[1], e_recv.at[1], (me, other_core))

    @pl.when(layer == 0)
    def _():
        edge_across().start()
        edge_beside(edge_ref.at[0]).start()
        edge[0] = edge_ref[0]

    def roles(tree):
        comb, root_z, root_y = tree
        along = jnp.logical_or(jnp.logical_not(comb), y == root_y)
        across = jnp.logical_or(comb, z == root_z)
        child = (
            exists[0] & along & (z <= root_z),
            exists[1] & along & (z >= root_z),
            across & (y == root_y),
        )
        up_z = along & (z != root_z)
        up_y = across & (y != root_y)
        parent = jnp.where(up_z, jnp.where(z < root_z, 1, 0), jnp.where(up_y, 2, 3))
        depth = jnp.abs(z - root_z) + jnp.abs(y - root_y)
        return child, parent, depth

    def neighbour(d):
        return me + jnp.where(d == 0, deltas[0], jnp.where(d == 1, deltas[1], deltas[2]))

    def facing(d):
        return jnp.where(d == 2, 2, 1 - d)

    def transfer(k, d, source):
        there = facing(d)
        return remote(
            buf.at[source, k], buf.at[there, k], send.at[d, k], recv.at[there, k],
            (neighbour(d), section),
        )

    def arrived(k, d):
        remote(
            buf.at[3, k], buf.at[d, k], send.at[0, k], recv.at[d, k], (me, other_core)
        ).wait_recv()

    def put(k, source):
        kk = k - 1
        low = 0
        for target, count, high in (
            (d_ref, n_d, ends[0]), (u_ref, n_u, ends[1]), (o_ref, n_o, ends[2]),
            (q_ref, n_q, chunks - 1),
        ):

            @pl.when((kk >= low) & (kk < high))
            def _():
                at = kk - low
                pltpu.make_async_copy(
                    buf.at[source, k],
                    target.at[
                        pl.ds(pl.multiple_of(at // count[1] * BLOCK, BLOCK), BLOCK),
                        pl.ds(pl.multiple_of(at % count[1] * side, BLOCK), side),
                    ],
                    out_sem.at[k],
                ).start()

            low = high

    def product(k):
        kd = k - 1
        in_d = kd < ends[0]
        ku = kd - ends[0]
        in_u = kd < ends[1]
        ko = kd - ends[1]
        in_o = kd < ends[2]
        kq = kd - ends[2]
        a_at = jnp.where(
            in_d,
            n_q[0] + n_o[0] + n_u[0] + kd // n_d[1],
            jnp.where(
                in_u,
                n_q[0] + n_o[0] + ku // n_u[1],
                jnp.where(in_o, n_q[0] + ko // n_o[1], kq // n_q[1]),
            ),
        )
        b_at = jnp.where(
            in_d,
            n_q[1] + n_o[1] + n_u[1] + kd % n_d[1],
            jnp.where(
                in_u,
                n_q[1] + n_o[1] + ku % n_u[1],
                jnp.where(in_o, n_q[1] + ko % n_o[1], kq % n_q[1]),
            ),
        )
        left = a_ref[:, pl.ds(pl.multiple_of(a_at * BLOCK, BLOCK), BLOCK)]
        right = b_ref[:, pl.ds(pl.multiple_of(b_at * side, BLOCK), side)]
        total[...] = lax.dot_general(
            left, right, (((0,), (0,)), ((), ())), preferred_element_type=F32
        )

    def climb(k, level):
        child, parent, depth = roles(tree_of(k))

        @pl.when((k >= 0) & (k < chunks) & (depth == DEPTH - level))
        def _():
            @pl.when(k == 0)
            def _():
                total[...] = small_ref[...]

            @pl.when(k > 0)
            def _():
                product(k)

            if level > 0:
                for d in range(3):

                    @pl.when(child[d])
                    def _():
                        arrived(k, d)
                        total[...] += buf[d, k].astype(F32)

            buf[3, k] = total[...].astype(BF)
            if level < DEPTH:
                transfer(k, parent, 3).start()
            else:
                for d in range(3):

                    @pl.when(child[d])
                    def _():
                        transfer(k, d, 3).start()

                put(k, 3)

    def descend(k, level):
        child, parent, depth = roles(tree_of(k))

        @pl.when((k >= 0) & (k < chunks) & (depth == level))
        def _():
            arrived(k, parent)
            for d in range(3):

                @pl.when(child[d])
                def _():
                    transfer(k, d, parent).start()

            put(k, parent)

    def settle(k):
        child, parent, depth = roles(tree_of(k))
        for d in range(3):

            @pl.when(child[d] | (parent == d))
            def _():
                transfer(k, d, 3).wait_send()

        @pl.when(k > 0)
        def _():
            pltpu.make_async_copy(
                buf.at[3, k], d_ref.at[pl.ds(0, BLOCK), pl.ds(0, side)], out_sem.at[k]
            ).wait()

    def advance(t):
        for level in range(DEPTH + 1):
            climb(t - level * HOP, level)
        for level in range(1, DEPTH + 1):
            descend(t - (DEPTH + level) * HOP, level)

    def slots_down(c, d):
        return remote(
            rows.at[0, c], rows.at[0, c], r_send.at[d, c], r_recv.at[0, c],
            (neighbour(d), section),
        )

    def slots_across(c):
        return remote(
            rows.at[0, c], rows.at[1, c], r_send.at[3, c], r_recv.at[1, c], (me, other_layer)
        )

    def slots_beside(c, kind):
        return remote(
            rows.at[kind, c], rows.at[2 + kind, c], r_send.at[4 + kind, c],
            r_recv.at[2 + kind, c], (me, other_core),
        )

    def slots_got(c, kind):
        remote(
            rows.at[kind, c], rows.at[kind, c], r_send.at[0, c], r_recv.at[kind, c],
            (me, other_core),
        ).wait_recv()

    def share_slots(c, level):
        child, parent, depth = roles(rooted_at(c))

        @pl.when((c >= 0) & (c < GROUP) & (depth == level))
        def _():
            if level > 0:
                slots_got(c, 0)
            for d in range(3):

                @pl.when(child[d])
                def _():
                    slots_down(c, d).start()

            slots_across(c).start()
            slots_beside(c, 0).start()

    def relay_slots(c):
        @pl.when((c >= 0) & (c < GROUP))
        def _():
            slots_got(c, 1)
            slots_beside(c, 1).start()

    def table_up(c, d):
        there = facing(d)
        return remote(
            piece.at[3, c], piece.at[there, c], t_send.at[d, c], t_recv.at[there, c],
            (neighbour(d), section),
        )

    def table_out(c, step):
        to = (section + step) % n_sections
        return remote(
            piece.at[3, c, pl.ds(to * table.shape[1], table.shape[1])], table.at[section],
            f_send.at[step], f_recv.at[section], (me, to),
        )

    def table_climb(c, level):
        child, parent, depth = roles(rooted_at(c))

        @pl.when((c >= 0) & (c < GROUP) & (depth == DEPTH + 1 - level))
        def _():
            at = c * BLOCK + lax.broadcasted_iota(jnp.int32, (BLOCK, edge.shape[1]), 0)
            for part in range(2):
                spots = box_ref[part]
                ones = (at == spots[0:1]).astype(F32) + (at == spots[1:2]).astype(F32)
                term = jnp.dot(ones.astype(BF), edge[part], preferred_element_type=F32)
                if part == 0:
                    total[...] = term
                else:
                    total[...] += term
            if level > 0:
                for d in range(3):

                    @pl.when(child[d])
                    def _():
                        remote(
                            piece.at[3, c], piece.at[d, c], t_send.at[0, c], t_recv.at[d, c],
                            (me, other_core),
                        ).wait_recv()
                        total[...] += piece[d, c].astype(F32)

            piece[3, c] = total[...].astype(BF)
            if level < DEPTH + 1:
                table_up(c, parent).start()
            else:
                for step in range(1, n_sections):
                    table_out(c, step).start()
                kept = table.shape[1]
                table[section] = piece[3, c, pl.ds(pl.multiple_of(section * kept, kept), kept)]

    def extras(t):
        c = t - EXTRA
        for level in range(DEPTH + 2):
            share_slots(c - level * HOP, level)
        relay_slots(c - (DEPTH + 3) * HOP)
        for level in range(DEPTH + 2):
            table_climb(c - GROUP - level * HOP, level)

    def settle_extras(c):
        child, parent, depth = roles(rooted_at(c))
        for d in range(3):

            @pl.when(child[d])
            def _():
                slots_down(c, d).wait_send()

            @pl.when(parent == d)
            def _():
                table_up(c, d).wait_send()

        slots_across(c).wait_send()
        for kind in range(2):
            slots_beside(c, kind).wait_send()
            slots_got(c, 2 + kind)

    def handed(step):
        return remote(
            gathered.at[0], gathered.at[step], g_send.at[step], g_recv.at[step],
            (me, (section + n_sections - step) % n_sections),
        )

    loop(0, EXTRA, advance)

    @pl.when(layer == 1)
    def _():
        edge_across().wait_recv()
        edge_beside(edge.at[0]).start()

    edge_beside(edge.at[0]).wait_recv()
    wanted = listed_ref[...] == lax.broadcasted_iota(jnp.int32, (slots, edge.shape[1]), 1)
    rows[0, place] = jnp.dot(
        wanted.astype(F32).astype(BF), edge[0], preferred_element_type=F32
    ).astype(BF)

    def both(t):
        advance(t)
        extras(t)

    middle = EXTRA + 2 * GROUP + (DEPTH + 3) * HOP
    loop(EXTRA, middle, both)
    mine = roles(tree_of(0))[1]
    kept_small = gathered.shape[1]
    gathered[0] = buf[mine, 0, :kept_small]
    for step in range(1, n_sections):
        handed(step).start()
    loop(middle, chunks + 2 * DEPTH * HOP, advance)
    loop(0, GROUP, settle_extras)
    for step in range(1, n_sections):
        handed(step).wait()
        table_out(place, step).wait_send()
        source = (section + n_sections - step) % n_sections
        remote(
            piece.at[3, 0, pl.ds(0, table.shape[1])], table.at[source], f_send.at[0],
            f_recv.at[source], (me, other_core),
        ).wait_recv()
    outs = (
        pltpu.make_async_copy(gathered, gathered_ref, last_sem.at[0]),
        pltpu.make_async_copy(rows, rows_ref, last_sem.at[1]),
        pltpu.make_async_copy(table, table_ref, last_sem.at[2]),
    )
    for copy in outs:
        copy.start()

    @pl.when(layer == 0)
    def _():
        edge_across().wait_send()

    edge_beside(edge.at[0]).wait_send()
    loop(0, chunks, settle)
    for copy in outs:
        copy.wait()


def reduced(a, b, small, edge, boxes, listed, counts, side):
    chunks = 1 + sum(count[0] * count[1] for count in counts)
    n_sections = lax.axis_size("section")
    kept = 32
    slots = listed.shape[0]
    page = edge.shape[1]
    any_space = pl.BlockSpec(memory_space=pl.ANY)
    in_vmem = pl.BlockSpec(memory_space=pltpu.VMEM)
    flops = 2 * a.shape[0] * BLOCK * side * chunks
    dma = pltpu.SemaphoreType.DMA
    return pl.pallas_call(
        functools.partial(reduce_kernel, counts),
        out_shape=tuple(
            jax.ShapeDtypeStruct((count[0] * BLOCK, count[1] * side), BF) for count in counts
        )
        + (
            jax.ShapeDtypeStruct((n_sections, kept, side), BF),
            jax.ShapeDtypeStruct((4, GROUP, slots, side), BF),
            jax.ShapeDtypeStruct((n_sections, BLOCK // n_sections, side), BF),
        ),
        in_specs=[in_vmem] * 6,
        out_specs=(any_space,) * 7,
        scratch_shapes=[
            pltpu.VMEM((4, chunks, BLOCK, side), BF),
            pltpu.VMEM((BLOCK, side), F32),
            pltpu.VMEM((n_sections, kept, side), BF),
            pltpu.VMEM((2, page, side), BF),
            pltpu.VMEM((4, GROUP, slots, side), BF),
            pltpu.VMEM((n_sections, BLOCK // n_sections, side), BF),
            pltpu.VMEM((4, GROUP, BLOCK, side), BF),
            dma((3, chunks)), dma((3, chunks)), dma((chunks,)),
            dma((n_sections,)), dma((n_sections,)),
            dma((2,)), dma((2,)),
            dma((6, GROUP)), dma((4, GROUP)),
            dma((3, GROUP)), dma((3, GROUP)),
            dma((n_sections,)), dma((n_sections,)),
            dma((3,)),
        ],
        compiler_params=pltpu.CompilerParams(
            collective_id=0, has_side_effects=True, vmem_limit_bytes=60 << 20
        ),
        cost_estimate=pl.CostEstimate(
            flops=flops, bytes_accessed=400 << 20, transcendentals=0
        ),
        name="gradient_sums",
    )(a, b, small, edge, boxes, listed)


ROWS = 256


def layer_kernel(
    x_ref, given_ref, q_own, o_own, u_own, d_own, qvb_ref, upb_ref, gains_ref, shifts_ref,
    a_ref, b_ref, y_ref, dx_ref, sums_ref, qvb_sum, upb_sum,
    wq, wo, wu, wd, wide, x_land, g_land, x_low, ctx, d_ctx, h_low, act, slope, qkv, d_qkv,
    da_low, df_low, probs, n_one, n_two, r_one, r_two, z, sent_low,
    w_local, w_send, w_recv, x_send, x_recv, g_send, g_recv, p_local, p_send, p_recv, io_sem,
):
    me = lax.axis_index("dp")
    section = lax.axis_index("section")
    n_sections = lax.axis_size("section")
    layer = section // 2
    half = section % 2
    beside = (me, section + 1 - 2 * half)
    across = (me, (section + 2) % n_sections)
    mesh_id = pl.DeviceIdType.MESH
    page, width = x_low.shape
    side = ctx.shape[2]
    units = act.shape[2]
    blocks = page // ROWS
    tile = 512
    scale = HEAD_DIM ** (-0.5)

    barrier = pltpu.get_barrier_semaphore()
    for device in (beside, across):
        pl.semaphore_signal(barrier, inc=1, device_id=device, device_id_type=mesh_id)
    pl.semaphore_wait(barrier, 2)

    def remote(source, target, sent, got, device):
        return pltpu.make_async_remote_copy(
            src_ref=source, dst_ref=target, send_sem=sent, recv_sem=got, device_id=device,
            device_id_type=mesh_id,
        )

    def weight_copies(i):
        source = (q_own, o_own, u_own, d_own)[i].at[0]
        target = (wq, wo, wu, wd)[i]
        return (
            pltpu.make_async_copy(source, target.at[0], w_local.at[i]),
            remote(source, target.at[1], w_send.at[i], w_recv.at[i], beside),
        )

    def weights_here(i):
        near, far = weight_copies(i)
        near.wait()
        far.wait_recv()

    x_copy = pltpu.make_async_copy(x_ref, wide, io_sem.at[0])
    given_copy = pltpu.make_async_copy(given_ref, g_land, io_sem.at[1])

    @pl.when(layer == 0)
    def _():
        x_copy.start()

    @pl.when(layer == 1)
    def _():
        given_copy.start()

    for i in range(4):
        near, far = weight_copies(i)
        far.start()
        near.start()

    def rows_of(block):
        return pl.ds(pl.multiple_of(block * ROWS, ROWS), ROWS)

    def x_move(block):
        rows = rows_of(block)
        return remote(
            sent_low.at[rows], x_land.at[rows], x_send.at[block], x_recv.at[block], across
        )

    def g_move(block):
        rows = rows_of(block)
        return remote(
            sent_low.at[rows], g_land.at[rows], g_send.at[block], g_recv.at[block], across
        )

    spans = (
        (a_ref, 0, width), (a_ref, width, side), (a_ref, width + side, width),
        (a_ref, 2 * width + side, units),
        (b_ref, 0, 3 * side), (b_ref, 3 * side, width), (b_ref, 3 * side + width, units),
        (b_ref, 3 * side + width + units, width),
    )

    def piece_copies(i):
        target, start, size = spans[i]
        source = (x_low, ctx, h_low, act, d_qkv, da_low, slope, df_low)[i]
        double = i in (1, 3, 4, 6)
        columns = pl.ds(start, size)
        return (
            pltpu.make_async_copy(
                source.at[0] if double else source, target.at[0, :, columns], p_local.at[i]
            ),
            remote(
                source.at[1] if double else source, target.at[1, :, columns], p_send.at[i],
                p_recv.at[i], beside,
            ),
        )

    def hand_out(*pieces):
        for i in pieces:
            near, far = piece_copies(i)
            far.start()
            near.start()

    def nt(left, right):
        return lax.dot_general(
            left, right, (((1,), (1,)), ((), ())), preferred_element_type=F32
        )

    def tn(left, right):
        return lax.dot_general(
            left, right, (((0,), (0,)), ((), ())), preferred_element_type=F32
        )

    def centred(values):
        center = values - jnp.mean(values, -1, keepdims=True)
        spread = jnp.mean(center * center, -1, keepdims=True)
        inverse = lax.rsqrt(spread + EPS)
        return center * inverse, inverse

    def pulled(grad, normed, inverse, gain):
        scaled = grad * gain
        return inverse * (
            scaled
            - jnp.mean(scaled, -1, keepdims=True)
            - normed * jnp.mean(scaled * normed, -1, keepdims=True)
        )

    def add_sum(row, values):
        sums_ref[row : row + 1] += jnp.sum(values, 0, keepdims=True)

    sums_ref[...] = jnp.zeros_like(sums_ref)
    upb_sum[...] = jnp.zeros_like(upb_sum)

    weights_here(0)

    @pl.when(layer == 0)
    def _():
        x_copy.wait()

    def project(block):
        rows = rows_of(block)

        @pl.when(layer == 1)
        def _():
            x_move(block).wait_recv()
            wide[rows] = x_land[rows].astype(F32)

        low = wide[rows].astype(BF)
        x_low[rows] = low
        for slot in range(2):
            for c in range(3):
                part = pl.ds(c * side, side)
                value = jnp.dot(low, wq[slot, :, part], preferred_element_type=F32)
                if c != 1:
                    value = value + qvb_ref[slot, c // 2 : c // 2 + 1]
                qkv[slot, rows, part] = value.astype(BF)

    loop(0, blocks, project)
    hand_out(0)

    lane = lax.broadcasted_iota(jnp.int32, (1, 2 * HEAD_DIM), 1)
    masks = ((lane < HEAD_DIM).astype(F32).astype(BF), (lane >= HEAD_DIM).astype(F32).astype(BF))
    first_lane = lax.broadcasted_iota(jnp.int32, (page, 2 * HEAD_DIM), 1) < HEAD_DIM
    first_row = lax.broadcasted_iota(jnp.int32, (2 * HEAD_DIM, page), 0) < HEAD_DIM
    pairs = side // (2 * HEAD_DIM)

    def lanes(i, third):
        at = third * side + (i % pairs) * 2 * HEAD_DIM
        return pl.ds(pl.multiple_of(at, 2 * HEAD_DIM), 2 * HEAD_DIM)

    def attend(i):
        slot = i // pairs
        queries = qkv[slot, :, lanes(i, 0)] * jnp.asarray(scale, BF)
        keys = qkv[slot, :, lanes(i, 1)]
        values = qkv[slot, :, lanes(i, 2)]
        found = []
        for e in range(2):
            scores = nt(keys * masks[e], queries)
            expo = jnp.exp(scores - jnp.max(scores, 0, keepdims=True))
            share = 1.0 / jnp.sum(expo, 0, keepdims=True)
            low = (expo * share).astype(BF)
            probs[2 * i + e] = low
            found.append(tn(values, low))
        ctx[slot, :, lanes(i, 0)] = jnp.where(first_row, found[0], found[1]).T.astype(BF)

    loop(0, 2 * pairs, attend)
    hand_out(1)
    for i in range(1, 4):
        weights_here(i)

    def feed(block):
        rows = rows_of(block)
        attended = (
            jnp.dot(ctx[0, rows], wo[0], preferred_element_type=F32)
            + jnp.dot(ctx[1, rows], wo[1], preferred_element_type=F32)
            + shifts_ref[0:1]
        )
        normed, inverse = centred(wide[rows] + attended)
        n_one[rows] = normed
        r_one[rows] = inverse
        hidden = normed * gains_ref[0:1] + shifts_ref[1:2]
        z[rows] = hidden
        h_low[rows] = hidden.astype(BF)
        for slot in range(2):
            for c in range(units // tile):
                part = pl.ds(c * tile, tile)
                upper = (
                    jnp.dot(h_low[rows], wu[slot, :, part], preferred_element_type=F32)
                    + upb_ref[slot : slot + 1, part]
                )
                below = 0.5 * (1.0 + lax.erf(upper * ROOT_HALF))
                act[slot, rows, part] = (upper * below).astype(BF)
                slope[slot, rows, part] = (
                    below + upper * jnp.exp(-0.5 * upper * upper) * INV_ROOT_TWO_PI
                ).astype(BF)
        mixed = (
            jnp.dot(act[0, rows], wd[0], preferred_element_type=F32)
            + jnp.dot(act[1, rows], wd[1], preferred_element_type=F32)
            + shifts_ref[2:3]
        )
        normed, inverse = centred(z[rows] + mixed)
        n_two[rows] = normed
        r_two[rows] = inverse
        output = normed * gains_ref[1:2] + shifts_ref[3:4]
        wide[rows] = output

        @pl.when(layer == 0)
        def _():
            sent_low[rows] = output.astype(BF)
            x_move(block).start()

    loop(0, blocks, feed)
    y_copy = pltpu.make_async_copy(wide, y_ref, io_sem.at[2])
    y_copy.start()
    hand_out(2, 3)

    @pl.when(layer == 1)
    def _():
        given_copy.wait()

    def feed_back(block):
        rows = rows_of(block)

        @pl.when(layer == 0)
        def _():
            g_move(block).wait_recv()

        grad = g_land[rows].astype(F32)
        normed = n_two[rows]
        add_sum(1, grad * normed)
        add_sum(5, grad)
        grad = pulled(grad, normed, r_two[rows], gains_ref[1:2])
        z[rows] = grad
        low = grad.astype(BF)
        df_low[rows] = low
        add_sum(4, low.astype(F32))
        for slot in range(2):
            for c in range(units // tile):
                part = pl.ds(c * tile, tile)
                term = nt(df_low[rows], wd[slot, part])
                term = (term * slope[slot, rows, part].astype(F32)).astype(BF)
                slope[slot, rows, part] = term
                upb_sum[slot : slot + 1, part] += jnp.sum(term.astype(F32), 0, keepdims=True)
        grad = z[rows] + nt(slope[0, rows], wu[0]) + nt(slope[1, rows], wu[1])
        normed = n_one[rows]
        add_sum(0, grad * normed)
        add_sum(3, grad)
        grad = pulled(grad, normed, r_one[rows], gains_ref[0:1])
        z[rows] = grad
        low = grad.astype(BF)
        da_low[rows] = low
        add_sum(2, low.astype(F32))
        for slot in range(2):
            d_ctx[slot, rows] = nt(da_low[rows], wo[slot]).astype(BF)

    loop(0, blocks, feed_back)
    hand_out(5, 6, 7)

    def attend_back(i):
        slot = i // pairs
        queries = qkv[slot, :, lanes(i, 0)]
        keys = qkv[slot, :, lanes(i, 1)]
        values = qkv[slot, :, lanes(i, 2)]
        grads = d_ctx[slot, :, lanes(i, 0)]
        d_q, d_k, d_v = [], [], []
        for e in range(2):
            low = probs[2 * i + e]
            share = low.astype(F32)
            term = share * nt(values * masks[e], grads)
            term = (term - share * jnp.sum(term, 0, keepdims=True)).astype(BF)
            d_k.append(jnp.dot(term, queries, preferred_element_type=F32))
            d_v.append(jnp.dot(low, grads, preferred_element_type=F32))
            d_q.append(tn(keys, term))
        d_qkv[slot, :, lanes(i, 0)] = (
            jnp.where(first_row, d_q[0], d_q[1]).T * scale
        ).astype(BF)
        d_qkv[slot, :, lanes(i, 1)] = (jnp.where(first_lane, d_k[0], d_k[1]) * scale).astype(BF)
        d_qkv[slot, :, lanes(i, 2)] = jnp.where(first_lane, d_v[0], d_v[1]).astype(BF)

    loop(0, 2 * pairs, attend_back)
    hand_out(4)

    def leave(block):
        rows = rows_of(block)
        grad = z[rows] + nt(d_qkv[0, rows], wq[0]) + nt(d_qkv[1, rows], wq[1])
        z[rows] = grad

        @pl.when(layer == 1)
        def _():
            sent_low[rows] = grad.astype(BF)
            g_move(block).start()

    loop(0, blocks, leave)
    dx_copy = pltpu.make_async_copy(z, dx_ref, io_sem.at[3])
    dx_copy.start()
    for slot in range(2):
        for i in range(2):
            columns = pl.ds(2 * i * side, side)
            qvb_sum[slot, i : i + 1] = jnp.sum(
                d_qkv[slot, :, columns].astype(F32), 0, keepdims=True
            )
    for block in range(blocks):

        @pl.when(layer == 0)
        def _():
            x_move(block).wait_send()

        @pl.when(layer == 1)
        def _():
            g_move(block).wait_send()

    for i in range(4):
        weight_copies(i)[1].wait_send()
    for i in range(8):
        near, far = piece_copies(i)
        near.wait()
        far.wait()
    y_copy.wait()
    dx_copy.wait()


def layered(x, given, weights, qvb, upb, gains, shifts):
    page, width = x.shape
    qkv_weight, out_weight, up_weight, down_weight = weights
    side = out_weight.shape[1]
    units = down_weight.shape[1]
    blocks = page // ROWS
    heads = 2 * side // HEAD_DIM
    any_space = pl.BlockSpec(memory_space=pl.ANY)
    in_vmem = pl.BlockSpec(memory_space=pltpu.VMEM)
    dma = pltpu.SemaphoreType.DMA
    vmem = pltpu.VMEM
    flops = 8 * page * width * (4 * width + 4 * units) * 2
    return pl.pallas_call(
        layer_kernel,
        out_shape=(
            jax.ShapeDtypeStruct((2, page, 2 * width + side + units), BF),
            jax.ShapeDtypeStruct((2, page, 3 * side + 2 * width + units), BF),
            jax.ShapeDtypeStruct((page, width), F32),
            jax.ShapeDtypeStruct((page, width), F32),
            jax.ShapeDtypeStruct((6, width), F32),
            jax.ShapeDtypeStruct((2, 2, side), F32),
            jax.ShapeDtypeStruct((2, units), F32),
        ),
        in_specs=[any_space] * 6 + [in_vmem] * 4,
        out_specs=(any_space,) * 4 + (in_vmem,) * 3,
        scratch_shapes=[
            vmem((2, width, 3 * side), BF), vmem((2, side, width), BF),
            vmem((2, width, units), BF), vmem((2, units, width), BF),
            vmem((page, width), F32), vmem((page, width), BF), vmem((page, width), BF),
            vmem((page, width), BF), vmem((2, page, side), BF), vmem((2, page, side), BF),
            vmem((page, width), BF), vmem((2, page, units), BF), vmem((2, page, units), BF),
            vmem((2, page, 3 * side), BF), vmem((2, page, 3 * side), BF),
            vmem((page, width), BF), vmem((page, width), BF), vmem((heads, page, page), BF),
            vmem((page, width), F32), vmem((page, width), F32),
            vmem((page, 1), F32), vmem((page, 1), F32),
            vmem((page, width), F32), vmem((page, width), BF),
            dma((4,)), dma((4,)), dma((4,)),
            dma((blocks,)), dma((blocks,)), dma((blocks,)), dma((blocks,)),
            dma((8,)), dma((8,)), dma((8,)), dma((4,)),
        ],
        compiler_params=pltpu.CompilerParams(
            collective_id=1, has_side_effects=True, vmem_limit_bytes=62 << 20
        ),
        cost_estimate=pl.CostEstimate(
            flops=flops, bytes_accessed=200 << 20, transcendentals=0
        ),
        name="layer_both_ways",
    )(x, given, *weights, qvb, upb, gains, shifts)


def on_device(
    word_embed, boxes, mask_pos, replace_ids, cotangent, layout_table, vocab_table, embed_gain,
    embed_shift, qkv_weight, qv_bias, out_weight, up_weight, up_bias, down_weight, layer_gains,
    layer_biases,
):
    section = lax.axis_index("section")
    layer = section // 2
    half = section % 2
    is_first = layer == 0
    quarter, width = word_embed.shape
    page = 2 * quarter
    side = qkv_weight.shape[2] // 3

    words_a = routed(word_embed, [(1, 0), (2, 1)])
    words_b = routed(word_embed, [(3, 1)])
    given_a = routed(cotangent, [(0, 2), (2, 3)])
    given_b = routed(cotangent, [(1, 2)])
    words = jnp.concatenate(
        [jnp.where(half == 0, word_embed, words_a), jnp.where(half == 0, words_a, words_b)], 0
    )
    given = jnp.concatenate(
        [given_a, jnp.where(half == 0, given_b, cotangent)], 0
    )

    qvb = jnp.stack([qv_bias[0], swapped(qv_bias[0])])
    upb = jnp.concatenate([up_bias, swapped(up_bias)])
    gains = lax.dynamic_index_in_dim(layer_gains, layer, 0, keepdims=False)
    shifts = lax.dynamic_index_in_dim(layer_biases, layer, 0, keepdims=False)

    listed = lax.dynamic_index_in_dim(mask_pos, half, 0, keepdims=False)
    ids = lax.dynamic_index_in_dim(replace_ids, half, 0, keepdims=False)
    slots = ids.shape[0]
    rows_held = vocab_table.shape[0]
    asked = lax.all_gather(ids, "dp", axis=0, tiled=True)
    held = jnp.arange(rows_held, dtype=jnp.int32) + lax.axis_index("dp") * rows_held
    picked = (asked[:, None] == held[None, :]).astype(BF)
    slot_rows = lax.psum_scatter(
        matmul(picked, vocab_table).astype(BF), "dp", scatter_dimension=0, tiled=True
    )

    places = jnp.arange(page, dtype=jnp.int32)
    chosen = (listed[:, None] == places[None, :]).astype(BF)
    marked = jnp.any(listed[:, None] == places[None, :], axis=0)
    replaced = matmul_left_t(chosen, slot_rows)
    box_rows = lax.dynamic_slice_in_dim(boxes, half * page, page, 1)
    coords = jnp.arange(layout_table.shape[1], dtype=jnp.int32)
    one_x, one_y = (
        (box_rows[a][:, None] == coords[None, :]).astype(BF)
        + (box_rows[a + 2][:, None] == coords[None, :]).astype(BF)
        for a in (0, 1)
    )
    summed = (
        jnp.where(marked[:, None], replaced, words.astype(F32))
        + matmul(one_x, layout_table[0])
        + matmul(one_y, layout_table[1])
    )
    hidden_in, normed_in, inverse_in = normalize(summed, embed_gain, embed_shift)

    left, right, output, grad_rows, sums_grad, qvb_grad, upb_grad = layered(
        hidden_in, given, (qkv_weight, out_weight, up_weight, down_weight), qvb, upb, gains, shifts
    )

    grad_summed, eg_grad, es_grad = normalize_back(grad_rows, normed_in, inverse_in, embed_gain)
    grad_low = jnp.where(is_first, grad_summed, 0.0).astype(BF)
    word_grad = jnp.where(marked[:, None], 0.0, grad_low.astype(F32))
    left, right = (array.reshape(2 * page, -1) for array in (left, right))
    hidden_units = up_bias.shape[1]
    counts = (
        (width // BLOCK, 3),
        (side // BLOCK, width // side),
        (width // BLOCK, hidden_units // side),
        (hidden_units // BLOCK, width // side),
    )
    flat = jnp.concatenate(
        [
            qvb_grad[0].reshape(-1), upb_grad[0], qvb_grad[1].reshape(-1), upb_grad[1],
            sums_grad.reshape(-1), eg_grad, es_grad,
        ]
    ).reshape(-1, side)
    small_in = jnp.pad(flat, ((0, BLOCK - flat.shape[0]), (0, 0)))
    edge = jnp.stack([grad_low[:, :side], grad_low[:, side:]])
    first, second = boxes[:, :page], boxes[:, page:]
    pair = jnp.stack([jnp.where(half == 0, first, second), jnp.where(half == 0, second, first)])
    pair = jnp.where(half == 0, pair[:, 0::2], pair[:, 1::2])
    *sums, gathered, slot_rows_all, table_rows = reduced(
        left, right, small_in, edge, pair, listed[:, None], counts, side
    )
    outer = lax.axis_size("dp") // GROUP
    if outer > 1:
        groups = [[i + GROUP * g for g in range(outer)] for i in range(GROUP)]
        *sums, gathered = lax.psum((*sums, gathered), "dp", axis_index_groups=groups)
        slot_rows_all = lax.all_gather(
            slot_rows_all, "dp", axis_index_groups=groups, axis=1, tiled=True
        )
        table_grad = jnp.stack([matmul_left_t(one_x, grad_low), matmul_left_t(one_y, grad_low)])
        table_part = lax.psum_scatter(
            table_grad.astype(BF), ("dp", "section"), scatter_dimension=1, tiled=True
        ).astype(F32)
    else:
        table_part = (
            table_rows.reshape(2, 2, -1, side).transpose(1, 2, 0, 3).reshape(2, -1, width)
        ).astype(F32)
    sums = [total.astype(F32)[None] for total in sums]

    other_asked = swapped(asked)
    count = rows_held // lax.axis_size("section")
    base = (lax.axis_index("dp") * lax.axis_size("section") + section) * count
    rows_here = jnp.arange(count, dtype=jnp.int32) + base
    all_ids = jnp.concatenate([asked, other_asked])
    ordered = slot_rows_all.reshape(2, 2, -1, side).transpose(0, 2, 1, 3)
    ordered = ordered.reshape(-1, width)
    found = matmul((rows_here[:, None] == all_ids[None, :]).astype(BF), ordered)
    vocab_part = jnp.where(
        is_first, found, jnp.concatenate([found[:, side:], found[:, :side]], 1)
    )

    parts = gathered.astype(F32)[:, : flat.shape[0]].reshape(4, -1)
    partner = parts[jnp.where(half == 0, 1, 3)]
    far_partner = parts[jnp.where(half == 0, 3, 1)]
    edge_at = 2 * side + hidden_units
    own = parts[0, :edge_at] + partner[edge_at : 2 * edge_at]
    in_order = jnp.stack([parts[0] + partner, parts[2] + far_partner])[:, 2 * edge_at :]
    by_layer = jnp.where(layer == 0, in_order, in_order[::-1])
    small = (
        by_layer[:, : 2 * width].reshape(2, 2, width),
        by_layer[:, 2 * width : 6 * width].reshape(2, 4, width),
        by_layer[0, 6 * width : 7 * width],
        by_layer[0, 7 * width :],
        own[: 2 * side].reshape(1, 2, side),
        own[2 * side :].reshape(1, hidden_units),
    )

    out_first = output[:quarter].astype(BF)
    out_second = output[quarter:].astype(BF)
    act_a = routed(out_first, [(2, 0), (3, 2)])
    act_b = routed(out_second, [(2, 1)])
    grad_first = word_grad[:quarter].astype(BF)
    grad_second = word_grad[quarter:].astype(BF)
    ing_a = routed(grad_second, [(0, 1), (1, 3)])
    ing_b = routed(grad_first, [(1, 2)])
    activations = jnp.where(
        section == 3,
        output[quarter:],
        jnp.where(section == 1, act_b, act_a).astype(F32),
    )
    input_grad = jnp.where(
        section == 0,
        word_grad[:quarter],
        jnp.where(section == 2, ing_b, ing_a).astype(F32),
    )
    return (
        activations, input_grad, table_part, vocab_part, small[2], small[3],
        sums[0],
        small[4],
        sums[1], sums[2],
        small[5],
        sums[3], small[0], small[1],
    )


def solution(mesh):
    both = ("dp", "section")
    by_section = P("section", None, None)
    return jax.shard_map(
        on_device,
        mesh=mesh,
        in_specs=(
            P(both, None), P(None, "dp"), P("dp", None), P("dp", None), P(both, None), P(),
            P("dp", None), P(), P(), by_section, by_section, by_section, by_section,
            P("section", None), by_section, P(), P(),
        ),
        out_specs=(
            P(both, None), P(both, None), P(None, both, None), P(both, None), P(), P(),
            by_section, by_section, by_section, by_section, P("section", None), by_section,
            P(), P(),
        ),
        check_vma=False,
    )
```

```python
import functools

import jax
import jax.numpy as jnp
from jax import lax
from jax.experimental import pallas as pl
from jax.experimental.pallas import tpu as pltpu
from jax.sharding import PartitionSpec as P

HEAD_DIM = 64
EPS = 1e-12
ROOT_HALF = 0.7071067811865476
INV_ROOT_TWO_PI = 0.3989422804014327
BF = jnp.bfloat16
F32 = jnp.float32


def routed(block, route):
    return lax.ppermute(block, "section", route)


SWAP = [(0, 1), (1, 0), (2, 3), (3, 2)]


def swapped(block):
    return routed(block, SWAP)


def matmul_left_t(left, right):
    return jnp.einsum("pa,pb->ab", left, right, preferred_element_type=F32)


GROUP = 8
BLOCK = 128
HOP = 4
DEPTH = 3
EXTRA = 20


def tree_of(k):
    turn = k % 8
    return turn < 4, 1 + turn % 2, (turn // 2) % 2


def rooted_at(c):
    return (c // 2) % 2 == 0, c // 2, c % 2


def loop(low, high, body):
    def step(k, carry):
        body(k)
        return carry

    lax.fori_loop(low, high, step, 0)


def reduce_kernel(
    counts, a_in, b_in, small_ref, edge_ref, mine_ref, box_ref, listed_ref,
    q_ref, o_ref, u_ref, d_ref, gathered_ref, rows_ref, table_ref, act_ref, ing_ref,
    a_ref, b_ref, buf, total, gathered, edge, rows, table, piece,
    send, recv, out_sem, g_send, g_recv, e_send, e_recv, r_send, r_recv, t_send, t_recv,
    f_send, f_recv, m_send, m_recv, last_sem, in_sem,
):
    loads = (
        pltpu.make_async_copy(a_in, a_ref, in_sem.at[0]),
        pltpu.make_async_copy(b_in, b_ref, in_sem.at[1]),
    )
    for copy in loads:
        copy.start()
    me = lax.axis_index("dp")
    section = lax.axis_index("section")
    n_sections = lax.axis_size("section")
    layer = section // 2
    half = section % 2
    other_core = section + 1 - 2 * half
    other_layer = (section + 2) % n_sections
    place = me % GROUP
    z = place // 2
    y = place % 2
    chunks = buf.shape[1]
    side = buf.shape[3]
    slots = rows.shape[2]
    n_q, n_o, n_u, n_d = counts
    ends = (n_d[0] * n_d[1],)
    ends += (ends[0] + n_u[0] * n_u[1],)
    ends += (ends[1] + n_o[0] * n_o[1],)
    mesh_id = pl.DeviceIdType.MESH
    deltas = (-2, 2, 1 - 2 * y)
    exists = (z > 0, z < GROUP // 2 - 1, y >= 0)

    barrier = pltpu.get_barrier_semaphore()
    for d in range(3):

        @pl.when(exists[d])
        def _():
            pl.semaphore_signal(
                barrier, inc=1, device_id=(me + deltas[d], section), device_id_type=mesh_id
            )

    for step in range(1, n_sections):
        pl.semaphore_signal(
            barrier, inc=1, device_id=(me, (section + step) % n_sections), device_id_type=mesh_id
        )
    pl.semaphore_wait(
        barrier,
        n_sections + jnp.where(exists[0], 1, 0) + jnp.where(exists[1], 1, 0),
    )

    def remote(source, target, sent, got, device):
        return pltpu.make_async_remote_copy(
            src_ref=source, dst_ref=target, send_sem=sent, recv_sem=got, device_id=device,
            device_id_type=mesh_id,
        )

    quarter = mine_ref.shape[0] // 2

    def spread(r, target, kind):
        return remote(
            mine_ref.at[pl.ds(r * quarter, quarter)], target, m_send.at[r], m_recv.at[kind],
            (me, 2 * half + r),
        )

    def keep(r, target):
        return pltpu.make_async_copy(
            mine_ref.at[pl.ds(r * quarter, quarter)], target, m_send.at[r]
        )

    for r in range(2):
        for kind, target in ((0, ing_ref), (1, act_ref)):

            @pl.when((layer == kind) & (section != 2 * half + r))
            def _():
                spread(r, target, kind).start()

            @pl.when((layer == kind) & (section == 2 * half + r))
            def _():
                keep(r, target).start()

    def edge_across():
        return remote(
            edge_ref.at[1], edge.at[0], e_send.at[0], e_recv.at[0], (me, other_layer)
        )

    def edge_beside(source):
        return remote(source, edge.at[1], e_send.at[1], e_recv.at[1], (me, other_core))

    @pl.when(layer == 0)
    def _():
        edge_across().start()
        edge_beside(edge_ref.at[0]).start()
        edge[0] = edge_ref[0]

    def roles(tree):
        comb, root_z, root_y = tree
        along = jnp.logical_or(jnp.logical_not(comb), y == root_y)
        across = jnp.logical_or(comb, z == root_z)
        child = (
            exists[0] & along & (z <= root_z),
            exists[1] & along & (z >= root_z),
            across & (y == root_y),
        )
        up_z = along & (z != root_z)
        up_y = across & (y != root_y)
        parent = jnp.where(up_z, jnp.where(z < root_z, 1, 0), jnp.where(up_y, 2, 3))
        depth = jnp.abs(z - root_z) + jnp.abs(y - root_y)
        return child, parent, depth

    def neighbour(d):
        return me + jnp.where(d == 0, deltas[0], jnp.where(d == 1, deltas[1], deltas[2]))

    def facing(d):
        return jnp.where(d == 2, 2, 1 - d)

    def transfer(k, d, source):
        there = facing(d)
        return remote(
            buf.at[source, k], buf.at[there, k], send.at[d, k], recv.at[there, k],
            (neighbour(d), section),
        )

    def arrived(k, d):
        remote(
            buf.at[3, k], buf.at[d, k], send.at[0, k], recv.at[d, k], (me, other_core)
        ).wait_recv()

    def put(k, source):
        kk = k - 1
        low = 0
        for target, count, high in (
            (d_ref, n_d, ends[0]), (u_ref, n_u, ends[1]), (o_ref, n_o, ends[2]),
            (q_ref, n_q, chunks - 1),
        ):

            @pl.when((kk >= low) & (kk < high))
            def _():
                at = kk - low
                pltpu.make_async_copy(
                    buf.at[source, k],
                    target.at[
                        pl.ds(pl.multiple_of(at // count[1] * BLOCK, BLOCK), BLOCK),
                        pl.ds(pl.multiple_of(at % count[1] * side, BLOCK), side),
                    ],
                    out_sem.at[k],
                ).start()

            low = high

    def product(k):
        kd = k - 1
        in_d = kd < ends[0]
        ku = kd - ends[0]
        in_u = kd < ends[1]
        ko = kd - ends[1]
        in_o = kd < ends[2]
        kq = kd - ends[2]
        a_at = jnp.where(
            in_d,
            n_q[0] + n_o[0] + n_u[0] + kd // n_d[1],
            jnp.where(
                in_u,
                n_q[0] + n_o[0] + ku // n_u[1],
                jnp.where(in_o, n_q[0] + ko // n_o[1], kq // n_q[1]),
            ),
        )
        b_at = jnp.where(
            in_d,
            n_q[1] + n_o[1] + n_u[1] + kd % n_d[1],
            jnp.where(
                in_u,
                n_q[1] + n_o[1] + ku % n_u[1],
                jnp.where(in_o, n_q[1] + ko % n_o[1], kq % n_q[1]),
            ),
        )
        left = a_ref[:, pl.ds(pl.multiple_of(a_at * BLOCK, BLOCK), BLOCK)]
        right = b_ref[:, pl.ds(pl.multiple_of(b_at * side, BLOCK), side)]
        total[...] = lax.dot_general(
            left, right, (((0,), (0,)), ((), ())), preferred_element_type=F32
        )

    def climb(k, level):
        child, parent, depth = roles(tree_of(k))

        @pl.when((k >= 0) & (k < chunks) & (depth == DEPTH - level))
        def _():
            @pl.when(k == 0)
            def _():
                total[...] = small_ref[...]

            @pl.when(k > 0)
            def _():
                product(k)

            if level > 0:
                for d in range(3):

                    @pl.when(child[d])
                    def _():
                        arrived(k, d)
                        total[...] += buf[d, k].astype(F32)

            buf[3, k] = total[...].astype(BF)
            if level < DEPTH:
                transfer(k, parent, 3).start()
            else:
                for d in range(3):

                    @pl.when(child[d])
                    def _():
                        transfer(k, d, 3).start()

                put(k, 3)

    def descend(k, level):
        child, parent, depth = roles(tree_of(k))

        @pl.when((k >= 0) & (k < chunks) & (depth == level))
        def _():
            arrived(k, parent)
            for d in range(3):

                @pl.when(child[d])
                def _():
                    transfer(k, d, parent).start()

            put(k, parent)

    def settle(k):
        child, parent, depth = roles(tree_of(k))
        for d in range(3):

            @pl.when(child[d] | (parent == d))
            def _():
                transfer(k, d, 3).wait_send()

        @pl.when(k > 0)
        def _():
            pltpu.make_async_copy(
                buf.at[3, k], d_ref.at[pl.ds(0, BLOCK), pl.ds(0, side)], out_sem.at[k]
            ).wait()

    def advance(t):
        for level in range(DEPTH + 1):
            climb(t - level * HOP, level)
        for level in range(1, DEPTH + 1):
            descend(t - (DEPTH + level) * HOP, level)

    def slots_down(c, d):
        return remote(
            rows.at[0, c], rows.at[0, c], r_send.at[d, c], r_recv.at[0, c],
            (neighbour(d), section),
        )

    def slots_across(c):
        return remote(
            rows.at[0, c], rows.at[1, c], r_send.at[3, c], r_recv.at[1, c], (me, other_layer)
        )

    def slots_beside(c, kind):
        return remote(
            rows.at[kind, c], rows.at[2 + kind, c], r_send.at[4 + kind, c],
            r_recv.at[2 + kind, c], (me, other_core),
        )

    def slots_got(c, kind):
        remote(
            rows.at[kind, c], rows.at[kind, c], r_send.at[0, c], r_recv.at[kind, c],
            (me, other_core),
        ).wait_recv()

    def share_slots(c, level):
        child, parent, depth = roles(rooted_at(c))

        @pl.when((c >= 0) & (c < GROUP) & (depth == level))
        def _():
            if level > 0:
                slots_got(c, 0)
            for d in range(3):

                @pl.when(child[d])
                def _():
                    slots_down(c, d).start()

            slots_across(c).start()
            slots_beside(c, 0).start()

    def relay_slots(c):
        @pl.when((c >= 0) & (c < GROUP))
        def _():
            slots_got(c, 1)
            slots_beside(c, 1).start()

    def table_up(c, d):
        there = facing(d)
        return remote(
            piece.at[3, c], piece.at[there, c], t_send.at[d, c], t_recv.at[there, c],
            (neighbour(d), section),
        )

    def table_out(c, step):
        to = (section + step) % n_sections
        return remote(
            piece.at[3, c, pl.ds(to * table.shape[1], table.shape[1])], table.at[section],
            f_send.at[step], f_recv.at[section], (me, to),
        )

    def table_climb(c, level):
        child, parent, depth = roles(rooted_at(c))

        @pl.when((c >= 0) & (c < GROUP) & (depth == DEPTH + 1 - level))
        def _():
            at = c * BLOCK + lax.broadcasted_iota(jnp.int32, (BLOCK, edge.shape[1]), 0)
            for part in range(2):
                spots = box_ref[part]
                ones = (at == spots[0:1]).astype(F32) + (at == spots[1:2]).astype(F32)
                term = jnp.dot(ones.astype(BF), edge[part], preferred_element_type=F32)
                if part == 0:
                    total[...] = term
                else:
                    total[...] += term
            if level > 0:
                for d in range(3):

                    @pl.when(child[d])
                    def _():
                        remote(
                            piece.at[3, c], piece.at[d, c], t_send.at[0, c], t_recv.at[d, c],
                            (me, other_core),
                        ).wait_recv()
                        total[...] += piece[d, c].astype(F32)

            piece[3, c] = total[...].astype(BF)
            if level < DEPTH + 1:
                table_up(c, parent).start()
            else:
                for step in range(1, n_sections):
                    table_out(c, step).start()
                kept = table.shape[1]
                table[section] = piece[3, c, pl.ds(pl.multiple_of(section * kept, kept), kept)]

    def extras(t):
        c = t - EXTRA
        for level in range(DEPTH + 2):
            share_slots(c - level * HOP, level)
        relay_slots(c - (DEPTH + 3) * HOP)
        for level in range(DEPTH + 2):
            table_climb(c - GROUP - level * HOP, level)

    def settle_extras(c):
        child, parent, depth = roles(rooted_at(c))
        for d in range(3):

            @pl.when(child[d])
            def _():
                slots_down(c, d).wait_send()

            @pl.when(parent == d)
            def _():
                table_up(c, d).wait_send()

        slots_across(c).wait_send()
        for kind in range(2):
            slots_beside(c, kind).wait_send()
            slots_got(c, 2 + kind)

    def handed(step):
        return remote(
            gathered.at[0], gathered.at[step], g_send.at[step], g_recv.at[step],
            (me, (section + n_sections - step) % n_sections),
        )

    for copy in loads:
        copy.wait()
    loop(0, EXTRA, advance)

    @pl.when(layer == 1)
    def _():
        edge_across().wait_recv()
        edge_beside(edge.at[0]).start()

    edge_beside(edge.at[0]).wait_recv()
    wanted = listed_ref[...] == lax.broadcasted_iota(jnp.int32, (slots, edge.shape[1]), 1)
    rows[0, place] = jnp.dot(
        wanted.astype(F32).astype(BF), edge[0], preferred_element_type=F32
    ).astype(BF)

    def both(t):
        advance(t)
        extras(t)

    middle = EXTRA + 2 * GROUP + (DEPTH + 3) * HOP
    loop(EXTRA, middle, both)
    mine = roles(tree_of(0))[1]
    kept_small = gathered.shape[1]
    gathered[0] = buf[mine, 0, :kept_small]
    for step in range(1, n_sections):
        handed(step).start()
    loop(middle, chunks + 2 * DEPTH * HOP, advance)
    loop(0, GROUP, settle_extras)
    for step in range(1, n_sections):
        handed(step).wait()
        table_out(place, step).wait_send()
        source = (section + n_sections - step) % n_sections
        remote(
            piece.at[3, 0, pl.ds(0, table.shape[1])], table.at[source], f_send.at[0],
            f_recv.at[source], (me, other_core),
        ).wait_recv()
    outs = (
        pltpu.make_async_copy(gathered, gathered_ref, last_sem.at[0]),
        pltpu.make_async_copy(rows, rows_ref, last_sem.at[1]),
        pltpu.make_async_copy(table, table_ref, last_sem.at[2]),
    )
    for copy in outs:
        copy.start()

    for r in range(2):
        for kind, target in ((0, ing_ref), (1, act_ref)):

            @pl.when((layer == kind) & (section != 2 * half + r))
            def _():
                spread(r, target, kind).wait_send()

            @pl.when((layer == kind) & (section == 2 * half + r))
            def _():
                keep(r, target).wait()

    for kind, target in ((0, ing_ref), (1, act_ref)):

        @pl.when(section != 2 * kind + layer)
        def _():
            spread(0, target, kind).wait_recv()

    @pl.when(layer == 0)
    def _():
        edge_across().wait_send()

    edge_beside(edge.at[0]).wait_send()
    loop(0, chunks, settle)
    for copy in outs:
        copy.wait()


def reduced(a, b, small, edge, mine, boxes, listed, counts, side):
    chunks = 1 + sum(count[0] * count[1] for count in counts)
    n_sections = lax.axis_size("section")
    kept = 32
    slots = listed.shape[0]
    page = edge.shape[1]
    any_space = pl.BlockSpec(memory_space=pl.ANY)
    in_vmem = pl.BlockSpec(memory_space=pltpu.VMEM)
    flops = 2 * a.shape[0] * BLOCK * side * chunks
    dma = pltpu.SemaphoreType.DMA
    return pl.pallas_call(
        functools.partial(reduce_kernel, counts),
        out_shape=tuple(
            jax.ShapeDtypeStruct((count[0] * BLOCK, count[1] * side), BF) for count in counts
        )
        + (
            jax.ShapeDtypeStruct((n_sections, kept, side), BF),
            jax.ShapeDtypeStruct((4, GROUP, slots, side), BF),
            jax.ShapeDtypeStruct((n_sections, BLOCK // n_sections, side), BF),
            jax.ShapeDtypeStruct((mine.shape[0] // 2, mine.shape[1]), BF),
            jax.ShapeDtypeStruct((mine.shape[0] // 2, mine.shape[1]), BF),
        ),
        in_specs=[any_space] * 2 + [in_vmem] * 2 + [any_space] + [in_vmem] * 2,
        out_specs=(any_space,) * 9,
        scratch_shapes=[
            pltpu.VMEM(a.shape, BF),
            pltpu.VMEM(b.shape, BF),
            pltpu.VMEM((4, chunks, BLOCK, side), BF),
            pltpu.VMEM((BLOCK, side), F32),
            pltpu.VMEM((n_sections, kept, side), BF),
            pltpu.VMEM((2, page, side), BF),
            pltpu.VMEM((4, GROUP, slots, side), BF),
            pltpu.VMEM((n_sections, BLOCK // n_sections, side), BF),
            pltpu.VMEM((4, GROUP, BLOCK, side), BF),
            dma((3, chunks)), dma((3, chunks)), dma((chunks,)),
            dma((n_sections,)), dma((n_sections,)),
            dma((2,)), dma((2,)),
            dma((6, GROUP)), dma((4, GROUP)),
            dma((3, GROUP)), dma((3, GROUP)),
            dma((n_sections,)), dma((n_sections,)),
            dma((2,)), dma((2,)),
            dma((3,)), dma((2,)),
        ],
        compiler_params=pltpu.CompilerParams(
            collective_id=0, has_side_effects=True, vmem_limit_bytes=60 << 20
        ),
        cost_estimate=pl.CostEstimate(
            flops=flops, bytes_accessed=400 << 20, transcendentals=0
        ),
        name="gradient_sums",
    )(a, b, small, edge, mine, boxes, listed)


ROWS = 256


def layer_kernel(
    x_ref, given_ref, norm_ref, column_ref, q_own, o_own, u_own, d_own, qvb_ref, upb_ref,
    gains_ref, shifts_ref, first_gain_ref,
    a_ref, b_ref, edge_ref, mine_ref, small_ref, sums_ref, upb_sum,
    wq, wo, wu, wd, wide, x_land, g_land, x_low, ctx, d_ctx, h_low, act, slope, qkv, d_qkv,
    da_low, df_low, probs, n_one, n_two, r_one, r_two, z, sent_low, columns,
    w_local, w_send, w_recv, x_send, x_recv, g_send, g_recv, p_local, p_send, p_recv, io_sem,
):
    me = lax.axis_index("dp")
    section = lax.axis_index("section")
    n_sections = lax.axis_size("section")
    layer = section // 2
    half = section % 2
    beside = (me, section + 1 - 2 * half)
    across = (me, (section + 2) % n_sections)
    mesh_id = pl.DeviceIdType.MESH
    page, width = x_low.shape
    side = ctx.shape[2]
    units = act.shape[2]
    blocks = page // ROWS
    tile = 512
    scale = HEAD_DIM ** (-0.5)

    barrier = pltpu.get_barrier_semaphore()
    for device in (beside, across):
        pl.semaphore_signal(barrier, inc=1, device_id=device, device_id_type=mesh_id)
    pl.semaphore_wait(barrier, 2)

    def remote(source, target, sent, got, device):
        return pltpu.make_async_remote_copy(
            src_ref=source, dst_ref=target, send_sem=sent, recv_sem=got, device_id=device,
            device_id_type=mesh_id,
        )

    def weight_copies(i):
        source = (q_own, o_own, u_own, d_own)[i].at[0]
        target = (wq, wo, wu, wd)[i]
        return (
            pltpu.make_async_copy(source, target.at[0], w_local.at[i]),
            remote(source, target.at[1], w_send.at[i], w_recv.at[i], beside),
        )

    def weights_here(i):
        near, far = weight_copies(i)
        near.wait()
        far.wait_recv()

    x_copy = pltpu.make_async_copy(x_ref, wide, io_sem.at[0])
    given_copy = pltpu.make_async_copy(given_ref, g_land, io_sem.at[1])

    @pl.when(layer == 0)
    def _():
        x_copy.start()

    @pl.when(layer == 1)
    def _():
        given_copy.start()

    for i in range(4):
        near, far = weight_copies(i)
        far.start()
        near.start()

    def rows_of(block):
        return pl.ds(pl.multiple_of(block * ROWS, ROWS), ROWS)

    def x_move(block):
        rows = rows_of(block)
        return remote(
            sent_low.at[rows], x_land.at[rows], x_send.at[block], x_recv.at[block], across
        )

    def g_move(block):
        rows = rows_of(block)
        return remote(
            sent_low.at[rows], g_land.at[rows], g_send.at[block], g_recv.at[block], across
        )

    spans = (
        (a_ref, 0, width), (a_ref, width, side), (a_ref, width + side, width),
        (a_ref, 2 * width + side, units),
        (b_ref, 0, 3 * side), (b_ref, 3 * side, width), (b_ref, 3 * side + width, units),
        (b_ref, 3 * side + width + units, width),
    )

    def piece_copies(i):
        target, start, size = spans[i]
        source = (x_low, ctx, h_low, act, d_qkv, da_low, slope, df_low)[i]
        double = i in (1, 3, 4, 6)
        columns = pl.ds(start, size)
        return (
            pltpu.make_async_copy(
                source.at[0] if double else source, target.at[0, :, columns], p_local.at[i]
            ),
            remote(
                source.at[1] if double else source, target.at[1, :, columns], p_send.at[i],
                p_recv.at[i], beside,
            ),
        )

    def hand_out(*pieces):
        for i in pieces:
            near, far = piece_copies(i)
            far.start()
            near.start()

    def nt(left, right):
        return lax.dot_general(
            left, right, (((1,), (1,)), ((), ())), preferred_element_type=F32
        )

    def tn(left, right):
        return lax.dot_general(
            left, right, (((0,), (0,)), ((), ())), preferred_element_type=F32
        )

    def centred(values):
        center = values - jnp.mean(values, -1, keepdims=True)
        spread = jnp.mean(center * center, -1, keepdims=True)
        inverse = lax.rsqrt(spread + EPS)
        return center * inverse, inverse

    def pulled(grad, normed, inverse, gain):
        scaled = grad * gain
        return inverse * (
            scaled
            - jnp.mean(scaled, -1, keepdims=True)
            - normed * jnp.mean(scaled * normed, -1, keepdims=True)
        )

    def add_sum(row, values):
        sums_ref[row : row + 1] += jnp.sum(values, 0, keepdims=True)

    sums_ref[...] = jnp.zeros_like(sums_ref)
    upb_sum[...] = jnp.zeros_like(upb_sum)

    weights_here(0)

    @pl.when(layer == 0)
    def _():
        x_copy.wait()

    def project(block):
        rows = rows_of(block)

        @pl.when(layer == 1)
        def _():
            x_move(block).wait_recv()
            wide[rows] = x_land[rows].astype(F32)

        low = wide[rows].astype(BF)
        x_low[rows] = low
        for slot in range(2):
            for c in range(3):
                part = pl.ds(c * side, side)
                value = jnp.dot(low, wq[slot, :, part], preferred_element_type=F32)
                if c != 1:
                    value = value + qvb_ref[slot, c // 2 : c // 2 + 1]
                qkv[slot, rows, part] = value.astype(BF)

    loop(0, blocks, project)
    hand_out(0)

    lane = lax.broadcasted_iota(jnp.int32, (1, 2 * HEAD_DIM), 1)
    masks = ((lane < HEAD_DIM).astype(F32).astype(BF), (lane >= HEAD_DIM).astype(F32).astype(BF))
    first_lane = lax.broadcasted_iota(jnp.int32, (page, 2 * HEAD_DIM), 1) < HEAD_DIM
    first_row = lax.broadcasted_iota(jnp.int32, (2 * HEAD_DIM, page), 0) < HEAD_DIM
    pairs = side // (2 * HEAD_DIM)

    def lanes(i, third):
        at = third * side + (i % pairs) * 2 * HEAD_DIM
        return pl.ds(pl.multiple_of(at, 2 * HEAD_DIM), 2 * HEAD_DIM)

    def attend(i):
        slot = i // pairs
        queries = qkv[slot, :, lanes(i, 0)] * jnp.asarray(scale, BF)
        keys = qkv[slot, :, lanes(i, 1)]
        values = qkv[slot, :, lanes(i, 2)]
        found = []
        for e in range(2):
            scores = nt(keys * masks[e], queries)
            expo = jnp.exp(scores - jnp.max(scores, 0, keepdims=True))
            share = 1.0 / jnp.sum(expo, 0, keepdims=True)
            low = (expo * share).astype(BF)
            probs[2 * i + e] = low
            found.append(tn(values, low))
        ctx[slot, :, lanes(i, 0)] = jnp.where(first_row, found[0], found[1]).T.astype(BF)

    loop(0, 2 * pairs, attend)
    hand_out(1)
    for i in range(1, 4):
        weights_here(i)

    def feed(block):
        rows = rows_of(block)
        attended = (
            jnp.dot(ctx[0, rows], wo[0], preferred_element_type=F32)
            + jnp.dot(ctx[1, rows], wo[1], preferred_element_type=F32)
            + shifts_ref[0:1]
        )
        normed, inverse = centred(wide[rows] + attended)
        n_one[rows] = normed
        r_one[rows] = inverse
        hidden = normed * gains_ref[0:1] + shifts_ref[1:2]
        z[rows] = hidden
        h_low[rows] = hidden.astype(BF)
        for slot in range(2):
            for c in range(units // tile):
                part = pl.ds(c * tile, tile)
                upper = (
                    jnp.dot(h_low[rows], wu[slot, :, part], preferred_element_type=F32)
                    + upb_ref[slot : slot + 1, part]
                )
                below = 0.5 * (1.0 + lax.erf(upper * ROOT_HALF))
                act[slot, rows, part] = (upper * below).astype(BF)
                slope[slot, rows, part] = (
                    below + upper * jnp.exp(-0.5 * upper * upper) * INV_ROOT_TWO_PI
                ).astype(BF)
        mixed = (
            jnp.dot(act[0, rows], wd[0], preferred_element_type=F32)
            + jnp.dot(act[1, rows], wd[1], preferred_element_type=F32)
            + shifts_ref[2:3]
        )
        normed, inverse = centred(z[rows] + mixed)
        n_two[rows] = normed
        r_two[rows] = inverse
        output = normed * gains_ref[1:2] + shifts_ref[3:4]
        sent_low[rows] = output.astype(BF)

        @pl.when(layer == 0)
        def _():
            x_move(block).start()

        @pl.when(layer == 1)
        def _():
            mine_ref[rows] = sent_low[rows]

    loop(0, blocks, feed)
    hand_out(2, 3)

    @pl.when(layer == 1)
    def _():
        given_copy.wait()

    def feed_back(block):
        rows = rows_of(block)

        @pl.when(layer == 0)
        def _():
            g_move(block).wait_recv()

        grad = g_land[rows].astype(F32)
        normed = n_two[rows]
        add_sum(1, grad * normed)
        add_sum(5, grad)
        grad = pulled(grad, normed, r_two[rows], gains_ref[1:2])
        z[rows] = grad
        low = grad.astype(BF)
        df_low[rows] = low
        add_sum(4, low.astype(F32))
        for slot in range(2):
            for c in range(units // tile):
                part = pl.ds(c * tile, tile)
                term = nt(df_low[rows], wd[slot, part])
                term = (term * slope[slot, rows, part].astype(F32)).astype(BF)
                slope[slot, rows, part] = term
                upb_sum[slot : slot + 1, part] += jnp.sum(term.astype(F32), 0, keepdims=True)
        grad = z[rows] + nt(slope[0, rows], wu[0]) + nt(slope[1, rows], wu[1])
        normed = n_one[rows]
        add_sum(0, grad * normed)
        add_sum(3, grad)
        grad = pulled(grad, normed, r_one[rows], gains_ref[0:1])
        z[rows] = grad
        low = grad.astype(BF)
        da_low[rows] = low
        add_sum(2, low.astype(F32))
        for slot in range(2):
            d_ctx[slot, rows] = nt(da_low[rows], wo[slot]).astype(BF)

    loop(0, blocks, feed_back)
    hand_out(5, 6, 7)
    norm_copy = pltpu.make_async_copy(norm_ref, n_two, io_sem.at[2])
    column_copy = pltpu.make_async_copy(column_ref, columns, io_sem.at[3])

    @pl.when(layer == 0)
    def _():
        norm_copy.start()
        column_copy.start()

    def attend_back(i):
        slot = i // pairs
        queries = qkv[slot, :, lanes(i, 0)]
        keys = qkv[slot, :, lanes(i, 1)]
        values = qkv[slot, :, lanes(i, 2)]
        grads = d_ctx[slot, :, lanes(i, 0)]
        d_q, d_k, d_v = [], [], []
        for e in range(2):
            low = probs[2 * i + e]
            share = low.astype(F32)
            term = share * nt(values * masks[e], grads)
            term = (term - share * jnp.sum(term, 0, keepdims=True)).astype(BF)
            d_k.append(jnp.dot(term, queries, preferred_element_type=F32))
            d_v.append(jnp.dot(low, grads, preferred_element_type=F32))
            d_q.append(tn(keys, term))
        d_qkv[slot, :, lanes(i, 0)] = (
            jnp.where(first_row, d_q[0], d_q[1]).T * scale
        ).astype(BF)
        d_qkv[slot, :, lanes(i, 1)] = (jnp.where(first_lane, d_k[0], d_k[1]) * scale).astype(BF)
        d_qkv[slot, :, lanes(i, 2)] = jnp.where(first_lane, d_v[0], d_v[1]).astype(BF)

    loop(0, 2 * pairs, attend_back)
    hand_out(4)

    @pl.when(layer == 0)
    def _():
        norm_copy.wait()
        column_copy.wait()

    def leave(block):
        rows = rows_of(block)
        grad = z[rows] + nt(d_qkv[0, rows], wq[0]) + nt(d_qkv[1, rows], wq[1])
        z[rows] = grad

        @pl.when(layer == 1)
        def _():
            sent_low[rows] = z[rows].astype(BF)
            g_move(block).start()

        @pl.when(layer == 0)
        def _():
            grad = z[rows]
            normed = n_two[rows]
            add_sum(6, grad * normed)
            add_sum(7, grad)
            low = pulled(grad, normed, columns[0, rows], first_gain_ref[...]).astype(BF)
            edge_ref[0, rows] = low[:, :side]
            edge_ref[1, rows] = low[:, side:]
            mine_ref[rows] = (low.astype(F32) * columns[1, rows]).astype(BF)

    loop(0, blocks, leave)
    small_ref[...] = jnp.zeros_like(small_ref)
    pieces = units // side
    for slot in range(2):
        for i in range(2):
            part = pl.ds(2 * i * side, side)
            at = slot * (2 + pieces) + i
            small_ref[at : at + 1] = jnp.sum(
                d_qkv[slot, :, part].astype(F32), 0, keepdims=True
            )
        for i in range(pieces):
            at = slot * (2 + pieces) + 2 + i
            small_ref[at : at + 1] = upb_sum[slot : slot + 1, pl.ds(i * side, side)]
    for i in range(8):
        for j in range(2):
            at = 2 * (2 + pieces) + 2 * i + j
            small_ref[at : at + 1] = sums_ref[i : i + 1, pl.ds(j * side, side)]
    for block in range(blocks):

        @pl.when(layer == 0)
        def _():
            x_move(block).wait_send()

        @pl.when(layer == 1)
        def _():
            g_move(block).wait_send()

    for i in range(4):
        weight_copies(i)[1].wait_send()
    for i in range(8):
        near, far = piece_copies(i)
        near.wait()
        far.wait()


def layered(x, given, norm, columns, weights, qvb, upb, gains, shifts, first_gain):
    page, width = x.shape
    qkv_weight, out_weight, up_weight, down_weight = weights
    side = out_weight.shape[1]
    units = down_weight.shape[1]
    blocks = page // ROWS
    heads = 2 * side // HEAD_DIM
    any_space = pl.BlockSpec(memory_space=pl.ANY)
    in_vmem = pl.BlockSpec(memory_space=pltpu.VMEM)
    dma = pltpu.SemaphoreType.DMA
    vmem = pltpu.VMEM
    flops = 8 * page * width * (4 * width + 4 * units) * 2
    return pl.pallas_call(
        layer_kernel,
        out_shape=(
            jax.ShapeDtypeStruct((2, page, 2 * width + side + units), BF),
            jax.ShapeDtypeStruct((2, page, 3 * side + 2 * width + units), BF),
            jax.ShapeDtypeStruct((2, page, side), BF),
            jax.ShapeDtypeStruct((page, width), BF),
            jax.ShapeDtypeStruct((BLOCK, side), F32),
        ),
        in_specs=[any_space] * 8 + [in_vmem] * 5,
        out_specs=(any_space,) * 2 + (in_vmem,) * 3,
        scratch_shapes=[
            vmem((8, width), F32), vmem((2, units), F32),
            vmem((2, width, 3 * side), BF), vmem((2, side, width), BF),
            vmem((2, width, units), BF), vmem((2, units, width), BF),
            vmem((page, width), F32), vmem((page, width), BF), vmem((page, width), BF),
            vmem((page, width), BF), vmem((2, page, side), BF), vmem((2, page, side), BF),
            vmem((page, width), BF), vmem((2, page, units), BF), vmem((2, page, units), BF),
            vmem((2, page, 3 * side), BF), vmem((2, page, 3 * side), BF),
            vmem((page, width), BF), vmem((page, width), BF), vmem((heads, page, page), BF),
            vmem((page, width), F32), vmem((page, width), F32),
            vmem((page, 1), F32), vmem((page, 1), F32),
            vmem((page, width), F32), vmem((page, width), BF), vmem((2, page, 1), F32),
            dma((4,)), dma((4,)), dma((4,)),
            dma((blocks,)), dma((blocks,)), dma((blocks,)), dma((blocks,)),
            dma((8,)), dma((8,)), dma((8,)), dma((4,)),
        ],
        compiler_params=pltpu.CompilerParams(
            collective_id=1, has_side_effects=True, vmem_limit_bytes=62 << 20
        ),
        cost_estimate=pl.CostEstimate(
            flops=flops, bytes_accessed=200 << 20, transcendentals=0
        ),
        name="layer_both_ways",
    )(x, given, norm, columns, *weights, qvb, upb, gains, shifts, first_gain)


def front_kernel(
    words_ref, cot_ref, ids_ref, listed_ref, box_ref, vocab_ref, table_ref, gain_ref, shift_ref,
    x_ref, given_ref, norm_ref, column_ref, ids_out,
    words, ids_all, vocab, spots, picks, land, other, sum_scratch, x_s, norm_s, column_s,
    w_send, w_recv, c_send, c_recv, i_send, i_recv, s_send, s_recv, o_send, o_recv, local,
):
    me = lax.axis_index("dp")
    section = lax.axis_index("section")
    n_sections = lax.axis_size("section")
    n_dp = ids_all.shape[0]
    layer = section // 2
    half = section % 2
    mesh_id = pl.DeviceIdType.MESH
    quarter = words_ref.shape[0]
    page, width = x_s.shape
    slots = picks.shape[1]
    side = picks.shape[2]
    held = vocab.shape[0]

    vocab_copy = pltpu.make_async_copy(
        vocab_ref.at[:, pl.ds(pl.multiple_of(layer * side, side), side)], vocab, local.at[0]
    )
    vocab_copy.start()

    barrier = pltpu.get_barrier_semaphore()

    def greet(step, carry):
        pl.semaphore_signal(
            barrier, inc=1, device_id=((me + step) % n_dp, section), device_id_type=mesh_id
        )
        return carry

    lax.fori_loop(1, n_dp, greet, 0)
    for step in range(1, n_sections):
        pl.semaphore_signal(
            barrier, inc=1, device_id=(me, (section + step) % n_sections), device_id_type=mesh_id
        )
    pl.semaphore_wait(barrier, n_dp - 1 + n_sections - 1)

    def remote(source, target, sent, got, device):
        return pltpu.make_async_remote_copy(
            src_ref=source, dst_ref=target, send_sem=sent, recv_sem=got, device_id=device,
            device_id_type=mesh_id,
        )

    def ids_move(step):
        return remote(
            ids_ref, ids_all.at[me], i_send.at[step], i_recv.at[me], ((me + step) % n_dp, section)
        )

    def ids_got(step):
        source = (me + step) % n_dp
        return remote(
            ids_ref, ids_all.at[source], i_send.at[0], i_recv.at[source],
            (me, (section + 1) % n_sections),
        )

    loop(1, n_dp, lambda step: ids_move(step).start())
    ids_all[me] = ids_ref[...]

    words_move = remote(
        words_ref, words.at[half], w_send, w_recv.at[half], (me, layer)
    )
    given_part = given_ref.at[pl.ds(pl.multiple_of(half * quarter, quarter), quarter)]
    given_move = remote(cot_ref, given_part, c_send, c_recv.at[half], (me, 2 + layer))
    given_keep = pltpu.make_async_copy(cot_ref, given_part, c_send)

    @pl.when(section != 0)
    def _():
        words_move.start()

    @pl.when(section == 0)
    def _():
        words[0] = words_ref[...]

    @pl.when(section != 3)
    def _():
        given_move.start()

    @pl.when(section == 3)
    def _():
        given_keep.start()

    loop(1, n_dp, lambda step: ids_got(step).wait_recv())
    lists = ids_all[...].astype(F32)
    lists = jnp.where(half == 0, lists[:, 0], lists[:, 1])
    sum_scratch[...] = jnp.zeros_like(sum_scratch)
    sum_scratch[0:n_dp] = lists
    across = sum_scratch[...].T
    at = (me * held + lax.broadcasted_iota(jnp.int32, (slots, held), 1)).astype(F32)
    for origin in range(n_dp):
        spots[origin * slots : (origin + 1) * slots] = (
            at == across[:slots, origin : origin + 1]
        ).astype(F32).astype(BF)
    vocab_copy.wait()
    found = jnp.dot(spots[...], vocab[...], preferred_element_type=F32).astype(BF)
    for origin in range(n_dp):
        picks[origin] = found[origin * slots : (origin + 1) * slots]

    def slots_move(step):
        to = (me + step) % n_dp
        return remote(
            picks.at[to], land.at[me], s_send.at[step], s_recv.at[me], (to, section)
        )

    def slots_got(step):
        source = (me + step) % n_dp
        return remote(
            picks.at[0], land.at[source], s_send.at[0], s_recv.at[source],
            (me, (section + 1) % n_sections),
        )

    loop(1, n_dp, lambda step: slots_move(step).start())
    land[me] = picks[me]

    @pl.when(layer == 0)
    def _():
        coords = lax.broadcasted_iota(jnp.int32, (table_ref.shape[1], page), 0)
        for kind in range(2):
            ones = (coords == box_ref[kind : kind + 1]).astype(F32) + (
                coords == box_ref[kind + 2 : kind + 3]
            ).astype(F32)
            term = lax.dot_general(
                ones.astype(BF), table_ref[kind], (((0,), (0,)), ((), ())),
                preferred_element_type=F32,
            )
            if kind == 0:
                x_s[...] = term
            else:
                x_s[...] += term

    loop(1, n_dp, lambda step: slots_got(step).wait_recv())
    mine = land[0]
    for origin in range(1, n_dp):
        mine = mine + land[origin]
    other[1] = mine
    other_move = remote(other.at[1], other.at[0], o_send, o_recv, (me, half))

    @pl.when(layer == 1)
    def _():
        other_move.start()

    @pl.when(layer == 0)
    def _():
        for r in range(2):

            @pl.when(section + r > 0)
            def _():
                remote(
                    words_ref, words.at[r], w_send, w_recv.at[r], (me, section + 1)
                ).wait_recv()

        chosen = (listed_ref[...] == lax.broadcasted_iota(jnp.int32, (slots, page), 1))
        chosen = chosen.astype(F32).astype(BF)

        def tn(right):
            return lax.dot_general(
                chosen, right, (((0,), (0,)), ((), ())), preferred_element_type=F32
            )

        marked = tn(jnp.ones((slots, BLOCK), BF))[:, 0:1]
        column_s[1] = 1.0 - marked
        other_move.wait_recv()
        for part, values in ((0, other[1]), (1, other[0])):
            columns = pl.ds(part * side, side)
            x_s[:, columns] += tn(values)
        for r in range(2):
            rows = pl.ds(r * quarter, quarter)
            kept = column_s[1, rows]
            summed = x_s[rows] + words[r].astype(F32) * kept
            center = summed - jnp.mean(summed, -1, keepdims=True)
            spread = jnp.mean(center * center, -1, keepdims=True)
            inverse = lax.rsqrt(spread + EPS)
            normed = center * inverse
            norm_s[rows] = normed
            column_s[0, rows] = inverse
            x_s[rows] = normed * gain_ref[...] + shift_ref[...]

    outs = (
        pltpu.make_async_copy(x_s, x_ref, local.at[1]),
        pltpu.make_async_copy(norm_s, norm_ref, local.at[2]),
        pltpu.make_async_copy(column_s, column_ref, local.at[3]),
    )
    ids_copy = pltpu.make_async_copy(ids_all, ids_out, local.at[4])
    ids_copy.start()

    @pl.when(layer == 0)
    def _():
        for copy in outs:
            copy.start()

    @pl.when(layer == 1)
    def _():
        other_move.wait_send()
        for r in range(2):

            @pl.when(section + r < 4)
            def _():
                remote(
                    cot_ref, given_ref.at[pl.ds(r * quarter, quarter)], c_send, c_recv.at[r],
                    (me, section - 1),
                ).wait_recv()

    @pl.when(section != 0)
    def _():
        words_move.wait_send()

    @pl.when(section != 3)
    def _():
        given_move.wait_send()

    @pl.when(section == 3)
    def _():
        given_keep.wait()

    loop(1, n_dp, lambda step: ids_move(step).wait_send())
    loop(1, n_dp, lambda step: slots_move(step).wait_send())
    ids_copy.wait()

    @pl.when(layer == 0)
    def _():
        for copy in outs:
            copy.wait()


def front(words, cot, ids, listed, boxes, vocab, table, gain, shift):
    quarter, width = words.shape
    page = 2 * quarter
    n_dp = lax.axis_size("dp")
    slots = listed.shape[0]
    held = vocab.shape[0]
    side = width // 2
    any_space = pl.BlockSpec(memory_space=pl.ANY)
    in_vmem = pl.BlockSpec(memory_space=pltpu.VMEM)
    dma = pltpu.SemaphoreType.DMA
    vmem = pltpu.VMEM
    return pl.pallas_call(
        front_kernel,
        out_shape=(
            jax.ShapeDtypeStruct((page, width), F32),
            jax.ShapeDtypeStruct((page, width), BF),
            jax.ShapeDtypeStruct((page, width), F32),
            jax.ShapeDtypeStruct((2, page, 1), F32),
            jax.ShapeDtypeStruct((n_dp, 2, BLOCK), jnp.int32),
        ),
        in_specs=[in_vmem, any_space, in_vmem, in_vmem, in_vmem, any_space] + [in_vmem] * 3,
        out_specs=(any_space,) * 5,
        scratch_shapes=[
            vmem((2, quarter, width), BF), vmem((n_dp, 2, BLOCK), jnp.int32),
            vmem((held, side), BF), vmem((n_dp * slots, held), BF),
            vmem((n_dp, slots, side), BF), vmem((n_dp, slots, side), BF),
            vmem((2, slots, side), BF), vmem((BLOCK, BLOCK), F32),
            vmem((page, width), F32), vmem((page, width), F32), vmem((2, page, 1), F32),
            dma, dma((2,)), dma, dma((2,)), dma((n_dp,)), dma((n_dp,)),
            dma((n_dp,)), dma((n_dp,)), dma, dma, dma((5,)),
        ],
        compiler_params=pltpu.CompilerParams(
            collective_id=2, has_side_effects=True, vmem_limit_bytes=60 << 20
        ),
        name="embedded_rows",
    )(words, cot, ids, listed, boxes, vocab, table, gain, shift)


def finish_kernel(
    pieces, q_in, o_in, u_in, d_in, rows_in, ids_ref, small_ref, table_ref, act_in, ing_in,
    act_ref, ing_ref, tab_ref, voc_ref, q_ref, qvb_ref, o_ref, u_ref, upb_ref, d_ref, own_ref,
    q_s, o_s, u_s, d_s, q_f, o_f, u_f, d_f, rows_s, in_sem, out_sem, rows_sem,
):
    section = lax.axis_index("section")
    layer = section // 2
    half = section % 2
    side = rows_s.shape[3]
    n_dp = rows_s.shape[1]
    rows_copy = pltpu.make_async_copy(rows_in, rows_s, rows_sem)
    rows_copy.start()
    moves = []
    for source, low, wide, target in (
        (d_in, d_s, d_f, d_ref), (u_in, u_s, u_f, u_ref), (q_in, q_s, q_f, q_ref),
        (o_in, o_s, o_f, o_ref),
    ):
        count = low.shape[0] // pieces
        for i in range(pieces):
            rows = pl.ds(i * count, count)
            moves.append((source.at[rows], low.at[rows], wide.at[rows], target.at[0, rows]))
    for i, (source, low, wide, target) in enumerate(moves):
        pltpu.make_async_copy(source, low, in_sem.at[i]).start()

    act_ref[...] = act_in[...].astype(F32)
    ing_ref[...] = ing_in[...].astype(F32)

    parts = small_ref[...].astype(F32)
    partner = jnp.where(half == 0, parts[1], parts[3])
    far_partner = jnp.where(half == 0, parts[3], parts[1])
    splits = d_in.shape[0] // side
    kept = 2 + splits
    own = parts[0, :kept] + partner[kept : 2 * kept]
    qvb_ref[0] = own[:2]
    for i in range(splits):
        upb_ref[0:1, pl.ds(i * side, side)] = own[2 + i : 3 + i]
    here = (parts[0] + partner)[2 * kept : 2 * kept + 16]
    there = (parts[2] + far_partner)[2 * kept : 2 * kept + 16]
    own_ref[0] = jnp.where(layer == 0, here, there)
    own_ref[1] = jnp.where(layer == 0, there, here)
    for l in range(2):
        for h in range(2):
            tab_ref[h, :, pl.ds(l * side, side)] = table_ref[2 * l + h].astype(F32)

    for i, (source, low, wide, target) in enumerate(moves):
        pltpu.make_async_copy(source, low, in_sem.at[i]).wait()
        wide[...] = low[...].astype(F32)
        pltpu.make_async_copy(wide, target, out_sem.at[i]).start()

    count = voc_ref.shape[0]
    base = (lax.axis_index("dp") * lax.axis_size("section") + section) * count
    rows_copy.wait()
    at = base + lax.broadcasted_iota(jnp.int32, (count, BLOCK), 0)
    for h in range(2):
        list_at = jnp.where(half == 0, h, 1 - h)
        for group in range(n_dp // 4):
            spots = []
            for origin in range(group * 4, group * 4 + 4):
                row = ids_ref[origin]
                row = jnp.where(list_at == 0, row[0:1], row[1:2])
                spots.append((at == row).astype(F32).astype(BF))
            spots = jnp.concatenate(spots, 1)
            for l in range(2):
                rows = rows_s[2 * h + l, group * 4 : group * 4 + 4].reshape(4 * BLOCK, side)
                term = jnp.dot(spots, rows, preferred_element_type=F32)
                columns = pl.ds(
                    pl.multiple_of(jnp.where(layer == 0, l, 1 - l) * side, side), side
                )
                if h == 0 and group == 0:
                    voc_ref[:, columns] = term
                else:
                    voc_ref[:, columns] += term

    for i, (source, low, wide, target) in enumerate(moves):
        pltpu.make_async_copy(wide, target, out_sem.at[i]).wait()


def finished(sums, rows, ids, small, tables, act, ing, count, side):
    any_space = pl.BlockSpec(memory_space=pl.ANY)
    in_vmem = pl.BlockSpec(memory_space=pltpu.VMEM)
    dma = pltpu.SemaphoreType.DMA
    vmem = pltpu.VMEM
    pieces = 6
    width = act.shape[1]
    units = sums[3].shape[0]
    shapes = [array.shape for array in sums]
    outs = [
        jax.ShapeDtypeStruct(shape, F32)
        for shape in (
            act.shape, ing.shape, (2, tables.shape[1], width), (count, width), (1, *shapes[0]),
            (1, 2, side), (1, *shapes[1]), (1, *shapes[2]), (1, units), (1, *shapes[3]),
            (2, 16, side),
        )
    ]
    specs = [in_vmem] * 4 + [any_space, in_vmem, any_space, any_space, in_vmem, any_space, in_vmem]
    return pl.pallas_call(
        functools.partial(finish_kernel, pieces),
        out_shape=outs,
        in_specs=[any_space] * 5 + [in_vmem] * 5,
        out_specs=specs,
        scratch_shapes=[vmem(shape, BF) for shape in shapes]
        + [vmem(shape, F32) for shape in shapes]
        + [vmem(rows.shape, BF), dma((4 * pieces,)), dma((4 * pieces,)), dma],
        compiler_params=pltpu.CompilerParams(vmem_limit_bytes=60 << 20),
        name="finished_outputs",
    )(*sums, rows, ids, small, tables, act, ing)


def on_device(
    word_embed, boxes, mask_pos, replace_ids, cotangent, layout_table, vocab_table, embed_gain,
    embed_shift, qkv_weight, qv_bias, out_weight, up_weight, up_bias, down_weight, layer_gains,
    layer_biases,
):
    section = lax.axis_index("section")
    layer = section // 2
    half = section % 2
    quarter, width = word_embed.shape
    page = 2 * quarter
    side = qkv_weight.shape[2] // 3
    units = up_bias.shape[1]

    qvb = jnp.stack([qv_bias[0], swapped(qv_bias[0])])
    upb = jnp.concatenate([up_bias, swapped(up_bias)])
    gains = lax.dynamic_index_in_dim(layer_gains, layer, 0, keepdims=False)
    shifts = lax.dynamic_index_in_dim(layer_biases, layer, 0, keepdims=False)
    slots = mask_pos.shape[1]
    listed = lax.dynamic_index_in_dim(mask_pos, half, 0, keepdims=False)[:, None]
    listed_wide = jnp.pad(listed, ((0, BLOCK - slots), (0, 0)), constant_values=-1)
    ids = jnp.pad(replace_ids, ((0, 0), (0, BLOCK - slots)), constant_values=-1)
    page_boxes = lax.dynamic_slice_in_dim(boxes, half * page, page, 1)

    hidden_in, given, norm_in, columns, all_ids = front(
        word_embed, cotangent, ids, listed, page_boxes, vocab_table, layout_table,
        embed_gain[None], embed_shift[None],
    )
    left, right, edge, mine, small = layered(
        hidden_in, given, norm_in, columns, (qkv_weight, out_weight, up_weight, down_weight),
        qvb, upb, gains, shifts, embed_gain[None],
    )
    left, right = (array.reshape(2 * page, -1) for array in (left, right))
    counts = (
        (width // BLOCK, 3),
        (side // BLOCK, width // side),
        (width // BLOCK, units // side),
        (units // BLOCK, width // side),
    )
    first, second = boxes[:, :page], boxes[:, page:]
    pair = jnp.stack([jnp.where(half == 0, first, second), jnp.where(half == 0, second, first)])
    pair = jnp.where(half == 0, pair[:, 0::2], pair[:, 1::2])
    *sums, gathered, slot_rows, table_rows, act, ing = reduced(
        left, right, small, edge, mine, pair, listed_wide, counts, side
    )
    outer = lax.axis_size("dp") // GROUP
    table_part = None
    if outer > 1:
        groups = [[i + GROUP * g for g in range(outer)] for i in range(GROUP)]
        *sums, gathered = lax.psum((*sums, gathered), "dp", axis_index_groups=groups)
        slot_rows = lax.all_gather(slot_rows, "dp", axis_index_groups=groups, axis=1, tiled=True)
        coords = jnp.arange(layout_table.shape[1], dtype=jnp.int32)
        grad_low = jnp.concatenate([edge[0], edge[1]], 1)
        grad_low = jnp.where(layer == 0, grad_low, jnp.zeros_like(grad_low))
        table_grad = jnp.stack(
            [
                matmul_left_t(
                    (page_boxes[a][:, None] == coords[None, :]).astype(BF)
                    + (page_boxes[a + 2][:, None] == coords[None, :]).astype(BF),
                    grad_low,
                )
                for a in (0, 1)
            ]
        )
        table_part = lax.psum_scatter(
            table_grad.astype(BF), ("dp", "section"), scatter_dimension=1, tiled=True
        ).astype(F32)
    count = vocab_table.shape[0] // lax.axis_size("section")
    act, ing, tables, vocab_part, q_sum, qvb_sum, o_sum, u_sum, upb_sum, d_sum, rest = finished(
        sums, slot_rows, all_ids, gathered, table_rows, act, ing, count, side
    )
    if table_part is None:
        table_part = tables
    gains_sum = rest[:, :4].reshape(2, 2, width)
    shifts_sum = rest[:, 4:12].reshape(2, 4, width)
    return (
        act, ing, table_part, vocab_part, rest[0, 12:14].reshape(width),
        rest[0, 14:16].reshape(width), q_sum, qvb_sum, o_sum, u_sum, upb_sum, d_sum, gains_sum,
        shifts_sum,
    )


def solution(mesh):
    both = ("dp", "section")
    by_section = P("section", None, None)
    return jax.shard_map(
        on_device,
        mesh=mesh,
        in_specs=(
            P(both, None), P(None, "dp"), P("dp", None), P("dp", None), P(both, None), P(),
            P("dp", None), P(), P(), by_section, by_section, by_section, by_section,
            P("section", None), by_section, P(), P(),
        ),
        out_specs=(
            P(both, None), P(both, None), P(None, both, None), P(both, None), P(), P(),
            by_section, by_section, by_section, by_section, P("section", None), by_section,
            P(), P(),
        ),
        check_vma=False,
    )
```

```python
import functools

import jax
import jax.numpy as jnp
from jax import lax
from jax.experimental import pallas as pl
from jax.experimental.pallas import tpu as pltpu
from jax.sharding import PartitionSpec as P

HEAD_DIM = 64
EPS = 1e-12
ROOT_HALF = 0.7071067811865476
INV_ROOT_TWO_PI = 0.3989422804014327
BF = jnp.bfloat16
F32 = jnp.float32


def matmul_left_t(left, right):
    return jnp.einsum("pa,pb->ab", left, right, preferred_element_type=F32)


GROUP = 8
BLOCK = 128
HOP = 4
DEPTH = 3
EXTRA = 20


def tree_of(k):
    turn = k % 8
    return turn < 4, 1 + turn % 2, (turn // 2) % 2


def rooted_at(c):
    return (c // 2) % 2 == 0, c // 2, c % 2


def loop(low, high, body):
    def step(k, carry):
        body(k)
        return carry

    lax.fori_loop(low, high, step, 0)


def reduce_kernel(
    counts, a_in, b_in, small_ref, edge_ref, mine_ref, box_ref, listed_ref,
    q_ref, o_ref, u_ref, d_ref, gathered_ref, rows_ref, table_ref, act_ref, ing_ref,
    a_ref, b_ref, square, buf, total, gathered, edge, rows, table, piece,
    send, recv, out_sem, g_send, g_recv, e_send, e_recv, r_send, r_recv, t_send, t_recv,
    f_send, f_recv, m_send, m_recv, last_sem, in_sem,
):
    loads = (
        pltpu.make_async_copy(a_in, a_ref, in_sem.at[0]),
        pltpu.make_async_copy(b_in, b_ref, in_sem.at[1]),
    )
    for copy in loads:
        copy.start()
    me = lax.axis_index("dp")
    section = lax.axis_index("section")
    n_sections = lax.axis_size("section")
    layer = section // 2
    half = section % 2
    other_core = section + 1 - 2 * half
    other_layer = (section + 2) % n_sections
    place = me % GROUP
    z = place // 2
    y = place % 2
    chunks = buf.shape[1]
    side = buf.shape[3]
    slots = rows.shape[2]
    n_q, n_o, n_u, n_d = counts
    ends = (n_d[0] * n_d[1],)
    ends += (ends[0] + n_u[0] * n_u[1],)
    ends += (ends[1] + n_o[0] * n_o[1],)
    mesh_id = pl.DeviceIdType.MESH
    deltas = (-2, 2, 1 - 2 * y)
    exists = (z > 0, z < GROUP // 2 - 1, y >= 0)

    barrier = pltpu.get_barrier_semaphore()
    for d in range(3):

        @pl.when(exists[d])
        def _():
            pl.semaphore_signal(
                barrier, inc=1, device_id=(me + deltas[d], section), device_id_type=mesh_id
            )

    for step in range(1, n_sections):
        pl.semaphore_signal(
            barrier, inc=1, device_id=(me, (section + step) % n_sections), device_id_type=mesh_id
        )
    pl.semaphore_wait(
        barrier,
        n_sections + jnp.where(exists[0], 1, 0) + jnp.where(exists[1], 1, 0),
    )

    def remote(source, target, sent, got, device):
        return pltpu.make_async_remote_copy(
            src_ref=source, dst_ref=target, send_sem=sent, recv_sem=got, device_id=device,
            device_id_type=mesh_id,
        )

    quarter = mine_ref.shape[0] // 2

    def spread(r, target, kind):
        return remote(
            mine_ref.at[pl.ds(r * quarter, quarter)], target, m_send.at[r], m_recv.at[kind],
            (me, 2 * half + r),
        )

    def keep(r, target):
        return pltpu.make_async_copy(
            mine_ref.at[pl.ds(r * quarter, quarter)], target, m_send.at[r]
        )

    for r in range(2):
        for kind, target in ((0, ing_ref), (1, act_ref)):

            @pl.when((layer == kind) & (section != 2 * half + r))
            def _():
                spread(r, target, kind).start()

            @pl.when((layer == kind) & (section == 2 * half + r))
            def _():
                keep(r, target).start()

    def edge_across():
        return remote(
            edge_ref.at[1], edge.at[0], e_send.at[0], e_recv.at[0], (me, other_layer)
        )

    def edge_beside(source):
        return remote(source, edge.at[1], e_send.at[1], e_recv.at[1], (me, other_core))

    @pl.when(layer == 0)
    def _():
        edge_across().start()
        edge_beside(edge_ref.at[0]).start()
        edge[0] = edge_ref[0]

    def roles(tree):
        comb, root_z, root_y = tree
        along = jnp.logical_or(jnp.logical_not(comb), y == root_y)
        across = jnp.logical_or(comb, z == root_z)
        child = (
            exists[0] & along & (z <= root_z),
            exists[1] & along & (z >= root_z),
            across & (y == root_y),
        )
        up_z = along & (z != root_z)
        up_y = across & (y != root_y)
        parent = jnp.where(up_z, jnp.where(z < root_z, 1, 0), jnp.where(up_y, 2, 3))
        depth = jnp.abs(z - root_z) + jnp.abs(y - root_y)
        return child, parent, depth

    def neighbour(d):
        return me + jnp.where(d == 0, deltas[0], jnp.where(d == 1, deltas[1], deltas[2]))

    def facing(d):
        return jnp.where(d == 2, 2, 1 - d)

    def transfer(k, d, source):
        there = facing(d)
        return remote(
            buf.at[source, k], buf.at[there, k], send.at[d, k], recv.at[there, k],
            (neighbour(d), section),
        )

    def arrived(k, d):
        remote(
            buf.at[3, k], buf.at[d, k], send.at[0, k], recv.at[d, k], (me, other_core)
        ).wait_recv()

    def put(k, source):
        kk = k - 1
        low = 0
        for target, count, high in (
            (d_ref, n_d, ends[0]), (u_ref, n_u, ends[1]), (o_ref, n_o, ends[2]),
            (q_ref, n_q, chunks - 1),
        ):

            @pl.when((kk >= low) & (kk < high))
            def _():
                at = kk - low
                pltpu.make_async_copy(
                    buf.at[source, k],
                    target.at[
                        pl.ds(pl.multiple_of(at // count[1] * BLOCK, BLOCK), BLOCK),
                        pl.ds(pl.multiple_of(at % count[1] * side, BLOCK), side),
                    ],
                    out_sem.at[k],
                ).start()

            low = high

    def product(k):
        kd = k - 1
        in_d = kd < ends[0]
        ku = kd - ends[0]
        in_u = kd < ends[1]
        ko = kd - ends[1]
        in_o = kd < ends[2]
        kq = kd - ends[2]
        a_at = jnp.where(
            in_d,
            n_q[0] + n_o[0] + n_u[0] + kd // n_d[1],
            jnp.where(
                in_u,
                n_q[0] + n_o[0] + ku // n_u[1],
                jnp.where(in_o, n_q[0] + ko // n_o[1], kq // n_q[1]),
            ),
        )
        b_at = jnp.where(
            in_d,
            n_q[1] + n_o[1] + n_u[1] + kd % n_d[1],
            jnp.where(
                in_u,
                n_q[1] + n_o[1] + ku % n_u[1],
                jnp.where(in_o, n_q[1] + ko % n_o[1], kq % n_q[1]),
            ),
        )
        left = a_ref[:, pl.ds(pl.multiple_of(a_at * BLOCK, BLOCK), BLOCK)]
        right = b_ref[:, pl.ds(pl.multiple_of(b_at * side, BLOCK), side)]
        total[...] = lax.dot_general(
            left, right, (((0,), (0,)), ((), ())), preferred_element_type=F32
        )

    def climb(k, level):
        child, parent, depth = roles(tree_of(k))

        @pl.when((k >= 0) & (k < chunks) & (depth == DEPTH - level))
        def _():
            @pl.when(k == 0)
            def _():
                total[...] = small_ref[...]

            @pl.when(k > 0)
            def _():
                product(k)

            if level > 0:
                for d in range(3):

                    @pl.when(child[d])
                    def _():
                        arrived(k, d)
                        total[...] += buf[d, k].astype(F32)

            buf[3, k] = total[...].astype(BF)
            if level < DEPTH:
                transfer(k, parent, 3).start()
            else:
                for d in range(3):

                    @pl.when(child[d])
                    def _():
                        transfer(k, d, 3).start()

                put(k, 3)

    def descend(k, level):
        child, parent, depth = roles(tree_of(k))

        @pl.when((k >= 0) & (k < chunks) & (depth == level))
        def _():
            arrived(k, parent)
            for d in range(3):

                @pl.when(child[d])
                def _():
                    transfer(k, d, parent).start()

            put(k, parent)

    def settle(k):
        child, parent, depth = roles(tree_of(k))
        for d in range(3):

            @pl.when(child[d] | (parent == d))
            def _():
                transfer(k, d, 3).wait_send()

        @pl.when(k > 0)
        def _():
            pltpu.make_async_copy(
                buf.at[3, k], d_ref.at[pl.ds(0, BLOCK), pl.ds(0, side)], out_sem.at[k]
            ).wait()

    def advance(t):
        for level in range(DEPTH + 1):
            climb(t - level * HOP, level)
        for level in range(1, DEPTH + 1):
            descend(t - (DEPTH + level) * HOP, level)

    def slots_down(c, d):
        return remote(
            rows.at[0, c], rows.at[0, c], r_send.at[d, c], r_recv.at[0, c],
            (neighbour(d), section),
        )

    def slots_across(c):
        return remote(
            rows.at[0, c], rows.at[1, c], r_send.at[3, c], r_recv.at[1, c], (me, other_layer)
        )

    def slots_beside(c, kind):
        return remote(
            rows.at[kind, c], rows.at[2 + kind, c], r_send.at[4 + kind, c],
            r_recv.at[2 + kind, c], (me, other_core),
        )

    def slots_got(c, kind):
        remote(
            rows.at[kind, c], rows.at[kind, c], r_send.at[0, c], r_recv.at[kind, c],
            (me, other_core),
        ).wait_recv()

    def share_slots(c, level):
        child, parent, depth = roles(rooted_at(c))

        @pl.when((c >= 0) & (c < GROUP) & (depth == level))
        def _():
            if level > 0:
                slots_got(c, 0)
            for d in range(3):

                @pl.when(child[d])
                def _():
                    slots_down(c, d).start()

            slots_across(c).start()
            slots_beside(c, 0).start()

    def relay_slots(c):
        @pl.when((c >= 0) & (c < GROUP))
        def _():
            slots_got(c, 1)
            slots_beside(c, 1).start()

    def table_up(c, d):
        there = facing(d)
        return remote(
            piece.at[3, c], piece.at[there, c], t_send.at[d, c], t_recv.at[there, c],
            (neighbour(d), section),
        )

    def table_out(c, step):
        to = (section + step) % n_sections
        return remote(
            piece.at[3, c, pl.ds(to * table.shape[1], table.shape[1])], table.at[section],
            f_send.at[step], f_recv.at[section], (me, to),
        )

    def table_climb(c, level):
        child, parent, depth = roles(rooted_at(c))

        @pl.when((c >= 0) & (c < GROUP) & (depth == DEPTH + 1 - level))
        def _():
            at = c * BLOCK + lax.broadcasted_iota(jnp.int32, (BLOCK, edge.shape[1]), 0)
            reach = edge.shape[1]
            for part in range(2):
                start = pl.multiple_of((half if part == 0 else 1 - half) * reach, reach)
                spots = box_ref[:, pl.ds(start, reach)]
                low_at = jnp.where(half == 0, spots[0:1], spots[1:2])
                high_at = jnp.where(half == 0, spots[2:3], spots[3:4])
                ones = (at == low_at).astype(F32) + (at == high_at).astype(F32)
                term = jnp.dot(ones.astype(BF), edge[part], preferred_element_type=F32)
                if part == 0:
                    total[...] = term
                else:
                    total[...] += term
            if level > 0:
                for d in range(3):

                    @pl.when(child[d])
                    def _():
                        remote(
                            piece.at[3, c], piece.at[d, c], t_send.at[0, c], t_recv.at[d, c],
                            (me, other_core),
                        ).wait_recv()
                        total[...] += piece[d, c].astype(F32)

            piece[3, c] = total[...].astype(BF)
            if level < DEPTH + 1:
                table_up(c, parent).start()
            else:
                for step in range(1, n_sections):
                    table_out(c, step).start()
                kept = table.shape[1]
                table[section] = piece[3, c, pl.ds(pl.multiple_of(section * kept, kept), kept)]

    def extras(t):
        c = t - EXTRA
        for level in range(DEPTH + 2):
            share_slots(c - level * HOP, level)
        relay_slots(c - (DEPTH + 3) * HOP)
        for level in range(DEPTH + 2):
            table_climb(c - GROUP - level * HOP, level)

    def settle_extras(c):
        child, parent, depth = roles(rooted_at(c))
        for d in range(3):

            @pl.when(child[d])
            def _():
                slots_down(c, d).wait_send()

            @pl.when(parent == d)
            def _():
                table_up(c, d).wait_send()

        slots_across(c).wait_send()
        for kind in range(2):
            slots_beside(c, kind).wait_send()
            slots_got(c, 2 + kind)

    def handed(step):
        return remote(
            gathered.at[0], gathered.at[step], g_send.at[step], g_recv.at[step],
            (me, (section + n_sections - step) % n_sections),
        )

    for copy in loads:
        copy.wait()
    loop(0, EXTRA, advance)

    @pl.when(layer == 1)
    def _():
        edge_across().wait_recv()
        edge_beside(edge.at[0]).start()

    edge_beside(edge.at[0]).wait_recv()
    used = listed_ref.shape[1]
    listed = listed_ref[...].astype(F32)
    square[...] = jnp.full_like(square, -1.0)
    square[0:1, :used] = jnp.where(half == 0, listed[0:1], listed[1:2])
    column = square[...].T[:, 0:1]
    wanted = column == lax.broadcasted_iota(jnp.int32, (slots, edge.shape[1]), 1).astype(F32)
    rows[0, place] = jnp.dot(
        wanted.astype(F32).astype(BF), edge[0], preferred_element_type=F32
    ).astype(BF)

    def both(t):
        advance(t)
        extras(t)

    middle = EXTRA + 2 * GROUP + (DEPTH + 3) * HOP
    loop(EXTRA, middle, both)
    mine = roles(tree_of(0))[1]
    kept_small = gathered.shape[1]
    gathered[0] = buf[mine, 0, :kept_small]
    for step in range(1, n_sections):
        handed(step).start()
    loop(middle, chunks + 2 * DEPTH * HOP, advance)
    loop(0, GROUP, settle_extras)
    for step in range(1, n_sections):
        handed(step).wait()
        table_out(place, step).wait_send()
        source = (section + n_sections - step) % n_sections
        remote(
            piece.at[3, 0, pl.ds(0, table.shape[1])], table.at[source], f_send.at[0],
            f_recv.at[source], (me, other_core),
        ).wait_recv()
    outs = (
        pltpu.make_async_copy(gathered, gathered_ref, last_sem.at[0]),
        pltpu.make_async_copy(rows, rows_ref, last_sem.at[1]),
        pltpu.make_async_copy(table, table_ref, last_sem.at[2]),
    )
    for copy in outs:
        copy.start()

    for r in range(2):
        for kind, target in ((0, ing_ref), (1, act_ref)):

            @pl.when((layer == kind) & (section != 2 * half + r))
            def _():
                spread(r, target, kind).wait_send()

            @pl.when((layer == kind) & (section == 2 * half + r))
            def _():
                keep(r, target).wait()

    for kind, target in ((0, ing_ref), (1, act_ref)):

        @pl.when(section != 2 * kind + layer)
        def _():
            spread(0, target, kind).wait_recv()

    @pl.when(layer == 0)
    def _():
        edge_across().wait_send()

    edge_beside(edge.at[0]).wait_send()
    loop(0, chunks, settle)
    for copy in outs:
        copy.wait()


def reduced(a, b, small, edge, mine, boxes, listed, counts, side):
    chunks = 1 + sum(count[0] * count[1] for count in counts)
    n_sections = lax.axis_size("section")
    kept = 32
    slots = BLOCK
    page = edge.shape[1]
    any_space = pl.BlockSpec(memory_space=pl.ANY)
    in_vmem = pl.BlockSpec(memory_space=pltpu.VMEM)
    flops = 2 * a.shape[0] * BLOCK * side * chunks
    dma = pltpu.SemaphoreType.DMA
    return pl.pallas_call(
        functools.partial(reduce_kernel, counts),
        out_shape=tuple(
            jax.ShapeDtypeStruct((count[0] * BLOCK, count[1] * side), BF) for count in counts
        )
        + (
            jax.ShapeDtypeStruct((n_sections, kept, side), BF),
            jax.ShapeDtypeStruct((4, GROUP, slots, side), BF),
            jax.ShapeDtypeStruct((n_sections, BLOCK // n_sections, side), BF),
            jax.ShapeDtypeStruct((mine.shape[0] // 2, mine.shape[1]), BF),
            jax.ShapeDtypeStruct((mine.shape[0] // 2, mine.shape[1]), BF),
        ),
        in_specs=[any_space] * 2 + [in_vmem] * 2 + [any_space] + [in_vmem] * 2,
        out_specs=(any_space,) * 9,
        scratch_shapes=[
            pltpu.VMEM(a.shape, BF),
            pltpu.VMEM(b.shape, BF),
            pltpu.VMEM((BLOCK, BLOCK), F32),
            pltpu.VMEM((4, chunks, BLOCK, side), BF),
            pltpu.VMEM((BLOCK, side), F32),
            pltpu.VMEM((n_sections, kept, side), BF),
            pltpu.VMEM((2, page, side), BF),
            pltpu.VMEM((4, GROUP, slots, side), BF),
            pltpu.VMEM((n_sections, BLOCK // n_sections, side), BF),
            pltpu.VMEM((4, GROUP, BLOCK, side), BF),
            dma((3, chunks)), dma((3, chunks)), dma((chunks,)),
            dma((n_sections,)), dma((n_sections,)),
            dma((2,)), dma((2,)),
            dma((6, GROUP)), dma((4, GROUP)),
            dma((3, GROUP)), dma((3, GROUP)),
            dma((n_sections,)), dma((n_sections,)),
            dma((2,)), dma((2,)),
            dma((3,)), dma((2,)),
        ],
        compiler_params=pltpu.CompilerParams(
            collective_id=0, has_side_effects=True, vmem_limit_bytes=60 << 20
        ),
        cost_estimate=pl.CostEstimate(
            flops=flops, bytes_accessed=400 << 20, transcendentals=0
        ),
        name="gradient_sums",
    )(a, b, small, edge, mine, boxes, listed)


ROWS = 256


def encoder_kernel(
    words_ref, cot_ref, ids_ref, mask_ref, box_ref, vocab_ref, table_ref, gain_ref, shift_ref,
    q_own, o_own, u_own, d_own, qvb_own, upb_own, gains_ref, shifts_ref,
    a_ref, b_ref, ids_out, edge_ref, mine_ref, small_ref,
    words, ids_all, ids_wide, vocab, spots, picks, land, other, square, norm_in, facts,
    sums_ref, upb_sum, qvb_ref, upb_ref,
    wq, wo, wu, wd, wide, x_land, g_land, x_low, ctx, d_ctx, h_low, act, slope, qkv, d_qkv,
    da_low, df_low, probs, n_one, n_two, r_one, r_two, z, sent_low,
    o_w_send, o_w_recv, c_send, c_recv, i_send, i_recv, s_send, s_recv, o_send, o_recv, local,
    w_local, w_send, w_recv, x_send, x_recv, g_send, g_recv, p_local, p_send, p_recv,
):
    me = lax.axis_index("dp")
    section = lax.axis_index("section")
    n_sections = lax.axis_size("section")
    n_dp = ids_all.shape[0]
    layer = section // 2
    half = section % 2
    mesh_id = pl.DeviceIdType.MESH
    quarter = words_ref.shape[0]
    page, width = x_low.shape
    units = act.shape[2]
    blocks = page // ROWS
    tile = 512
    scale = HEAD_DIM ** (-0.5)
    beside = (me, section + 1 - 2 * half)
    across = (me, (section + 2) % n_sections)
    slots = picks.shape[1]
    side = picks.shape[2]
    held = vocab.shape[0]

    vocab_copy = pltpu.make_async_copy(
        vocab_ref.at[:, pl.ds(pl.multiple_of(layer * side, side), side)], vocab, local.at[0]
    )
    vocab_copy.start()
    table_copies = [
        pltpu.make_async_copy(
            table_ref.at[kind, pl.ds(part * page, page)],
            act.at[kind, :, pl.ds(part * width, width)],
            local.at[2 + 2 * kind + part],
        )
        for kind in range(2)
        for part in range(2)
    ]

    @pl.when(layer == 0)
    def _():
        for copy in table_copies:
            copy.start()

    ids_wide[...] = jnp.full_like(ids_wide, -1)
    ids_wide[:, :slots] = ids_ref[...]

    barrier = pltpu.get_barrier_semaphore()

    def greet(step, carry):
        pl.semaphore_signal(
            barrier, inc=1, device_id=((me + step) % n_dp, section), device_id_type=mesh_id
        )
        return carry

    lax.fori_loop(1, n_dp, greet, 0)
    for step in range(1, n_sections):
        pl.semaphore_signal(
            barrier, inc=1, device_id=(me, (section + step) % n_sections), device_id_type=mesh_id
        )
    pl.semaphore_wait(barrier, n_dp - 1 + n_sections - 1)

    def remote(source, target, sent, got, device):
        return pltpu.make_async_remote_copy(
            src_ref=source, dst_ref=target, send_sem=sent, recv_sem=got, device_id=device,
            device_id_type=mesh_id,
        )

    def weight_copies(i):
        source = (q_own, o_own, u_own, d_own, qvb_own, upb_own)[i].at[0]
        target = (wq, wo, wu, wd, qvb_ref, upb_ref)[i]
        return (
            pltpu.make_async_copy(source, target.at[0], w_local.at[i]),
            remote(source, target.at[1], w_send.at[i], w_recv.at[i], beside),
        )

    def weights_here(i):
        near, far = weight_copies(i)
        near.wait()
        far.wait_recv()

    def ids_move(step):
        return remote(
            ids_wide, ids_all.at[me], i_send.at[step], i_recv.at[me], ((me + step) % n_dp, section)
        )

    def ids_got(step):
        source = (me + step) % n_dp
        return remote(
            ids_wide, ids_all.at[source], i_send.at[0], i_recv.at[source],
            (me, (section + 1) % n_sections),
        )

    loop(1, n_dp, lambda step: ids_move(step).start())
    ids_all[me] = ids_wide[...]

    words_move = remote(
        words_ref, words.at[half], o_w_send, o_w_recv.at[half], (me, layer)
    )
    given_part = g_land.at[pl.ds(pl.multiple_of(half * quarter, quarter), quarter)]
    given_move = remote(cot_ref, given_part, c_send, c_recv.at[half], (me, 2 + layer))
    given_keep = pltpu.make_async_copy(cot_ref, given_part, c_send)

    @pl.when(section != 0)
    def _():
        words_move.start()

    @pl.when(section == 0)
    def _():
        words[0] = words_ref[...]

    @pl.when(section != 3)
    def _():
        given_move.start()

    @pl.when(section == 3)
    def _():
        given_keep.start()

    for i in (0, 4, 5, 1, 2, 3):
        near, far = weight_copies(i)
        far.start()
        near.start()

    loop(1, n_dp, lambda step: ids_got(step).wait_recv())
    lists = ids_all[...].astype(F32)
    lists = jnp.where(half == 0, lists[:, 0], lists[:, 1])
    square[...] = jnp.zeros_like(square)
    square[0:n_dp] = lists
    listed = mask_ref[...].astype(F32)
    square[n_dp : n_dp + 1, :slots] = jnp.where(half == 0, listed[0:1], listed[1:2])
    turned = square[...].T
    at = (me * held + lax.broadcasted_iota(jnp.int32, (slots, held), 1)).astype(F32)
    for origin in range(n_dp):
        spots[origin * slots : (origin + 1) * slots] = (
            at == turned[:slots, origin : origin + 1]
        ).astype(F32).astype(BF)
    vocab_copy.wait()
    found = jnp.dot(spots[...], vocab[...], preferred_element_type=F32).astype(BF)
    for origin in range(n_dp):
        picks[origin] = found[origin * slots : (origin + 1) * slots]

    def slots_move(step):
        to = (me + step) % n_dp
        return remote(
            picks.at[to], land.at[me], s_send.at[step], s_recv.at[me], (to, section)
        )

    def slots_got(step):
        source = (me + step) % n_dp
        return remote(
            picks.at[0], land.at[source], s_send.at[0], s_recv.at[source],
            (me, (section + 1) % n_sections),
        )

    loop(1, n_dp, lambda step: slots_move(step).start())
    land[me] = picks[me]

    @pl.when(layer == 0)
    def _():
        for copy in table_copies:
            copy.wait()
        coords = lax.broadcasted_iota(jnp.int32, (page, page), 0)
        for kind in range(2):
            low_at, high_at = (
                box_ref[i : i + 1, pl.ds(pl.multiple_of(half * page, page), page)]
                for i in (kind, kind + 2)
            )
            for part in range(2):
                at = coords + part * page
                ones = (at == low_at).astype(F32) + (at == high_at).astype(F32)
                term = lax.dot_general(
                    ones.astype(BF), act[kind, :, pl.ds(part * width, width)],
                    (((0,), (0,)), ((), ())), preferred_element_type=F32,
                )
                if kind + part == 0:
                    wide[...] = term
                else:
                    wide[...] += term

    loop(1, n_dp, lambda step: slots_got(step).wait_recv())
    mine = land[0]
    for origin in range(1, n_dp):
        mine = mine + land[origin]
    other[1] = mine
    other_move = remote(other.at[1], other.at[0], o_send, o_recv, (me, half))

    @pl.when(layer == 1)
    def _():
        other_move.start()

    @pl.when(layer == 0)
    def _():
        for r in range(2):

            @pl.when(section + r > 0)
            def _():
                remote(
                    words_ref, words.at[r], o_w_send, o_w_recv.at[r], (me, section + 1)
                ).wait_recv()

        places = lax.broadcasted_iota(jnp.int32, (slots, page), 1).astype(F32)
        chosen = (turned[:slots, n_dp : n_dp + 1] == places).astype(F32).astype(BF)

        def spread_out(right):
            return lax.dot_general(
                chosen, right, (((0,), (0,)), ((), ())), preferred_element_type=F32
            )

        marked = spread_out(jnp.ones((slots, BLOCK), BF))[:, 0:1]
        facts[1] = 1.0 - marked
        other_move.wait_recv()
        for part, values in ((0, other[1]), (1, other[0])):
            columns = pl.ds(part * side, side)
            wide[:, columns] += spread_out(values)
        for r in range(2):
            rows = pl.ds(r * quarter, quarter)
            kept = facts[1, rows]
            summed = wide[rows] + words[r].astype(F32) * kept
            center = summed - jnp.mean(summed, -1, keepdims=True)
            spread = jnp.mean(center * center, -1, keepdims=True)
            inverse = lax.rsqrt(spread + EPS)
            normed = center * inverse
            norm_in[rows] = normed
            facts[0, rows] = inverse
            wide[rows] = normed * gain_ref[...][None] + shift_ref[...][None]

    ids_copy = pltpu.make_async_copy(ids_all, ids_out, local.at[1])
    ids_copy.start()

    @pl.when(layer == 1)
    def _():
        for r in range(2):

            @pl.when(section + r < 4)
            def _():
                remote(
                    cot_ref, g_land.at[pl.ds(r * quarter, quarter)], c_send, c_recv.at[r],
                    (me, section - 1),
                ).wait_recv()

    @pl.when(section == 3)
    def _():
        given_keep.wait()

    def rows_of(block):
        return pl.ds(pl.multiple_of(block * ROWS, ROWS), ROWS)

    def x_move(block):
        rows = rows_of(block)
        return remote(
            sent_low.at[rows], x_land.at[rows], x_send.at[block], x_recv.at[block], across
        )

    def g_move(block):
        rows = rows_of(block)
        return remote(
            sent_low.at[rows], g_land.at[rows], g_send.at[block], g_recv.at[block], across
        )

    spans = (
        (a_ref, 0, width), (a_ref, width, side), (a_ref, width + side, width),
        (a_ref, 2 * width + side, units),
        (b_ref, 0, 3 * side), (b_ref, 3 * side, width), (b_ref, 3 * side + width, units),
        (b_ref, 3 * side + width + units, width),
    )

    def piece_copies(i):
        target, start, size = spans[i]
        source = (x_low, ctx, h_low, act, d_qkv, da_low, slope, df_low)[i]
        double = i in (1, 3, 4, 6)
        columns = pl.ds(start, size)
        return (
            pltpu.make_async_copy(
                source.at[0] if double else source, target.at[0, :, columns], p_local.at[i]
            ),
            remote(
                source.at[1] if double else source, target.at[1, :, columns], p_send.at[i],
                p_recv.at[i], beside,
            ),
        )

    def hand_out(*pieces):
        for i in pieces:
            near, far = piece_copies(i)
            far.start()
            near.start()

    def nt(left, right):
        return lax.dot_general(
            left, right, (((1,), (1,)), ((), ())), preferred_element_type=F32
        )

    def tn(left, right):
        return lax.dot_general(
            left, right, (((0,), (0,)), ((), ())), preferred_element_type=F32
        )

    def centred(values):
        center = values - jnp.mean(values, -1, keepdims=True)
        spread = jnp.mean(center * center, -1, keepdims=True)
        inverse = lax.rsqrt(spread + EPS)
        return center * inverse, inverse

    def pulled(grad, normed, inverse, gain):
        scaled = grad * gain
        return inverse * (
            scaled
            - jnp.mean(scaled, -1, keepdims=True)
            - normed * jnp.mean(scaled * normed, -1, keepdims=True)
        )

    def add_sum(row, values):
        sums_ref[row : row + 1] += jnp.sum(values, 0, keepdims=True)

    sums_ref[...] = jnp.zeros_like(sums_ref)
    upb_sum[...] = jnp.zeros_like(upb_sum)

    for i in (0, 4, 5):
        weights_here(i)

    def project(block):
        rows = rows_of(block)

        @pl.when(layer == 1)
        def _():
            x_move(block).wait_recv()
            wide[rows] = x_land[rows].astype(F32)

        low = wide[rows].astype(BF)
        x_low[rows] = low
        for slot in range(2):
            for c in range(3):
                part = pl.ds(c * side, side)
                value = jnp.dot(low, wq[slot, :, part], preferred_element_type=F32)
                if c != 1:
                    value = value + qvb_ref[slot, c // 2 : c // 2 + 1]
                qkv[slot, rows, part] = value.astype(BF)

    loop(0, blocks, project)
    hand_out(0)

    lane = lax.broadcasted_iota(jnp.int32, (1, 2 * HEAD_DIM), 1)
    masks = ((lane < HEAD_DIM).astype(F32).astype(BF), (lane >= HEAD_DIM).astype(F32).astype(BF))
    first_lane = lax.broadcasted_iota(jnp.int32, (page, 2 * HEAD_DIM), 1) < HEAD_DIM
    first_row = lax.broadcasted_iota(jnp.int32, (2 * HEAD_DIM, page), 0) < HEAD_DIM
    pairs = side // (2 * HEAD_DIM)

    def lanes(i, third):
        at = third * side + (i % pairs) * 2 * HEAD_DIM
        return pl.ds(pl.multiple_of(at, 2 * HEAD_DIM), 2 * HEAD_DIM)

    def attend(i):
        slot = i // pairs
        queries = qkv[slot, :, lanes(i, 0)] * jnp.asarray(scale, BF)
        keys = qkv[slot, :, lanes(i, 1)]
        values = qkv[slot, :, lanes(i, 2)]
        found = []
        for e in range(2):
            scores = nt(keys * masks[e], queries)
            expo = jnp.exp(scores - jnp.max(scores, 0, keepdims=True))
            share = 1.0 / jnp.sum(expo, 0, keepdims=True)
            low = (expo * share).astype(BF)
            probs[2 * i + e] = low
            found.append(tn(values, low))
        ctx[slot, :, lanes(i, 0)] = jnp.where(first_row, found[0], found[1]).T.astype(BF)

    loop(0, 2 * pairs, attend)
    hand_out(1)
    for i in range(1, 4):
        weights_here(i)

    def feed(block):
        rows = rows_of(block)
        attended = (
            jnp.dot(ctx[0, rows], wo[0], preferred_element_type=F32)
            + jnp.dot(ctx[1, rows], wo[1], preferred_element_type=F32)
            + shifts_ref[layer, 0:1]
        )
        normed, inverse = centred(wide[rows] + attended)
        n_one[rows] = normed
        r_one[rows] = inverse
        hidden = normed * gains_ref[layer, 0:1] + shifts_ref[layer, 1:2]
        z[rows] = hidden
        h_low[rows] = hidden.astype(BF)
        for slot in range(2):
            for c in range(units // tile):
                part = pl.ds(c * tile, tile)
                upper = (
                    jnp.dot(h_low[rows], wu[slot, :, part], preferred_element_type=F32)
                    + upb_ref[slot, :, part]
                )
                below = 0.5 * (1.0 + lax.erf(upper * ROOT_HALF))
                act[slot, rows, part] = (upper * below).astype(BF)
                slope[slot, rows, part] = (
                    below + upper * jnp.exp(-0.5 * upper * upper) * INV_ROOT_TWO_PI
                ).astype(BF)
        mixed = (
            jnp.dot(act[0, rows], wd[0], preferred_element_type=F32)
            + jnp.dot(act[1, rows], wd[1], preferred_element_type=F32)
            + shifts_ref[layer, 2:3]
        )
        normed, inverse = centred(z[rows] + mixed)
        n_two[rows] = normed
        r_two[rows] = inverse
        output = normed * gains_ref[layer, 1:2] + shifts_ref[layer, 3:4]
        sent_low[rows] = output.astype(BF)

        @pl.when(layer == 0)
        def _():
            x_move(block).start()

        @pl.when(layer == 1)
        def _():
            mine_ref[rows] = sent_low[rows]

    loop(0, blocks, feed)
    hand_out(2, 3)

    def feed_back(block):
        rows = rows_of(block)

        @pl.when(layer == 0)
        def _():
            g_move(block).wait_recv()

        grad = g_land[rows].astype(F32)
        normed = n_two[rows]
        add_sum(1, grad * normed)
        add_sum(5, grad)
        grad = pulled(grad, normed, r_two[rows], gains_ref[layer, 1:2])
        z[rows] = grad
        low = grad.astype(BF)
        df_low[rows] = low
        add_sum(4, low.astype(F32))
        for slot in range(2):
            for c in range(units // tile):
                part = pl.ds(c * tile, tile)
                term = nt(df_low[rows], wd[slot, part])
                term = (term * slope[slot, rows, part].astype(F32)).astype(BF)
                slope[slot, rows, part] = term
                upb_sum[slot : slot + 1, part] += jnp.sum(term.astype(F32), 0, keepdims=True)
        grad = z[rows] + nt(slope[0, rows], wu[0]) + nt(slope[1, rows], wu[1])
        normed = n_one[rows]
        add_sum(0, grad * normed)
        add_sum(3, grad)
        grad = pulled(grad, normed, r_one[rows], gains_ref[layer, 0:1])
        z[rows] = grad
        low = grad.astype(BF)
        da_low[rows] = low
        add_sum(2, low.astype(F32))
        for slot in range(2):
            d_ctx[slot, rows] = nt(da_low[rows], wo[slot]).astype(BF)

    loop(0, blocks, feed_back)
    hand_out(5, 6, 7)

    def attend_back(i):
        slot = i // pairs
        queries = qkv[slot, :, lanes(i, 0)]
        keys = qkv[slot, :, lanes(i, 1)]
        values = qkv[slot, :, lanes(i, 2)]
        grads = d_ctx[slot, :, lanes(i, 0)]
        d_q, d_k, d_v = [], [], []
        for e in range(2):
            low = probs[2 * i + e]
            share = low.astype(F32)
            term = share * nt(values * masks[e], grads)
            term = (term - share * jnp.sum(term, 0, keepdims=True)).astype(BF)
            d_k.append(jnp.dot(term, queries, preferred_element_type=F32))
            d_v.append(jnp.dot(low, grads, preferred_element_type=F32))
            d_q.append(tn(keys, term))
        d_qkv[slot, :, lanes(i, 0)] = (
            jnp.where(first_row, d_q[0], d_q[1]).T * scale
        ).astype(BF)
        d_qkv[slot, :, lanes(i, 1)] = (jnp.where(first_lane, d_k[0], d_k[1]) * scale).astype(BF)
        d_qkv[slot, :, lanes(i, 2)] = jnp.where(first_lane, d_v[0], d_v[1]).astype(BF)

    loop(0, 2 * pairs, attend_back)
    hand_out(4)

    def leave(block):
        rows = rows_of(block)
        grad = z[rows] + nt(d_qkv[0, rows], wq[0]) + nt(d_qkv[1, rows], wq[1])
        z[rows] = grad

        @pl.when(layer == 1)
        def _():
            sent_low[rows] = z[rows].astype(BF)
            g_move(block).start()

        @pl.when(layer == 0)
        def _():
            grad = z[rows]
            normed = norm_in[rows]
            add_sum(6, grad * normed)
            add_sum(7, grad)
            low = pulled(grad, normed, facts[0, rows], gain_ref[...][None]).astype(BF)
            edge_ref[0, rows] = low[:, :side]
            edge_ref[1, rows] = low[:, side:]
            mine_ref[rows] = (low.astype(F32) * facts[1, rows]).astype(BF)

    loop(0, blocks, leave)
    small_ref[...] = jnp.zeros_like(small_ref)
    pieces = units // side
    for slot in range(2):
        for i in range(2):
            part = pl.ds(2 * i * side, side)
            at = slot * (2 + pieces) + i
            small_ref[at : at + 1] = jnp.sum(
                d_qkv[slot, :, part].astype(F32), 0, keepdims=True
            )
        for i in range(pieces):
            at = slot * (2 + pieces) + 2 + i
            small_ref[at : at + 1] = upb_sum[slot : slot + 1, pl.ds(i * side, side)]
    for i in range(8):
        for j in range(2):
            at = 2 * (2 + pieces) + 2 * i + j
            small_ref[at : at + 1] = sums_ref[i : i + 1, pl.ds(j * side, side)]
    for block in range(blocks):

        @pl.when(layer == 0)
        def _():
            x_move(block).wait_send()

        @pl.when(layer == 1)
        def _():
            g_move(block).wait_send()

    for i in range(6):
        weight_copies(i)[1].wait_send()
    for i in range(8):
        near, far = piece_copies(i)
        near.wait()
        far.wait()


    @pl.when(layer == 1)
    def _():
        other_move.wait_send()

    @pl.when(section != 0)
    def _():
        words_move.wait_send()

    @pl.when(section != 3)
    def _():
        given_move.wait_send()

    loop(1, n_dp, lambda step: ids_move(step).wait_send())
    loop(1, n_dp, lambda step: slots_move(step).wait_send())
    ids_copy.wait()


def encoded(
    words, cot, ids, mask, boxes, vocab, table, gain, shift, weights, qvb, upb, gains, shifts
):
    quarter, width = words.shape
    page = 2 * quarter
    n_dp = lax.axis_size("dp")
    slots = ids.shape[1]
    held = vocab.shape[0]
    side = width // 2
    units = weights[3].shape[1]
    blocks = page // ROWS
    heads = width // HEAD_DIM
    any_space = pl.BlockSpec(memory_space=pl.ANY)
    in_vmem = pl.BlockSpec(memory_space=pltpu.VMEM)
    dma = pltpu.SemaphoreType.DMA
    vmem = pltpu.VMEM
    flops = 8 * page * width * (4 * width + 4 * units) * 2
    return pl.pallas_call(
        encoder_kernel,
        out_shape=(
            jax.ShapeDtypeStruct((2, page, 2 * width + side + units), BF),
            jax.ShapeDtypeStruct((2, page, 3 * side + 2 * width + units), BF),
            jax.ShapeDtypeStruct((n_dp, 2, BLOCK), jnp.int32),
            jax.ShapeDtypeStruct((2, page, side), BF),
            jax.ShapeDtypeStruct((page, width), BF),
            jax.ShapeDtypeStruct((BLOCK, side), F32),
        ),
        in_specs=[in_vmem, any_space] + [in_vmem] * 3 + [any_space] * 2 + [in_vmem] * 2
        + [any_space] * 6 + [in_vmem] * 2,
        out_specs=(any_space,) * 3 + (in_vmem,) * 3,
        scratch_shapes=[
            vmem((2, quarter, width), BF), vmem((n_dp, 2, BLOCK), jnp.int32),
            vmem((2, BLOCK), jnp.int32),
            vmem((held, side), BF), vmem((n_dp * slots, held), BF),
            vmem((n_dp, slots, side), BF), vmem((n_dp, slots, side), BF),
            vmem((2, slots, side), BF), vmem((BLOCK, BLOCK), F32),
            vmem((page, width), F32), vmem((2, page, 1), F32),
            vmem((8, width), F32), vmem((2, units), F32),
            vmem((2, 2, side), F32), vmem((2, 1, units), F32),
            vmem((2, width, 3 * side), BF), vmem((2, side, width), BF),
            vmem((2, width, units), BF), vmem((2, units, width), BF),
            vmem((page, width), F32), vmem((page, width), BF), vmem((page, width), BF),
            vmem((page, width), BF), vmem((2, page, side), BF), vmem((2, page, side), BF),
            vmem((page, width), BF), vmem((2, page, units), BF), vmem((2, page, units), BF),
            vmem((2, page, 3 * side), BF), vmem((2, page, 3 * side), BF),
            vmem((page, width), BF), vmem((page, width), BF), vmem((heads, page, page), BF),
            vmem((page, width), F32), vmem((page, width), F32),
            vmem((page, 1), F32), vmem((page, 1), F32),
            vmem((page, width), F32), vmem((page, width), BF),
            dma, dma((2,)), dma, dma((2,)), dma((n_dp,)), dma((n_dp,)),
            dma((n_dp,)), dma((n_dp,)), dma, dma, dma((6,)),
            dma((6,)), dma((6,)), dma((6,)),
            dma((blocks,)), dma((blocks,)), dma((blocks,)), dma((blocks,)),
            dma((8,)), dma((8,)), dma((8,)),
        ],
        compiler_params=pltpu.CompilerParams(
            collective_id=1, has_side_effects=True, vmem_limit_bytes=63 << 20
        ),
        cost_estimate=pl.CostEstimate(
            flops=flops, bytes_accessed=200 << 20, transcendentals=0
        ),
        name="encoder_both_ways",
    )(words, cot, ids, mask, boxes, vocab, table, gain, shift, *weights, qvb, upb, gains, shifts)


def finish_kernel(
    pieces, q_in, o_in, u_in, d_in, rows_in, ids_ref, small_ref, table_ref, act_in, ing_in,
    act_ref, ing_ref, tab_ref, voc_ref, q_ref, qvb_ref, o_ref, u_ref, upb_ref, d_ref, gains_ref,
    shifts_ref, eg_ref, es_ref,
    q_s, o_s, u_s, d_s, q_f, o_f, u_f, d_f, rows_s, in_sem, out_sem, rows_sem,
):
    section = lax.axis_index("section")
    layer = section // 2
    half = section % 2
    side = rows_s.shape[3]
    n_dp = rows_s.shape[1]
    rows_copy = pltpu.make_async_copy(rows_in, rows_s, rows_sem)
    rows_copy.start()
    moves = []
    for source, low, wide, target in (
        (d_in, d_s, d_f, d_ref), (u_in, u_s, u_f, u_ref), (q_in, q_s, q_f, q_ref),
        (o_in, o_s, o_f, o_ref),
    ):
        count = low.shape[0] // pieces
        for i in range(pieces):
            rows = pl.ds(i * count, count)
            moves.append((source.at[rows], low.at[rows], wide.at[rows], target.at[0, rows]))
    for i, (source, low, wide, target) in enumerate(moves):
        pltpu.make_async_copy(source, low, in_sem.at[i]).start()

    act_ref[...] = act_in[...].astype(F32)
    ing_ref[...] = ing_in[...].astype(F32)

    parts = small_ref[...].astype(F32)
    partner = jnp.where(half == 0, parts[1], parts[3])
    far_partner = jnp.where(half == 0, parts[3], parts[1])
    splits = d_in.shape[0] // side
    kept = 2 + splits
    own = parts[0, :kept] + partner[kept : 2 * kept]
    qvb_ref[0] = own[:2]
    for i in range(splits):
        upb_ref[0:1, pl.ds(i * side, side)] = own[2 + i : 3 + i]
    here = (parts[0] + partner)[2 * kept : 2 * kept + 16]
    there = (parts[2] + far_partner)[2 * kept : 2 * kept + 16]
    in_order = (jnp.where(layer == 0, here, there), jnp.where(layer == 0, there, here))
    for j in range(2):
        columns = pl.ds(j * side, side)
        for l in range(2):
            for i in range(2):
                at = 2 * i + j
                gains_ref[l, i : i + 1, columns] = in_order[l][at : at + 1]
            for i in range(4):
                at = 4 + 2 * i + j
                shifts_ref[l, i : i + 1, columns] = in_order[l][at : at + 1]
        eg_ref[columns] = in_order[0][12 + j]
        es_ref[columns] = in_order[0][14 + j]
    for l in range(2):
        for h in range(2):
            tab_ref[h, :, pl.ds(l * side, side)] = table_ref[2 * l + h].astype(F32)

    for i, (source, low, wide, target) in enumerate(moves):
        pltpu.make_async_copy(source, low, in_sem.at[i]).wait()
        wide[...] = low[...].astype(F32)
        pltpu.make_async_copy(wide, target, out_sem.at[i]).start()

    count = voc_ref.shape[0]
    base = (lax.axis_index("dp") * lax.axis_size("section") + section) * count
    rows_copy.wait()
    at = base + lax.broadcasted_iota(jnp.int32, (count, BLOCK), 0)
    for h in range(2):
        list_at = jnp.where(half == 0, h, 1 - h)
        for group in range(n_dp // 4):
            spots = []
            for origin in range(group * 4, group * 4 + 4):
                row = ids_ref[origin]
                row = jnp.where(list_at == 0, row[0:1], row[1:2])
                spots.append((at == row).astype(F32).astype(BF))
            spots = jnp.concatenate(spots, 1)
            for l in range(2):
                rows = rows_s[2 * h + l, group * 4 : group * 4 + 4].reshape(4 * BLOCK, side)
                term = jnp.dot(spots, rows, preferred_element_type=F32)
                columns = pl.ds(
                    pl.multiple_of(jnp.where(layer == 0, l, 1 - l) * side, side), side
                )
                if h == 0 and group == 0:
                    voc_ref[:, columns] = term
                else:
                    voc_ref[:, columns] += term

    for i, (source, low, wide, target) in enumerate(moves):
        pltpu.make_async_copy(wide, target, out_sem.at[i]).wait()


def finished(sums, rows, ids, small, tables, act, ing, count, side):
    any_space = pl.BlockSpec(memory_space=pl.ANY)
    in_vmem = pl.BlockSpec(memory_space=pltpu.VMEM)
    dma = pltpu.SemaphoreType.DMA
    vmem = pltpu.VMEM
    pieces = 6
    width = act.shape[1]
    units = sums[3].shape[0]
    shapes = [array.shape for array in sums]
    outs = [
        jax.ShapeDtypeStruct(shape, F32)
        for shape in (
            act.shape, ing.shape, (2, tables.shape[1], width), (count, width), (1, *shapes[0]),
            (1, 2, side), (1, *shapes[1]), (1, *shapes[2]), (1, units), (1, *shapes[3]),
            (2, 2, width), (2, 4, width), (width,), (width,),
        )
    ]
    specs = [in_vmem] * 4 + [any_space, in_vmem, any_space, any_space, in_vmem, any_space] + [in_vmem] * 4
    return pl.pallas_call(
        functools.partial(finish_kernel, pieces),
        out_shape=outs,
        in_specs=[any_space] * 5 + [in_vmem] * 5,
        out_specs=specs,
        scratch_shapes=[vmem(shape, BF) for shape in shapes]
        + [vmem(shape, F32) for shape in shapes]
        + [vmem(rows.shape, BF), dma((4 * pieces,)), dma((4 * pieces,)), dma],
        compiler_params=pltpu.CompilerParams(vmem_limit_bytes=60 << 20),
        name="finished_outputs",
    )(*sums, rows, ids, small, tables, act, ing)


def on_device(
    word_embed, boxes, mask_pos, replace_ids, cotangent, layout_table, vocab_table, embed_gain,
    embed_shift, qkv_weight, qv_bias, out_weight, up_weight, up_bias, down_weight, layer_gains,
    layer_biases,
):
    section = lax.axis_index("section")
    layer = section // 2
    half = section % 2
    quarter, width = word_embed.shape
    page = 2 * quarter
    side = qkv_weight.shape[2] // 3
    units = up_bias.shape[1]

    left, right, all_ids, edge, mine, small = encoded(
        word_embed, cotangent, replace_ids, mask_pos, boxes, vocab_table, layout_table,
        embed_gain, embed_shift, (qkv_weight, out_weight, up_weight, down_weight), qv_bias,
        up_bias[:, None], layer_gains, layer_biases,
    )
    left, right = (array.reshape(2 * page, -1) for array in (left, right))
    counts = (
        (width // BLOCK, 3),
        (side // BLOCK, width // side),
        (width // BLOCK, units // side),
        (units // BLOCK, width // side),
    )
    *sums, gathered, slot_rows, table_rows, act, ing = reduced(
        left, right, small, edge, mine, boxes, mask_pos, counts, side
    )
    outer = lax.axis_size("dp") // GROUP
    table_part = None
    if outer > 1:
        groups = [[i + GROUP * g for g in range(outer)] for i in range(GROUP)]
        *sums, gathered = lax.psum((*sums, gathered), "dp", axis_index_groups=groups)
        slot_rows = lax.all_gather(slot_rows, "dp", axis_index_groups=groups, axis=1, tiled=True)
        coords = jnp.arange(layout_table.shape[1], dtype=jnp.int32)
        page_boxes = lax.dynamic_slice_in_dim(boxes, half * page, page, 1)
        grad_low = jnp.concatenate([edge[0], edge[1]], 1)
        grad_low = jnp.where(layer == 0, grad_low, jnp.zeros_like(grad_low))
        table_grad = jnp.stack(
            [
                matmul_left_t(
                    (page_boxes[a][:, None] == coords[None, :]).astype(BF)
                    + (page_boxes[a + 2][:, None] == coords[None, :]).astype(BF),
                    grad_low,
                )
                for a in (0, 1)
            ]
        )
        table_part = lax.psum_scatter(
            table_grad.astype(BF), ("dp", "section"), scatter_dimension=1, tiled=True
        ).astype(F32)
    count = vocab_table.shape[0] // lax.axis_size("section")
    act, ing, tables, vocab_part, *rest = finished(
        sums, slot_rows, all_ids, gathered, table_rows, act, ing, count, side
    )
    if table_part is None:
        table_part = tables
    *layer_sums, gains_sum, shifts_sum, gain_sum, shift_sum = rest
    return (
        act, ing, table_part, vocab_part, gain_sum, shift_sum, *layer_sums, gains_sum, shifts_sum,
    )


def solution(mesh):
    both = ("dp", "section")
    by_section = P("section", None, None)
    return jax.shard_map(
        on_device,
        mesh=mesh,
        in_specs=(
            P(both, None), P(None, "dp"), P("dp", None), P("dp", None), P(both, None), P(),
            P("dp", None), P(), P(), by_section, by_section, by_section, by_section,
            P("section", None), by_section, P(), P(),
        ),
        out_specs=(
            P(both, None), P(both, None), P(None, both, None), P(both, None), P(), P(),
            by_section, by_section, by_section, by_section, P("section", None), by_section,
            P(), P(),
        ),
        check_vma=False,
    )
```

```python
import functools

import jax
import jax.numpy as jnp
from jax import lax
from jax.experimental import pallas as pl
from jax.experimental.pallas import tpu as pltpu
from jax.sharding import PartitionSpec as P

HEAD_DIM = 64
EPS = 1e-12
ROOT_HALF = 0.7071067811865476
INV_ROOT_TWO_PI = 0.3989422804014327
BF = jnp.bfloat16
F32 = jnp.float32


def matmul_left_t(left, right):
    return jnp.einsum("pa,pb->ab", left, right, preferred_element_type=F32)


GROUP = 8
BLOCK = 128
HOP = 4
DEPTH = 3
FIRST = 20
EXTRA = 36
GUESTS = 6


def tree_of(k):
    turn = k % 8
    return turn < 4, 1 + turn % 2, (turn // 2) % 2


def rooted_at(c):
    return (c // 2) % 2 == 0, c // 2, c % 2


def loop(low, high, body):
    def step(k, carry):
        body(k)
        return carry

    lax.fori_loop(low, high, step, 0)


def reduce_kernel(
    counts, a_in, b_in, small_ref, edge_ref, mine_ref, box_ref, listed_ref, ids_ref,
    q_ref, o_ref, u_ref, d_ref, gathered_ref, rows_ref, table_ref, act_ref, ing_ref, voc_ref,
    a_ref, b_ref, square, buf, total, gathered, edge, rows, table, piece,
    send, recv, out_sem, g_send, g_recv, e_send, e_recv, r_send, r_recv, t_send, t_recv,
    f_send, f_recv, m_send, m_recv, last_sem, in_sem, voc, entered,
    away_send, away_recv, back_send, back_recv,
):
    a_cut = a_ref.shape[1] - counts[3][0] * BLOCK
    b_cut = b_ref.shape[1] - counts[3][1] * buf.shape[3]
    loads = []
    for columns_a, columns_b in (
        (pl.ds(a_cut, a_ref.shape[1] - a_cut), pl.ds(b_cut, b_ref.shape[1] - b_cut)),
        (pl.ds(0, a_cut), pl.ds(0, b_cut)),
    ):
        for source, target, columns in ((a_in, a_ref, columns_a), (b_in, b_ref, columns_b)):
            loads.append(
                pltpu.make_async_copy(
                    source.at[:, columns], target.at[:, columns], in_sem.at[len(loads)]
                )
            )
    for copy in loads:
        copy.start()
    me = lax.axis_index("dp")
    section = lax.axis_index("section")
    n_sections = lax.axis_size("section")
    layer = section // 2
    half = section % 2
    other_core = section + 1 - 2 * half
    other_layer = (section + 2) % n_sections
    place = me % GROUP
    z = place // 2
    y = place % 2
    chunks = buf.shape[1] - GUESTS
    limit = jnp.where(layer == 0, chunks - GUESTS, chunks + GUESTS)
    side = buf.shape[3]
    slots = rows.shape[2]
    n_q, n_o, n_u, n_d = counts
    ends = (n_d[0] * n_d[1],)
    ends += (ends[0] + n_u[0] * n_u[1],)
    ends += (ends[1] + n_o[0] * n_o[1],)
    mesh_id = pl.DeviceIdType.MESH
    deltas = (-2, 2, 1 - 2 * y)
    exists = (z > 0, z < GROUP // 2 - 1, y >= 0)

    barrier = pltpu.get_barrier_semaphore()
    for d in range(3):

        @pl.when(exists[d])
        def _():
            pl.semaphore_signal(
                barrier, inc=1, device_id=(me + deltas[d], section), device_id_type=mesh_id
            )

    pl.semaphore_signal(barrier, inc=1, device_id=(me, other_core), device_id_type=mesh_id)

    @pl.when(layer == 1)
    def _():
        for h in range(2):
            pl.semaphore_signal(barrier, inc=1, device_id=(me, h), device_id_type=mesh_id)

    around = 2 + jnp.where(exists[0], 1, 0) + jnp.where(exists[1], 1, 0)
    pl.semaphore_wait(barrier, around + jnp.where(layer == 0, 2, 0))

    @pl.when(layer == 0)
    def _():
        for h in range(2):
            pl.semaphore_signal(entered, inc=1, device_id=(me, 2 + h), device_id_type=mesh_id)

    def remote(source, target, sent, got, device):
        return pltpu.make_async_remote_copy(
            src_ref=source, dst_ref=target, send_sem=sent, recv_sem=got, device_id=device,
            device_id_type=mesh_id,
        )

    quarter = mine_ref.shape[0] // 2

    def spread(r, target, kind):
        return remote(
            mine_ref.at[pl.ds(r * quarter, quarter)], target, m_send.at[r], m_recv.at[kind],
            (me, 2 * half + r),
        )

    def keep(r, target):
        return pltpu.make_async_copy(
            mine_ref.at[pl.ds(r * quarter, quarter)], target, m_send.at[r]
        )

    def spread_all(kind, target):
        for r in range(2):

            @pl.when((layer == kind) & (section != 2 * half + r))
            def _():
                spread(r, target, kind).start()

            @pl.when((layer == kind) & (section == 2 * half + r))
            def _():
                keep(r, target).start()

    def edge_across():
        return remote(
            edge_ref.at[1], edge.at[0], e_send.at[0], e_recv.at[0], (me, other_layer)
        )

    def edge_beside(source):
        return remote(source, edge.at[1], e_send.at[1], e_recv.at[1], (me, other_core))

    @pl.when(layer == 0)
    def _():
        edge_across().start()
        edge_beside(edge_ref.at[0]).start()
        edge[0] = edge_ref[0]

    def roles(tree):
        comb, root_z, root_y = tree
        along = jnp.logical_or(jnp.logical_not(comb), y == root_y)
        across = jnp.logical_or(comb, z == root_z)
        child = (
            exists[0] & along & (z <= root_z),
            exists[1] & along & (z >= root_z),
            across & (y == root_y),
        )
        up_z = along & (z != root_z)
        up_y = across & (y != root_y)
        parent = jnp.where(up_z, jnp.where(z < root_z, 1, 0), jnp.where(up_y, 2, 3))
        depth = jnp.abs(z - root_z) + jnp.abs(y - root_y)
        return child, parent, depth

    def neighbour(d):
        return me + jnp.where(d == 0, deltas[0], jnp.where(d == 1, deltas[1], deltas[2]))

    def facing(d):
        return jnp.where(d == 2, 2, 1 - d)

    def transfer(k, d, source):
        there = facing(d)
        return remote(
            buf.at[source, k], buf.at[there, k], send.at[d, k], recv.at[there, k],
            (neighbour(d), section),
        )

    def arrived(k, d):
        remote(
            buf.at[3, k], buf.at[d, k], send.at[0, k], recv.at[d, k], (me, other_core)
        ).wait_recv()

    def put(k, source):
        kk = k - 1
        low = 0
        for target, count, high in (
            (d_ref, n_d, ends[0]), (u_ref, n_u, ends[1]), (o_ref, n_o, ends[2]),
            (q_ref, n_q, chunks - 1),
        ):

            @pl.when((kk >= low) & (kk < high))
            def _():
                at = kk - low
                pltpu.make_async_copy(
                    buf.at[source, k],
                    target.at[
                        pl.ds(pl.multiple_of(at // count[1] * BLOCK, BLOCK), BLOCK),
                        pl.ds(pl.multiple_of(at % count[1] * side, BLOCK), side),
                    ],
                    out_sem.at[k],
                ).start()

            low = high

    def product(k):
        kd = k - 1
        in_d = kd < ends[0]
        ku = kd - ends[0]
        in_u = kd < ends[1]
        ko = kd - ends[1]
        in_o = kd < ends[2]
        kq = kd - ends[2]
        a_at = jnp.where(
            in_d,
            n_q[0] + n_o[0] + n_u[0] + kd // n_d[1],
            jnp.where(
                in_u,
                n_q[0] + n_o[0] + ku // n_u[1],
                jnp.where(in_o, n_q[0] + ko // n_o[1], kq // n_q[1]),
            ),
        )
        b_at = jnp.where(
            in_d,
            n_q[1] + n_o[1] + n_u[1] + kd % n_d[1],
            jnp.where(
                in_u,
                n_q[1] + n_o[1] + ku % n_u[1],
                jnp.where(in_o, n_q[1] + ko % n_o[1], kq % n_q[1]),
            ),
        )
        left = a_ref[:, pl.ds(pl.multiple_of(a_at * BLOCK, BLOCK), BLOCK)]
        right = b_ref[:, pl.ds(pl.multiple_of(b_at * side, BLOCK), side)]
        total[...] = lax.dot_general(
            left, right, (((0,), (0,)), ((), ())), preferred_element_type=F32
        )

    def away(g):
        return remote(
            buf.at[3, chunks - GUESTS + g], buf.at[3, chunks + g], away_send.at[g],
            away_recv.at[g], (me, other_layer),
        )

    def back(g, source):
        return remote(
            buf.at[source, chunks + g], buf.at[0, chunks - GUESTS + g], back_send.at[g],
            back_recv.at[g], (me, other_layer),
        )

    def finish(k, source):
        @pl.when(k < chunks)
        def _():
            put(k, source)

        @pl.when(k >= chunks)
        def _():
            back(k - chunks, source).start()

    def send_away(g):
        k = chunks - GUESTS + g
        product(k)
        buf[3, k] = total[...].astype(BF)
        away(g).start()

    def receive_back(g):
        back(g, 3).wait_recv()
        put(chunks - GUESTS + g, 0)

    def climb(k, level):
        child, parent, depth = roles(tree_of(k))

        @pl.when((k >= 0) & (k < limit) & (depth == DEPTH - level))
        def _():
            @pl.when(k == 0)
            def _():
                total[...] = small_ref[...]

            @pl.when((k > 0) & (k < chunks))
            def _():
                product(k)

            @pl.when(k >= chunks)
            def _():
                away(k - chunks).wait_recv()
                total[...] = buf[3, k].astype(F32)

            if level > 0:
                for d in range(3):

                    @pl.when(child[d])
                    def _():
                        arrived(k, d)
                        total[...] += buf[d, k].astype(F32)

            buf[3, k] = total[...].astype(BF)
            if level < DEPTH:
                transfer(k, parent, 3).start()
            else:
                for d in range(3):

                    @pl.when(child[d])
                    def _():
                        transfer(k, d, 3).start()

                finish(k, 3)

    def descend(k, level):
        child, parent, depth = roles(tree_of(k))

        @pl.when((k >= 0) & (k < limit) & (depth == level))
        def _():
            arrived(k, parent)
            for d in range(3):

                @pl.when(child[d])
                def _():
                    transfer(k, d, parent).start()

            finish(k, parent)

    def settle(k):
        child, parent, depth = roles(tree_of(k))
        for d in range(3):

            @pl.when(child[d] | (parent == d))
            def _():
                transfer(k, d, 3).wait_send()

        @pl.when((k > 0) & (k < chunks))
        def _():
            pltpu.make_async_copy(
                buf.at[3, k], d_ref.at[pl.ds(0, BLOCK), pl.ds(0, side)], out_sem.at[k]
            ).wait()

    def advance(t):
        for level in range(DEPTH + 1):
            climb(t - level * HOP, level)
        for level in range(1, DEPTH + 1):
            descend(t - (DEPTH + level) * HOP, level)

    def settle_away(g):
        pltpu.make_async_copy(
            buf.at[0, chunks - GUESTS + g], d_ref.at[pl.ds(0, BLOCK), pl.ds(0, side)],
            out_sem.at[chunks - GUESTS + g],
        ).wait()
        away(g).wait_send()

    def slots_down(c, d):
        return remote(
            rows.at[0, c], rows.at[0, c], r_send.at[d, c], r_recv.at[0, c],
            (neighbour(d), section),
        )

    def slots_across(c):
        return remote(
            rows.at[0, c], rows.at[1, c], r_send.at[3, c], r_recv.at[1, c], (me, other_layer)
        )

    def slots_beside(c, kind):
        return remote(
            rows.at[kind, c], rows.at[2 + kind, c], r_send.at[4 + kind, c],
            r_recv.at[2 + kind, c], (me, other_core),
        )

    def slots_got(c, kind):
        remote(
            rows.at[kind, c], rows.at[kind, c], r_send.at[0, c], r_recv.at[kind, c],
            (me, other_core),
        ).wait_recv()

    def share_slots(c, level):
        child, parent, depth = roles(rooted_at(c))

        @pl.when((c >= 0) & (c < GROUP) & (depth == level))
        def _():
            if level > 0:
                slots_got(c, 0)
            for d in range(3):

                @pl.when(child[d])
                def _():
                    slots_down(c, d).start()

            slots_across(c).start()
            slots_beside(c, 0).start()

    def relay_slots(c):
        @pl.when((c >= 0) & (c < GROUP))
        def _():
            slots_got(c, 1)
            slots_beside(c, 1).start()

    def table_up(c, d):
        there = facing(d)
        return remote(
            piece.at[3, c], piece.at[there, c], t_send.at[d, c], t_recv.at[there, c],
            (neighbour(d), section),
        )

    def table_out(c, step):
        to = (section + step) % n_sections
        return remote(
            piece.at[3, c, pl.ds(to * table.shape[1], table.shape[1])], table.at[section],
            f_send.at[step], f_recv.at[section], (me, to),
        )

    def table_climb(c, level):
        child, parent, depth = roles(rooted_at(c))

        @pl.when((c >= 0) & (c < GROUP) & (depth == DEPTH + 1 - level))
        def _():
            at = c * BLOCK + lax.broadcasted_iota(jnp.int32, (BLOCK, edge.shape[1]), 0)
            reach = edge.shape[1]
            for part in range(2):
                start = pl.multiple_of((half if part == 0 else 1 - half) * reach, reach)
                spots = box_ref[:, pl.ds(start, reach)]
                low_at = jnp.where(half == 0, spots[0:1], spots[1:2])
                high_at = jnp.where(half == 0, spots[2:3], spots[3:4])
                ones = (at == low_at).astype(F32) + (at == high_at).astype(F32)
                term = jnp.dot(ones.astype(BF), edge[part], preferred_element_type=F32)
                if part == 0:
                    total[...] = term
                else:
                    total[...] += term
            if level > 0:
                for d in range(3):

                    @pl.when(child[d])
                    def _():
                        remote(
                            piece.at[3, c], piece.at[d, c], t_send.at[0, c], t_recv.at[d, c],
                            (me, other_core),
                        ).wait_recv()
                        total[...] += piece[d, c].astype(F32)

            piece[3, c] = total[...].astype(BF)
            if level < DEPTH + 1:
                table_up(c, parent).start()
            else:
                for step in range(1, n_sections):
                    table_out(c, step).start()
                kept = table.shape[1]
                table[section] = piece[3, c, pl.ds(pl.multiple_of(section * kept, kept), kept)]

    def extras(t):
        c = t - EXTRA
        for level in range(DEPTH + 2):
            share_slots(c - level * HOP, level)
        relay_slots(c - (DEPTH + 3) * HOP)
        for level in range(DEPTH + 2):
            table_climb(c - GROUP - level * HOP, level)

    def settle_extras(c):
        child, parent, depth = roles(rooted_at(c))
        for d in range(3):

            @pl.when(child[d])
            def _():
                slots_down(c, d).wait_send()

            @pl.when(parent == d)
            def _():
                table_up(c, d).wait_send()

        slots_across(c).wait_send()
        for kind in range(2):
            slots_beside(c, kind).wait_send()

    count = voc.shape[0]
    base = (me * n_sections + section) * count

    def tokens(n):
        at = base + lax.broadcasted_iota(jnp.int32, (count, BLOCK), 0)
        first = lax.rem(half + n // 2, 2) == 0
        spots = []
        for origin in range(GROUP):
            row = ids_ref[origin]
            spots.append((at == jnp.where(first, row[0:1], row[1:2])).astype(F32).astype(BF))
        spots = jnp.concatenate(spots, 1)
        held = rows[n].reshape(GROUP * slots, side)
        term = jnp.dot(spots, held, preferred_element_type=F32)
        columns = pl.ds(pl.multiple_of(lax.rem(layer + n, 2) * side, side), side)

        @pl.when(n < 2)
        def _():
            voc[:, columns] = term

        @pl.when(n >= 2)
        def _():
            voc[:, columns] += term

    def handed(step):
        return remote(
            gathered.at[0], gathered.at[step], g_send.at[step], g_recv.at[step],
            (me, (section + n_sections - step) % n_sections),
        )

    for copy in loads[:2]:
        copy.wait()
    loop(0, FIRST, advance)
    for copy in loads[2:]:
        copy.wait()

    @pl.when(layer == 0)
    def _():
        loop(0, GUESTS, send_away)

    spread_all(0, ing_ref)
    loop(FIRST, EXTRA, advance)

    @pl.when(layer == 1)
    def _():
        pl.semaphore_wait(entered, 2)
        edge_across().wait_recv()
        edge_beside(edge.at[0]).start()

    spread_all(1, act_ref)
    edge_beside(edge.at[0]).wait_recv()
    used = listed_ref.shape[1]
    listed = listed_ref[...].astype(F32)
    square[...] = jnp.full_like(square, -1.0)
    square[0:1, :used] = jnp.where(half == 0, listed[0:1], listed[1:2])
    column = square[...].T[:, 0:1]
    wanted = column == lax.broadcasted_iota(jnp.int32, (slots, edge.shape[1]), 1).astype(F32)
    rows[0, place] = jnp.dot(
        wanted.astype(F32).astype(BF), edge[0], preferred_element_type=F32
    ).astype(BF)

    def both(t):
        advance(t)
        extras(t)

    middle = EXTRA + 2 * GROUP + (DEPTH + 3) * HOP
    loop(EXTRA, middle, both)
    mine = roles(tree_of(0))[1]
    kept_small = gathered.shape[1]
    gathered[0] = buf[mine, 0, :kept_small]
    for step in range(1, n_sections):
        handed(step).start()
    for c in range(GROUP):
        for kind in range(2):
            slots_got(c, 2 + kind)

    def late(t):
        advance(t)
        n = t - middle - 2

        @pl.when((n >= 0) & (n < 4))
        def _():
            tokens(n)

    loop(middle, limit + 2 * DEPTH * HOP, late)
    loop(0, GROUP, settle_extras)
    for step in range(1, n_sections):
        handed(step).wait()
        table_out(place, step).wait_send()
        source = (section + n_sections - step) % n_sections
        remote(
            piece.at[3, 0, pl.ds(0, table.shape[1])], table.at[source], f_send.at[0],
            f_recv.at[source], (me, other_core),
        ).wait_recv()
    outs = (
        pltpu.make_async_copy(gathered, gathered_ref, last_sem.at[0]),
        pltpu.make_async_copy(rows, rows_ref, last_sem.at[1]),
        pltpu.make_async_copy(table, table_ref, last_sem.at[2]),
        pltpu.make_async_copy(voc, voc_ref, last_sem.at[3]),
    )
    for copy in outs:
        copy.start()

    for r in range(2):
        for kind, target in ((0, ing_ref), (1, act_ref)):

            @pl.when((layer == kind) & (section != 2 * half + r))
            def _():
                spread(r, target, kind).wait_send()

            @pl.when((layer == kind) & (section == 2 * half + r))
            def _():
                keep(r, target).wait()

    for kind, target in ((0, ing_ref), (1, act_ref)):

        @pl.when(section != 2 * kind + layer)
        def _():
            spread(0, target, kind).wait_recv()

    @pl.when(layer == 0)
    def _():
        edge_across().wait_send()

    edge_beside(edge.at[0]).wait_send()
    loop(0, limit, settle)

    @pl.when(layer == 0)
    def _():
        loop(0, GUESTS, receive_back)
        loop(0, GUESTS, settle_away)

    @pl.when(layer == 1)
    def _():
        loop(0, GUESTS, lambda g: back(g, 3).wait_send())

    for copy in outs:
        copy.wait()


def reduced(a, b, small, edge, mine, boxes, listed, ids, count, counts, side):
    chunks = 1 + sum(count[0] * count[1] for count in counts)
    n_sections = lax.axis_size("section")
    kept = 32
    slots = BLOCK
    page = edge.shape[1]
    any_space = pl.BlockSpec(memory_space=pl.ANY)
    in_vmem = pl.BlockSpec(memory_space=pltpu.VMEM)
    flops = 2 * a.shape[0] * BLOCK * side * chunks
    dma = pltpu.SemaphoreType.DMA
    return pl.pallas_call(
        functools.partial(reduce_kernel, counts),
        out_shape=tuple(
            jax.ShapeDtypeStruct((count[0] * BLOCK, count[1] * side), BF) for count in counts
        )
        + (
            jax.ShapeDtypeStruct((n_sections, kept, side), BF),
            jax.ShapeDtypeStruct((4, GROUP, slots, side), BF),
            jax.ShapeDtypeStruct((n_sections, BLOCK // n_sections, side), BF),
            jax.ShapeDtypeStruct((mine.shape[0] // 2, mine.shape[1]), BF),
            jax.ShapeDtypeStruct((mine.shape[0] // 2, mine.shape[1]), BF),
            jax.ShapeDtypeStruct((count, mine.shape[1]), F32),
        ),
        in_specs=[any_space] * 2 + [in_vmem] * 2 + [any_space] + [in_vmem] * 3,
        out_specs=(any_space,) * 10,
        scratch_shapes=[
            pltpu.VMEM(a.shape, BF),
            pltpu.VMEM(b.shape, BF),
            pltpu.VMEM((BLOCK, BLOCK), F32),
            pltpu.VMEM((4, chunks + GUESTS, BLOCK, side), BF),
            pltpu.VMEM((BLOCK, side), F32),
            pltpu.VMEM((n_sections, kept, side), BF),
            pltpu.VMEM((2, page, side), BF),
            pltpu.VMEM((4, GROUP, slots, side), BF),
            pltpu.VMEM((n_sections, BLOCK // n_sections, side), BF),
            pltpu.VMEM((4, GROUP, BLOCK, side), BF),
            dma((3, chunks + GUESTS)), dma((3, chunks + GUESTS)), dma((chunks,)),
            dma((n_sections,)), dma((n_sections,)),
            dma((2,)), dma((2,)),
            dma((6, GROUP)), dma((4, GROUP)),
            dma((3, GROUP)), dma((3, GROUP)),
            dma((n_sections,)), dma((n_sections,)),
            dma((2,)), dma((2,)),
            dma((4,)), dma((4,)),
            pltpu.VMEM((count, mine.shape[1]), F32),
            pltpu.SemaphoreType.REGULAR,
            dma((GUESTS,)), dma((GUESTS,)), dma((GUESTS,)), dma((GUESTS,)),
        ],
        compiler_params=pltpu.CompilerParams(
            collective_id=0, has_side_effects=True, vmem_limit_bytes=60 << 20
        ),
        cost_estimate=pl.CostEstimate(
            flops=flops, bytes_accessed=400 << 20, transcendentals=0
        ),
        name="gradient_sums",
    )(a, b, small, edge, mine, boxes, listed, ids)


ROWS = 256


def encoder_kernel(
    words_ref, cot_ref, ids_ref, mask_ref, box_ref, vocab_ref, table_ref, gain_ref, shift_ref,
    q_own, o_own, u_own, d_own, qvb_own, upb_own, gains_ref, shifts_ref,
    a_ref, b_ref, ids_out, edge_ref, mine_ref, small_ref,
    words, ids_all, ids_wide, vocab, spots, picks, land, other, square, norm_in, facts,
    sums_ref, upb_sum, qvb_ref, upb_ref,
    wq, wo, wu, wd, wide, x_land, g_land, x_low, ctx, d_ctx, h_low, act, slope, qkv, d_qkv,
    da_low, df_low, probs, n_one, n_two, r_one, r_two, z, sent_low,
    o_w_send, o_w_recv, c_send, c_recv, i_send, i_recv, s_send, s_recv, o_send, o_recv, local,
    w_local, w_send, w_recv, x_send, x_recv, g_send, g_recv, p_local, p_send, p_recv,
):
    me = lax.axis_index("dp")
    section = lax.axis_index("section")
    n_sections = lax.axis_size("section")
    n_dp = ids_all.shape[0]
    layer = section // 2
    half = section % 2
    mesh_id = pl.DeviceIdType.MESH
    quarter = words_ref.shape[0]
    page, width = x_low.shape
    units = act.shape[2]
    blocks = page // ROWS
    tile = 512
    scale = HEAD_DIM ** (-0.5)
    beside = (me, section + 1 - 2 * half)
    across = (me, (section + 2) % n_sections)
    slots = picks.shape[1]
    side = picks.shape[2]
    held = vocab.shape[0]

    vocab_copy = pltpu.make_async_copy(
        vocab_ref.at[:, pl.ds(pl.multiple_of(layer * side, side), side)], vocab, local.at[0]
    )
    vocab_copy.start()
    table_copies = [
        pltpu.make_async_copy(
            table_ref.at[kind, pl.ds(part * page, page)],
            act.at[kind, :, pl.ds(part * width, width)],
            local.at[2 + 2 * kind + part],
        )
        for kind in range(2)
        for part in range(2)
    ]

    @pl.when(layer == 0)
    def _():
        for copy in table_copies:
            copy.start()

    ids_wide[...] = jnp.full_like(ids_wide, -1)
    ids_wide[:, :slots] = ids_ref[...]

    barrier = pltpu.get_barrier_semaphore()

    def greet(step, carry):
        pl.semaphore_signal(
            barrier, inc=1, device_id=((me + step) % n_dp, section), device_id_type=mesh_id
        )
        return carry

    lax.fori_loop(1, n_dp, greet, 0)
    for step in range(1, n_sections):
        pl.semaphore_signal(
            barrier, inc=1, device_id=(me, (section + step) % n_sections), device_id_type=mesh_id
        )
    pl.semaphore_wait(barrier, n_dp - 1 + n_sections - 1)

    def remote(source, target, sent, got, device):
        return pltpu.make_async_remote_copy(
            src_ref=source, dst_ref=target, send_sem=sent, recv_sem=got, device_id=device,
            device_id_type=mesh_id,
        )

    def weight_copies(i):
        source = (q_own, o_own, u_own, d_own, qvb_own, upb_own)[i].at[0]
        target = (wq, wo, wu, wd, qvb_ref, upb_ref)[i]
        return (
            pltpu.make_async_copy(source, target.at[0], w_local.at[i]),
            remote(source, target.at[1], w_send.at[i], w_recv.at[i], beside),
        )

    def weights_here(i):
        near, far = weight_copies(i)
        near.wait()
        far.wait_recv()

    def ids_move(step):
        return remote(
            ids_wide, ids_all.at[me], i_send.at[step], i_recv.at[me], ((me + step) % n_dp, section)
        )

    def ids_got(step):
        source = (me + step) % n_dp
        return remote(
            ids_wide, ids_all.at[source], i_send.at[0], i_recv.at[source],
            (me, (section + 1) % n_sections),
        )

    loop(1, n_dp, lambda step: ids_move(step).start())
    ids_all[me] = ids_wide[...]

    words_move = remote(
        words_ref, words.at[half], o_w_send, o_w_recv.at[half], (me, layer)
    )
    given_part = g_land.at[pl.ds(pl.multiple_of(half * quarter, quarter), quarter)]
    given_move = remote(cot_ref, given_part, c_send, c_recv.at[half], (me, 2 + layer))
    given_keep = pltpu.make_async_copy(cot_ref, given_part, c_send)

    @pl.when(section != 0)
    def _():
        words_move.start()

    @pl.when(section == 0)
    def _():
        words[0] = words_ref[...]

    @pl.when(section != 3)
    def _():
        given_move.start()

    @pl.when(section == 3)
    def _():
        given_keep.start()

    for i in (0, 4, 5, 1, 2, 3):
        near, far = weight_copies(i)
        far.start()
        near.start()

    loop(1, n_dp, lambda step: ids_got(step).wait_recv())
    lists = ids_all[...].astype(F32)
    lists = jnp.where(half == 0, lists[:, 0], lists[:, 1])
    square[...] = jnp.zeros_like(square)
    square[0:n_dp] = lists
    listed = mask_ref[...].astype(F32)
    square[n_dp : n_dp + 1, :slots] = jnp.where(half == 0, listed[0:1], listed[1:2])
    turned = square[...].T
    at = (me * held + lax.broadcasted_iota(jnp.int32, (slots, held), 1)).astype(F32)
    for origin in range(n_dp):
        spots[origin * slots : (origin + 1) * slots] = (
            at == turned[:slots, origin : origin + 1]
        ).astype(F32).astype(BF)
    vocab_copy.wait()
    found = jnp.dot(spots[...], vocab[...], preferred_element_type=F32).astype(BF)
    for origin in range(n_dp):
        picks[origin] = found[origin * slots : (origin + 1) * slots]

    def slots_move(step):
        to = (me + step) % n_dp
        return remote(
            picks.at[to], land.at[me], s_send.at[step], s_recv.at[me], (to, section)
        )

    def slots_got(step):
        source = (me + step) % n_dp
        return remote(
            picks.at[0], land.at[source], s_send.at[0], s_recv.at[source],
            (me, (section + 1) % n_sections),
        )

    loop(1, n_dp, lambda step: slots_move(step).start())
    land[me] = picks[me]

    @pl.when(layer == 0)
    def _():
        for copy in table_copies:
            copy.wait()
        coords = lax.broadcasted_iota(jnp.int32, (page, page), 0)
        for kind in range(2):
            low_at, high_at = (
                box_ref[i : i + 1, pl.ds(pl.multiple_of(half * page, page), page)]
                for i in (kind, kind + 2)
            )
            for part in range(2):
                at = coords + part * page
                ones = (at == low_at).astype(F32) + (at == high_at).astype(F32)
                term = lax.dot_general(
                    ones.astype(BF), act[kind, :, pl.ds(part * width, width)],
                    (((0,), (0,)), ((), ())), preferred_element_type=F32,
                )
                if kind + part == 0:
                    wide[...] = term
                else:
                    wide[...] += term

    loop(1, n_dp, lambda step: slots_got(step).wait_recv())
    mine = land[0]
    for origin in range(1, n_dp):
        mine = mine + land[origin]
    other[1] = mine
    other_move = remote(other.at[1], other.at[0], o_send, o_recv, (me, half))

    @pl.when(layer == 1)
    def _():
        other_move.start()

    @pl.when(layer == 0)
    def _():
        for r in range(2):

            @pl.when(section + r > 0)
            def _():
                remote(
                    words_ref, words.at[r], o_w_send, o_w_recv.at[r], (me, section + 1)
                ).wait_recv()

        places = lax.broadcasted_iota(jnp.int32, (slots, page), 1).astype(F32)
        chosen = (turned[:slots, n_dp : n_dp + 1] == places).astype(F32).astype(BF)

        def spread_out(right):
            return lax.dot_general(
                chosen, right, (((0,), (0,)), ((), ())), preferred_element_type=F32
            )

        marked = spread_out(jnp.ones((slots, BLOCK), BF))[:, 0:1]
        facts[1] = 1.0 - marked
        other_move.wait_recv()
        for part, values in ((0, other[1]), (1, other[0])):
            columns = pl.ds(part * side, side)
            wide[:, columns] += spread_out(values)
        for r in range(2):
            rows = pl.ds(r * quarter, quarter)
            kept = facts[1, rows]
            summed = wide[rows] + words[r].astype(F32) * kept
            center = summed - jnp.mean(summed, -1, keepdims=True)
            spread = jnp.mean(center * center, -1, keepdims=True)
            inverse = lax.rsqrt(spread + EPS)
            normed = center * inverse
            norm_in[rows] = normed
            facts[0, rows] = inverse
            wide[rows] = normed * gain_ref[...][None] + shift_ref[...][None]

    ids_copy = pltpu.make_async_copy(ids_all, ids_out, local.at[1])
    ids_copy.start()

    @pl.when(layer == 1)
    def _():
        for r in range(2):

            @pl.when(section + r < 4)
            def _():
                remote(
                    cot_ref, g_land.at[pl.ds(r * quarter, quarter)], c_send, c_recv.at[r],
                    (me, section - 1),
                ).wait_recv()

    @pl.when(section == 3)
    def _():
        given_keep.wait()

    def rows_of(block):
        return pl.ds(pl.multiple_of(block * ROWS, ROWS), ROWS)

    def x_move(block):
        rows = rows_of(block)
        return remote(
            sent_low.at[rows], x_land.at[rows], x_send.at[block], x_recv.at[block], across
        )

    def g_move(block):
        rows = rows_of(block)
        return remote(
            sent_low.at[rows], g_land.at[rows], g_send.at[block], g_recv.at[block], across
        )

    spans = (
        (a_ref, 0, width), (a_ref, width, side), (a_ref, width + side, width),
        (a_ref, 2 * width + side, units),
        (b_ref, 0, 3 * side), (b_ref, 3 * side, width), (b_ref, 3 * side + width, units),
        (b_ref, 3 * side + width + units, width),
    )

    def piece_copies(i):
        target, start, size = spans[i]
        source = (x_low, ctx, h_low, act, d_qkv, da_low, slope, df_low)[i]
        double = i in (1, 3, 4, 6)
        columns = pl.ds(start, size)
        return (
            pltpu.make_async_copy(
                source.at[0] if double else source, target.at[0, :, columns], p_local.at[i]
            ),
            remote(
                source.at[1] if double else source, target.at[1, :, columns], p_send.at[i],
                p_recv.at[i], beside,
            ),
        )

    def hand_out(*pieces):
        for i in pieces:
            near, far = piece_copies(i)
            far.start()
            near.start()

    def nt(left, right):
        return lax.dot_general(
            left, right, (((1,), (1,)), ((), ())), preferred_element_type=F32
        )

    def tn(left, right):
        return lax.dot_general(
            left, right, (((0,), (0,)), ((), ())), preferred_element_type=F32
        )

    def centred(values):
        center = values - jnp.mean(values, -1, keepdims=True)
        spread = jnp.mean(center * center, -1, keepdims=True)
        inverse = lax.rsqrt(spread + EPS)
        return center * inverse, inverse

    def pulled(grad, normed, inverse, gain):
        scaled = grad * gain
        return inverse * (
            scaled
            - jnp.mean(scaled, -1, keepdims=True)
            - normed * jnp.mean(scaled * normed, -1, keepdims=True)
        )

    def add_sum(row, values):
        sums_ref[row : row + 1] += jnp.sum(values, 0, keepdims=True)

    sums_ref[...] = jnp.zeros_like(sums_ref)
    upb_sum[...] = jnp.zeros_like(upb_sum)

    for i in (0, 4, 5):
        weights_here(i)

    def project(block):
        rows = rows_of(block)

        @pl.when(layer == 1)
        def _():
            x_move(block).wait_recv()
            wide[rows] = x_land[rows].astype(F32)

        low = wide[rows].astype(BF)
        x_low[rows] = low
        for slot in range(2):
            for c in range(3):
                part = pl.ds(c * side, side)
                value = jnp.dot(low, wq[slot, :, part], preferred_element_type=F32)
                if c != 1:
                    value = value + qvb_ref[slot, c // 2 : c // 2 + 1]
                qkv[slot, rows, part] = value.astype(BF)

    loop(0, blocks, project)
    hand_out(0)

    lane = lax.broadcasted_iota(jnp.int32, (1, 2 * HEAD_DIM), 1)
    masks = ((lane < HEAD_DIM).astype(F32).astype(BF), (lane >= HEAD_DIM).astype(F32).astype(BF))
    first_lane = lax.broadcasted_iota(jnp.int32, (page, 2 * HEAD_DIM), 1) < HEAD_DIM
    first_row = lax.broadcasted_iota(jnp.int32, (2 * HEAD_DIM, page), 0) < HEAD_DIM
    pairs = side // (2 * HEAD_DIM)

    def lanes(i, third):
        at = third * side + (i % pairs) * 2 * HEAD_DIM
        return pl.ds(pl.multiple_of(at, 2 * HEAD_DIM), 2 * HEAD_DIM)

    def attend(i):
        slot = i // pairs
        queries = qkv[slot, :, lanes(i, 0)] * jnp.asarray(scale, BF)
        keys = qkv[slot, :, lanes(i, 1)]
        values = qkv[slot, :, lanes(i, 2)]
        found = []
        for e in range(2):
            scores = nt(keys * masks[e], queries)
            expo = jnp.exp(scores - jnp.max(scores, 0, keepdims=True))
            share = 1.0 / jnp.sum(expo, 0, keepdims=True)
            low = (expo * share).astype(BF)
            probs[2 * i + e] = low
            found.append(tn(values, low))
        ctx[slot, :, lanes(i, 0)] = jnp.where(first_row, found[0], found[1]).T.astype(BF)

    loop(0, 2 * pairs, attend)
    hand_out(1)
    for i in range(1, 4):
        weights_here(i)

    def feed(block):
        rows = rows_of(block)
        attended = (
            jnp.dot(ctx[0, rows], wo[0], preferred_element_type=F32)
            + jnp.dot(ctx[1, rows], wo[1], preferred_element_type=F32)
            + shifts_ref[layer, 0:1]
        )
        normed, inverse = centred(wide[rows] + attended)
        n_one[rows] = normed
        r_one[rows] = inverse
        hidden = normed * gains_ref[layer, 0:1] + shifts_ref[layer, 1:2]
        z[rows] = hidden
        h_low[rows] = hidden.astype(BF)
        for slot in range(2):
            for c in range(units // tile):
                part = pl.ds(c * tile, tile)
                upper = (
                    jnp.dot(h_low[rows], wu[slot, :, part], preferred_element_type=F32)
                    + upb_ref[slot, :, part]
                )
                below = 0.5 * (1.0 + lax.erf(upper * ROOT_HALF))
                act[slot, rows, part] = (upper * below).astype(BF)
                slope[slot, rows, part] = (
                    below + upper * jnp.exp(-0.5 * upper * upper) * INV_ROOT_TWO_PI
                ).astype(BF)
        mixed = (
            jnp.dot(act[0, rows], wd[0], preferred_element_type=F32)
            + jnp.dot(act[1, rows], wd[1], preferred_element_type=F32)
            + shifts_ref[layer, 2:3]
        )
        normed, inverse = centred(z[rows] + mixed)
        n_two[rows] = normed
        r_two[rows] = inverse
        output = normed * gains_ref[layer, 1:2] + shifts_ref[layer, 3:4]
        sent_low[rows] = output.astype(BF)

        @pl.when(layer == 0)
        def _():
            x_move(block).start()

        @pl.when(layer == 1)
        def _():
            mine_ref[rows] = sent_low[rows]

    loop(0, blocks, feed)
    hand_out(2, 3)

    def feed_back(block):
        rows = rows_of(block)

        @pl.when(layer == 0)
        def _():
            g_move(block).wait_recv()

        grad = g_land[rows].astype(F32)
        normed = n_two[rows]
        add_sum(1, grad * normed)
        add_sum(5, grad)
        grad = pulled(grad, normed, r_two[rows], gains_ref[layer, 1:2])
        z[rows] = grad
        low = grad.astype(BF)
        df_low[rows] = low
        add_sum(4, low.astype(F32))
        for slot in range(2):
            for c in range(units // tile):
                part = pl.ds(c * tile, tile)
                term = nt(df_low[rows], wd[slot, part])
                term = (term * slope[slot, rows, part].astype(F32)).astype(BF)
                slope[slot, rows, part] = term
                upb_sum[slot : slot + 1, part] += jnp.sum(term.astype(F32), 0, keepdims=True)
        grad = z[rows] + nt(slope[0, rows], wu[0]) + nt(slope[1, rows], wu[1])
        normed = n_one[rows]
        add_sum(0, grad * normed)
        add_sum(3, grad)
        grad = pulled(grad, normed, r_one[rows], gains_ref[layer, 0:1])
        z[rows] = grad
        low = grad.astype(BF)
        da_low[rows] = low
        add_sum(2, low.astype(F32))
        for slot in range(2):
            d_ctx[slot, rows] = nt(da_low[rows], wo[slot]).astype(BF)

    loop(0, blocks, feed_back)
    hand_out(5, 6, 7)

    def attend_back(i):
        slot = i // pairs
        queries = qkv[slot, :, lanes(i, 0)]
        keys = qkv[slot, :, lanes(i, 1)]
        values = qkv[slot, :, lanes(i, 2)]
        grads = d_ctx[slot, :, lanes(i, 0)]
        d_q, d_k, d_v = [], [], []
        for e in range(2):
            low = probs[2 * i + e]
            share = low.astype(F32)
            term = share * nt(values * masks[e], grads)
            term = (term - share * jnp.sum(term, 0, keepdims=True)).astype(BF)
            d_k.append(jnp.dot(term, queries, preferred_element_type=F32))
            d_v.append(jnp.dot(low, grads, preferred_element_type=F32))
            d_q.append(tn(keys, term))
        d_qkv[slot, :, lanes(i, 0)] = (
            jnp.where(first_row, d_q[0], d_q[1]).T * scale
        ).astype(BF)
        d_qkv[slot, :, lanes(i, 1)] = (jnp.where(first_lane, d_k[0], d_k[1]) * scale).astype(BF)
        d_qkv[slot, :, lanes(i, 2)] = jnp.where(first_lane, d_v[0], d_v[1]).astype(BF)

    loop(0, 2 * pairs, attend_back)
    hand_out(4)

    def leave(block):
        rows = rows_of(block)
        grad = z[rows] + nt(d_qkv[0, rows], wq[0]) + nt(d_qkv[1, rows], wq[1])
        z[rows] = grad

        @pl.when(layer == 1)
        def _():
            sent_low[rows] = z[rows].astype(BF)
            g_move(block).start()

        @pl.when(layer == 0)
        def _():
            grad = z[rows]
            normed = norm_in[rows]
            add_sum(6, grad * normed)
            add_sum(7, grad)
            low = pulled(grad, normed, facts[0, rows], gain_ref[...][None]).astype(BF)
            edge_ref[0, rows] = low[:, :side]
            edge_ref[1, rows] = low[:, side:]
            mine_ref[rows] = (low.astype(F32) * facts[1, rows]).astype(BF)

    loop(0, blocks, leave)
    small_ref[...] = jnp.zeros_like(small_ref)
    pieces = units // side
    for slot in range(2):
        for i in range(2):
            part = pl.ds(2 * i * side, side)
            at = slot * (2 + pieces) + i
            small_ref[at : at + 1] = jnp.sum(
                d_qkv[slot, :, part].astype(F32), 0, keepdims=True
            )
        for i in range(pieces):
            at = slot * (2 + pieces) + 2 + i
            small_ref[at : at + 1] = upb_sum[slot : slot + 1, pl.ds(i * side, side)]
    for i in range(8):
        for j in range(2):
            at = 2 * (2 + pieces) + 2 * i + j
            small_ref[at : at + 1] = sums_ref[i : i + 1, pl.ds(j * side, side)]
    for block in range(blocks):

        @pl.when(layer == 0)
        def _():
            x_move(block).wait_send()

        @pl.when(layer == 1)
        def _():
            g_move(block).wait_send()

    for i in range(6):
        weight_copies(i)[1].wait_send()
    for i in range(8):
        near, far = piece_copies(i)
        near.wait()
        far.wait()


    @pl.when(layer == 1)
    def _():
        other_move.wait_send()

    @pl.when(section != 0)
    def _():
        words_move.wait_send()

    @pl.when(section != 3)
    def _():
        given_move.wait_send()

    loop(1, n_dp, lambda step: ids_move(step).wait_send())
    loop(1, n_dp, lambda step: slots_move(step).wait_send())
    ids_copy.wait()


def encoded(
    words, cot, ids, mask, boxes, vocab, table, gain, shift, weights, qvb, upb, gains, shifts
):
    quarter, width = words.shape
    page = 2 * quarter
    n_dp = lax.axis_size("dp")
    slots = ids.shape[1]
    held = vocab.shape[0]
    side = width // 2
    units = weights[3].shape[1]
    blocks = page // ROWS
    heads = width // HEAD_DIM
    any_space = pl.BlockSpec(memory_space=pl.ANY)
    in_vmem = pl.BlockSpec(memory_space=pltpu.VMEM)
    dma = pltpu.SemaphoreType.DMA
    vmem = pltpu.VMEM
    flops = 8 * page * width * (4 * width + 4 * units) * 2
    return pl.pallas_call(
        encoder_kernel,
        out_shape=(
            jax.ShapeDtypeStruct((2, page, 2 * width + side + units), BF),
            jax.ShapeDtypeStruct((2, page, 3 * side + 2 * width + units), BF),
            jax.ShapeDtypeStruct((n_dp, 2, BLOCK), jnp.int32),
            jax.ShapeDtypeStruct((2, page, side), BF),
            jax.ShapeDtypeStruct((page, width), BF),
            jax.ShapeDtypeStruct((BLOCK, side), F32),
        ),
        in_specs=[in_vmem, any_space] + [in_vmem] * 3 + [any_space] * 2 + [in_vmem] * 2
        + [any_space] * 6 + [in_vmem] * 2,
        out_specs=(any_space,) * 3 + (in_vmem,) * 3,
        scratch_shapes=[
            vmem((2, quarter, width), BF), vmem((n_dp, 2, BLOCK), jnp.int32),
            vmem((2, BLOCK), jnp.int32),
            vmem((held, side), BF), vmem((n_dp * slots, held), BF),
            vmem((n_dp, slots, side), BF), vmem((n_dp, slots, side), BF),
            vmem((2, slots, side), BF), vmem((BLOCK, BLOCK), F32),
            vmem((page, width), F32), vmem((2, page, 1), F32),
            vmem((8, width), F32), vmem((2, units), F32),
            vmem((2, 2, side), F32), vmem((2, 1, units), F32),
            vmem((2, width, 3 * side), BF), vmem((2, side, width), BF),
            vmem((2, width, units), BF), vmem((2, units, width), BF),
            vmem((page, width), F32), vmem((page, width), BF), vmem((page, width), BF),
            vmem((page, width), BF), vmem((2, page, side), BF), vmem((2, page, side), BF),
            vmem((page, width), BF), vmem((2, page, units), BF), vmem((2, page, units), BF),
            vmem((2, page, 3 * side), BF), vmem((2, page, 3 * side), BF),
            vmem((page, width), BF), vmem((page, width), BF), vmem((heads, page, page), BF),
            vmem((page, width), F32), vmem((page, width), F32),
            vmem((page, 1), F32), vmem((page, 1), F32),
            vmem((page, width), F32), vmem((page, width), BF),
            dma, dma((2,)), dma, dma((2,)), dma((n_dp,)), dma((n_dp,)),
            dma((n_dp,)), dma((n_dp,)), dma, dma, dma((6,)),
            dma((6,)), dma((6,)), dma((6,)),
            dma((blocks,)), dma((blocks,)), dma((blocks,)), dma((blocks,)),
            dma((8,)), dma((8,)), dma((8,)),
        ],
        compiler_params=pltpu.CompilerParams(
            collective_id=1, has_side_effects=True, vmem_limit_bytes=63 << 20
        ),
        cost_estimate=pl.CostEstimate(
            flops=flops, bytes_accessed=200 << 20, transcendentals=0
        ),
        name="encoder_both_ways",
    )(words, cot, ids, mask, boxes, vocab, table, gain, shift, *weights, qvb, upb, gains, shifts)


def finish_kernel(
    pieces, q_in, o_in, u_in, d_in, voc_in, small_ref, table_ref, act_in, ing_in,
    act_ref, ing_ref, tab_ref, voc_ref, q_ref, qvb_ref, o_ref, u_ref, upb_ref, d_ref, gains_ref,
    shifts_ref, eg_ref, es_ref,
    q_s, o_s, u_s, d_s, q_f, o_f, u_f, d_f, in_sem, out_sem, voc_s, voc_sem,
):
    section = lax.axis_index("section")
    layer = section // 2
    half = section % 2
    side = table_ref.shape[2]
    voc_copy = pltpu.make_async_copy(voc_in, voc_s, voc_sem.at[0])
    voc_copy.start()
    moves = []
    for source, low, wide, target in (
        (d_in, d_s, d_f, d_ref), (u_in, u_s, u_f, u_ref), (q_in, q_s, q_f, q_ref),
        (o_in, o_s, o_f, o_ref),
    ):
        count = low.shape[0] // pieces
        for i in range(pieces):
            rows = pl.ds(i * count, count)
            moves.append((source.at[rows], low.at[rows], wide.at[rows], target.at[0, rows]))
    for i, (source, low, wide, target) in enumerate(moves):
        pltpu.make_async_copy(source, low, in_sem.at[i]).start()

    voc_copy.wait()
    voc_out = pltpu.make_async_copy(voc_s, voc_ref, voc_sem.at[1])
    voc_out.start()
    act_ref[...] = act_in[...].astype(F32)
    ing_ref[...] = ing_in[...].astype(F32)

    parts = small_ref[...].astype(F32)
    partner = jnp.where(half == 0, parts[1], parts[3])
    far_partner = jnp.where(half == 0, parts[3], parts[1])
    splits = d_in.shape[0] // side
    kept = 2 + splits
    own = parts[0, :kept] + partner[kept : 2 * kept]
    qvb_ref[0] = own[:2]
    for i in range(splits):
        upb_ref[0:1, pl.ds(i * side, side)] = own[2 + i : 3 + i]
    here = (parts[0] + partner)[2 * kept : 2 * kept + 16]
    there = (parts[2] + far_partner)[2 * kept : 2 * kept + 16]
    in_order = (jnp.where(layer == 0, here, there), jnp.where(layer == 0, there, here))
    for j in range(2):
        columns = pl.ds(j * side, side)
        for l in range(2):
            for i in range(2):
                at = 2 * i + j
                gains_ref[l, i : i + 1, columns] = in_order[l][at : at + 1]
            for i in range(4):
                at = 4 + 2 * i + j
                shifts_ref[l, i : i + 1, columns] = in_order[l][at : at + 1]
        eg_ref[columns] = in_order[0][12 + j]
        es_ref[columns] = in_order[0][14 + j]
    for l in range(2):
        for h in range(2):
            tab_ref[h, :, pl.ds(l * side, side)] = table_ref[2 * l + h].astype(F32)

    for i, (source, low, wide, target) in enumerate(moves):
        pltpu.make_async_copy(source, low, in_sem.at[i]).wait()
        wide[...] = low[...].astype(F32)
        pltpu.make_async_copy(wide, target, out_sem.at[i]).start()

    for i, (source, low, wide, target) in enumerate(moves):
        pltpu.make_async_copy(wide, target, out_sem.at[i]).wait()
    voc_out.wait()


def finished(sums, voc, small, tables, act, ing, side):
    any_space = pl.BlockSpec(memory_space=pl.ANY)
    in_vmem = pl.BlockSpec(memory_space=pltpu.VMEM)
    dma = pltpu.SemaphoreType.DMA
    vmem = pltpu.VMEM
    pieces = 6
    width = act.shape[1]
    units = sums[3].shape[0]
    shapes = [array.shape for array in sums]
    outs = [
        jax.ShapeDtypeStruct(shape, F32)
        for shape in (
            act.shape, ing.shape, (2, tables.shape[1], width), voc.shape, (1, *shapes[0]),
            (1, 2, side), (1, *shapes[1]), (1, *shapes[2]), (1, units), (1, *shapes[3]),
            (2, 2, width), (2, 4, width), (width,), (width,),
        )
    ]
    specs = [in_vmem] * 3 + [any_space] * 2 + [in_vmem, any_space, any_space, in_vmem, any_space] + [in_vmem] * 4
    return pl.pallas_call(
        functools.partial(finish_kernel, pieces),
        out_shape=outs,
        in_specs=[any_space] * 5 + [in_vmem] * 4,
        out_specs=specs,
        scratch_shapes=[vmem(shape, BF) for shape in shapes]
        + [vmem(shape, F32) for shape in shapes]
        + [dma((4 * pieces,)), dma((4 * pieces,)), vmem(voc.shape, F32), dma((2,))],
        compiler_params=pltpu.CompilerParams(vmem_limit_bytes=60 << 20),
        name="finished_outputs",
    )(*sums, voc, small, tables, act, ing)


def on_device(
    word_embed, boxes, mask_pos, replace_ids, cotangent, layout_table, vocab_table, embed_gain,
    embed_shift, qkv_weight, qv_bias, out_weight, up_weight, up_bias, down_weight, layer_gains,
    layer_biases,
):
    section = lax.axis_index("section")
    layer = section // 2
    half = section % 2
    quarter, width = word_embed.shape
    page = 2 * quarter
    side = qkv_weight.shape[2] // 3
    units = up_bias.shape[1]

    left, right, all_ids, edge, mine, small = encoded(
        word_embed, cotangent, replace_ids, mask_pos, boxes, vocab_table, layout_table,
        embed_gain, embed_shift, (qkv_weight, out_weight, up_weight, down_weight), qv_bias,
        up_bias[:, None], layer_gains, layer_biases,
    )
    left, right = (array.reshape(2 * page, -1) for array in (left, right))
    counts = (
        (width // BLOCK, 3),
        (side // BLOCK, width // side),
        (width // BLOCK, units // side),
        (units // BLOCK, width // side),
    )
    count = vocab_table.shape[0] // lax.axis_size("section")
    *sums, gathered, slot_rows, table_rows, act, ing, voc = reduced(
        left, right, small, edge, mine, boxes, mask_pos, all_ids, count, counts, side
    )
    outer = lax.axis_size("dp") // GROUP
    table_part = None
    if outer > 1:
        groups = [[i + GROUP * g for g in range(outer)] for i in range(GROUP)]
        *sums, gathered = lax.psum((*sums, gathered), "dp", axis_index_groups=groups)
        slot_rows = lax.all_gather(slot_rows, "dp", axis_index_groups=groups, axis=1, tiled=True)
        here = jnp.arange(count, dtype=jnp.int32)
        here = here + (lax.axis_index("dp") * lax.axis_size("section") + section) * count
        ordered_ids = jnp.where(half == 0, all_ids, all_ids[:, ::-1])
        ordered_ids = ordered_ids.transpose(1, 0, 2).reshape(-1)
        held = slot_rows.reshape(2, 2, -1, side).transpose(0, 2, 1, 3).reshape(-1, width)
        voc = jnp.dot(
            (here[:, None] == ordered_ids[None]).astype(BF), held, preferred_element_type=F32
        )
        voc = jnp.where(layer == 0, voc, jnp.roll(voc, side, 1))
        coords = jnp.arange(layout_table.shape[1], dtype=jnp.int32)
        page_boxes = lax.dynamic_slice_in_dim(boxes, half * page, page, 1)
        grad_low = jnp.concatenate([edge[0], edge[1]], 1)
        grad_low = jnp.where(layer == 0, grad_low, jnp.zeros_like(grad_low))
        table_grad = jnp.stack(
            [
                matmul_left_t(
                    (page_boxes[a][:, None] == coords[None, :]).astype(BF)
                    + (page_boxes[a + 2][:, None] == coords[None, :]).astype(BF),
                    grad_low,
                )
                for a in (0, 1)
            ]
        )
        table_part = lax.psum_scatter(
            table_grad.astype(BF), ("dp", "section"), scatter_dimension=1, tiled=True
        ).astype(F32)
    act, ing, tables, vocab_part, *rest = finished(
        sums, voc, gathered, table_rows, act, ing, side
    )
    if table_part is None:
        table_part = tables
    *layer_sums, gains_sum, shifts_sum, gain_sum, shift_sum = rest
    return (
        act, ing, table_part, vocab_part, gain_sum, shift_sum, *layer_sums, gains_sum, shifts_sum,
    )


def solution(mesh):
    both = ("dp", "section")
    by_section = P("section", None, None)
    return jax.shard_map(
        on_device,
        mesh=mesh,
        in_specs=(
            P(both, None), P(None, "dp"), P("dp", None), P("dp", None), P(both, None), P(),
            P("dp", None), P(), P(), by_section, by_section, by_section, by_section,
            P("section", None), by_section, P(), P(),
        ),
        out_specs=(
            P(both, None), P(both, None), P(None, both, None), P(both, None), P(), P(),
            by_section, by_section, by_section, by_section, P("section", None), by_section,
            P(), P(),
        ),
        check_vma=False,
    )
```

```python
import functools

import jax
import jax.numpy as jnp
from jax import lax
from jax.experimental import pallas as pl
from jax.experimental.pallas import tpu as pltpu
from jax.sharding import PartitionSpec as P

HEAD_DIM = 64
EPS = 1e-12
ROOT_HALF = 0.7071067811865476
INV_ROOT_TWO_PI = 0.3989422804014327
BF = jnp.bfloat16
F32 = jnp.float32


def matmul_left_t(left, right):
    return jnp.einsum("pa,pb->ab", left, right, preferred_element_type=F32)


GROUP = 8
BLOCK = 128
HOP = 5
DEPTH = 4
FIRST = 20
EXTRA = 36
GUESTS = 6
SETTLED = 9


def tree_of(k):
    lines = lax.div(4 * k, 10)
    comb = lax.rem(4 * k, 10) < 6
    pick = jnp.where(comb, k - lines, lines)
    root_z = 3 * lax.rem(pick, 2)
    near = lax.rem(lax.div(pick, 4), 2)
    rung = jnp.where(comb, root_z, jnp.where(root_z == 0, near, 3 - near))
    return comb, root_z, lax.rem(lax.div(pick, 2), 2), rung


def rooted_at(c):
    line = lax.div(c, 2)
    return lax.rem(line, 2) == 0, line, lax.rem(c, 2), line


def loop(low, high, body):
    def step(k, carry):
        body(k)
        return carry

    lax.fori_loop(low, high, step, 0)


def reduce_kernel(
    counts, a_in, b_in, small_ref, edge_ref, mine_ref, box_ref, listed_ref, ids_ref,
    q_ref, o_ref, u_ref, d_ref, gathered_ref, rows_ref, table_ref, act_ref, ing_ref, voc_ref,
    a_ref, b_ref, square, buf, total, gathered, edge, rows, table, piece,
    send, recv, out_sem, g_send, g_recv, e_send, e_recv, r_send, r_recv, t_send, t_recv,
    f_send, f_recv, m_send, m_recv, last_sem, in_sem, voc, entered,
    away_send, away_recv, back_send, back_recv,
):
    a_cut = a_ref.shape[1] - counts[3][0] * BLOCK
    b_cut = b_ref.shape[1] - counts[3][1] * buf.shape[3]
    loads = []
    for columns_a, columns_b in (
        (pl.ds(a_cut, a_ref.shape[1] - a_cut), pl.ds(b_cut, b_ref.shape[1] - b_cut)),
        (pl.ds(0, a_cut), pl.ds(0, b_cut)),
    ):
        for source, target, columns in ((a_in, a_ref, columns_a), (b_in, b_ref, columns_b)):
            loads.append(
                pltpu.make_async_copy(
                    source.at[:, columns], target.at[:, columns], in_sem.at[len(loads)]
                )
            )
    for copy in loads:
        copy.start()
    me = lax.axis_index("dp")
    section = lax.axis_index("section")
    n_sections = lax.axis_size("section")
    layer = section // 2
    half = section % 2
    other_core = section + 1 - 2 * half
    other_layer = (section + 2) % n_sections
    place = me % GROUP
    z = place // 2
    y = place % 2
    chunks = buf.shape[1] - GUESTS
    limit = jnp.where(layer == 0, chunks - GUESTS, chunks + GUESTS)
    side = buf.shape[3]
    slots = rows.shape[2]
    n_q, n_o, n_u, n_d = counts
    ends = (n_d[0] * n_d[1],)
    ends += (ends[0] + n_u[0] * n_u[1],)
    ends += (ends[1] + n_o[0] * n_o[1],)
    mesh_id = pl.DeviceIdType.MESH
    deltas = (-2, 2, 1 - 2 * y)
    exists = (z > 0, z < GROUP // 2 - 1, y >= 0)

    barrier = pltpu.get_barrier_semaphore()
    for d in range(3):

        @pl.when(exists[d])
        def _():
            pl.semaphore_signal(
                barrier, inc=1, device_id=(me + deltas[d], section), device_id_type=mesh_id
            )

    pl.semaphore_signal(barrier, inc=1, device_id=(me, other_core), device_id_type=mesh_id)

    @pl.when(layer == 1)
    def _():
        for h in range(2):
            pl.semaphore_signal(barrier, inc=1, device_id=(me, h), device_id_type=mesh_id)

    around = 2 + jnp.where(exists[0], 1, 0) + jnp.where(exists[1], 1, 0)
    pl.semaphore_wait(barrier, around + jnp.where(layer == 0, 2, 0))

    @pl.when(layer == 0)
    def _():
        for h in range(2):
            pl.semaphore_signal(entered, inc=1, device_id=(me, 2 + h), device_id_type=mesh_id)

    def remote(source, target, sent, got, device):
        return pltpu.make_async_remote_copy(
            src_ref=source, dst_ref=target, send_sem=sent, recv_sem=got, device_id=device,
            device_id_type=mesh_id,
        )

    quarter = mine_ref.shape[0] // 2

    def spread(r, target, kind):
        return remote(
            mine_ref.at[pl.ds(r * quarter, quarter)], target, m_send.at[r], m_recv.at[kind],
            (me, 2 * half + r),
        )

    def keep(r, target):
        return pltpu.make_async_copy(
            mine_ref.at[pl.ds(r * quarter, quarter)], target, m_send.at[r]
        )

    def spread_all(kind, target):
        for r in range(2):

            @pl.when((layer == kind) & (section != 2 * half + r))
            def _():
                spread(r, target, kind).start()

            @pl.when((layer == kind) & (section == 2 * half + r))
            def _():
                keep(r, target).start()

    def edge_across():
        return remote(
            edge_ref.at[1], edge.at[0], e_send.at[0], e_recv.at[0], (me, other_layer)
        )

    def edge_beside(source):
        return remote(source, edge.at[1], e_send.at[1], e_recv.at[1], (me, other_core))

    @pl.when(layer == 0)
    def _():
        edge_across().start()
        edge_beside(edge_ref.at[0]).start()
        edge[0] = edge_ref[0]

    def roles(tree):
        comb, root_z, root_y, rung = tree
        along = jnp.logical_or(jnp.logical_not(comb), y == root_y)
        across = jnp.logical_or(comb, z == rung)
        pivot = jnp.where(y == root_y, root_z, rung)
        child = (
            exists[0] & along & (z <= pivot),
            exists[1] & along & (z >= pivot),
            across & (y == root_y),
        )
        up_z = along & (z != pivot)
        up_y = across & (y != root_y)
        parent = jnp.where(up_z, jnp.where(z < pivot, 1, 0), jnp.where(up_y, 2, 3))
        return child, parent

    def depth_of(k):
        comb, root_z, root_y, rung = tree_of(jnp.maximum(k, 0))
        beyond = jnp.abs(z - rung) + 1 + jnp.abs(rung - root_z)
        return jnp.where(y == root_y, jnp.abs(z - root_z), beyond)

    def depth_from(c):
        return jnp.abs(z - lax.div(c, 2)) + jnp.abs(y - lax.rem(c, 2))

    def neighbour(d):
        return me + jnp.where(d == 0, deltas[0], jnp.where(d == 1, deltas[1], deltas[2]))

    def facing(d):
        return jnp.where(d == 2, 2, 1 - d)

    def transfer(k, d, source):
        there = facing(d)
        return remote(
            buf.at[source, k], buf.at[there, k], send.at[d, k], recv.at[there, k],
            (neighbour(d), section),
        )

    def arrived(k, d):
        remote(
            buf.at[3, k], buf.at[d, k], send.at[0, k], recv.at[d, k], (me, other_core)
        ).wait_recv()

    def put(k, source):
        kk = k - 1
        low = 0
        for target, count, high in (
            (d_ref, n_d, ends[0]), (u_ref, n_u, ends[1]), (o_ref, n_o, ends[2]),
            (q_ref, n_q, chunks - 1),
        ):

            @pl.when((kk >= low) & (kk < high))
            def _():
                at = kk - low
                pltpu.make_async_copy(
                    buf.at[source, k],
                    target.at[
                        pl.ds(pl.multiple_of(at // count[1] * BLOCK, BLOCK), BLOCK),
                        pl.ds(pl.multiple_of(at % count[1] * side, BLOCK), side),
                    ],
                    out_sem.at[k],
                ).start()

            low = high

    def product(k):
        kd = k - 1
        in_d = kd < ends[0]
        ku = kd - ends[0]
        in_u = kd < ends[1]
        ko = kd - ends[1]
        in_o = kd < ends[2]
        kq = kd - ends[2]
        a_at = jnp.where(
            in_d,
            n_q[0] + n_o[0] + n_u[0] + kd // n_d[1],
            jnp.where(
                in_u,
                n_q[0] + n_o[0] + ku // n_u[1],
                jnp.where(in_o, n_q[0] + ko // n_o[1], kq // n_q[1]),
            ),
        )
        b_at = jnp.where(
            in_d,
            n_q[1] + n_o[1] + n_u[1] + kd % n_d[1],
            jnp.where(
                in_u,
                n_q[1] + n_o[1] + ku % n_u[1],
                jnp.where(in_o, n_q[1] + ko % n_o[1], kq % n_q[1]),
            ),
        )
        left = a_ref[:, pl.ds(pl.multiple_of(a_at * BLOCK, BLOCK), BLOCK)]
        right = b_ref[:, pl.ds(pl.multiple_of(b_at * side, BLOCK), side)]
        total[...] = lax.dot_general(
            left, right, (((0,), (0,)), ((), ())), preferred_element_type=F32
        )

    def away(g):
        return remote(
            buf.at[3, chunks - GUESTS + g], buf.at[3, chunks + g], away_send.at[g],
            away_recv.at[g], (me, other_layer),
        )

    def back(g, source):
        return remote(
            buf.at[source, chunks + g], buf.at[0, chunks - GUESTS + g], back_send.at[g],
            back_recv.at[g], (me, other_layer),
        )

    def finish(k, source):
        @pl.when(k < chunks)
        def _():
            put(k, source)

        @pl.when(k >= chunks)
        def _():
            back(k - chunks, source).start()

    def send_away(g):
        k = chunks - GUESTS + g
        product(k)
        buf[3, k] = total[...].astype(BF)
        away(g).start()

    def receive_back(g):
        back(g, 3).wait_recv()
        put(chunks - GUESTS + g, 0)

    def prepare(k):
        @pl.when((k > 0) & (k < jnp.minimum(limit, chunks)))
        def _():
            product(k)
            buf[3, k] = total[...].astype(BF)

    def climb(k, level):
        @pl.when((k >= 0) & (k < limit) & (depth_of(k) == DEPTH - level))
        def _():
            child, parent = roles(tree_of(k))

            @pl.when(k >= chunks)
            def _():
                away(k - chunks).wait_recv()

            if level > 0:

                @pl.when(child[0] | child[1] | child[2])
                def _():
                    total[...] = buf[3, k].astype(F32)
                    for d in range(3):

                        @pl.when(child[d])
                        def _():
                            arrived(k, d)
                            total[...] += buf[d, k].astype(F32)

                    buf[3, k] = total[...].astype(BF)

            if level < DEPTH:
                transfer(k, parent, 3).start()
            else:
                for d in range(3):

                    @pl.when(child[d])
                    def _():
                        transfer(k, d, 3).start()

                finish(k, 3)

    def descend(k, level):
        @pl.when((k >= 0) & (k < limit) & (depth_of(k) == level))
        def _():
            child, parent = roles(tree_of(k))
            arrived(k, parent)
            for d in range(3):

                @pl.when(child[d])
                def _():
                    transfer(k, d, parent).start()

            finish(k, parent)

    def settle(k):
        child, parent = roles(tree_of(k))
        for d in range(3):

            @pl.when(child[d] | (parent == d))
            def _():
                transfer(k, d, 3).wait_send()

        @pl.when((k > 0) & (k < chunks))
        def _():
            pltpu.make_async_copy(
                buf.at[3, k], d_ref.at[pl.ds(0, BLOCK), pl.ds(0, side)], out_sem.at[k]
            ).wait()

    def advance(t):
        old = t - SETTLED * HOP

        @pl.when((old >= 0) & (old < limit))
        def _():
            settle(old)

        for level in range(DEPTH + 1):
            climb(t - level * HOP, level)
        for level in range(1, DEPTH + 1):
            descend(t - (DEPTH + level) * HOP, level)
        prepare(t + 1)

    def settle_away(g):
        pltpu.make_async_copy(
            buf.at[0, chunks - GUESTS + g], d_ref.at[pl.ds(0, BLOCK), pl.ds(0, side)],
            out_sem.at[chunks - GUESTS + g],
        ).wait()
        away(g).wait_send()

    def slots_down(c, d):
        return remote(
            rows.at[0, c], rows.at[0, c], r_send.at[d, c], r_recv.at[0, c],
            (neighbour(d), section),
        )

    def slots_across(c):
        return remote(
            rows.at[0, c], rows.at[1, c], r_send.at[3, c], r_recv.at[1, c], (me, other_layer)
        )

    def slots_beside(c, kind):
        return remote(
            rows.at[kind, c], rows.at[2 + kind, c], r_send.at[4 + kind, c],
            r_recv.at[2 + kind, c], (me, other_core),
        )

    def slots_got(c, kind):
        remote(
            rows.at[kind, c], rows.at[kind, c], r_send.at[0, c], r_recv.at[kind, c],
            (me, other_core),
        ).wait_recv()

    def share_slots(c, level):
        @pl.when((c >= 0) & (c < GROUP) & (depth_from(c) == level))
        def _():
            child, parent = roles(rooted_at(c))
            if level > 0:
                slots_got(c, 0)
            for d in range(3):

                @pl.when(child[d])
                def _():
                    slots_down(c, d).start()

            slots_across(c).start()
            slots_beside(c, 0).start()

    def relay_slots(c):
        @pl.when((c >= 0) & (c < GROUP))
        def _():
            slots_got(c, 1)
            slots_beside(c, 1).start()

    def table_up(c, d):
        there = facing(d)
        return remote(
            piece.at[3, c], piece.at[there, c], t_send.at[d, c], t_recv.at[there, c],
            (neighbour(d), section),
        )

    def table_out(c, step):
        to = (section + step) % n_sections
        return remote(
            piece.at[3, c, pl.ds(to * table.shape[1], table.shape[1])], table.at[section],
            f_send.at[step], f_recv.at[section], (me, to),
        )

    def table_climb(c, level):
        @pl.when((c >= 0) & (c < GROUP) & (depth_from(c) == DEPTH - level))
        def _():
            child, parent = roles(rooted_at(c))
            at = c * BLOCK + lax.broadcasted_iota(jnp.int32, (BLOCK, edge.shape[1]), 0)
            reach = edge.shape[1]
            for part in range(2):
                start = pl.multiple_of((half if part == 0 else 1 - half) * reach, reach)
                spots = box_ref[:, pl.ds(start, reach)]
                low_at = jnp.where(half == 0, spots[0:1], spots[1:2])
                high_at = jnp.where(half == 0, spots[2:3], spots[3:4])
                ones = (at == low_at).astype(F32) + (at == high_at).astype(F32)
                term = jnp.dot(ones.astype(BF), edge[part], preferred_element_type=F32)
                if part == 0:
                    total[...] = term
                else:
                    total[...] += term
            if level > 0:
                for d in range(3):

                    @pl.when(child[d])
                    def _():
                        remote(
                            piece.at[3, c], piece.at[d, c], t_send.at[0, c], t_recv.at[d, c],
                            (me, other_core),
                        ).wait_recv()
                        total[...] += piece[d, c].astype(F32)

            piece[3, c] = total[...].astype(BF)
            if level < DEPTH:
                table_up(c, parent).start()
            else:
                for step in range(1, n_sections):
                    table_out(c, step).start()
                kept = table.shape[1]
                table[section] = piece[3, c, pl.ds(pl.multiple_of(section * kept, kept), kept)]

    def extras(t):
        c = t - EXTRA
        for level in range(DEPTH + 1):
            share_slots(c - level * HOP, level)
        relay_slots(c - (DEPTH + 2) * HOP)
        for level in range(DEPTH + 1):
            table_climb(c - GROUP - level * HOP, level)

    def settle_extras(c):
        child, parent = roles(rooted_at(c))
        for d in range(3):

            @pl.when(child[d])
            def _():
                slots_down(c, d).wait_send()

            @pl.when(parent == d)
            def _():
                table_up(c, d).wait_send()

        slots_across(c).wait_send()
        for kind in range(2):
            slots_beside(c, kind).wait_send()

    count = voc.shape[0]
    base = (me * n_sections + section) * count

    def tokens(n):
        at = base + lax.broadcasted_iota(jnp.int32, (count, BLOCK), 0)
        first = lax.rem(half + n // 2, 2) == 0
        spots = []
        for origin in range(GROUP):
            row = ids_ref[origin]
            spots.append((at == jnp.where(first, row[0:1], row[1:2])).astype(F32).astype(BF))
        spots = jnp.concatenate(spots, 1)
        held = rows[n].reshape(GROUP * slots, side)
        term = jnp.dot(spots, held, preferred_element_type=F32)
        columns = pl.ds(pl.multiple_of(lax.rem(layer + n, 2) * side, side), side)

        @pl.when(n < 2)
        def _():
            voc[:, columns] = term

        @pl.when(n >= 2)
        def _():
            voc[:, columns] += term

    def handed(step):
        return remote(
            gathered.at[0], gathered.at[step], g_send.at[step], g_recv.at[step],
            (me, (section + n_sections - step) % n_sections),
        )

    for copy in loads[:2]:
        copy.wait()
    buf[3, 0] = small_ref[...].astype(BF)
    loop(0, FIRST, advance)
    for copy in loads[2:]:
        copy.wait()

    @pl.when(layer == 0)
    def _():
        loop(0, GUESTS, send_away)

    spread_all(0, ing_ref)
    loop(FIRST, EXTRA, advance)

    @pl.when(layer == 1)
    def _():
        pl.semaphore_wait(entered, 2)
        edge_across().wait_recv()
        edge_beside(edge.at[0]).start()

    spread_all(1, act_ref)
    edge_beside(edge.at[0]).wait_recv()
    used = listed_ref.shape[1]
    listed = listed_ref[...].astype(F32)
    square[...] = jnp.full_like(square, -1.0)
    square[0:1, :used] = jnp.where(half == 0, listed[0:1], listed[1:2])
    column = square[...].T[:, 0:1]
    wanted = column == lax.broadcasted_iota(jnp.int32, (slots, edge.shape[1]), 1).astype(F32)
    rows[0, place] = jnp.dot(
        wanted.astype(F32).astype(BF), edge[0], preferred_element_type=F32
    ).astype(BF)

    def both(t):
        advance(t)
        extras(t)

    middle = EXTRA + 2 * GROUP + (DEPTH + 2) * HOP
    loop(EXTRA, middle, both)
    mine = roles(tree_of(0))[1]
    kept_small = gathered.shape[1]
    gathered[0] = buf[mine, 0, :kept_small]
    for step in range(1, n_sections):
        handed(step).start()
    for c in range(GROUP):
        for kind in range(2):
            slots_got(c, 2 + kind)

    def late(t):
        advance(t)
        n = t - middle - 2

        @pl.when((n >= 0) & (n < 4))
        def _():
            tokens(n)

        @pl.when((n >= 4) & (n < 4 + GROUP))
        def _():
            settle_extras(n - 4)

    loop(middle, limit + 2 * DEPTH * HOP, late)
    for step in range(1, n_sections):
        handed(step).wait()
        table_out(place, step).wait_send()
        source = (section + n_sections - step) % n_sections
        remote(
            piece.at[3, 0, pl.ds(0, table.shape[1])], table.at[source], f_send.at[0],
            f_recv.at[source], (me, other_core),
        ).wait_recv()
    outs = (
        pltpu.make_async_copy(gathered, gathered_ref, last_sem.at[0]),
        pltpu.make_async_copy(rows, rows_ref, last_sem.at[1]),
        pltpu.make_async_copy(table, table_ref, last_sem.at[2]),
        pltpu.make_async_copy(voc, voc_ref, last_sem.at[3]),
    )
    for copy in outs:
        copy.start()

    for r in range(2):
        for kind, target in ((0, ing_ref), (1, act_ref)):

            @pl.when((layer == kind) & (section != 2 * half + r))
            def _():
                spread(r, target, kind).wait_send()

            @pl.when((layer == kind) & (section == 2 * half + r))
            def _():
                keep(r, target).wait()

    for kind, target in ((0, ing_ref), (1, act_ref)):

        @pl.when(section != 2 * kind + layer)
        def _():
            spread(0, target, kind).wait_recv()

    @pl.when(layer == 0)
    def _():
        edge_across().wait_send()

    edge_beside(edge.at[0]).wait_send()
    loop(limit - (SETTLED - 2 * DEPTH) * HOP, limit, settle)

    @pl.when(layer == 0)
    def _():
        loop(0, GUESTS, receive_back)
        loop(0, GUESTS, settle_away)

    @pl.when(layer == 1)
    def _():
        loop(0, GUESTS, lambda g: back(g, 3).wait_send())

    for copy in outs:
        copy.wait()


def reduced(a, b, small, edge, mine, boxes, listed, ids, count, counts, side):
    chunks = 1 + sum(count[0] * count[1] for count in counts)
    n_sections = lax.axis_size("section")
    kept = 32
    slots = BLOCK
    page = edge.shape[1]
    any_space = pl.BlockSpec(memory_space=pl.ANY)
    in_vmem = pl.BlockSpec(memory_space=pltpu.VMEM)
    flops = 2 * a.shape[0] * BLOCK * side * chunks
    dma = pltpu.SemaphoreType.DMA
    return pl.pallas_call(
        functools.partial(reduce_kernel, counts),
        out_shape=tuple(
            jax.ShapeDtypeStruct((count[0] * BLOCK, count[1] * side), BF) for count in counts
        )
        + (
            jax.ShapeDtypeStruct((n_sections, kept, side), BF),
            jax.ShapeDtypeStruct((4, GROUP, slots, side), BF),
            jax.ShapeDtypeStruct((n_sections, BLOCK // n_sections, side), BF),
            jax.ShapeDtypeStruct((mine.shape[0] // 2, mine.shape[1]), BF),
            jax.ShapeDtypeStruct((mine.shape[0] // 2, mine.shape[1]), BF),
            jax.ShapeDtypeStruct((count, mine.shape[1]), F32),
        ),
        in_specs=[any_space] * 2 + [in_vmem] * 2 + [any_space] + [in_vmem] * 3,
        out_specs=(any_space,) * 10,
        scratch_shapes=[
            pltpu.VMEM(a.shape, BF),
            pltpu.VMEM(b.shape, BF),
            pltpu.VMEM((BLOCK, BLOCK), F32),
            pltpu.VMEM((4, chunks + GUESTS, BLOCK, side), BF),
            pltpu.VMEM((BLOCK, side), F32),
            pltpu.VMEM((n_sections, kept, side), BF),
            pltpu.VMEM((2, page, side), BF),
            pltpu.VMEM((4, GROUP, slots, side), BF),
            pltpu.VMEM((n_sections, BLOCK // n_sections, side), BF),
            pltpu.VMEM((4, GROUP, BLOCK, side), BF),
            dma((3, chunks + GUESTS)), dma((3, chunks + GUESTS)), dma((chunks,)),
            dma((n_sections,)), dma((n_sections,)),
            dma((2,)), dma((2,)),
            dma((6, GROUP)), dma((4, GROUP)),
            dma((3, GROUP)), dma((3, GROUP)),
            dma((n_sections,)), dma((n_sections,)),
            dma((2,)), dma((2,)),
            dma((4,)), dma((4,)),
            pltpu.VMEM((count, mine.shape[1]), F32),
            pltpu.SemaphoreType.REGULAR,
            dma((GUESTS,)), dma((GUESTS,)), dma((GUESTS,)), dma((GUESTS,)),
        ],
        compiler_params=pltpu.CompilerParams(
            collective_id=0, has_side_effects=True, vmem_limit_bytes=60 << 20
        ),
        cost_estimate=pl.CostEstimate(
            flops=flops, bytes_accessed=400 << 20, transcendentals=0
        ),
        name="gradient_sums",
    )(a, b, small, edge, mine, boxes, listed, ids)


ROWS = 256


def encoder_kernel(
    words_ref, cot_ref, ids_ref, mask_ref, box_ref, vocab_ref, table_ref, gain_ref, shift_ref,
    q_own, o_own, u_own, d_own, qvb_own, upb_own, gains_ref, shifts_ref,
    a_ref, b_ref, ids_out, edge_ref, mine_ref, small_ref,
    words, ids_all, ids_wide, vocab, spots, picks, land, other, square, norm_in, facts,
    sums_ref, upb_sum, qvb_ref, upb_ref,
    wq, wo, wu, wd, wide, x_land, g_land, x_low, ctx, d_ctx, h_low, act, slope, qkv, d_qkv,
    da_low, df_low, probs, n_one, n_two, r_one, r_two, z, sent_low,
    o_w_send, o_w_recv, c_send, c_recv, i_send, i_recv, s_send, s_recv, o_send, o_recv, local,
    w_local, w_send, w_recv, x_send, x_recv, g_send, g_recv, p_local, p_send, p_recv,
):
    me = lax.axis_index("dp")
    section = lax.axis_index("section")
    n_sections = lax.axis_size("section")
    n_dp = ids_all.shape[0]
    layer = section // 2
    half = section % 2
    mesh_id = pl.DeviceIdType.MESH
    quarter = words_ref.shape[0]
    page, width = x_low.shape
    units = act.shape[2]
    blocks = page // ROWS
    tile = 512
    scale = HEAD_DIM ** (-0.5)
    beside = (me, section + 1 - 2 * half)
    across = (me, (section + 2) % n_sections)
    slots = picks.shape[1]
    side = picks.shape[2]
    held = vocab.shape[0]

    vocab_copy = pltpu.make_async_copy(
        vocab_ref.at[:, pl.ds(pl.multiple_of(layer * side, side), side)], vocab, local.at[0]
    )
    vocab_copy.start()
    table_copies = [
        pltpu.make_async_copy(
            table_ref.at[kind, pl.ds(part * page, page)],
            act.at[kind, :, pl.ds(part * width, width)],
            local.at[2 + 2 * kind + part],
        )
        for kind in range(2)
        for part in range(2)
    ]

    @pl.when(layer == 0)
    def _():
        for copy in table_copies:
            copy.start()

    ids_wide[...] = jnp.full_like(ids_wide, -1)
    ids_wide[:, :slots] = ids_ref[...]

    barrier = pltpu.get_barrier_semaphore()

    def greet(step, carry):
        pl.semaphore_signal(
            barrier, inc=1, device_id=((me + step) % n_dp, section), device_id_type=mesh_id
        )
        return carry

    lax.fori_loop(1, n_dp, greet, 0)
    for step in range(1, n_sections):
        pl.semaphore_signal(
            barrier, inc=1, device_id=(me, (section + step) % n_sections), device_id_type=mesh_id
        )
    pl.semaphore_wait(barrier, n_dp - 1 + n_sections - 1)

    def remote(source, target, sent, got, device):
        return pltpu.make_async_remote_copy(
            src_ref=source, dst_ref=target, send_sem=sent, recv_sem=got, device_id=device,
            device_id_type=mesh_id,
        )

    def weight_copies(i):
        source = (q_own, o_own, u_own, d_own, qvb_own, upb_own)[i].at[0]
        target = (wq, wo, wu, wd, qvb_ref, upb_ref)[i]
        return (
            pltpu.make_async_copy(source, target.at[0], w_local.at[i]),
            remote(source, target.at[1], w_send.at[i], w_recv.at[i], beside),
        )

    def weights_here(i):
        near, far = weight_copies(i)
        near.wait()
        far.wait_recv()

    def ids_move(step):
        return remote(
            ids_wide, ids_all.at[me], i_send.at[step], i_recv.at[me], ((me + step) % n_dp, section)
        )

    def ids_got(step):
        source = (me + step) % n_dp
        return remote(
            ids_wide, ids_all.at[source], i_send.at[0], i_recv.at[source],
            (me, (section + 1) % n_sections),
        )

    loop(1, n_dp, lambda step: ids_move(step).start())
    ids_all[me] = ids_wide[...]

    words_move = remote(
        words_ref, words.at[half], o_w_send, o_w_recv.at[half], (me, layer)
    )
    given_part = g_land.at[pl.ds(pl.multiple_of(half * quarter, quarter), quarter)]
    given_move = remote(cot_ref, given_part, c_send, c_recv.at[half], (me, 2 + layer))
    given_keep = pltpu.make_async_copy(cot_ref, given_part, c_send)

    @pl.when(section != 0)
    def _():
        words_move.start()

    @pl.when(section == 0)
    def _():
        words[0] = words_ref[...]

    @pl.when(section != 3)
    def _():
        given_move.start()

    @pl.when(section == 3)
    def _():
        given_keep.start()

    for i in (0, 4, 5, 1, 2, 3):
        near, far = weight_copies(i)
        far.start()
        near.start()

    loop(1, n_dp, lambda step: ids_got(step).wait_recv())
    lists = ids_all[...].astype(F32)
    lists = jnp.where(half == 0, lists[:, 0], lists[:, 1])
    square[...] = jnp.zeros_like(square)
    square[0:n_dp] = lists
    listed = mask_ref[...].astype(F32)
    square[n_dp : n_dp + 1, :slots] = jnp.where(half == 0, listed[0:1], listed[1:2])
    turned = square[...].T
    at = (me * held + lax.broadcasted_iota(jnp.int32, (slots, held), 1)).astype(F32)
    for origin in range(n_dp):
        spots[origin * slots : (origin + 1) * slots] = (
            at == turned[:slots, origin : origin + 1]
        ).astype(F32).astype(BF)
    vocab_copy.wait()
    found = jnp.dot(spots[...], vocab[...], preferred_element_type=F32).astype(BF)
    for origin in range(n_dp):
        picks[origin] = found[origin * slots : (origin + 1) * slots]

    lines = n_dp // 2
    line, lane_of = me // 2, me % 2

    def slots_beside(at):
        return remote(
            picks.at[2 * at + 1 - lane_of], land.at[at], s_send.at[at], s_recv.at[at],
            (me + 1 - 2 * lane_of, section),
        )

    def slots_along(step):
        to = (line + step) % lines
        return remote(
            picks.at[2 * to + lane_of], land.at[lines + line], s_send.at[lines + to],
            s_recv.at[lines + line], (2 * to + lane_of, section),
        )

    def slots_got(step):
        source = (line + step) % lines
        return remote(
            picks.at[0], land.at[lines + source], s_send.at[0], s_recv.at[lines + source],
            (me, (section + 1) % n_sections),
        )

    def pass_on(step):
        to = (line + step) % lines
        slots_beside(to).wait_recv()
        picks[2 * to + lane_of] = picks[2 * to + lane_of] + land[to]

        @pl.when(step < lines)
        def _():
            slots_along(step).start()

    loop(1, lines + 1, lambda step: slots_beside((line + step) % lines).start())
    loop(1, lines + 1, pass_on)
    land[lines + line] = picks[me]

    @pl.when(layer == 0)
    def _():
        for copy in table_copies:
            copy.wait()
        coords = lax.broadcasted_iota(jnp.int32, (page, page), 0)
        for kind in range(2):
            low_at, high_at = (
                box_ref[i : i + 1, pl.ds(pl.multiple_of(half * page, page), page)]
                for i in (kind, kind + 2)
            )
            for part in range(2):
                at = coords + part * page
                ones = (at == low_at).astype(F32) + (at == high_at).astype(F32)
                term = lax.dot_general(
                    ones.astype(BF), act[kind, :, pl.ds(part * width, width)],
                    (((0,), (0,)), ((), ())), preferred_element_type=F32,
                )
                if kind + part == 0:
                    wide[...] = term
                else:
                    wide[...] += term

    loop(1, lines, lambda step: slots_got(step).wait_recv())
    mine = land[lines]
    for origin in range(1, lines):
        mine = mine + land[lines + origin]
    other[1] = mine
    other_move = remote(other.at[1], other.at[0], o_send, o_recv, (me, half))

    @pl.when(layer == 1)
    def _():
        other_move.start()

    @pl.when(layer == 0)
    def _():
        for r in range(2):

            @pl.when(section + r > 0)
            def _():
                remote(
                    words_ref, words.at[r], o_w_send, o_w_recv.at[r], (me, section + 1)
                ).wait_recv()

        places = lax.broadcasted_iota(jnp.int32, (slots, page), 1).astype(F32)
        chosen = (turned[:slots, n_dp : n_dp + 1] == places).astype(F32).astype(BF)

        def spread_out(right):
            return lax.dot_general(
                chosen, right, (((0,), (0,)), ((), ())), preferred_element_type=F32
            )

        marked = spread_out(jnp.ones((slots, BLOCK), BF))[:, 0:1]
        facts[1] = 1.0 - marked
        other_move.wait_recv()
        for part, values in ((0, other[1]), (1, other[0])):
            columns = pl.ds(part * side, side)
            wide[:, columns] += spread_out(values)
        for r in range(2):
            rows = pl.ds(r * quarter, quarter)
            kept = facts[1, rows]
            summed = wide[rows] + words[r].astype(F32) * kept
            center = summed - jnp.mean(summed, -1, keepdims=True)
            spread = jnp.mean(center * center, -1, keepdims=True)
            inverse = lax.rsqrt(spread + EPS)
            normed = center * inverse
            norm_in[rows] = normed
            facts[0, rows] = inverse
            wide[rows] = normed * gain_ref[...][None] + shift_ref[...][None]

    ids_copy = pltpu.make_async_copy(ids_all, ids_out, local.at[1])
    ids_copy.start()

    @pl.when(layer == 1)
    def _():
        for r in range(2):

            @pl.when(section + r < 4)
            def _():
                remote(
                    cot_ref, g_land.at[pl.ds(r * quarter, quarter)], c_send, c_recv.at[r],
                    (me, section - 1),
                ).wait_recv()

    @pl.when(section == 3)
    def _():
        given_keep.wait()

    def rows_of(block):
        return pl.ds(pl.multiple_of(block * ROWS, ROWS), ROWS)

    def x_move(block):
        rows = rows_of(block)
        return remote(
            sent_low.at[rows], x_land.at[rows], x_send.at[block], x_recv.at[block], across
        )

    def g_move(block):
        rows = rows_of(block)
        return remote(
            sent_low.at[rows], g_land.at[rows], g_send.at[block], g_recv.at[block], across
        )

    spans = (
        (a_ref, 0, width), (a_ref, width, side), (a_ref, width + side, width),
        (a_ref, 2 * width + side, units),
        (b_ref, 0, 3 * side), (b_ref, 3 * side, width), (b_ref, 3 * side + width, units),
        (b_ref, 3 * side + width + units, width),
    )

    def piece_copies(i):
        target, start, size = spans[i]
        source = (x_low, ctx, h_low, act, d_qkv, da_low, slope, df_low)[i]
        double = i in (1, 3, 4, 6)
        columns = pl.ds(start, size)
        return (
            pltpu.make_async_copy(
                source.at[0] if double else source, target.at[0, :, columns], p_local.at[i]
            ),
            remote(
                source.at[1] if double else source, target.at[1, :, columns], p_send.at[i],
                p_recv.at[i], beside,
            ),
        )

    def hand_out(*pieces):
        for i in pieces:
            near, far = piece_copies(i)
            far.start()
            near.start()

    def nt(left, right):
        return lax.dot_general(
            left, right, (((1,), (1,)), ((), ())), preferred_element_type=F32
        )

    def tn(left, right):
        return lax.dot_general(
            left, right, (((0,), (0,)), ((), ())), preferred_element_type=F32
        )

    def centred(values):
        center = values - jnp.mean(values, -1, keepdims=True)
        spread = jnp.mean(center * center, -1, keepdims=True)
        inverse = lax.rsqrt(spread + EPS)
        return center * inverse, inverse

    def pulled(grad, normed, inverse, gain):
        scaled = grad * gain
        return inverse * (
            scaled
            - jnp.mean(scaled, -1, keepdims=True)
            - normed * jnp.mean(scaled * normed, -1, keepdims=True)
        )

    def add_sum(row, values):
        sums_ref[row : row + 1] += jnp.sum(values, 0, keepdims=True)

    sums_ref[...] = jnp.zeros_like(sums_ref)
    upb_sum[...] = jnp.zeros_like(upb_sum)

    for i in (0, 4, 5):
        weights_here(i)

    def project(block):
        rows = rows_of(block)

        @pl.when(layer == 1)
        def _():
            x_move(block).wait_recv()
            wide[rows] = x_land[rows].astype(F32)

        low = wide[rows].astype(BF)
        x_low[rows] = low
        for slot in range(2):
            for c in range(3):
                part = pl.ds(c * side, side)
                value = jnp.dot(low, wq[slot, :, part], preferred_element_type=F32)
                if c != 1:
                    value = value + qvb_ref[slot, c // 2 : c // 2 + 1]
                qkv[slot, rows, part] = value.astype(BF)

    loop(0, blocks, project)
    hand_out(0)

    lane = lax.broadcasted_iota(jnp.int32, (1, 2 * HEAD_DIM), 1)
    masks = ((lane < HEAD_DIM).astype(F32).astype(BF), (lane >= HEAD_DIM).astype(F32).astype(BF))
    first_lane = lax.broadcasted_iota(jnp.int32, (page, 2 * HEAD_DIM), 1) < HEAD_DIM
    first_row = lax.broadcasted_iota(jnp.int32, (2 * HEAD_DIM, page), 0) < HEAD_DIM
    pairs = side // (2 * HEAD_DIM)

    def lanes(i, third):
        at = third * side + (i % pairs) * 2 * HEAD_DIM
        return pl.ds(pl.multiple_of(at, 2 * HEAD_DIM), 2 * HEAD_DIM)

    def attend(i):
        slot = i // pairs
        queries = qkv[slot, :, lanes(i, 0)] * jnp.asarray(scale, BF)
        keys = qkv[slot, :, lanes(i, 1)]
        values = qkv[slot, :, lanes(i, 2)]
        found = []
        for e in range(2):
            scores = nt(keys * masks[e], queries)
            expo = jnp.exp(scores - jnp.max(scores, 0, keepdims=True))
            share = 1.0 / jnp.sum(expo, 0, keepdims=True)
            low = (expo * share).astype(BF)
            probs[2 * i + e] = low
            found.append(tn(values, low))
        ctx[slot, :, lanes(i, 0)] = jnp.where(first_row, found[0], found[1]).T.astype(BF)

    loop(0, 2 * pairs, attend)
    hand_out(1)
    for i in range(1, 4):
        weights_here(i)

    def feed(block):
        rows = rows_of(block)
        attended = (
            jnp.dot(ctx[0, rows], wo[0], preferred_element_type=F32)
            + jnp.dot(ctx[1, rows], wo[1], preferred_element_type=F32)
            + shifts_ref[layer, 0:1]
        )
        normed, inverse = centred(wide[rows] + attended)
        n_one[rows] = normed
        r_one[rows] = inverse
        hidden = normed * gains_ref[layer, 0:1] + shifts_ref[layer, 1:2]
        z[rows] = hidden
        h_low[rows] = hidden.astype(BF)
        for slot in range(2):
            for c in range(units // tile):
                part = pl.ds(c * tile, tile)
                upper = (
                    jnp.dot(h_low[rows], wu[slot, :, part], preferred_element_type=F32)
                    + upb_ref[slot, :, part]
                )
                below = 0.5 * (1.0 + lax.erf(upper * ROOT_HALF))
                act[slot, rows, part] = (upper * below).astype(BF)
                slope[slot, rows, part] = (
                    below + upper * jnp.exp(-0.5 * upper * upper) * INV_ROOT_TWO_PI
                ).astype(BF)
        mixed = (
            jnp.dot(act[0, rows], wd[0], preferred_element_type=F32)
            + jnp.dot(act[1, rows], wd[1], preferred_element_type=F32)
            + shifts_ref[layer, 2:3]
        )
        normed, inverse = centred(z[rows] + mixed)
        n_two[rows] = normed
        r_two[rows] = inverse
        output = normed * gains_ref[layer, 1:2] + shifts_ref[layer, 3:4]
        sent_low[rows] = output.astype(BF)

        @pl.when(layer == 0)
        def _():
            x_move(block).start()

        @pl.when(layer == 1)
        def _():
            mine_ref[rows] = sent_low[rows]

    loop(0, blocks, feed)
    hand_out(2, 3)

    def feed_back(block):
        rows = rows_of(block)

        @pl.when(layer == 0)
        def _():
            g_move(block).wait_recv()

        grad = g_land[rows].astype(F32)
        normed = n_two[rows]
        add_sum(1, grad * normed)
        add_sum(5, grad)
        grad = pulled(grad, normed, r_two[rows], gains_ref[layer, 1:2])
        z[rows] = grad
        low = grad.astype(BF)
        df_low[rows] = low
        add_sum(4, low.astype(F32))
        for slot in range(2):
            for c in range(units // tile):
                part = pl.ds(c * tile, tile)
                term = nt(df_low[rows], wd[slot, part])
                term = (term * slope[slot, rows, part].astype(F32)).astype(BF)
                slope[slot, rows, part] = term
                upb_sum[slot : slot + 1, part] += jnp.sum(term.astype(F32), 0, keepdims=True)
        grad = z[rows] + nt(slope[0, rows], wu[0]) + nt(slope[1, rows], wu[1])
        normed = n_one[rows]
        add_sum(0, grad * normed)
        add_sum(3, grad)
        grad = pulled(grad, normed, r_one[rows], gains_ref[layer, 0:1])
        z[rows] = grad
        low = grad.astype(BF)
        da_low[rows] = low
        add_sum(2, low.astype(F32))
        for slot in range(2):
            d_ctx[slot, rows] = nt(da_low[rows], wo[slot]).astype(BF)

    loop(0, blocks, feed_back)
    hand_out(5, 6, 7)

    def attend_back(i):
        slot = i // pairs
        queries = qkv[slot, :, lanes(i, 0)]
        keys = qkv[slot, :, lanes(i, 1)]
        values = qkv[slot, :, lanes(i, 2)]
        grads = d_ctx[slot, :, lanes(i, 0)]
        d_q, d_k, d_v = [], [], []
        for e in range(2):
            low = probs[2 * i + e]
            share = low.astype(F32)
            term = share * nt(values * masks[e], grads)
            term = (term - share * jnp.sum(term, 0, keepdims=True)).astype(BF)
            d_k.append(jnp.dot(term, queries, preferred_element_type=F32))
            d_v.append(jnp.dot(low, grads, preferred_element_type=F32))
            d_q.append(tn(keys, term))
        d_qkv[slot, :, lanes(i, 0)] = (
            jnp.where(first_row, d_q[0], d_q[1]).T * scale
        ).astype(BF)
        d_qkv[slot, :, lanes(i, 1)] = (jnp.where(first_lane, d_k[0], d_k[1]) * scale).astype(BF)
        d_qkv[slot, :, lanes(i, 2)] = jnp.where(first_lane, d_v[0], d_v[1]).astype(BF)

    loop(0, 2 * pairs, attend_back)
    hand_out(4)

    def leave(block):
        rows = rows_of(block)
        grad = z[rows] + nt(d_qkv[0, rows], wq[0]) + nt(d_qkv[1, rows], wq[1])
        z[rows] = grad

        @pl.when(layer == 1)
        def _():
            sent_low[rows] = z[rows].astype(BF)
            g_move(block).start()

        @pl.when(layer == 0)
        def _():
            grad = z[rows]
            normed = norm_in[rows]
            add_sum(6, grad * normed)
            add_sum(7, grad)
            low = pulled(grad, normed, facts[0, rows], gain_ref[...][None]).astype(BF)
            edge_ref[0, rows] = low[:, :side]
            edge_ref[1, rows] = low[:, side:]
            mine_ref[rows] = (low.astype(F32) * facts[1, rows]).astype(BF)

    loop(0, blocks, leave)
    small_ref[...] = jnp.zeros_like(small_ref)
    pieces = units // side
    for slot in range(2):
        for i in range(2):
            part = pl.ds(2 * i * side, side)
            at = slot * (2 + pieces) + i
            small_ref[at : at + 1] = jnp.sum(
                d_qkv[slot, :, part].astype(F32), 0, keepdims=True
            )
        for i in range(pieces):
            at = slot * (2 + pieces) + 2 + i
            small_ref[at : at + 1] = upb_sum[slot : slot + 1, pl.ds(i * side, side)]
    for i in range(8):
        for j in range(2):
            at = 2 * (2 + pieces) + 2 * i + j
            small_ref[at : at + 1] = sums_ref[i : i + 1, pl.ds(j * side, side)]
    for block in range(blocks):

        @pl.when(layer == 0)
        def _():
            x_move(block).wait_send()

        @pl.when(layer == 1)
        def _():
            g_move(block).wait_send()

    for i in range(6):
        weight_copies(i)[1].wait_send()
    for i in range(8):
        near, far = piece_copies(i)
        near.wait()
        far.wait()


    @pl.when(layer == 1)
    def _():
        other_move.wait_send()

    @pl.when(section != 0)
    def _():
        words_move.wait_send()

    @pl.when(section != 3)
    def _():
        given_move.wait_send()

    loop(1, n_dp, lambda step: ids_move(step).wait_send())
    loop(0, lines, lambda at: slots_beside(at).wait_send())
    loop(1, lines, lambda step: slots_along(step).wait_send())
    ids_copy.wait()


def encoded(
    words, cot, ids, mask, boxes, vocab, table, gain, shift, weights, qvb, upb, gains, shifts
):
    quarter, width = words.shape
    page = 2 * quarter
    n_dp = lax.axis_size("dp")
    slots = ids.shape[1]
    held = vocab.shape[0]
    side = width // 2
    units = weights[3].shape[1]
    blocks = page // ROWS
    heads = width // HEAD_DIM
    any_space = pl.BlockSpec(memory_space=pl.ANY)
    in_vmem = pl.BlockSpec(memory_space=pltpu.VMEM)
    dma = pltpu.SemaphoreType.DMA
    vmem = pltpu.VMEM
    flops = 8 * page * width * (4 * width + 4 * units) * 2
    return pl.pallas_call(
        encoder_kernel,
        out_shape=(
            jax.ShapeDtypeStruct((2, page, 2 * width + side + units), BF),
            jax.ShapeDtypeStruct((2, page, 3 * side + 2 * width + units), BF),
            jax.ShapeDtypeStruct((n_dp, 2, BLOCK), jnp.int32),
            jax.ShapeDtypeStruct((2, page, side), BF),
            jax.ShapeDtypeStruct((page, width), BF),
            jax.ShapeDtypeStruct((BLOCK, side), F32),
        ),
        in_specs=[in_vmem, any_space] + [in_vmem] * 3 + [any_space] * 2 + [in_vmem] * 2
        + [any_space] * 6 + [in_vmem] * 2,
        out_specs=(any_space,) * 3 + (in_vmem,) * 3,
        scratch_shapes=[
            vmem((2, quarter, width), BF), vmem((n_dp, 2, BLOCK), jnp.int32),
            vmem((2, BLOCK), jnp.int32),
            vmem((held, side), BF), vmem((n_dp * slots, held), BF),
            vmem((n_dp, slots, side), BF), vmem((n_dp, slots, side), BF),
            vmem((2, slots, side), BF), vmem((BLOCK, BLOCK), F32),
            vmem((page, width), F32), vmem((2, page, 1), F32),
            vmem((8, width), F32), vmem((2, units), F32),
            vmem((2, 2, side), F32), vmem((2, 1, units), F32),
            vmem((2, width, 3 * side), BF), vmem((2, side, width), BF),
            vmem((2, width, units), BF), vmem((2, units, width), BF),
            vmem((page, width), F32), vmem((page, width), BF), vmem((page, width), BF),
            vmem((page, width), BF), vmem((2, page, side), BF), vmem((2, page, side), BF),
            vmem((page, width), BF), vmem((2, page, units), BF), vmem((2, page, units), BF),
            vmem((2, page, 3 * side), BF), vmem((2, page, 3 * side), BF),
            vmem((page, width), BF), vmem((page, width), BF), vmem((heads, page, page), BF),
            vmem((page, width), F32), vmem((page, width), F32),
            vmem((page, 1), F32), vmem((page, 1), F32),
            vmem((page, width), F32), vmem((page, width), BF),
            dma, dma((2,)), dma, dma((2,)), dma((n_dp,)), dma((n_dp,)),
            dma((n_dp,)), dma((n_dp,)), dma, dma, dma((6,)),
            dma((6,)), dma((6,)), dma((6,)),
            dma((blocks,)), dma((blocks,)), dma((blocks,)), dma((blocks,)),
            dma((8,)), dma((8,)), dma((8,)),
        ],
        compiler_params=pltpu.CompilerParams(
            collective_id=1, has_side_effects=True, vmem_limit_bytes=63 << 20
        ),
        cost_estimate=pl.CostEstimate(
            flops=flops, bytes_accessed=200 << 20, transcendentals=0
        ),
        name="encoder_both_ways",
    )(words, cot, ids, mask, boxes, vocab, table, gain, shift, *weights, qvb, upb, gains, shifts)


def finish_kernel(
    pieces, q_in, o_in, u_in, d_in, voc_in, small_ref, table_ref, act_in, ing_in,
    act_ref, ing_ref, tab_ref, voc_ref, q_ref, qvb_ref, o_ref, u_ref, upb_ref, d_ref, gains_ref,
    shifts_ref, eg_ref, es_ref,
    q_s, o_s, u_s, d_s, q_f, o_f, u_f, d_f, act_s, ing_s, act_f, ing_f, in_sem, out_sem, voc_s, voc_sem,
):
    section = lax.axis_index("section")
    layer = section // 2
    half = section % 2
    side = table_ref.shape[2]
    voc_copy = pltpu.make_async_copy(voc_in, voc_s, voc_sem.at[0])
    voc_copy.start()
    moves = []
    for source, low, wide, target in (
        (d_in, d_s, d_f, d_ref), (u_in, u_s, u_f, u_ref), (q_in, q_s, q_f, q_ref),
        (o_in, o_s, o_f, o_ref),
    ):
        count = low.shape[0] // pieces
        for i in range(pieces):
            rows = pl.ds(i * count, count)
            moves.append((source.at[rows], low.at[rows], wide.at[rows], target.at[0, rows]))
    moves.append((act_in, act_s, act_f, act_ref))
    moves.append((ing_in, ing_s, ing_f, ing_ref))
    for i, (source, low, wide, target) in enumerate(moves):
        pltpu.make_async_copy(source, low, in_sem.at[i]).start()


    parts = small_ref[...].astype(F32)
    partner = jnp.where(half == 0, parts[1], parts[3])
    far_partner = jnp.where(half == 0, parts[3], parts[1])
    splits = d_in.shape[0] // side
    kept = 2 + splits
    own = parts[0, :kept] + partner[kept : 2 * kept]
    qvb_ref[0] = own[:2]
    for i in range(splits):
        upb_ref[0:1, pl.ds(i * side, side)] = own[2 + i : 3 + i]
    here = (parts[0] + partner)[2 * kept : 2 * kept + 16]
    there = (parts[2] + far_partner)[2 * kept : 2 * kept + 16]
    in_order = (jnp.where(layer == 0, here, there), jnp.where(layer == 0, there, here))
    for j in range(2):
        columns = pl.ds(j * side, side)
        for l in range(2):
            for i in range(2):
                at = 2 * i + j
                gains_ref[l, i : i + 1, columns] = in_order[l][at : at + 1]
            for i in range(4):
                at = 4 + 2 * i + j
                shifts_ref[l, i : i + 1, columns] = in_order[l][at : at + 1]
        eg_ref[columns] = in_order[0][12 + j]
        es_ref[columns] = in_order[0][14 + j]
    for l in range(2):
        for h in range(2):
            tab_ref[h, :, pl.ds(l * side, side)] = table_ref[2 * l + h].astype(F32)

    voc_copy.wait()
    voc_out = pltpu.make_async_copy(voc_s, voc_ref, voc_sem.at[1])
    voc_out.start()
    for i, (source, low, wide, target) in enumerate(moves):
        pltpu.make_async_copy(source, low, in_sem.at[i]).wait()
        wide[...] = low[...].astype(F32)
        pltpu.make_async_copy(wide, target, out_sem.at[i]).start()

    for i, (source, low, wide, target) in enumerate(moves):
        pltpu.make_async_copy(wide, target, out_sem.at[i]).wait()
    voc_out.wait()


def finished(sums, voc, small, tables, act, ing, side):
    any_space = pl.BlockSpec(memory_space=pl.ANY)
    in_vmem = pl.BlockSpec(memory_space=pltpu.VMEM)
    dma = pltpu.SemaphoreType.DMA
    vmem = pltpu.VMEM
    pieces = 6
    width = act.shape[1]
    units = sums[3].shape[0]
    shapes = [array.shape for array in sums]
    outs = [
        jax.ShapeDtypeStruct(shape, F32)
        for shape in (
            act.shape, ing.shape, (2, tables.shape[1], width), voc.shape, (1, *shapes[0]),
            (1, 2, side), (1, *shapes[1]), (1, *shapes[2]), (1, units), (1, *shapes[3]),
            (2, 2, width), (2, 4, width), (width,), (width,),
        )
    ]
    specs = [any_space] * 2 + [in_vmem] + [any_space] * 2 + [in_vmem, any_space, any_space, in_vmem, any_space] + [in_vmem] * 4
    return pl.pallas_call(
        functools.partial(finish_kernel, pieces),
        out_shape=outs,
        in_specs=[any_space] * 5 + [in_vmem] * 2 + [any_space] * 2,
        out_specs=specs,
        scratch_shapes=[vmem(shape, BF) for shape in shapes]
        + [vmem(shape, F32) for shape in shapes]
        + [vmem(act.shape, BF)] * 2
        + [vmem(act.shape, F32)] * 2
        + [dma((4 * pieces + 2,)), dma((4 * pieces + 2,)), vmem(voc.shape, F32), dma((2,))],
        compiler_params=pltpu.CompilerParams(vmem_limit_bytes=60 << 20),
        name="finished_outputs",
    )(*sums, voc, small, tables, act, ing)


def on_device(
    word_embed, boxes, mask_pos, replace_ids, cotangent, layout_table, vocab_table, embed_gain,
    embed_shift, qkv_weight, qv_bias, out_weight, up_weight, up_bias, down_weight, layer_gains,
    layer_biases,
):
    section = lax.axis_index("section")
    layer = section // 2
    half = section % 2
    quarter, width = word_embed.shape
    page = 2 * quarter
    side = qkv_weight.shape[2] // 3
    units = up_bias.shape[1]

    left, right, all_ids, edge, mine, small = encoded(
        word_embed, cotangent, replace_ids, mask_pos, boxes, vocab_table, layout_table,
        embed_gain, embed_shift, (qkv_weight, out_weight, up_weight, down_weight), qv_bias,
        up_bias[:, None], layer_gains, layer_biases,
    )
    left, right = (array.reshape(2 * page, -1) for array in (left, right))
    counts = (
        (width // BLOCK, 3),
        (side // BLOCK, width // side),
        (width // BLOCK, units // side),
        (units // BLOCK, width // side),
    )
    count = vocab_table.shape[0] // lax.axis_size("section")
    *sums, gathered, slot_rows, table_rows, act, ing, voc = reduced(
        left, right, small, edge, mine, boxes, mask_pos, all_ids, count, counts, side
    )
    outer = lax.axis_size("dp") // GROUP
    table_part = None
    if outer > 1:
        groups = [[i + GROUP * g for g in range(outer)] for i in range(GROUP)]
        *sums, gathered = lax.psum((*sums, gathered), "dp", axis_index_groups=groups)
        slot_rows = lax.all_gather(slot_rows, "dp", axis_index_groups=groups, axis=1, tiled=True)
        here = jnp.arange(count, dtype=jnp.int32)
        here = here + (lax.axis_index("dp") * lax.axis_size("section") + section) * count
        ordered_ids = jnp.where(half == 0, all_ids, all_ids[:, ::-1])
        ordered_ids = ordered_ids.transpose(1, 0, 2).reshape(-1)
        held = slot_rows.reshape(2, 2, -1, side).transpose(0, 2, 1, 3).reshape(-1, width)
        voc = jnp.dot(
            (here[:, None] == ordered_ids[None]).astype(BF), held, preferred_element_type=F32
        )
        voc = jnp.where(layer == 0, voc, jnp.roll(voc, side, 1))
        coords = jnp.arange(layout_table.shape[1], dtype=jnp.int32)
        page_boxes = lax.dynamic_slice_in_dim(boxes, half * page, page, 1)
        grad_low = jnp.concatenate([edge[0], edge[1]], 1)
        grad_low = jnp.where(layer == 0, grad_low, jnp.zeros_like(grad_low))
        table_grad = jnp.stack(
            [
                matmul_left_t(
                    (page_boxes[a][:, None] == coords[None, :]).astype(BF)
                    + (page_boxes[a + 2][:, None] == coords[None, :]).astype(BF),
                    grad_low,
                )
                for a in (0, 1)
            ]
        )
        table_part = lax.psum_scatter(
            table_grad.astype(BF), ("dp", "section"), scatter_dimension=1, tiled=True
        ).astype(F32)
    act, ing, tables, vocab_part, *rest = finished(
        sums, voc, gathered, table_rows, act, ing, side
    )
    if table_part is None:
        table_part = tables
    *layer_sums, gains_sum, shifts_sum, gain_sum, shift_sum = rest
    return (
        act, ing, table_part, vocab_part, gain_sum, shift_sum, *layer_sums, gains_sum, shifts_sum,
    )


def solution(mesh):
    both = ("dp", "section")
    by_section = P("section", None, None)
    return jax.shard_map(
        on_device,
        mesh=mesh,
        in_specs=(
            P(both, None), P(None, "dp"), P("dp", None), P("dp", None), P(both, None), P(),
            P("dp", None), P(), P(), by_section, by_section, by_section, by_section,
            P("section", None), by_section, P(), P(),
        ),
        out_specs=(
            P(both, None), P(both, None), P(None, both, None), P(both, None), P(), P(),
            by_section, by_section, by_section, by_section, P("section", None), by_section,
            P(), P(),
        ),
        check_vma=False,
    )
```

```python
import functools

import jax
import jax.numpy as jnp
from jax import lax
from jax.experimental import pallas as pl
from jax.experimental.pallas import tpu as pltpu
from jax.sharding import PartitionSpec as P

HEAD_DIM = 64
EPS = 1e-12
ROOT_HALF = 0.7071067811865476
INV_ROOT_TWO_PI = 0.3989422804014327
BF = jnp.bfloat16
F32 = jnp.float32


def matmul_left_t(left, right):
    return jnp.einsum("pa,pb->ab", left, right, preferred_element_type=F32)


GROUP = 8
BLOCK = 128
HOP = 5
DEPTH = 4
FIRST = 20
EXTRA = 36
GUESTS = 6
SETTLED = 9


def tree_of(k):
    lines = lax.div(4 * k, 10)
    comb = lax.rem(4 * k, 10) < 6
    pick = jnp.where(comb, k - lines, lines)
    root_z = 3 * lax.rem(pick, 2)
    near = lax.rem(lax.div(pick, 4), 2)
    rung = jnp.where(comb, root_z, jnp.where(root_z == 0, near, 3 - near))
    return comb, root_z, lax.rem(lax.div(pick, 2), 2), rung


def rooted_at(c):
    line = lax.div(c, 2)
    return lax.rem(line, 2) == 0, line, lax.rem(c, 2), line


def loop(low, high, body):
    def step(k, carry):
        body(k)
        return carry

    lax.fori_loop(low, high, step, 0)


def reduce_kernel(
    counts, a_in, b_in, small_ref, edge_ref, mine_ref, box_ref, listed_ref, ids_ref,
    q_ref, o_ref, u_ref, d_ref, gathered_ref, rows_ref, table_ref, act_ref, ing_ref, voc_ref,
    a_ref, b_ref, square, buf, total, gathered, edge, rows, table, piece,
    send, recv, out_sem, g_send, g_recv, e_send, e_recv, r_send, r_recv, t_send, t_recv,
    f_send, f_recv, m_send, m_recv, last_sem, in_sem, voc, entered,
    away_send, away_recv, back_send, back_recv,
):
    a_cut = a_ref.shape[1] - counts[3][0] * BLOCK
    b_cut = b_ref.shape[1] - counts[3][1] * buf.shape[3]
    loads = []
    for columns_a, columns_b in (
        (pl.ds(a_cut, a_ref.shape[1] - a_cut), pl.ds(b_cut, b_ref.shape[1] - b_cut)),
        (pl.ds(0, a_cut), pl.ds(0, b_cut)),
    ):
        for source, target, columns in ((a_in, a_ref, columns_a), (b_in, b_ref, columns_b)):
            loads.append(
                pltpu.make_async_copy(
                    source.at[:, columns], target.at[:, columns], in_sem.at[len(loads)]
                )
            )
    for copy in loads:
        copy.start()
    me = lax.axis_index("dp")
    section = lax.axis_index("section")
    n_sections = lax.axis_size("section")
    layer = section // 2
    half = section % 2
    other_core = section + 1 - 2 * half
    other_layer = (section + 2) % n_sections
    place = me % GROUP
    z = place // 2
    y = place % 2
    chunks = buf.shape[1] - GUESTS
    limit = jnp.where(layer == 0, chunks - GUESTS, chunks + GUESTS)
    side = buf.shape[3]
    slots = rows.shape[2]
    n_q, n_o, n_u, n_d = counts
    ends = (n_d[0] * n_d[1],)
    ends += (ends[0] + n_u[0] * n_u[1],)
    ends += (ends[1] + n_o[0] * n_o[1],)
    mesh_id = pl.DeviceIdType.MESH
    deltas = (-2, 2, 1 - 2 * y)
    exists = (z > 0, z < GROUP // 2 - 1, y >= 0)

    barrier = pltpu.get_barrier_semaphore()
    for d in range(3):

        @pl.when(exists[d])
        def _():
            pl.semaphore_signal(
                barrier, inc=1, device_id=(me + deltas[d], section), device_id_type=mesh_id
            )

    pl.semaphore_signal(barrier, inc=1, device_id=(me, other_core), device_id_type=mesh_id)

    @pl.when(layer == 1)
    def _():
        for h in range(2):
            pl.semaphore_signal(barrier, inc=1, device_id=(me, h), device_id_type=mesh_id)

    around = 2 + jnp.where(exists[0], 1, 0) + jnp.where(exists[1], 1, 0)
    pl.semaphore_wait(barrier, around + jnp.where(layer == 0, 2, 0))

    @pl.when(layer == 0)
    def _():
        for h in range(2):
            pl.semaphore_signal(entered, inc=1, device_id=(me, 2 + h), device_id_type=mesh_id)

    def remote(source, target, sent, got, device):
        return pltpu.make_async_remote_copy(
            src_ref=source, dst_ref=target, send_sem=sent, recv_sem=got, device_id=device,
            device_id_type=mesh_id,
        )

    quarter = mine_ref.shape[0] // 2

    def spread(r, target, kind):
        return remote(
            mine_ref.at[pl.ds(r * quarter, quarter)], target, m_send.at[r], m_recv.at[kind],
            (me, 2 * half + r),
        )

    def keep(r, target):
        return pltpu.make_async_copy(
            mine_ref.at[pl.ds(r * quarter, quarter)], target, m_send.at[r]
        )

    def spread_all(kind, target):
        for r in range(2):

            @pl.when((layer == kind) & (section != 2 * half + r))
            def _():
                spread(r, target, kind).start()

            @pl.when((layer == kind) & (section == 2 * half + r))
            def _():
                keep(r, target).start()

    def edge_across():
        return remote(
            edge_ref.at[1], edge.at[0], e_send.at[0], e_recv.at[0], (me, other_layer)
        )

    def edge_beside(source):
        return remote(source, edge.at[1], e_send.at[1], e_recv.at[1], (me, other_core))

    @pl.when(layer == 0)
    def _():
        edge_across().start()
        edge_beside(edge_ref.at[0]).start()
        edge[0] = edge_ref[0]

    def roles(tree):
        comb, root_z, root_y, rung = tree
        along = jnp.logical_or(jnp.logical_not(comb), y == root_y)
        across = jnp.logical_or(comb, z == rung)
        pivot = jnp.where(y == root_y, root_z, rung)
        child = (
            exists[0] & along & (z <= pivot),
            exists[1] & along & (z >= pivot),
            across & (y == root_y),
        )
        up_z = along & (z != pivot)
        up_y = across & (y != root_y)
        parent = jnp.where(up_z, jnp.where(z < pivot, 1, 0), jnp.where(up_y, 2, 3))
        return child, parent

    def depth_of(k):
        comb, root_z, root_y, rung = tree_of(jnp.maximum(k, 0))
        beyond = jnp.abs(z - rung) + 1 + jnp.abs(rung - root_z)
        return jnp.where(y == root_y, jnp.abs(z - root_z), beyond)

    def depth_from(c):
        return jnp.abs(z - lax.div(c, 2)) + jnp.abs(y - lax.rem(c, 2))

    def neighbour(d):
        return me + jnp.where(d == 0, deltas[0], jnp.where(d == 1, deltas[1], deltas[2]))

    def facing(d):
        return jnp.where(d == 2, 2, 1 - d)

    def transfer(k, d, source):
        there = facing(d)
        return remote(
            buf.at[source, k], buf.at[there, k], send.at[d, k], recv.at[there, k],
            (neighbour(d), section),
        )

    def arrived(k, d):
        remote(
            buf.at[3, k], buf.at[d, k], send.at[0, k], recv.at[d, k], (me, other_core)
        ).wait_recv()

    def put(k, source):
        kk = k - 1
        low = 0
        for target, count, high in (
            (d_ref, n_d, ends[0]), (u_ref, n_u, ends[1]), (o_ref, n_o, ends[2]),
            (q_ref, n_q, chunks - 1),
        ):

            @pl.when((kk >= low) & (kk < high))
            def _():
                at = kk - low
                pltpu.make_async_copy(
                    buf.at[source, k],
                    target.at[
                        pl.ds(pl.multiple_of(at // count[1] * BLOCK, BLOCK), BLOCK),
                        pl.ds(pl.multiple_of(at % count[1] * side, BLOCK), side),
                    ],
                    out_sem.at[k],
                ).start()

            low = high

    def product(k):
        kd = k - 1
        in_d = kd < ends[0]
        ku = kd - ends[0]
        in_u = kd < ends[1]
        ko = kd - ends[1]
        in_o = kd < ends[2]
        kq = kd - ends[2]
        a_at = jnp.where(
            in_d,
            n_q[0] + n_o[0] + n_u[0] + kd // n_d[1],
            jnp.where(
                in_u,
                n_q[0] + n_o[0] + ku // n_u[1],
                jnp.where(in_o, n_q[0] + ko // n_o[1], kq // n_q[1]),
            ),
        )
        b_at = jnp.where(
            in_d,
            n_q[1] + n_o[1] + n_u[1] + kd % n_d[1],
            jnp.where(
                in_u,
                n_q[1] + n_o[1] + ku % n_u[1],
                jnp.where(in_o, n_q[1] + ko % n_o[1], kq % n_q[1]),
            ),
        )
        left = a_ref[:, pl.ds(pl.multiple_of(a_at * BLOCK, BLOCK), BLOCK)]
        right = b_ref[:, pl.ds(pl.multiple_of(b_at * side, BLOCK), side)]
        total[...] = lax.dot_general(
            left, right, (((0,), (0,)), ((), ())), preferred_element_type=F32
        )

    def away(g):
        return remote(
            buf.at[3, chunks - GUESTS + g], buf.at[3, chunks + g], away_send.at[g],
            away_recv.at[g], (me, other_layer),
        )

    def back(g, source):
        return remote(
            buf.at[source, chunks + g], buf.at[0, chunks - GUESTS + g], back_send.at[g],
            back_recv.at[g], (me, other_layer),
        )

    def finish(k, source):
        @pl.when(k < chunks)
        def _():
            put(k, source)

        @pl.when(k >= chunks)
        def _():
            back(k - chunks, source).start()

    def send_away(g):
        k = chunks - GUESTS + g
        product(k)
        buf[3, k] = total[...].astype(BF)
        away(g).start()

    def receive_back(g):
        back(g, 3).wait_recv()
        put(chunks - GUESTS + g, 0)

    def prepare(k):
        @pl.when((k > 0) & (k < jnp.minimum(limit, chunks)))
        def _():
            product(k)
            buf[3, k] = total[...].astype(BF)

    def climb(k, level):
        @pl.when((k >= 0) & (k < limit) & (depth_of(k) == DEPTH - level))
        def _():
            child, parent = roles(tree_of(k))

            @pl.when(k >= chunks)
            def _():
                away(k - chunks).wait_recv()

            if level > 0:

                @pl.when(child[0] | child[1] | child[2])
                def _():
                    total[...] = buf[3, k].astype(F32)
                    for d in range(3):

                        @pl.when(child[d])
                        def _():
                            arrived(k, d)
                            total[...] += buf[d, k].astype(F32)

                    buf[3, k] = total[...].astype(BF)

            if level < DEPTH:
                transfer(k, parent, 3).start()
            else:
                for d in range(3):

                    @pl.when(child[d])
                    def _():
                        transfer(k, d, 3).start()

                finish(k, 3)

    def descend(k, level):
        @pl.when((k >= 0) & (k < limit) & (depth_of(k) == level))
        def _():
            child, parent = roles(tree_of(k))
            arrived(k, parent)
            for d in range(3):

                @pl.when(child[d])
                def _():
                    transfer(k, d, parent).start()

            finish(k, parent)

    def settle(k):
        child, parent = roles(tree_of(k))
        for d in range(3):

            @pl.when(child[d] | (parent == d))
            def _():
                transfer(k, d, 3).wait_send()

        @pl.when((k > 0) & (k < chunks))
        def _():
            pltpu.make_async_copy(
                buf.at[3, k], d_ref.at[pl.ds(0, BLOCK), pl.ds(0, side)], out_sem.at[k]
            ).wait()

    def advance(t):
        old = t - SETTLED * HOP

        @pl.when((old >= 0) & (old < limit))
        def _():
            settle(old)

        for level in range(DEPTH + 1):
            climb(t - level * HOP, level)
        for level in range(1, DEPTH + 1):
            descend(t - (DEPTH + level) * HOP, level)
        prepare(t + 1)

    def settle_away(g):
        pltpu.make_async_copy(
            buf.at[0, chunks - GUESTS + g], d_ref.at[pl.ds(0, BLOCK), pl.ds(0, side)],
            out_sem.at[chunks - GUESTS + g],
        ).wait()
        away(g).wait_send()

    used = listed_ref.shape[1]

    def filled(kind, c):
        return rows.at[kind, c, pl.ds(0, used)]

    def slots_down(c, d):
        return remote(
            filled(0, c), filled(0, c), r_send.at[d, c], r_recv.at[0, c], (neighbour(d), section)
        )

    def slots_across(c):
        return remote(
            filled(0, c), filled(1, c), r_send.at[3, c], r_recv.at[1, c], (me, other_layer)
        )

    def slots_beside(c, kind):
        return remote(
            filled(kind, c), filled(2 + kind, c), r_send.at[4 + kind, c], r_recv.at[2 + kind, c],
            (me, other_core),
        )

    def slots_got(c, kind):
        remote(
            filled(kind, c), filled(kind, c), r_send.at[0, c], r_recv.at[kind, c],
            (me, other_core),
        ).wait_recv()

    def share_slots(c, level):
        @pl.when((c >= 0) & (c < GROUP) & (depth_from(c) == level))
        def _():
            child, parent = roles(rooted_at(c))
            if level > 0:
                slots_got(c, 0)
            for d in range(3):

                @pl.when(child[d])
                def _():
                    slots_down(c, d).start()

            slots_across(c).start()
            slots_beside(c, 0).start()

    def relay_slots(c):
        @pl.when((c >= 0) & (c < GROUP))
        def _():
            slots_got(c, 1)
            slots_beside(c, 1).start()

    def table_up(c, d):
        there = facing(d)
        return remote(
            piece.at[3, c], piece.at[there, c], t_send.at[d, c], t_recv.at[there, c],
            (neighbour(d), section),
        )

    def table_out(c, step):
        to = (section + step) % n_sections
        return remote(
            piece.at[3, c, pl.ds(to * table.shape[1], table.shape[1])], table.at[section],
            f_send.at[step], f_recv.at[section], (me, to),
        )

    def table_climb(c, level):
        @pl.when((c >= 0) & (c < GROUP) & (depth_from(c) == DEPTH - level))
        def _():
            child, parent = roles(rooted_at(c))
            at = c * BLOCK + lax.broadcasted_iota(jnp.int32, (BLOCK, edge.shape[1]), 0)
            reach = edge.shape[1]
            for part in range(2):
                start = pl.multiple_of((half if part == 0 else 1 - half) * reach, reach)
                spots = box_ref[:, pl.ds(start, reach)]
                low_at = jnp.where(half == 0, spots[0:1], spots[1:2])
                high_at = jnp.where(half == 0, spots[2:3], spots[3:4])
                ones = (at == low_at).astype(F32) + (at == high_at).astype(F32)
                term = jnp.dot(ones.astype(BF), edge[part], preferred_element_type=F32)
                if part == 0:
                    total[...] = term
                else:
                    total[...] += term
            if level > 0:
                for d in range(3):

                    @pl.when(child[d])
                    def _():
                        remote(
                            piece.at[3, c], piece.at[d, c], t_send.at[0, c], t_recv.at[d, c],
                            (me, other_core),
                        ).wait_recv()
                        total[...] += piece[d, c].astype(F32)

            piece[3, c] = total[...].astype(BF)
            if level < DEPTH:
                table_up(c, parent).start()
            else:
                for step in range(1, n_sections):
                    table_out(c, step).start()
                kept = table.shape[1]
                table[section] = piece[3, c, pl.ds(pl.multiple_of(section * kept, kept), kept)]

    def extras(t):
        c = t - EXTRA
        for level in range(DEPTH + 1):
            share_slots(c - level * HOP, level)
        relay_slots(c - (DEPTH + 2) * HOP)
        for level in range(DEPTH + 1):
            table_climb(c - GROUP - level * HOP, level)

    def settle_extras(c):
        child, parent = roles(rooted_at(c))
        for d in range(3):

            @pl.when(child[d])
            def _():
                slots_down(c, d).wait_send()

            @pl.when(parent == d)
            def _():
                table_up(c, d).wait_send()

        slots_across(c).wait_send()
        for kind in range(2):
            slots_beside(c, kind).wait_send()

    count = voc.shape[0]
    base = (me * n_sections + section) * count

    def tokens(n):
        at = base + lax.broadcasted_iota(jnp.int32, (count, BLOCK), 0)
        first = lax.rem(half + n // 2, 2) == 0
        spots = []
        for origin in range(GROUP):
            row = ids_ref[origin]
            spots.append((at == jnp.where(first, row[0:1], row[1:2])).astype(F32).astype(BF))
        spots = jnp.concatenate(spots, 1)
        held = rows[n].reshape(GROUP * slots, side)
        term = jnp.dot(spots, held, preferred_element_type=F32)
        columns = pl.ds(pl.multiple_of(lax.rem(layer + n, 2) * side, side), side)

        @pl.when(n < 2)
        def _():
            voc[:, columns] = term

        @pl.when(n >= 2)
        def _():
            voc[:, columns] += term

    def handed(step):
        return remote(
            gathered.at[0], gathered.at[step], g_send.at[step], g_recv.at[step],
            (me, (section + n_sections - step) % n_sections),
        )

    for copy in loads[:2]:
        copy.wait()
    buf[3, 0] = small_ref[...].astype(BF)
    loop(0, FIRST, advance)
    for copy in loads[2:]:
        copy.wait()

    @pl.when(layer == 0)
    def _():
        loop(0, GUESTS, send_away)

    spread_all(0, ing_ref)
    loop(FIRST, EXTRA, advance)

    @pl.when(layer == 1)
    def _():
        pl.semaphore_wait(entered, 2)
        edge_across().wait_recv()
        edge_beside(edge.at[0]).start()

    spread_all(1, act_ref)
    edge_beside(edge.at[0]).wait_recv()
    listed = listed_ref[...].astype(F32)
    square[...] = jnp.full_like(square, -1.0)
    square[0:1, :used] = jnp.where(half == 0, listed[0:1], listed[1:2])
    column = square[...].T[:, 0:1]
    wanted = column == lax.broadcasted_iota(jnp.int32, (slots, edge.shape[1]), 1).astype(F32)
    for kind in range(4):
        for c in range(GROUP):
            rows[kind, c, used:] = jnp.zeros((slots - used, side), BF)
    found = jnp.dot(wanted.astype(F32).astype(BF), edge[0], preferred_element_type=F32)
    rows[0, place, :used] = found[:used].astype(BF)

    def both(t):
        advance(t)
        extras(t)

    middle = EXTRA + 2 * GROUP + (DEPTH + 2) * HOP
    loop(EXTRA, middle, both)
    mine = roles(tree_of(0))[1]
    kept_small = gathered.shape[1]
    gathered[0] = buf[mine, 0, :kept_small]
    for step in range(1, n_sections):
        handed(step).start()
    for c in range(GROUP):
        for kind in range(2):
            slots_got(c, 2 + kind)

    def late(t):
        advance(t)
        n = t - middle - 2

        @pl.when((n >= 0) & (n < 4))
        def _():
            tokens(n)

        @pl.when((n >= 4) & (n < 4 + GROUP))
        def _():
            settle_extras(n - 4)

    loop(middle, limit + 2 * DEPTH * HOP, late)
    for step in range(1, n_sections):
        handed(step).wait()
        table_out(place, step).wait_send()
        source = (section + n_sections - step) % n_sections
        remote(
            piece.at[3, 0, pl.ds(0, table.shape[1])], table.at[source], f_send.at[0],
            f_recv.at[source], (me, other_core),
        ).wait_recv()
    outs = (
        pltpu.make_async_copy(gathered, gathered_ref, last_sem.at[0]),
        pltpu.make_async_copy(rows, rows_ref, last_sem.at[1]),
        pltpu.make_async_copy(table, table_ref, last_sem.at[2]),
        pltpu.make_async_copy(voc, voc_ref, last_sem.at[3]),
    )
    for copy in outs:
        copy.start()

    for r in range(2):
        for kind, target in ((0, ing_ref), (1, act_ref)):

            @pl.when((layer == kind) & (section != 2 * half + r))
            def _():
                spread(r, target, kind).wait_send()

            @pl.when((layer == kind) & (section == 2 * half + r))
            def _():
                keep(r, target).wait()

    for kind, target in ((0, ing_ref), (1, act_ref)):

        @pl.when(section != 2 * kind + layer)
        def _():
            spread(0, target, kind).wait_recv()

    @pl.when(layer == 0)
    def _():
        edge_across().wait_send()

    edge_beside(edge.at[0]).wait_send()
    loop(limit - (SETTLED - 2 * DEPTH) * HOP, limit, settle)

    @pl.when(layer == 0)
    def _():
        loop(0, GUESTS, receive_back)
        loop(0, GUESTS, settle_away)

    @pl.when(layer == 1)
    def _():
        loop(0, GUESTS, lambda g: back(g, 3).wait_send())

    for copy in outs:
        copy.wait()


def reduced(a, b, small, edge, mine, boxes, listed, ids, count, counts, side):
    chunks = 1 + sum(count[0] * count[1] for count in counts)
    n_sections = lax.axis_size("section")
    kept = 32
    slots = BLOCK
    page = edge.shape[1]
    any_space = pl.BlockSpec(memory_space=pl.ANY)
    in_vmem = pl.BlockSpec(memory_space=pltpu.VMEM)
    flops = 2 * a.shape[0] * BLOCK * side * chunks
    dma = pltpu.SemaphoreType.DMA
    return pl.pallas_call(
        functools.partial(reduce_kernel, counts),
        out_shape=tuple(
            jax.ShapeDtypeStruct((count[0] * BLOCK, count[1] * side), BF) for count in counts
        )
        + (
            jax.ShapeDtypeStruct((n_sections, kept, side), BF),
            jax.ShapeDtypeStruct((4, GROUP, slots, side), BF),
            jax.ShapeDtypeStruct((n_sections, BLOCK // n_sections, side), BF),
            jax.ShapeDtypeStruct((mine.shape[0] // 2, mine.shape[1]), BF),
            jax.ShapeDtypeStruct((mine.shape[0] // 2, mine.shape[1]), BF),
            jax.ShapeDtypeStruct((count, mine.shape[1]), F32),
        ),
        in_specs=[any_space] * 2 + [in_vmem] * 2 + [any_space] + [in_vmem] * 3,
        out_specs=(any_space,) * 10,
        scratch_shapes=[
            pltpu.VMEM(a.shape, BF),
            pltpu.VMEM(b.shape, BF),
            pltpu.VMEM((BLOCK, BLOCK), F32),
            pltpu.VMEM((4, chunks + GUESTS, BLOCK, side), BF),
            pltpu.VMEM((BLOCK, side), F32),
            pltpu.VMEM((n_sections, kept, side), BF),
            pltpu.VMEM((2, page, side), BF),
            pltpu.VMEM((4, GROUP, slots, side), BF),
            pltpu.VMEM((n_sections, BLOCK // n_sections, side), BF),
            pltpu.VMEM((4, GROUP, BLOCK, side), BF),
            dma((3, chunks + GUESTS)), dma((3, chunks + GUESTS)), dma((chunks,)),
            dma((n_sections,)), dma((n_sections,)),
            dma((2,)), dma((2,)),
            dma((6, GROUP)), dma((4, GROUP)),
            dma((3, GROUP)), dma((3, GROUP)),
            dma((n_sections,)), dma((n_sections,)),
            dma((2,)), dma((2,)),
            dma((4,)), dma((4,)),
            pltpu.VMEM((count, mine.shape[1]), F32),
            pltpu.SemaphoreType.REGULAR,
            dma((GUESTS,)), dma((GUESTS,)), dma((GUESTS,)), dma((GUESTS,)),
        ],
        compiler_params=pltpu.CompilerParams(
            collective_id=0, has_side_effects=True, vmem_limit_bytes=60 << 20
        ),
        cost_estimate=pl.CostEstimate(
            flops=flops, bytes_accessed=400 << 20, transcendentals=0
        ),
        name="gradient_sums",
    )(a, b, small, edge, mine, boxes, listed, ids)


ROWS = 256


def encoder_kernel(
    words_ref, cot_ref, ids_ref, mask_ref, box_ref, vocab_ref, table_ref, gain_ref, shift_ref,
    q_own, o_own, u_own, d_own, qvb_own, upb_own, gains_ref, shifts_ref,
    a_ref, b_ref, ids_out, edge_ref, mine_ref, small_ref,
    words, ids_all, ids_wide, vocab, spots, picks, land, other, square, norm_in, facts,
    sums_ref, upb_sum, qvb_ref, upb_ref,
    wq, wo, wu, wd, wide, x_land, g_land, x_low, ctx, d_ctx, h_low, act, slope, qkv, d_qkv,
    da_low, df_low, probs, n_one, n_two, r_one, r_two, z, sent_low,
    o_w_send, o_w_recv, c_send, c_recv, i_send, i_recv, s_send, s_recv, o_send, o_recv, local,
    w_local, w_send, w_recv, x_send, x_recv, g_send, g_recv, p_local, p_send, p_recv,
):
    me = lax.axis_index("dp")
    section = lax.axis_index("section")
    n_sections = lax.axis_size("section")
    n_dp = ids_all.shape[0]
    layer = section // 2
    half = section % 2
    mesh_id = pl.DeviceIdType.MESH
    quarter = words_ref.shape[0]
    page, width = x_low.shape
    units = act.shape[2]
    blocks = page // ROWS
    tile = 512
    scale = HEAD_DIM ** (-0.5)
    beside = (me, section + 1 - 2 * half)
    across = (me, (section + 2) % n_sections)
    slots = picks.shape[1]
    side = picks.shape[2]
    held = vocab.shape[0]

    vocab_copy = pltpu.make_async_copy(
        vocab_ref.at[:, pl.ds(pl.multiple_of(layer * side, side), side)], vocab, local.at[0]
    )
    vocab_copy.start()
    table_copies = [
        pltpu.make_async_copy(
            table_ref.at[kind, pl.ds(part * page, page)],
            act.at[kind, :, pl.ds(part * width, width)],
            local.at[2 + 2 * kind + part],
        )
        for kind in range(2)
        for part in range(2)
    ]

    @pl.when(layer == 0)
    def _():
        for copy in table_copies:
            copy.start()

    ids_wide[...] = jnp.full_like(ids_wide, -1)
    ids_wide[:, :slots] = ids_ref[...]

    barrier = pltpu.get_barrier_semaphore()

    def greet(step, carry):
        pl.semaphore_signal(
            barrier, inc=1, device_id=((me + step) % n_dp, section), device_id_type=mesh_id
        )
        return carry

    lax.fori_loop(1, n_dp, greet, 0)
    for step in range(1, n_sections):
        pl.semaphore_signal(
            barrier, inc=1, device_id=(me, (section + step) % n_sections), device_id_type=mesh_id
        )
    pl.semaphore_wait(barrier, n_dp - 1 + n_sections - 1)

    def remote(source, target, sent, got, device):
        return pltpu.make_async_remote_copy(
            src_ref=source, dst_ref=target, send_sem=sent, recv_sem=got, device_id=device,
            device_id_type=mesh_id,
        )

    def weight_copies(i):
        source = (q_own, o_own, u_own, d_own, qvb_own, upb_own)[i].at[0]
        target = (wq, wo, wu, wd, qvb_ref, upb_ref)[i]
        return (
            pltpu.make_async_copy(source, target.at[0], w_local.at[i]),
            remote(source, target.at[1], w_send.at[i], w_recv.at[i], beside),
        )

    def weights_here(i):
        near, far = weight_copies(i)
        near.wait()
        far.wait_recv()

    def ids_move(step):
        return remote(
            ids_wide, ids_all.at[me], i_send.at[step], i_recv.at[me], ((me + step) % n_dp, section)
        )

    def ids_got(step):
        source = (me + step) % n_dp
        return remote(
            ids_wide, ids_all.at[source], i_send.at[0], i_recv.at[source],
            (me, (section + 1) % n_sections),
        )

    loop(1, n_dp, lambda step: ids_move(step).start())
    ids_all[me] = ids_wide[...]

    words_move = remote(
        words_ref, words.at[half], o_w_send, o_w_recv.at[half], (me, layer)
    )
    given_part = g_land.at[pl.ds(pl.multiple_of(half * quarter, quarter), quarter)]
    given_move = remote(cot_ref, given_part, c_send, c_recv.at[half], (me, 2 + layer))
    given_keep = pltpu.make_async_copy(cot_ref, given_part, c_send)

    @pl.when(section != 0)
    def _():
        words_move.start()

    @pl.when(section == 0)
    def _():
        words[0] = words_ref[...]

    @pl.when(section != 3)
    def _():
        given_move.start()

    @pl.when(section == 3)
    def _():
        given_keep.start()

    for i in (0, 4, 5, 1, 2, 3):
        near, far = weight_copies(i)
        far.start()
        near.start()

    loop(1, n_dp, lambda step: ids_got(step).wait_recv())
    lists = ids_all[...].astype(F32)
    lists = jnp.where(half == 0, lists[:, 0], lists[:, 1])
    square[...] = jnp.zeros_like(square)
    square[0:n_dp] = lists
    listed = mask_ref[...].astype(F32)
    square[n_dp : n_dp + 1, :slots] = jnp.where(half == 0, listed[0:1], listed[1:2])
    turned = square[...].T
    at = (me * held + lax.broadcasted_iota(jnp.int32, (slots, held), 1)).astype(F32)
    for origin in range(n_dp):
        spots[origin * slots : (origin + 1) * slots] = (
            at == turned[:slots, origin : origin + 1]
        ).astype(F32).astype(BF)
    vocab_copy.wait()
    found = jnp.dot(spots[...], vocab[...], preferred_element_type=F32).astype(BF)
    for origin in range(n_dp):
        picks[origin] = found[origin * slots : (origin + 1) * slots]

    lines = n_dp // 2
    line, lane_of = me // 2, me % 2

    def slots_beside(at):
        return remote(
            picks.at[2 * at + 1 - lane_of], land.at[at], s_send.at[at], s_recv.at[at],
            (me + 1 - 2 * lane_of, section),
        )

    def slots_along(step):
        to = (line + step) % lines
        return remote(
            picks.at[2 * to + lane_of], land.at[lines + line], s_send.at[lines + to],
            s_recv.at[lines + line], (2 * to + lane_of, section),
        )

    def slots_got(step):
        source = (line + step) % lines
        return remote(
            picks.at[0], land.at[lines + source], s_send.at[0], s_recv.at[lines + source],
            (me, (section + 1) % n_sections),
        )

    def pass_on(step):
        to = (line + step) % lines
        slots_beside(to).wait_recv()
        picks[2 * to + lane_of] = picks[2 * to + lane_of] + land[to]

        @pl.when(step < lines)
        def _():
            slots_along(step).start()

    loop(1, lines + 1, lambda step: slots_beside((line + step) % lines).start())
    loop(1, lines + 1, pass_on)
    land[lines + line] = picks[me]

    @pl.when(layer == 0)
    def _():
        for copy in table_copies:
            copy.wait()
        coords = lax.broadcasted_iota(jnp.int32, (page, page), 0)
        for kind in range(2):
            low_at, high_at = (
                box_ref[i : i + 1, pl.ds(pl.multiple_of(half * page, page), page)]
                for i in (kind, kind + 2)
            )
            for part in range(2):
                at = coords + part * page
                ones = (at == low_at).astype(F32) + (at == high_at).astype(F32)
                term = lax.dot_general(
                    ones.astype(BF), act[kind, :, pl.ds(part * width, width)],
                    (((0,), (0,)), ((), ())), preferred_element_type=F32,
                )
                if kind + part == 0:
                    wide[...] = term
                else:
                    wide[...] += term

    loop(1, lines, lambda step: slots_got(step).wait_recv())
    mine = land[lines]
    for origin in range(1, lines):
        mine = mine + land[lines + origin]
    other[1] = mine
    other_move = remote(other.at[1], other.at[0], o_send, o_recv, (me, half))

    @pl.when(layer == 1)
    def _():
        other_move.start()

    @pl.when(layer == 0)
    def _():
        for r in range(2):

            @pl.when(section + r > 0)
            def _():
                remote(
                    words_ref, words.at[r], o_w_send, o_w_recv.at[r], (me, section + 1)
                ).wait_recv()

        places = lax.broadcasted_iota(jnp.int32, (slots, page), 1).astype(F32)
        chosen = (turned[:slots, n_dp : n_dp + 1] == places).astype(F32).astype(BF)

        def spread_out(right):
            return lax.dot_general(
                chosen, right, (((0,), (0,)), ((), ())), preferred_element_type=F32
            )

        marked = spread_out(jnp.ones((slots, BLOCK), BF))[:, 0:1]
        facts[1] = 1.0 - marked
        other_move.wait_recv()
        for part, values in ((0, other[1]), (1, other[0])):
            columns = pl.ds(part * side, side)
            wide[:, columns] += spread_out(values)
        for r in range(2):
            rows = pl.ds(r * quarter, quarter)
            kept = facts[1, rows]
            summed = wide[rows] + words[r].astype(F32) * kept
            center = summed - jnp.mean(summed, -1, keepdims=True)
            spread = jnp.mean(center * center, -1, keepdims=True)
            inverse = lax.rsqrt(spread + EPS)
            normed = center * inverse
            norm_in[rows] = normed
            facts[0, rows] = inverse
            wide[rows] = normed * gain_ref[...][None] + shift_ref[...][None]

    ids_copy = pltpu.make_async_copy(ids_all, ids_out, local.at[1])
    ids_copy.start()

    @pl.when(layer == 1)
    def _():
        for r in range(2):

            @pl.when(section + r < 4)
            def _():
                remote(
                    cot_ref, g_land.at[pl.ds(r * quarter, quarter)], c_send, c_recv.at[r],
                    (me, section - 1),
                ).wait_recv()

    @pl.when(section == 3)
    def _():
        given_keep.wait()

    def rows_of(block):
        return pl.ds(pl.multiple_of(block * ROWS, ROWS), ROWS)

    def x_move(block):
        rows = rows_of(block)
        return remote(
            sent_low.at[rows], x_land.at[rows], x_send.at[block], x_recv.at[block], across
        )

    def g_move(block):
        rows = rows_of(block)
        return remote(
            sent_low.at[rows], g_land.at[rows], g_send.at[block], g_recv.at[block], across
        )

    spans = (
        (a_ref, 0, width), (a_ref, width, side), (a_ref, width + side, width),
        (a_ref, 2 * width + side, units),
        (b_ref, 0, 3 * side), (b_ref, 3 * side, width), (b_ref, 3 * side + width, units),
        (b_ref, 3 * side + width + units, width),
    )

    def piece_copies(i):
        target, start, size = spans[i]
        source = (x_low, ctx, h_low, act, d_qkv, da_low, slope, df_low)[i]
        double = i in (1, 3, 4, 6)
        columns = pl.ds(start, size)
        return (
            pltpu.make_async_copy(
                source.at[0] if double else source, target.at[0, :, columns], p_local.at[i]
            ),
            remote(
                source.at[1] if double else source, target.at[1, :, columns], p_send.at[i],
                p_recv.at[i], beside,
            ),
        )

    def hand_out(*pieces):
        for i in pieces:
            near, far = piece_copies(i)
            far.start()
            near.start()

    def nt(left, right):
        return lax.dot_general(
            left, right, (((1,), (1,)), ((), ())), preferred_element_type=F32
        )

    def tn(left, right):
        return lax.dot_general(
            left, right, (((0,), (0,)), ((), ())), preferred_element_type=F32
        )

    def centred(values):
        center = values - jnp.mean(values, -1, keepdims=True)
        spread = jnp.mean(center * center, -1, keepdims=True)
        inverse = lax.rsqrt(spread + EPS)
        return center * inverse, inverse

    def pulled(grad, normed, inverse, gain):
        scaled = grad * gain
        return inverse * (
            scaled
            - jnp.mean(scaled, -1, keepdims=True)
            - normed * jnp.mean(scaled * normed, -1, keepdims=True)
        )

    def add_sum(row, values):
        sums_ref[row : row + 1] += jnp.sum(values, 0, keepdims=True)

    sums_ref[...] = jnp.zeros_like(sums_ref)
    upb_sum[...] = jnp.zeros_like(upb_sum)

    for i in (0, 4, 5):
        weights_here(i)

    def project(block):
        rows = rows_of(block)

        @pl.when(layer == 1)
        def _():
            x_move(block).wait_recv()
            wide[rows] = x_land[rows].astype(F32)

        low = wide[rows].astype(BF)
        x_low[rows] = low
        for slot in range(2):
            for c in range(3):
                part = pl.ds(c * side, side)
                value = jnp.dot(low, wq[slot, :, part], preferred_element_type=F32)
                if c != 1:
                    value = value + qvb_ref[slot, c // 2 : c // 2 + 1]
                qkv[slot, rows, part] = value.astype(BF)

    loop(0, blocks, project)
    hand_out(0)

    lane = lax.broadcasted_iota(jnp.int32, (1, 2 * HEAD_DIM), 1)
    masks = ((lane < HEAD_DIM).astype(F32).astype(BF), (lane >= HEAD_DIM).astype(F32).astype(BF))
    first_lane = lax.broadcasted_iota(jnp.int32, (page, 2 * HEAD_DIM), 1) < HEAD_DIM
    first_row = lax.broadcasted_iota(jnp.int32, (2 * HEAD_DIM, page), 0) < HEAD_DIM
    pairs = side // (2 * HEAD_DIM)

    def lanes(i, third):
        at = third * side + (i % pairs) * 2 * HEAD_DIM
        return pl.ds(pl.multiple_of(at, 2 * HEAD_DIM), 2 * HEAD_DIM)

    def attend(i):
        slot = i // pairs
        queries = qkv[slot, :, lanes(i, 0)] * jnp.asarray(scale, BF)
        keys = qkv[slot, :, lanes(i, 1)]
        values = qkv[slot, :, lanes(i, 2)]
        found = []
        for e in range(2):
            scores = nt(keys * masks[e], queries)
            expo = jnp.exp(scores - jnp.max(scores, 0, keepdims=True))
            share = 1.0 / jnp.sum(expo, 0, keepdims=True)
            low = (expo * share).astype(BF)
            probs[2 * i + e] = low
            found.append(tn(values, low))
        ctx[slot, :, lanes(i, 0)] = jnp.where(first_row, found[0], found[1]).T.astype(BF)

    loop(0, 2 * pairs, attend)
    hand_out(1)
    for i in range(1, 4):
        weights_here(i)

    def feed(block):
        rows = rows_of(block)
        attended = (
            jnp.dot(ctx[0, rows], wo[0], preferred_element_type=F32)
            + jnp.dot(ctx[1, rows], wo[1], preferred_element_type=F32)
            + shifts_ref[layer, 0:1]
        )
        normed, inverse = centred(wide[rows] + attended)
        n_one[rows] = normed
        r_one[rows] = inverse
        hidden = normed * gains_ref[layer, 0:1] + shifts_ref[layer, 1:2]
        z[rows] = hidden
        h_low[rows] = hidden.astype(BF)
        for slot in range(2):
            for c in range(units // tile):
                part = pl.ds(c * tile, tile)
                upper = (
                    jnp.dot(h_low[rows], wu[slot, :, part], preferred_element_type=F32)
                    + upb_ref[slot, :, part]
                )
                below = 0.5 * (1.0 + lax.erf(upper * ROOT_HALF))
                act[slot, rows, part] = (upper * below).astype(BF)
                slope[slot, rows, part] = (
                    below + upper * jnp.exp(-0.5 * upper * upper) * INV_ROOT_TWO_PI
                ).astype(BF)
        mixed = (
            jnp.dot(act[0, rows], wd[0], preferred_element_type=F32)
            + jnp.dot(act[1, rows], wd[1], preferred_element_type=F32)
            + shifts_ref[layer, 2:3]
        )
        normed, inverse = centred(z[rows] + mixed)
        n_two[rows] = normed
        r_two[rows] = inverse
        output = normed * gains_ref[layer, 1:2] + shifts_ref[layer, 3:4]
        sent_low[rows] = output.astype(BF)

        @pl.when(layer == 0)
        def _():
            x_move(block).start()

        @pl.when(layer == 1)
        def _():
            mine_ref[rows] = sent_low[rows]

    loop(0, blocks, feed)
    hand_out(2, 3)

    def feed_back(block):
        rows = rows_of(block)

        @pl.when(layer == 0)
        def _():
            g_move(block).wait_recv()

        grad = g_land[rows].astype(F32)
        normed = n_two[rows]
        add_sum(1, grad * normed)
        add_sum(5, grad)
        grad = pulled(grad, normed, r_two[rows], gains_ref[layer, 1:2])
        z[rows] = grad
        low = grad.astype(BF)
        df_low[rows] = low
        add_sum(4, low.astype(F32))
        for slot in range(2):
            for c in range(units // tile):
                part = pl.ds(c * tile, tile)
                term = nt(df_low[rows], wd[slot, part])
                term = (term * slope[slot, rows, part].astype(F32)).astype(BF)
                slope[slot, rows, part] = term
                upb_sum[slot : slot + 1, part] += jnp.sum(term.astype(F32), 0, keepdims=True)
        grad = z[rows] + nt(slope[0, rows], wu[0]) + nt(slope[1, rows], wu[1])
        normed = n_one[rows]
        add_sum(0, grad * normed)
        add_sum(3, grad)
        grad = pulled(grad, normed, r_one[rows], gains_ref[layer, 0:1])
        z[rows] = grad
        low = grad.astype(BF)
        da_low[rows] = low
        add_sum(2, low.astype(F32))
        for slot in range(2):
            d_ctx[slot, rows] = nt(da_low[rows], wo[slot]).astype(BF)

    loop(0, blocks, feed_back)
    hand_out(5, 6, 7)

    def attend_back(i):
        slot = i // pairs
        queries = qkv[slot, :, lanes(i, 0)]
        keys = qkv[slot, :, lanes(i, 1)]
        values = qkv[slot, :, lanes(i, 2)]
        grads = d_ctx[slot, :, lanes(i, 0)]
        d_q, d_k, d_v = [], [], []
        for e in range(2):
            low = probs[2 * i + e]
            share = low.astype(F32)
            term = share * nt(values * masks[e], grads)
            term = (term - share * jnp.sum(term, 0, keepdims=True)).astype(BF)
            d_k.append(jnp.dot(term, queries, preferred_element_type=F32))
            d_v.append(jnp.dot(low, grads, preferred_element_type=F32))
            d_q.append(tn(keys, term))
        d_qkv[slot, :, lanes(i, 0)] = (
            jnp.where(first_row, d_q[0], d_q[1]).T * scale
        ).astype(BF)
        d_qkv[slot, :, lanes(i, 1)] = (jnp.where(first_lane, d_k[0], d_k[1]) * scale).astype(BF)
        d_qkv[slot, :, lanes(i, 2)] = jnp.where(first_lane, d_v[0], d_v[1]).astype(BF)

    loop(0, 2 * pairs, attend_back)
    hand_out(4)

    def leave(block):
        rows = rows_of(block)
        grad = z[rows] + nt(d_qkv[0, rows], wq[0]) + nt(d_qkv[1, rows], wq[1])
        z[rows] = grad

        @pl.when(layer == 1)
        def _():
            sent_low[rows] = z[rows].astype(BF)
            g_move(block).start()

        @pl.when(layer == 0)
        def _():
            grad = z[rows]
            normed = norm_in[rows]
            add_sum(6, grad * normed)
            add_sum(7, grad)
            low = pulled(grad, normed, facts[0, rows], gain_ref[...][None]).astype(BF)
            edge_ref[0, rows] = low[:, :side]
            edge_ref[1, rows] = low[:, side:]
            mine_ref[rows] = (low.astype(F32) * facts[1, rows]).astype(BF)

    loop(0, blocks, leave)
    small_ref[...] = jnp.zeros_like(small_ref)
    pieces = units // side
    for slot in range(2):
        for i in range(2):
            part = pl.ds(2 * i * side, side)
            at = slot * (2 + pieces) + i
            small_ref[at : at + 1] = jnp.sum(
                d_qkv[slot, :, part].astype(F32), 0, keepdims=True
            )
        for i in range(pieces):
            at = slot * (2 + pieces) + 2 + i
            small_ref[at : at + 1] = upb_sum[slot : slot + 1, pl.ds(i * side, side)]
    for i in range(8):
        for j in range(2):
            at = 2 * (2 + pieces) + 2 * i + j
            small_ref[at : at + 1] = sums_ref[i : i + 1, pl.ds(j * side, side)]
    for block in range(blocks):

        @pl.when(layer == 0)
        def _():
            x_move(block).wait_send()

        @pl.when(layer == 1)
        def _():
            g_move(block).wait_send()

    for i in range(6):
        weight_copies(i)[1].wait_send()
    for i in range(8):
        near, far = piece_copies(i)
        near.wait()
        far.wait()


    @pl.when(layer == 1)
    def _():
        other_move.wait_send()

    @pl.when(section != 0)
    def _():
        words_move.wait_send()

    @pl.when(section != 3)
    def _():
        given_move.wait_send()

    loop(1, n_dp, lambda step: ids_move(step).wait_send())
    loop(0, lines, lambda at: slots_beside(at).wait_send())
    loop(1, lines, lambda step: slots_along(step).wait_send())
    ids_copy.wait()


def encoded(
    words, cot, ids, mask, boxes, vocab, table, gain, shift, weights, qvb, upb, gains, shifts
):
    quarter, width = words.shape
    page = 2 * quarter
    n_dp = lax.axis_size("dp")
    slots = ids.shape[1]
    held = vocab.shape[0]
    side = width // 2
    units = weights[3].shape[1]
    blocks = page // ROWS
    heads = width // HEAD_DIM
    any_space = pl.BlockSpec(memory_space=pl.ANY)
    in_vmem = pl.BlockSpec(memory_space=pltpu.VMEM)
    dma = pltpu.SemaphoreType.DMA
    vmem = pltpu.VMEM
    flops = 8 * page * width * (4 * width + 4 * units) * 2
    return pl.pallas_call(
        encoder_kernel,
        out_shape=(
            jax.ShapeDtypeStruct((2, page, 2 * width + side + units), BF),
            jax.ShapeDtypeStruct((2, page, 3 * side + 2 * width + units), BF),
            jax.ShapeDtypeStruct((n_dp, 2, BLOCK), jnp.int32),
            jax.ShapeDtypeStruct((2, page, side), BF),
            jax.ShapeDtypeStruct((page, width), BF),
            jax.ShapeDtypeStruct((BLOCK, side), F32),
        ),
        in_specs=[in_vmem, any_space] + [in_vmem] * 3 + [any_space] * 2 + [in_vmem] * 2
        + [any_space] * 6 + [in_vmem] * 2,
        out_specs=(any_space,) * 3 + (in_vmem,) * 3,
        scratch_shapes=[
            vmem((2, quarter, width), BF), vmem((n_dp, 2, BLOCK), jnp.int32),
            vmem((2, BLOCK), jnp.int32),
            vmem((held, side), BF), vmem((n_dp * slots, held), BF),
            vmem((n_dp, slots, side), BF), vmem((n_dp, slots, side), BF),
            vmem((2, slots, side), BF), vmem((BLOCK, BLOCK), F32),
            vmem((page, width), F32), vmem((2, page, 1), F32),
            vmem((8, width), F32), vmem((2, units), F32),
            vmem((2, 2, side), F32), vmem((2, 1, units), F32),
            vmem((2, width, 3 * side), BF), vmem((2, side, width), BF),
            vmem((2, width, units), BF), vmem((2, units, width), BF),
            vmem((page, width), F32), vmem((page, width), BF), vmem((page, width), BF),
            vmem((page, width), BF), vmem((2, page, side), BF), vmem((2, page, side), BF),
            vmem((page, width), BF), vmem((2, page, units), BF), vmem((2, page, units), BF),
            vmem((2, page, 3 * side), BF), vmem((2, page, 3 * side), BF),
            vmem((page, width), BF), vmem((page, width), BF), vmem((heads, page, page), BF),
            vmem((page, width), F32), vmem((page, width), F32),
            vmem((page, 1), F32), vmem((page, 1), F32),
            vmem((page, width), F32), vmem((page, width), BF),
            dma, dma((2,)), dma, dma((2,)), dma((n_dp,)), dma((n_dp,)),
            dma((n_dp,)), dma((n_dp,)), dma, dma, dma((6,)),
            dma((6,)), dma((6,)), dma((6,)),
            dma((blocks,)), dma((blocks,)), dma((blocks,)), dma((blocks,)),
            dma((8,)), dma((8,)), dma((8,)),
        ],
        compiler_params=pltpu.CompilerParams(
            collective_id=1, has_side_effects=True, vmem_limit_bytes=63 << 20
        ),
        cost_estimate=pl.CostEstimate(
            flops=flops, bytes_accessed=200 << 20, transcendentals=0
        ),
        name="encoder_both_ways",
    )(words, cot, ids, mask, boxes, vocab, table, gain, shift, *weights, qvb, upb, gains, shifts)


def finish_kernel(
    pieces, q_in, o_in, u_in, d_in, voc_in, small_ref, table_ref, act_in, ing_in,
    act_ref, ing_ref, tab_ref, voc_ref, q_ref, qvb_ref, o_ref, u_ref, upb_ref, d_ref, gains_ref,
    shifts_ref, eg_ref, es_ref,
    q_s, o_s, u_s, d_s, q_f, o_f, u_f, d_f, act_s, ing_s, act_f, ing_f, in_sem, out_sem, voc_s, voc_sem,
):
    section = lax.axis_index("section")
    layer = section // 2
    half = section % 2
    side = table_ref.shape[2]
    voc_copy = pltpu.make_async_copy(voc_in, voc_s, voc_sem.at[0])
    voc_copy.start()
    moves = []
    for source, low, wide, target in (
        (d_in, d_s, d_f, d_ref), (u_in, u_s, u_f, u_ref), (q_in, q_s, q_f, q_ref),
        (o_in, o_s, o_f, o_ref),
    ):
        count = low.shape[0] // pieces
        for i in range(pieces):
            rows = pl.ds(i * count, count)
            moves.append((source.at[rows], low.at[rows], wide.at[rows], target.at[0, rows]))
    moves.append((act_in, act_s, act_f, act_ref))
    moves.append((ing_in, ing_s, ing_f, ing_ref))
    for i, (source, low, wide, target) in enumerate(moves):
        pltpu.make_async_copy(source, low, in_sem.at[i]).start()


    parts = small_ref[...].astype(F32)
    partner = jnp.where(half == 0, parts[1], parts[3])
    far_partner = jnp.where(half == 0, parts[3], parts[1])
    splits = d_in.shape[0] // side
    kept = 2 + splits
    own = parts[0, :kept] + partner[kept : 2 * kept]
    qvb_ref[0] = own[:2]
    for i in range(splits):
        upb_ref[0:1, pl.ds(i * side, side)] = own[2 + i : 3 + i]
    here = (parts[0] + partner)[2 * kept : 2 * kept + 16]
    there = (parts[2] + far_partner)[2 * kept : 2 * kept + 16]
    in_order = (jnp.where(layer == 0, here, there), jnp.where(layer == 0, there, here))
    for j in range(2):
        columns = pl.ds(j * side, side)
        for l in range(2):
            for i in range(2):
                at = 2 * i + j
                gains_ref[l, i : i + 1, columns] = in_order[l][at : at + 1]
            for i in range(4):
                at = 4 + 2 * i + j
                shifts_ref[l, i : i + 1, columns] = in_order[l][at : at + 1]
        eg_ref[columns] = in_order[0][12 + j]
        es_ref[columns] = in_order[0][14 + j]
    for l in range(2):
        for h in range(2):
            tab_ref[h, :, pl.ds(l * side, side)] = table_ref[2 * l + h].astype(F32)

    voc_copy.wait()
    voc_out = pltpu.make_async_copy(voc_s, voc_ref, voc_sem.at[1])
    voc_out.start()
    for i, (source, low, wide, target) in enumerate(moves):
        pltpu.make_async_copy(source, low, in_sem.at[i]).wait()
        wide[...] = low[...].astype(F32)
        pltpu.make_async_copy(wide, target, out_sem.at[i]).start()

    for i, (source, low, wide, target) in enumerate(moves):
        pltpu.make_async_copy(wide, target, out_sem.at[i]).wait()
    voc_out.wait()


def finished(sums, voc, small, tables, act, ing, side):
    any_space = pl.BlockSpec(memory_space=pl.ANY)
    in_vmem = pl.BlockSpec(memory_space=pltpu.VMEM)
    dma = pltpu.SemaphoreType.DMA
    vmem = pltpu.VMEM
    pieces = 4
    width = act.shape[1]
    units = sums[3].shape[0]
    shapes = [array.shape for array in sums]
    outs = [
        jax.ShapeDtypeStruct(shape, F32)
        for shape in (
            act.shape, ing.shape, (2, tables.shape[1], width), voc.shape, (1, *shapes[0]),
            (1, 2, side), (1, *shapes[1]), (1, *shapes[2]), (1, units), (1, *shapes[3]),
            (2, 2, width), (2, 4, width), (width,), (width,),
        )
    ]
    specs = [any_space] * 2 + [in_vmem] + [any_space] * 2 + [in_vmem, any_space, any_space, in_vmem, any_space] + [in_vmem] * 4
    return pl.pallas_call(
        functools.partial(finish_kernel, pieces),
        out_shape=outs,
        in_specs=[any_space] * 5 + [in_vmem] * 2 + [any_space] * 2,
        out_specs=specs,
        scratch_shapes=[vmem(shape, BF) for shape in shapes]
        + [vmem(shape, F32) for shape in shapes]
        + [vmem(act.shape, BF)] * 2
        + [vmem(act.shape, F32)] * 2
        + [dma((4 * pieces + 2,)), dma((4 * pieces + 2,)), vmem(voc.shape, F32), dma((2,))],
        compiler_params=pltpu.CompilerParams(vmem_limit_bytes=60 << 20),
        name="finished_outputs",
    )(*sums, voc, small, tables, act, ing)


def on_device(
    word_embed, boxes, mask_pos, replace_ids, cotangent, layout_table, vocab_table, embed_gain,
    embed_shift, qkv_weight, qv_bias, out_weight, up_weight, up_bias, down_weight, layer_gains,
    layer_biases,
):
    section = lax.axis_index("section")
    layer = section // 2
    half = section % 2
    quarter, width = word_embed.shape
    page = 2 * quarter
    side = qkv_weight.shape[2] // 3
    units = up_bias.shape[1]

    left, right, all_ids, edge, mine, small = encoded(
        word_embed, cotangent, replace_ids, mask_pos, boxes, vocab_table, layout_table,
        embed_gain, embed_shift, (qkv_weight, out_weight, up_weight, down_weight), qv_bias,
        up_bias[:, None], layer_gains, layer_biases,
    )
    left, right = (array.reshape(2 * page, -1) for array in (left, right))
    counts = (
        (width // BLOCK, 3),
        (side // BLOCK, width // side),
        (width // BLOCK, units // side),
        (units // BLOCK, width // side),
    )
    count = vocab_table.shape[0] // lax.axis_size("section")
    *sums, gathered, slot_rows, table_rows, act, ing, voc = reduced(
        left, right, small, edge, mine, boxes, mask_pos, all_ids, count, counts, side
    )
    outer = lax.axis_size("dp") // GROUP
    table_part = None
    if outer > 1:
        groups = [[i + GROUP * g for g in range(outer)] for i in range(GROUP)]
        *sums, gathered = lax.psum((*sums, gathered), "dp", axis_index_groups=groups)
        slot_rows = lax.all_gather(slot_rows, "dp", axis_index_groups=groups, axis=1, tiled=True)
        here = jnp.arange(count, dtype=jnp.int32)
        here = here + (lax.axis_index("dp") * lax.axis_size("section") + section) * count
        ordered_ids = jnp.where(half == 0, all_ids, all_ids[:, ::-1])
        ordered_ids = ordered_ids.transpose(1, 0, 2).reshape(-1)
        held = slot_rows.reshape(2, 2, -1, side).transpose(0, 2, 1, 3).reshape(-1, width)
        voc = jnp.dot(
            (here[:, None] == ordered_ids[None]).astype(BF), held, preferred_element_type=F32
        )
        voc = jnp.where(layer == 0, voc, jnp.roll(voc, side, 1))
        coords = jnp.arange(layout_table.shape[1], dtype=jnp.int32)
        page_boxes = lax.dynamic_slice_in_dim(boxes, half * page, page, 1)
        grad_low = jnp.concatenate([edge[0], edge[1]], 1)
        grad_low = jnp.where(layer == 0, grad_low, jnp.zeros_like(grad_low))
        table_grad = jnp.stack(
            [
                matmul_left_t(
                    (page_boxes[a][:, None] == coords[None, :]).astype(BF)
                    + (page_boxes[a + 2][:, None] == coords[None, :]).astype(BF),
                    grad_low,
                )
                for a in (0, 1)
            ]
        )
        table_part = lax.psum_scatter(
            table_grad.astype(BF), ("dp", "section"), scatter_dimension=1, tiled=True
        ).astype(F32)
    act, ing, tables, vocab_part, *rest = finished(
        sums, voc, gathered, table_rows, act, ing, side
    )
    if table_part is None:
        table_part = tables
    *layer_sums, gains_sum, shifts_sum, gain_sum, shift_sum = rest
    return (
        act, ing, table_part, vocab_part, gain_sum, shift_sum, *layer_sums, gains_sum, shifts_sum,
    )


def solution(mesh):
    both = ("dp", "section")
    by_section = P("section", None, None)
    return jax.shard_map(
        on_device,
        mesh=mesh,
        in_specs=(
            P(both, None), P(None, "dp"), P("dp", None), P("dp", None), P(both, None), P(),
            P("dp", None), P(), P(), by_section, by_section, by_section, by_section,
            P("section", None), by_section, P(), P(),
        ),
        out_specs=(
            P(both, None), P(both, None), P(None, both, None), P(both, None), P(), P(),
            by_section, by_section, by_section, by_section, P("section", None), by_section,
            P(), P(),
        ),
        check_vma=False,
    )
```

```python
import functools

import jax
import jax.numpy as jnp
from jax import lax
from jax.experimental import pallas as pl
from jax.experimental.pallas import tpu as pltpu
from jax.sharding import PartitionSpec as P

HEAD_DIM = 64
EPS = 1e-12
ROOT_HALF = 0.7071067811865476
INV_ROOT_TWO_PI = 0.3989422804014327
BF = jnp.bfloat16
F32 = jnp.float32


def matmul_left_t(left, right):
    return jnp.einsum("pa,pb->ab", left, right, preferred_element_type=F32)


GROUP = 8
BLOCK = 128
HOP = 5
DEPTH = 4
FIRST = 20
EXTRA = 36
GUESTS = 7
SETTLED = 9


def tree_of(k):
    lines = lax.div(4 * k, 10)
    comb = lax.rem(4 * k, 10) < 6
    pick = jnp.where(comb, k - lines, lines)
    root_z = 3 * lax.rem(pick, 2)
    near = lax.rem(lax.div(pick, 4), 2)
    rung = jnp.where(comb, root_z, jnp.where(root_z == 0, near, 3 - near))
    return comb, root_z, lax.rem(lax.div(pick, 2), 2), rung


def rooted_at(c):
    line = lax.div(c, 2)
    return lax.rem(line, 2) == 0, line, lax.rem(c, 2), line


def loop(low, high, body):
    def step(k, carry):
        body(k)
        return carry

    lax.fori_loop(low, high, step, 0)


def reduce_kernel(
    counts, a_in, b_in, small_ref, edge_ref, mine_ref, box_ref, listed_ref, ids_ref,
    q_ref, o_ref, u_ref, d_ref, gathered_ref, rows_ref, table_ref, act_ref, ing_ref, voc_ref,
    a_ref, b_ref, square, buf, total, gathered, edge, rows, table, piece,
    send, recv, out_sem, g_send, g_recv, e_send, e_recv, r_send, r_recv, t_send, t_recv,
    f_send, f_recv, m_send, m_recv, last_sem, in_sem, voc, entered,
    away_send, away_recv, back_send, back_recv,
):
    a_cut = a_ref.shape[1] - counts[3][0] * BLOCK
    b_cut = b_ref.shape[1] - counts[3][1] * buf.shape[3]
    loads = []
    for columns_a, columns_b in (
        (pl.ds(a_cut, a_ref.shape[1] - a_cut), pl.ds(b_cut, b_ref.shape[1] - b_cut)),
        (pl.ds(0, a_cut), pl.ds(0, b_cut)),
    ):
        for source, target, columns in ((a_in, a_ref, columns_a), (b_in, b_ref, columns_b)):
            loads.append(
                pltpu.make_async_copy(
                    source.at[:, columns], target.at[:, columns], in_sem.at[len(loads)]
                )
            )
    for copy in loads:
        copy.start()
    me = lax.axis_index("dp")
    section = lax.axis_index("section")
    n_sections = lax.axis_size("section")
    layer = section // 2
    half = section % 2
    other_core = section + 1 - 2 * half
    other_layer = (section + 2) % n_sections
    place = me % GROUP
    z = place // 2
    y = place % 2
    chunks = buf.shape[1] - GUESTS
    limit = jnp.where(layer == 0, chunks - GUESTS, chunks + GUESTS)
    side = buf.shape[3]
    slots = rows.shape[2]
    n_q, n_o, n_u, n_d = counts
    ends = (n_d[0] * n_d[1],)
    ends += (ends[0] + n_u[0] * n_u[1],)
    ends += (ends[1] + n_o[0] * n_o[1],)
    mesh_id = pl.DeviceIdType.MESH
    deltas = (-2, 2, 1 - 2 * y)
    exists = (z > 0, z < GROUP // 2 - 1, y >= 0)

    barrier = pltpu.get_barrier_semaphore()
    for d in range(3):

        @pl.when(exists[d])
        def _():
            pl.semaphore_signal(
                barrier, inc=1, device_id=(me + deltas[d], section), device_id_type=mesh_id
            )

    pl.semaphore_signal(barrier, inc=1, device_id=(me, other_core), device_id_type=mesh_id)

    @pl.when(layer == 1)
    def _():
        for h in range(2):
            pl.semaphore_signal(barrier, inc=1, device_id=(me, h), device_id_type=mesh_id)

    around = 2 + jnp.where(exists[0], 1, 0) + jnp.where(exists[1], 1, 0)
    pl.semaphore_wait(barrier, around + jnp.where(layer == 0, 2, 0))

    @pl.when(layer == 0)
    def _():
        for h in range(2):
            pl.semaphore_signal(entered, inc=1, device_id=(me, 2 + h), device_id_type=mesh_id)

    def remote(source, target, sent, got, device):
        return pltpu.make_async_remote_copy(
            src_ref=source, dst_ref=target, send_sem=sent, recv_sem=got, device_id=device,
            device_id_type=mesh_id,
        )

    quarter = mine_ref.shape[0] // 2

    def spread(r, target, kind):
        return remote(
            mine_ref.at[pl.ds(r * quarter, quarter)], target, m_send.at[r], m_recv.at[kind],
            (me, 2 * half + r),
        )

    def keep(r, target):
        return pltpu.make_async_copy(
            mine_ref.at[pl.ds(r * quarter, quarter)], target, m_send.at[r]
        )

    def spread_all(kind, target):
        for r in range(2):

            @pl.when((layer == kind) & (section != 2 * half + r))
            def _():
                spread(r, target, kind).start()

            @pl.when((layer == kind) & (section == 2 * half + r))
            def _():
                keep(r, target).start()

    def edge_across():
        return remote(
            edge_ref.at[1], edge.at[0], e_send.at[0], e_recv.at[0], (me, other_layer)
        )

    def edge_beside(source):
        return remote(source, edge.at[1], e_send.at[1], e_recv.at[1], (me, other_core))

    @pl.when(layer == 0)
    def _():
        edge_across().start()
        edge_beside(edge_ref.at[0]).start()
        edge[0] = edge_ref[0]

    def roles(tree):
        comb, root_z, root_y, rung = tree
        along = jnp.logical_or(jnp.logical_not(comb), y == root_y)
        across = jnp.logical_or(comb, z == rung)
        pivot = jnp.where(y == root_y, root_z, rung)
        child = (
            exists[0] & along & (z <= pivot),
            exists[1] & along & (z >= pivot),
            across & (y == root_y),
        )
        up_z = along & (z != pivot)
        up_y = across & (y != root_y)
        parent = jnp.where(up_z, jnp.where(z < pivot, 1, 0), jnp.where(up_y, 2, 3))
        return child, parent

    def depth_of(k):
        comb, root_z, root_y, rung = tree_of(jnp.maximum(k, 0))
        beyond = jnp.abs(z - rung) + 1 + jnp.abs(rung - root_z)
        return jnp.where(y == root_y, jnp.abs(z - root_z), beyond)

    def depth_from(c):
        return jnp.abs(z - lax.div(c, 2)) + jnp.abs(y - lax.rem(c, 2))

    def neighbour(d):
        return me + jnp.where(d == 0, deltas[0], jnp.where(d == 1, deltas[1], deltas[2]))

    def facing(d):
        return jnp.where(d == 2, 2, 1 - d)

    def transfer(k, d, source):
        there = facing(d)
        return remote(
            buf.at[source, k], buf.at[there, k], send.at[d, k], recv.at[there, k],
            (neighbour(d), section),
        )

    def arrived(k, d):
        remote(
            buf.at[3, k], buf.at[d, k], send.at[0, k], recv.at[d, k], (me, other_core)
        ).wait_recv()

    def put(k, source):
        kk = k - 1
        low = 0
        for target, count, high in (
            (d_ref, n_d, ends[0]), (u_ref, n_u, ends[1]), (o_ref, n_o, ends[2]),
            (q_ref, n_q, chunks - 1),
        ):

            @pl.when((kk >= low) & (kk < high))
            def _():
                at = kk - low
                pltpu.make_async_copy(
                    buf.at[source, k],
                    target.at[
                        pl.ds(pl.multiple_of(at // count[1] * BLOCK, BLOCK), BLOCK),
                        pl.ds(pl.multiple_of(at % count[1] * side, BLOCK), side),
                    ],
                    out_sem.at[k],
                ).start()

            low = high

    def product(k):
        kd = k - 1
        in_d = kd < ends[0]
        ku = kd - ends[0]
        in_u = kd < ends[1]
        ko = kd - ends[1]
        in_o = kd < ends[2]
        kq = kd - ends[2]
        a_at = jnp.where(
            in_d,
            n_q[0] + n_o[0] + n_u[0] + kd // n_d[1],
            jnp.where(
                in_u,
                n_q[0] + n_o[0] + ku // n_u[1],
                jnp.where(in_o, n_q[0] + ko // n_o[1], kq // n_q[1]),
            ),
        )
        b_at = jnp.where(
            in_d,
            n_q[1] + n_o[1] + n_u[1] + kd % n_d[1],
            jnp.where(
                in_u,
                n_q[1] + n_o[1] + ku % n_u[1],
                jnp.where(in_o, n_q[1] + ko % n_o[1], kq % n_q[1]),
            ),
        )
        left = a_ref[:, pl.ds(pl.multiple_of(a_at * BLOCK, BLOCK), BLOCK)]
        right = b_ref[:, pl.ds(pl.multiple_of(b_at * side, BLOCK), side)]
        total[...] = lax.dot_general(
            left, right, (((0,), (0,)), ((), ())), preferred_element_type=F32
        )

    def away(g):
        return remote(
            buf.at[3, chunks - GUESTS + g], buf.at[3, chunks + g], away_send.at[g],
            away_recv.at[g], (me, other_layer),
        )

    def back(g, source):
        return remote(
            buf.at[source, chunks + g], buf.at[0, chunks - GUESTS + g], back_send.at[g],
            back_recv.at[g], (me, other_layer),
        )

    def finish(k, source):
        @pl.when(k < chunks)
        def _():
            put(k, source)

        @pl.when(k >= chunks)
        def _():
            back(k - chunks, source).start()

    def send_away(g):
        k = chunks - GUESTS + g
        product(k)
        buf[3, k] = total[...].astype(BF)
        away(g).start()

    def receive_back(g):
        back(g, 3).wait_recv()
        put(chunks - GUESTS + g, 0)

    def prepare(k):
        @pl.when((k > 0) & (k < jnp.minimum(limit, chunks)))
        def _():
            product(k)
            buf[3, k] = total[...].astype(BF)

    def climb(k, level):
        @pl.when((k >= 0) & (k < limit) & (depth_of(k) == DEPTH - level))
        def _():
            child, parent = roles(tree_of(k))

            @pl.when(k >= chunks)
            def _():
                away(k - chunks).wait_recv()

            if level > 0:

                @pl.when(child[0] | child[1] | child[2])
                def _():
                    total[...] = buf[3, k].astype(F32)
                    for d in range(3):

                        @pl.when(child[d])
                        def _():
                            arrived(k, d)
                            total[...] += buf[d, k].astype(F32)

                    buf[3, k] = total[...].astype(BF)

            if level < DEPTH:
                transfer(k, parent, 3).start()
            else:
                for d in range(3):

                    @pl.when(child[d])
                    def _():
                        transfer(k, d, 3).start()

                finish(k, 3)

    def descend(k, level):
        @pl.when((k >= 0) & (k < limit) & (depth_of(k) == level))
        def _():
            child, parent = roles(tree_of(k))
            arrived(k, parent)
            for d in range(3):

                @pl.when(child[d])
                def _():
                    transfer(k, d, parent).start()

            finish(k, parent)

    def settle(k):
        child, parent = roles(tree_of(k))
        for d in range(3):

            @pl.when(child[d] | (parent == d))
            def _():
                transfer(k, d, 3).wait_send()

        @pl.when((k > 0) & (k < chunks))
        def _():
            pltpu.make_async_copy(
                buf.at[3, k], d_ref.at[pl.ds(0, BLOCK), pl.ds(0, side)], out_sem.at[k]
            ).wait()

    def advance(t):
        old = t - SETTLED * HOP

        @pl.when((old >= 0) & (old < limit))
        def _():
            settle(old)

        for level in range(DEPTH + 1):
            climb(t - level * HOP, level)
        for level in range(1, DEPTH + 1):
            descend(t - (DEPTH + level) * HOP, level)
        prepare(t + 1)

    def settle_away(g):
        pltpu.make_async_copy(
            buf.at[0, chunks - GUESTS + g], d_ref.at[pl.ds(0, BLOCK), pl.ds(0, side)],
            out_sem.at[chunks - GUESTS + g],
        ).wait()
        away(g).wait_send()

    used = listed_ref.shape[1]

    def filled(kind, c):
        return rows.at[kind, c, pl.ds(0, used)]

    def slots_down(c, d):
        return remote(
            filled(0, c), filled(0, c), r_send.at[d, c], r_recv.at[0, c], (neighbour(d), section)
        )

    def slots_across(c):
        return remote(
            filled(0, c), filled(1, c), r_send.at[3, c], r_recv.at[1, c], (me, other_layer)
        )

    def slots_beside(c, kind):
        return remote(
            filled(kind, c), filled(2 + kind, c), r_send.at[4 + kind, c], r_recv.at[2 + kind, c],
            (me, other_core),
        )

    def slots_got(c, kind):
        remote(
            filled(kind, c), filled(kind, c), r_send.at[0, c], r_recv.at[kind, c],
            (me, other_core),
        ).wait_recv()

    def share_slots(c, level):
        @pl.when((c >= 0) & (c < GROUP) & (depth_from(c) == level))
        def _():
            child, parent = roles(rooted_at(c))
            if level > 0:
                slots_got(c, 0)
            for d in range(3):

                @pl.when(child[d])
                def _():
                    slots_down(c, d).start()

            slots_across(c).start()
            slots_beside(c, 0).start()

    def relay_slots(c):
        @pl.when((c >= 0) & (c < GROUP))
        def _():
            slots_got(c, 1)
            slots_beside(c, 1).start()

    def table_up(c, d):
        there = facing(d)
        return remote(
            piece.at[3, c], piece.at[there, c], t_send.at[d, c], t_recv.at[there, c],
            (neighbour(d), section),
        )

    def table_out(c, step):
        to = (section + step) % n_sections
        return remote(
            piece.at[3, c, pl.ds(to * table.shape[1], table.shape[1])], table.at[section],
            f_send.at[step], f_recv.at[section], (me, to),
        )

    def table_climb(c, level):
        @pl.when((c >= 0) & (c < GROUP) & (depth_from(c) == DEPTH - level))
        def _():
            child, parent = roles(rooted_at(c))
            at = c * BLOCK + lax.broadcasted_iota(jnp.int32, (BLOCK, edge.shape[1]), 0)
            reach = edge.shape[1]
            for part in range(2):
                start = pl.multiple_of((half if part == 0 else 1 - half) * reach, reach)
                spots = box_ref[:, pl.ds(start, reach)]
                low_at = jnp.where(half == 0, spots[0:1], spots[1:2])
                high_at = jnp.where(half == 0, spots[2:3], spots[3:4])
                ones = (at == low_at).astype(F32) + (at == high_at).astype(F32)
                term = jnp.dot(ones.astype(BF), edge[part], preferred_element_type=F32)
                if part == 0:
                    total[...] = term
                else:
                    total[...] += term
            if level > 0:
                for d in range(3):

                    @pl.when(child[d])
                    def _():
                        remote(
                            piece.at[3, c], piece.at[d, c], t_send.at[0, c], t_recv.at[d, c],
                            (me, other_core),
                        ).wait_recv()
                        total[...] += piece[d, c].astype(F32)

            piece[3, c] = total[...].astype(BF)
            if level < DEPTH:
                table_up(c, parent).start()
            else:
                for step in range(1, n_sections):
                    table_out(c, step).start()
                kept = table.shape[1]
                table[section] = piece[3, c, pl.ds(pl.multiple_of(section * kept, kept), kept)]

    def extras(t):
        c = t - EXTRA
        for level in range(DEPTH + 1):
            share_slots(c - level * HOP, level)
        relay_slots(c - (DEPTH + 2) * HOP)
        for level in range(DEPTH + 1):
            table_climb(c - GROUP - level * HOP, level)

    def settle_extras(c):
        child, parent = roles(rooted_at(c))
        for d in range(3):

            @pl.when(child[d])
            def _():
                slots_down(c, d).wait_send()

            @pl.when(parent == d)
            def _():
                table_up(c, d).wait_send()

        slots_across(c).wait_send()
        for kind in range(2):
            slots_beside(c, kind).wait_send()

    count = voc.shape[0]
    base = (me * n_sections + section) * count

    def tokens(n):
        at = base + lax.broadcasted_iota(jnp.int32, (count, BLOCK), 0)
        first = lax.rem(half + n // 2, 2) == 0
        spots = []
        for origin in range(GROUP):
            row = ids_ref[origin]
            spots.append((at == jnp.where(first, row[0:1], row[1:2])).astype(F32).astype(BF))
        spots = jnp.concatenate(spots, 1)
        held = rows[n].reshape(GROUP * slots, side)
        term = jnp.dot(spots, held, preferred_element_type=F32)
        columns = pl.ds(pl.multiple_of(lax.rem(layer + n, 2) * side, side), side)

        @pl.when(n < 2)
        def _():
            voc[:, columns] = term

        @pl.when(n >= 2)
        def _():
            voc[:, columns] += term

    def handed(step):
        return remote(
            gathered.at[0], gathered.at[step], g_send.at[step], g_recv.at[step],
            (me, (section + n_sections - step) % n_sections),
        )

    for copy in loads[:2]:
        copy.wait()
    buf[3, 0] = small_ref[...].astype(BF)
    loop(0, FIRST, advance)
    for copy in loads[2:]:
        copy.wait()

    @pl.when(layer == 0)
    def _():
        loop(0, GUESTS, send_away)

    spread_all(0, ing_ref)
    loop(FIRST, EXTRA, advance)

    @pl.when(layer == 1)
    def _():
        pl.semaphore_wait(entered, 2)
        edge_across().wait_recv()
        edge_beside(edge.at[0]).start()

    spread_all(1, act_ref)
    edge_beside(edge.at[0]).wait_recv()
    listed = listed_ref[...].astype(F32)
    square[...] = jnp.full_like(square, -1.0)
    square[0:1, :used] = jnp.where(half == 0, listed[0:1], listed[1:2])
    column = square[...].T[:, 0:1]
    wanted = column == lax.broadcasted_iota(jnp.int32, (slots, edge.shape[1]), 1).astype(F32)
    for kind in range(4):
        for c in range(GROUP):
            rows[kind, c, used:] = jnp.zeros((slots - used, side), BF)
    found = jnp.dot(wanted.astype(F32).astype(BF), edge[0], preferred_element_type=F32)
    rows[0, place, :used] = found[:used].astype(BF)

    def both(t):
        advance(t)
        extras(t)

    middle = EXTRA + 2 * GROUP + (DEPTH + 2) * HOP
    loop(EXTRA, middle, both)
    mine = roles(tree_of(0))[1]
    kept_small = gathered.shape[1]
    gathered[0] = buf[mine, 0, :kept_small]
    for step in range(1, n_sections):
        handed(step).start()
    for c in range(GROUP):
        for kind in range(2):
            slots_got(c, 2 + kind)

    def late(t):
        advance(t)
        n = t - middle - 2

        @pl.when((n >= 0) & (n < 4))
        def _():
            tokens(n)

        @pl.when((n >= 4) & (n < 4 + GROUP))
        def _():
            settle_extras(n - 4)

    loop(middle, limit + 2 * DEPTH * HOP, late)
    for step in range(1, n_sections):
        handed(step).wait()
        table_out(place, step).wait_send()
        source = (section + n_sections - step) % n_sections
        remote(
            piece.at[3, 0, pl.ds(0, table.shape[1])], table.at[source], f_send.at[0],
            f_recv.at[source], (me, other_core),
        ).wait_recv()
    outs = (
        pltpu.make_async_copy(gathered, gathered_ref, last_sem.at[0]),
        pltpu.make_async_copy(rows, rows_ref, last_sem.at[1]),
        pltpu.make_async_copy(table, table_ref, last_sem.at[2]),
        pltpu.make_async_copy(voc, voc_ref, last_sem.at[3]),
    )
    for copy in outs:
        copy.start()

    for r in range(2):
        for kind, target in ((0, ing_ref), (1, act_ref)):

            @pl.when((layer == kind) & (section != 2 * half + r))
            def _():
                spread(r, target, kind).wait_send()

            @pl.when((layer == kind) & (section == 2 * half + r))
            def _():
                keep(r, target).wait()

    for kind, target in ((0, ing_ref), (1, act_ref)):

        @pl.when(section != 2 * kind + layer)
        def _():
            spread(0, target, kind).wait_recv()

    @pl.when(layer == 0)
    def _():
        edge_across().wait_send()

    edge_beside(edge.at[0]).wait_send()
    loop(limit - (SETTLED - 2 * DEPTH) * HOP, limit, settle)

    @pl.when(layer == 0)
    def _():
        loop(0, GUESTS, receive_back)
        loop(0, GUESTS, settle_away)

    @pl.when(layer == 1)
    def _():
        loop(0, GUESTS, lambda g: back(g, 3).wait_send())

    for copy in outs:
        copy.wait()


def reduced(a, b, small, edge, mine, boxes, listed, ids, count, counts, side):
    chunks = 1 + sum(count[0] * count[1] for count in counts)
    n_sections = lax.axis_size("section")
    kept = 32
    slots = BLOCK
    page = edge.shape[1]
    any_space = pl.BlockSpec(memory_space=pl.ANY)
    in_vmem = pl.BlockSpec(memory_space=pltpu.VMEM)
    flops = 2 * a.shape[0] * BLOCK * side * chunks
    dma = pltpu.SemaphoreType.DMA
    return pl.pallas_call(
        functools.partial(reduce_kernel, counts),
        out_shape=tuple(
            jax.ShapeDtypeStruct((count[0] * BLOCK, count[1] * side), BF) for count in counts
        )
        + (
            jax.ShapeDtypeStruct((n_sections, kept, side), BF),
            jax.ShapeDtypeStruct((4, GROUP, slots, side), BF),
            jax.ShapeDtypeStruct((n_sections, BLOCK // n_sections, side), BF),
            jax.ShapeDtypeStruct((mine.shape[0] // 2, mine.shape[1]), BF),
            jax.ShapeDtypeStruct((mine.shape[0] // 2, mine.shape[1]), BF),
            jax.ShapeDtypeStruct((count, mine.shape[1]), F32),
        ),
        in_specs=[any_space] * 2 + [in_vmem] * 2 + [any_space] + [in_vmem] * 3,
        out_specs=(any_space,) * 10,
        scratch_shapes=[
            pltpu.VMEM(a.shape, BF),
            pltpu.VMEM(b.shape, BF),
            pltpu.VMEM((BLOCK, BLOCK), F32),
            pltpu.VMEM((4, chunks + GUESTS, BLOCK, side), BF),
            pltpu.VMEM((BLOCK, side), F32),
            pltpu.VMEM((n_sections, kept, side), BF),
            pltpu.VMEM((2, page, side), BF),
            pltpu.VMEM((4, GROUP, slots, side), BF),
            pltpu.VMEM((n_sections, BLOCK // n_sections, side), BF),
            pltpu.VMEM((4, GROUP, BLOCK, side), BF),
            dma((3, chunks + GUESTS)), dma((3, chunks + GUESTS)), dma((chunks,)),
            dma((n_sections,)), dma((n_sections,)),
            dma((2,)), dma((2,)),
            dma((6, GROUP)), dma((4, GROUP)),
            dma((3, GROUP)), dma((3, GROUP)),
            dma((n_sections,)), dma((n_sections,)),
            dma((2,)), dma((2,)),
            dma((4,)), dma((4,)),
            pltpu.VMEM((count, mine.shape[1]), F32),
            pltpu.SemaphoreType.REGULAR,
            dma((GUESTS,)), dma((GUESTS,)), dma((GUESTS,)), dma((GUESTS,)),
        ],
        compiler_params=pltpu.CompilerParams(
            collective_id=0, has_side_effects=True, vmem_limit_bytes=60 << 20
        ),
        cost_estimate=pl.CostEstimate(
            flops=flops, bytes_accessed=400 << 20, transcendentals=0
        ),
        name="gradient_sums",
    )(a, b, small, edge, mine, boxes, listed, ids)


ROWS = 256


def encoder_kernel(
    words_ref, cot_ref, ids_ref, mask_ref, box_ref, vocab_ref, table_ref, gain_ref, shift_ref,
    q_own, o_own, u_own, d_own, qvb_own, upb_own, gains_ref, shifts_ref,
    a_ref, b_ref, ids_out, edge_ref, mine_ref, small_ref,
    words, ids_all, ids_wide, vocab, spots, picks, land, other, square, norm_in, facts,
    sums_ref, upb_sum, qvb_ref, upb_ref,
    wq, wo, wu, wd, wide, x_land, g_land, x_low, ctx, d_ctx, h_low, act, slope, qkv, d_qkv,
    da_low, df_low, probs, n_one, n_two, r_one, r_two, z, sent_low,
    o_w_send, o_w_recv, c_send, c_recv, i_send, i_recv, s_send, s_recv, o_send, o_recv, local,
    w_local, w_send, w_recv, x_send, x_recv, g_send, g_recv, p_local, p_send, p_recv,
):
    me = lax.axis_index("dp")
    section = lax.axis_index("section")
    n_sections = lax.axis_size("section")
    n_dp = ids_all.shape[0]
    layer = section // 2
    half = section % 2
    mesh_id = pl.DeviceIdType.MESH
    quarter = words_ref.shape[0]
    page, width = x_low.shape
    units = act.shape[2]
    blocks = page // ROWS
    tile = 512
    scale = HEAD_DIM ** (-0.5)
    beside = (me, section + 1 - 2 * half)
    across = (me, (section + 2) % n_sections)
    slots = picks.shape[1]
    side = picks.shape[2]
    held = vocab.shape[0]

    vocab_copy = pltpu.make_async_copy(
        vocab_ref.at[:, pl.ds(pl.multiple_of(layer * side, side), side)], vocab, local.at[0]
    )
    vocab_copy.start()
    table_copies = [
        pltpu.make_async_copy(
            table_ref.at[kind, pl.ds(part * page, page)],
            act.at[kind, :, pl.ds(part * width, width)],
            local.at[2 + 2 * kind + part],
        )
        for kind in range(2)
        for part in range(2)
    ]

    @pl.when(layer == 0)
    def _():
        for copy in table_copies:
            copy.start()

    ids_wide[...] = jnp.full_like(ids_wide, -1)
    ids_wide[:, :slots] = ids_ref[...]

    barrier = pltpu.get_barrier_semaphore()

    def greet(step, carry):
        pl.semaphore_signal(
            barrier, inc=1, device_id=((me + step) % n_dp, section), device_id_type=mesh_id
        )
        return carry

    lax.fori_loop(1, n_dp, greet, 0)
    for step in range(1, n_sections):
        pl.semaphore_signal(
            barrier, inc=1, device_id=(me, (section + step) % n_sections), device_id_type=mesh_id
        )
    pl.semaphore_wait(barrier, n_dp - 1 + n_sections - 1)

    def remote(source, target, sent, got, device):
        return pltpu.make_async_remote_copy(
            src_ref=source, dst_ref=target, send_sem=sent, recv_sem=got, device_id=device,
            device_id_type=mesh_id,
        )

    def weight_copies(i):
        source = (q_own, o_own, u_own, d_own, qvb_own, upb_own)[i].at[0]
        target = (wq, wo, wu, wd, qvb_ref, upb_ref)[i]
        return (
            pltpu.make_async_copy(source, target.at[0], w_local.at[i]),
            remote(source, target.at[1], w_send.at[i], w_recv.at[i], beside),
        )

    def weights_here(i):
        near, far = weight_copies(i)
        near.wait()
        far.wait_recv()

    def ids_move(step):
        return remote(
            ids_wide, ids_all.at[me], i_send.at[step], i_recv.at[me], ((me + step) % n_dp, section)
        )

    def ids_got(step):
        source = (me + step) % n_dp
        return remote(
            ids_wide, ids_all.at[source], i_send.at[0], i_recv.at[source],
            (me, (section + 1) % n_sections),
        )

    loop(1, n_dp, lambda step: ids_move(step).start())
    ids_all[me] = ids_wide[...]

    words_move = remote(
        words_ref, words.at[half], o_w_send, o_w_recv.at[half], (me, layer)
    )
    given_part = g_land.at[pl.ds(pl.multiple_of(half * quarter, quarter), quarter)]
    given_move = remote(cot_ref, given_part, c_send, c_recv.at[half], (me, 2 + layer))
    given_keep = pltpu.make_async_copy(cot_ref, given_part, c_send)

    @pl.when(section != 0)
    def _():
        words_move.start()

    @pl.when(section == 0)
    def _():
        words[0] = words_ref[...]

    @pl.when(section != 3)
    def _():
        given_move.start()

    @pl.when(section == 3)
    def _():
        given_keep.start()

    for i in (0, 4, 5, 1, 2, 3):
        near, far = weight_copies(i)
        far.start()
        near.start()

    loop(1, n_dp, lambda step: ids_got(step).wait_recv())
    lists = ids_all[...].astype(F32)
    lists = jnp.where(half == 0, lists[:, 0], lists[:, 1])
    square[...] = jnp.zeros_like(square)
    square[0:n_dp] = lists
    listed = mask_ref[...].astype(F32)
    square[n_dp : n_dp + 1, :slots] = jnp.where(half == 0, listed[0:1], listed[1:2])
    turned = square[...].T
    at = (me * held + lax.broadcasted_iota(jnp.int32, (slots, held), 1)).astype(F32)
    for origin in range(n_dp):
        spots[origin * slots : (origin + 1) * slots] = (
            at == turned[:slots, origin : origin + 1]
        ).astype(F32).astype(BF)
    vocab_copy.wait()
    found = jnp.dot(spots[...], vocab[...], preferred_element_type=F32).astype(BF)
    for origin in range(n_dp):
        picks[origin] = found[origin * slots : (origin + 1) * slots]

    lines = n_dp // 2
    line, lane_of = me // 2, me % 2

    def slots_beside(at):
        return remote(
            picks.at[2 * at + 1 - lane_of], land.at[at], s_send.at[at], s_recv.at[at],
            (me + 1 - 2 * lane_of, section),
        )

    def slots_along(step):
        to = (line + step) % lines
        return remote(
            picks.at[2 * to + lane_of], land.at[lines + line], s_send.at[lines + to],
            s_recv.at[lines + line], (2 * to + lane_of, section),
        )

    def slots_got(step):
        source = (line + step) % lines
        return remote(
            picks.at[0], land.at[lines + source], s_send.at[0], s_recv.at[lines + source],
            (me, (section + 1) % n_sections),
        )

    def pass_on(step):
        to = (line + step) % lines
        slots_beside(to).wait_recv()
        picks[2 * to + lane_of] = picks[2 * to + lane_of] + land[to]

        @pl.when(step < lines)
        def _():
            slots_along(step).start()

    loop(1, lines + 1, lambda step: slots_beside((line + step) % lines).start())
    loop(1, lines + 1, pass_on)
    land[lines + line] = picks[me]

    @pl.when(layer == 0)
    def _():
        for copy in table_copies:
            copy.wait()
        coords = lax.broadcasted_iota(jnp.int32, (page, page), 0)
        for kind in range(2):
            low_at, high_at = (
                box_ref[i : i + 1, pl.ds(pl.multiple_of(half * page, page), page)]
                for i in (kind, kind + 2)
            )
            for part in range(2):
                at = coords + part * page
                ones = (at == low_at).astype(F32) + (at == high_at).astype(F32)
                term = lax.dot_general(
                    ones.astype(BF), act[kind, :, pl.ds(part * width, width)],
                    (((0,), (0,)), ((), ())), preferred_element_type=F32,
                )
                if kind + part == 0:
                    wide[...] = term
                else:
                    wide[...] += term

    loop(1, lines, lambda step: slots_got(step).wait_recv())
    mine = land[lines]
    for origin in range(1, lines):
        mine = mine + land[lines + origin]
    other[1] = mine
    other_move = remote(other.at[1], other.at[0], o_send, o_recv, (me, half))

    @pl.when(layer == 1)
    def _():
        other_move.start()

    @pl.when(layer == 0)
    def _():
        for r in range(2):

            @pl.when(section + r > 0)
            def _():
                remote(
                    words_ref, words.at[r], o_w_send, o_w_recv.at[r], (me, section + 1)
                ).wait_recv()

        places = lax.broadcasted_iota(jnp.int32, (slots, page), 1).astype(F32)
        chosen = (turned[:slots, n_dp : n_dp + 1] == places).astype(F32).astype(BF)

        def spread_out(right):
            return lax.dot_general(
                chosen, right, (((0,), (0,)), ((), ())), preferred_element_type=F32
            )

        marked = spread_out(jnp.ones((slots, BLOCK), BF))[:, 0:1]
        facts[1] = 1.0 - marked
        other_move.wait_recv()
        for part, values in ((0, other[1]), (1, other[0])):
            columns = pl.ds(part * side, side)
            wide[:, columns] += spread_out(values)
        for r in range(2):
            rows = pl.ds(r * quarter, quarter)
            kept = facts[1, rows]
            summed = wide[rows] + words[r].astype(F32) * kept
            center = summed - jnp.mean(summed, -1, keepdims=True)
            spread = jnp.mean(center * center, -1, keepdims=True)
            inverse = lax.rsqrt(spread + EPS)
            normed = center * inverse
            norm_in[rows] = normed
            facts[0, rows] = inverse
            wide[rows] = normed * gain_ref[...][None] + shift_ref[...][None]

    ids_copy = pltpu.make_async_copy(ids_all, ids_out, local.at[1])
    ids_copy.start()

    @pl.when(layer == 1)
    def _():
        for r in range(2):

            @pl.when(section + r < 4)
            def _():
                remote(
                    cot_ref, g_land.at[pl.ds(r * quarter, quarter)], c_send, c_recv.at[r],
                    (me, section - 1),
                ).wait_recv()

    @pl.when(section == 3)
    def _():
        given_keep.wait()

    def rows_of(block):
        return pl.ds(pl.multiple_of(block * ROWS, ROWS), ROWS)

    def x_move(block):
        rows = rows_of(block)
        return remote(
            sent_low.at[rows], x_land.at[rows], x_send.at[block], x_recv.at[block], across
        )

    def g_move(block):
        rows = rows_of(block)
        return remote(
            sent_low.at[rows], g_land.at[rows], g_send.at[block], g_recv.at[block], across
        )

    spans = (
        (a_ref, 0, width), (a_ref, width, side), (a_ref, width + side, width),
        (a_ref, 2 * width + side, units),
        (b_ref, 0, 3 * side), (b_ref, 3 * side, width), (b_ref, 3 * side + width, units),
        (b_ref, 3 * side + width + units, width),
    )

    def piece_copies(i):
        target, start, size = spans[i]
        source = (x_low, ctx, h_low, act, d_qkv, da_low, slope, df_low)[i]
        double = i in (1, 3, 4, 6)
        columns = pl.ds(start, size)
        return (
            pltpu.make_async_copy(
                source.at[0] if double else source, target.at[0, :, columns], p_local.at[i]
            ),
            remote(
                source.at[1] if double else source, target.at[1, :, columns], p_send.at[i],
                p_recv.at[i], beside,
            ),
        )

    def hand_out(*pieces):
        for i in pieces:
            near, far = piece_copies(i)
            far.start()
            near.start()

    def nt(left, right):
        return lax.dot_general(
            left, right, (((1,), (1,)), ((), ())), preferred_element_type=F32
        )

    def tn(left, right):
        return lax.dot_general(
            left, right, (((0,), (0,)), ((), ())), preferred_element_type=F32
        )

    def centred(values):
        center = values - jnp.mean(values, -1, keepdims=True)
        spread = jnp.mean(center * center, -1, keepdims=True)
        inverse = lax.rsqrt(spread + EPS)
        return center * inverse, inverse

    def pulled(grad, normed, inverse, gain):
        scaled = grad * gain
        return inverse * (
            scaled
            - jnp.mean(scaled, -1, keepdims=True)
            - normed * jnp.mean(scaled * normed, -1, keepdims=True)
        )

    def add_sum(row, values):
        sums_ref[row : row + 1] += jnp.sum(values, 0, keepdims=True)

    sums_ref[...] = jnp.zeros_like(sums_ref)
    upb_sum[...] = jnp.zeros_like(upb_sum)

    for i in (0, 4, 5):
        weights_here(i)

    def project(block):
        rows = rows_of(block)

        @pl.when(layer == 1)
        def _():
            x_move(block).wait_recv()
            wide[rows] = x_land[rows].astype(F32)

        low = wide[rows].astype(BF)
        x_low[rows] = low
        for slot in range(2):
            for c in range(3):
                part = pl.ds(c * side, side)
                value = jnp.dot(low, wq[slot, :, part], preferred_element_type=F32)
                if c != 1:
                    value = value + qvb_ref[slot, c // 2 : c // 2 + 1]
                qkv[slot, rows, part] = value.astype(BF)

    loop(0, blocks, project)
    hand_out(0)

    lane = lax.broadcasted_iota(jnp.int32, (1, 2 * HEAD_DIM), 1)
    masks = ((lane < HEAD_DIM).astype(F32).astype(BF), (lane >= HEAD_DIM).astype(F32).astype(BF))
    first_lane = lax.broadcasted_iota(jnp.int32, (page, 2 * HEAD_DIM), 1) < HEAD_DIM
    first_row = lax.broadcasted_iota(jnp.int32, (2 * HEAD_DIM, page), 0) < HEAD_DIM
    pairs = side // (2 * HEAD_DIM)

    def lanes(i, third):
        at = third * side + (i % pairs) * 2 * HEAD_DIM
        return pl.ds(pl.multiple_of(at, 2 * HEAD_DIM), 2 * HEAD_DIM)

    def attend(i):
        slot = i // pairs
        queries = qkv[slot, :, lanes(i, 0)] * jnp.asarray(scale, BF)
        keys = qkv[slot, :, lanes(i, 1)]
        values = qkv[slot, :, lanes(i, 2)]
        found = []
        for e in range(2):
            scores = nt(keys * masks[e], queries)
            expo = jnp.exp(scores - jnp.max(scores, 0, keepdims=True))
            share = 1.0 / jnp.sum(expo, 0, keepdims=True)
            low = (expo * share).astype(BF)
            probs[2 * i + e] = low
            found.append(tn(values, low))
        ctx[slot, :, lanes(i, 0)] = jnp.where(first_row, found[0], found[1]).T.astype(BF)

    loop(0, 2 * pairs, attend)
    hand_out(1)
    for i in range(1, 4):
        weights_here(i)

    def feed(block):
        rows = rows_of(block)
        attended = (
            jnp.dot(ctx[0, rows], wo[0], preferred_element_type=F32)
            + jnp.dot(ctx[1, rows], wo[1], preferred_element_type=F32)
            + shifts_ref[layer, 0:1]
        )
        normed, inverse = centred(wide[rows] + attended)
        n_one[rows] = normed
        r_one[rows] = inverse
        hidden = normed * gains_ref[layer, 0:1] + shifts_ref[layer, 1:2]
        z[rows] = hidden
        h_low[rows] = hidden.astype(BF)
        for slot in range(2):
            for c in range(units // tile):
                part = pl.ds(c * tile, tile)
                upper = (
                    jnp.dot(h_low[rows], wu[slot, :, part], preferred_element_type=F32)
                    + upb_ref[slot, :, part]
                )
                below = 0.5 * (1.0 + lax.erf(upper * ROOT_HALF))
                act[slot, rows, part] = (upper * below).astype(BF)
                slope[slot, rows, part] = (
                    below + upper * jnp.exp(-0.5 * upper * upper) * INV_ROOT_TWO_PI
                ).astype(BF)
        mixed = (
            jnp.dot(act[0, rows], wd[0], preferred_element_type=F32)
            + jnp.dot(act[1, rows], wd[1], preferred_element_type=F32)
            + shifts_ref[layer, 2:3]
        )
        normed, inverse = centred(z[rows] + mixed)
        n_two[rows] = normed
        r_two[rows] = inverse
        output = normed * gains_ref[layer, 1:2] + shifts_ref[layer, 3:4]
        sent_low[rows] = output.astype(BF)

        @pl.when(layer == 0)
        def _():
            x_move(block).start()

        @pl.when(layer == 1)
        def _():
            mine_ref[rows] = sent_low[rows]

    loop(0, blocks, feed)
    hand_out(2, 3)

    def feed_back(block):
        rows = rows_of(block)

        @pl.when(layer == 0)
        def _():
            g_move(block).wait_recv()

        grad = g_land[rows].astype(F32)
        normed = n_two[rows]
        add_sum(1, grad * normed)
        add_sum(5, grad)
        grad = pulled(grad, normed, r_two[rows], gains_ref[layer, 1:2])
        z[rows] = grad
        low = grad.astype(BF)
        df_low[rows] = low
        add_sum(4, low.astype(F32))
        for slot in range(2):
            for c in range(units // tile):
                part = pl.ds(c * tile, tile)
                term = nt(df_low[rows], wd[slot, part])
                term = (term * slope[slot, rows, part].astype(F32)).astype(BF)
                slope[slot, rows, part] = term
                upb_sum[slot : slot + 1, part] += jnp.sum(term.astype(F32), 0, keepdims=True)
        grad = z[rows] + nt(slope[0, rows], wu[0]) + nt(slope[1, rows], wu[1])
        normed = n_one[rows]
        add_sum(0, grad * normed)
        add_sum(3, grad)
        grad = pulled(grad, normed, r_one[rows], gains_ref[layer, 0:1])
        z[rows] = grad
        low = grad.astype(BF)
        da_low[rows] = low
        add_sum(2, low.astype(F32))
        for slot in range(2):
            d_ctx[slot, rows] = nt(da_low[rows], wo[slot]).astype(BF)

    loop(0, blocks, feed_back)
    hand_out(5, 6, 7)

    def attend_back(i):
        slot = i // pairs
        queries = qkv[slot, :, lanes(i, 0)]
        keys = qkv[slot, :, lanes(i, 1)]
        values = qkv[slot, :, lanes(i, 2)]
        grads = d_ctx[slot, :, lanes(i, 0)]
        d_q, d_k, d_v = [], [], []
        for e in range(2):
            low = probs[2 * i + e]
            share = low.astype(F32)
            term = share * nt(values * masks[e], grads)
            term = (term - share * jnp.sum(term, 0, keepdims=True)).astype(BF)
            d_k.append(jnp.dot(term, queries, preferred_element_type=F32))
            d_v.append(jnp.dot(low, grads, preferred_element_type=F32))
            d_q.append(tn(keys, term))
        d_qkv[slot, :, lanes(i, 0)] = (
            jnp.where(first_row, d_q[0], d_q[1]).T * scale
        ).astype(BF)
        d_qkv[slot, :, lanes(i, 1)] = (jnp.where(first_lane, d_k[0], d_k[1]) * scale).astype(BF)
        d_qkv[slot, :, lanes(i, 2)] = jnp.where(first_lane, d_v[0], d_v[1]).astype(BF)

    loop(0, 2 * pairs, attend_back)
    hand_out(4)

    def leave(block):
        rows = rows_of(block)
        grad = z[rows] + nt(d_qkv[0, rows], wq[0]) + nt(d_qkv[1, rows], wq[1])
        z[rows] = grad

        @pl.when(layer == 1)
        def _():
            sent_low[rows] = z[rows].astype(BF)
            g_move(block).start()

        @pl.when(layer == 0)
        def _():
            grad = z[rows]
            normed = norm_in[rows]
            add_sum(6, grad * normed)
            add_sum(7, grad)
            low = pulled(grad, normed, facts[0, rows], gain_ref[...][None]).astype(BF)
            edge_ref[0, rows] = low[:, :side]
            edge_ref[1, rows] = low[:, side:]
            mine_ref[rows] = (low.astype(F32) * facts[1, rows]).astype(BF)

    loop(0, blocks, leave)
    small_ref[...] = jnp.zeros_like(small_ref)
    pieces = units // side
    for slot in range(2):
        for i in range(2):
            part = pl.ds(2 * i * side, side)
            at = slot * (2 + pieces) + i
            small_ref[at : at + 1] = jnp.sum(
                d_qkv[slot, :, part].astype(F32), 0, keepdims=True
            )
        for i in range(pieces):
            at = slot * (2 + pieces) + 2 + i
            small_ref[at : at + 1] = upb_sum[slot : slot + 1, pl.ds(i * side, side)]
    for i in range(8):
        for j in range(2):
            at = 2 * (2 + pieces) + 2 * i + j
            small_ref[at : at + 1] = sums_ref[i : i + 1, pl.ds(j * side, side)]
    for block in range(blocks):

        @pl.when(layer == 0)
        def _():
            x_move(block).wait_send()

        @pl.when(layer == 1)
        def _():
            g_move(block).wait_send()

    for i in range(6):
        weight_copies(i)[1].wait_send()
    for i in range(8):
        near, far = piece_copies(i)
        near.wait()
        far.wait()


    @pl.when(layer == 1)
    def _():
        other_move.wait_send()

    @pl.when(section != 0)
    def _():
        words_move.wait_send()

    @pl.when(section != 3)
    def _():
        given_move.wait_send()

    loop(1, n_dp, lambda step: ids_move(step).wait_send())
    loop(0, lines, lambda at: slots_beside(at).wait_send())
    loop(1, lines, lambda step: slots_along(step).wait_send())
    ids_copy.wait()


def encoded(
    words, cot, ids, mask, boxes, vocab, table, gain, shift, weights, qvb, upb, gains, shifts
):
    quarter, width = words.shape
    page = 2 * quarter
    n_dp = lax.axis_size("dp")
    slots = ids.shape[1]
    held = vocab.shape[0]
    side = width // 2
    units = weights[3].shape[1]
    blocks = page // ROWS
    heads = width // HEAD_DIM
    any_space = pl.BlockSpec(memory_space=pl.ANY)
    in_vmem = pl.BlockSpec(memory_space=pltpu.VMEM)
    dma = pltpu.SemaphoreType.DMA
    vmem = pltpu.VMEM
    flops = 8 * page * width * (4 * width + 4 * units) * 2
    return pl.pallas_call(
        encoder_kernel,
        out_shape=(
            jax.ShapeDtypeStruct((2, page, 2 * width + side + units), BF),
            jax.ShapeDtypeStruct((2, page, 3 * side + 2 * width + units), BF),
            jax.ShapeDtypeStruct((n_dp, 2, BLOCK), jnp.int32),
            jax.ShapeDtypeStruct((2, page, side), BF),
            jax.ShapeDtypeStruct((page, width), BF),
            jax.ShapeDtypeStruct((BLOCK, side), F32),
        ),
        in_specs=[in_vmem, any_space] + [in_vmem] * 3 + [any_space] * 2 + [in_vmem] * 2
        + [any_space] * 6 + [in_vmem] * 2,
        out_specs=(any_space,) * 3 + (in_vmem,) * 3,
        scratch_shapes=[
            vmem((2, quarter, width), BF), vmem((n_dp, 2, BLOCK), jnp.int32),
            vmem((2, BLOCK), jnp.int32),
            vmem((held, side), BF), vmem((n_dp * slots, held), BF),
            vmem((n_dp, slots, side), BF), vmem((n_dp, slots, side), BF),
            vmem((2, slots, side), BF), vmem((BLOCK, BLOCK), F32),
            vmem((page, width), F32), vmem((2, page, 1), F32),
            vmem((8, width), F32), vmem((2, units), F32),
            vmem((2, 2, side), F32), vmem((2, 1, units), F32),
            vmem((2, width, 3 * side), BF), vmem((2, side, width), BF),
            vmem((2, width, units), BF), vmem((2, units, width), BF),
            vmem((page, width), F32), vmem((page, width), BF), vmem((page, width), BF),
            vmem((page, width), BF), vmem((2, page, side), BF), vmem((2, page, side), BF),
            vmem((page, width), BF), vmem((2, page, units), BF), vmem((2, page, units), BF),
            vmem((2, page, 3 * side), BF), vmem((2, page, 3 * side), BF),
            vmem((page, width), BF), vmem((page, width), BF), vmem((heads, page, page), BF),
            vmem((page, width), F32), vmem((page, width), F32),
            vmem((page, 1), F32), vmem((page, 1), F32),
            vmem((page, width), F32), vmem((page, width), BF),
            dma, dma((2,)), dma, dma((2,)), dma((n_dp,)), dma((n_dp,)),
            dma((n_dp,)), dma((n_dp,)), dma, dma, dma((6,)),
            dma((6,)), dma((6,)), dma((6,)),
            dma((blocks,)), dma((blocks,)), dma((blocks,)), dma((blocks,)),
            dma((8,)), dma((8,)), dma((8,)),
        ],
        compiler_params=pltpu.CompilerParams(
            collective_id=1, has_side_effects=True, vmem_limit_bytes=63 << 20
        ),
        cost_estimate=pl.CostEstimate(
            flops=flops, bytes_accessed=200 << 20, transcendentals=0
        ),
        name="encoder_both_ways",
    )(words, cot, ids, mask, boxes, vocab, table, gain, shift, *weights, qvb, upb, gains, shifts)


def finish_kernel(
    pieces, q_in, o_in, u_in, d_in, voc_in, small_ref, table_ref, act_in, ing_in,
    act_ref, ing_ref, tab_ref, voc_ref, q_ref, qvb_ref, o_ref, u_ref, upb_ref, d_ref, gains_ref,
    shifts_ref, eg_ref, es_ref,
    q_s, o_s, u_s, d_s, q_f, o_f, u_f, d_f, act_s, ing_s, act_f, ing_f, in_sem, out_sem, voc_s, voc_sem,
):
    section = lax.axis_index("section")
    layer = section // 2
    half = section % 2
    side = table_ref.shape[2]
    voc_copy = pltpu.make_async_copy(voc_in, voc_s, voc_sem.at[0])
    voc_copy.start()
    moves = []
    for source, low, wide, target in (
        (d_in, d_s, d_f, d_ref), (u_in, u_s, u_f, u_ref), (q_in, q_s, q_f, q_ref),
        (o_in, o_s, o_f, o_ref),
    ):
        count = low.shape[0] // pieces
        for i in range(pieces):
            rows = pl.ds(i * count, count)
            moves.append((source.at[rows], low.at[rows], wide.at[rows], target.at[0, rows]))
    moves.append((act_in, act_s, act_f, act_ref))
    moves.append((ing_in, ing_s, ing_f, ing_ref))
    for i, (source, low, wide, target) in enumerate(moves):
        pltpu.make_async_copy(source, low, in_sem.at[i]).start()


    parts = small_ref[...].astype(F32)
    partner = jnp.where(half == 0, parts[1], parts[3])
    far_partner = jnp.where(half == 0, parts[3], parts[1])
    splits = d_in.shape[0] // side
    kept = 2 + splits
    own = parts[0, :kept] + partner[kept : 2 * kept]
    qvb_ref[0] = own[:2]
    for i in range(splits):
        upb_ref[0:1, pl.ds(i * side, side)] = own[2 + i : 3 + i]
    here = (parts[0] + partner)[2 * kept : 2 * kept + 16]
    there = (parts[2] + far_partner)[2 * kept : 2 * kept + 16]
    in_order = (jnp.where(layer == 0, here, there), jnp.where(layer == 0, there, here))
    for j in range(2):
        columns = pl.ds(j * side, side)
        for l in range(2):
            for i in range(2):
                at = 2 * i + j
                gains_ref[l, i : i + 1, columns] = in_order[l][at : at + 1]
            for i in range(4):
                at = 4 + 2 * i + j
                shifts_ref[l, i : i + 1, columns] = in_order[l][at : at + 1]
        eg_ref[columns] = in_order[0][12 + j]
        es_ref[columns] = in_order[0][14 + j]
    for l in range(2):
        for h in range(2):
            tab_ref[h, :, pl.ds(l * side, side)] = table_ref[2 * l + h].astype(F32)

    voc_copy.wait()
    voc_out = pltpu.make_async_copy(voc_s, voc_ref, voc_sem.at[1])
    voc_out.start()
    for i, (source, low, wide, target) in enumerate(moves):
        pltpu.make_async_copy(source, low, in_sem.at[i]).wait()
        wide[...] = low[...].astype(F32)
        pltpu.make_async_copy(wide, target, out_sem.at[i]).start()

    for i, (source, low, wide, target) in enumerate(moves):
        pltpu.make_async_copy(wide, target, out_sem.at[i]).wait()
    voc_out.wait()


def finished(sums, voc, small, tables, act, ing, side):
    any_space = pl.BlockSpec(memory_space=pl.ANY)
    in_vmem = pl.BlockSpec(memory_space=pltpu.VMEM)
    dma = pltpu.SemaphoreType.DMA
    vmem = pltpu.VMEM
    pieces = 4
    width = act.shape[1]
    units = sums[3].shape[0]
    shapes = [array.shape for array in sums]
    outs = [
        jax.ShapeDtypeStruct(shape, F32)
        for shape in (
            act.shape, ing.shape, (2, tables.shape[1], width), voc.shape, (1, *shapes[0]),
            (1, 2, side), (1, *shapes[1]), (1, *shapes[2]), (1, units), (1, *shapes[3]),
            (2, 2, width), (2, 4, width), (width,), (width,),
        )
    ]
    specs = [any_space] * 2 + [in_vmem] + [any_space] * 2 + [in_vmem, any_space, any_space, in_vmem, any_space] + [in_vmem] * 4
    return pl.pallas_call(
        functools.partial(finish_kernel, pieces),
        out_shape=outs,
        in_specs=[any_space] * 5 + [in_vmem] * 2 + [any_space] * 2,
        out_specs=specs,
        scratch_shapes=[vmem(shape, BF) for shape in shapes]
        + [vmem(shape, F32) for shape in shapes]
        + [vmem(act.shape, BF)] * 2
        + [vmem(act.shape, F32)] * 2
        + [dma((4 * pieces + 2,)), dma((4 * pieces + 2,)), vmem(voc.shape, F32), dma((2,))],
        compiler_params=pltpu.CompilerParams(vmem_limit_bytes=60 << 20),
        name="finished_outputs",
    )(*sums, voc, small, tables, act, ing)


def on_device(
    word_embed, boxes, mask_pos, replace_ids, cotangent, layout_table, vocab_table, embed_gain,
    embed_shift, qkv_weight, qv_bias, out_weight, up_weight, up_bias, down_weight, layer_gains,
    layer_biases,
):
    section = lax.axis_index("section")
    layer = section // 2
    half = section % 2
    quarter, width = word_embed.shape
    page = 2 * quarter
    side = qkv_weight.shape[2] // 3
    units = up_bias.shape[1]

    left, right, all_ids, edge, mine, small = encoded(
        word_embed, cotangent, replace_ids, mask_pos, boxes, vocab_table, layout_table,
        embed_gain, embed_shift, (qkv_weight, out_weight, up_weight, down_weight), qv_bias,
        up_bias[:, None], layer_gains, layer_biases,
    )
    left, right = (array.reshape(2 * page, -1) for array in (left, right))
    counts = (
        (width // BLOCK, 3),
        (side // BLOCK, width // side),
        (width // BLOCK, units // side),
        (units // BLOCK, width // side),
    )
    count = vocab_table.shape[0] // lax.axis_size("section")
    *sums, gathered, slot_rows, table_rows, act, ing, voc = reduced(
        left, right, small, edge, mine, boxes, mask_pos, all_ids, count, counts, side
    )
    outer = lax.axis_size("dp") // GROUP
    table_part = None
    if outer > 1:
        groups = [[i + GROUP * g for g in range(outer)] for i in range(GROUP)]
        *sums, gathered = lax.psum((*sums, gathered), "dp", axis_index_groups=groups)
        slot_rows = lax.all_gather(slot_rows, "dp", axis_index_groups=groups, axis=1, tiled=True)
        here = jnp.arange(count, dtype=jnp.int32)
        here = here + (lax.axis_index("dp") * lax.axis_size("section") + section) * count
        ordered_ids = jnp.where(half == 0, all_ids, all_ids[:, ::-1])
        ordered_ids = ordered_ids.transpose(1, 0, 2).reshape(-1)
        held = slot_rows.reshape(2, 2, -1, side).transpose(0, 2, 1, 3).reshape(-1, width)
        voc = jnp.dot(
            (here[:, None] == ordered_ids[None]).astype(BF), held, preferred_element_type=F32
        )
        voc = jnp.where(layer == 0, voc, jnp.roll(voc, side, 1))
        coords = jnp.arange(layout_table.shape[1], dtype=jnp.int32)
        page_boxes = lax.dynamic_slice_in_dim(boxes, half * page, page, 1)
        grad_low = jnp.concatenate([edge[0], edge[1]], 1)
        grad_low = jnp.where(layer == 0, grad_low, jnp.zeros_like(grad_low))
        table_grad = jnp.stack(
            [
                matmul_left_t(
                    (page_boxes[a][:, None] == coords[None, :]).astype(BF)
                    + (page_boxes[a + 2][:, None] == coords[None, :]).astype(BF),
                    grad_low,
                )
                for a in (0, 1)
            ]
        )
        table_part = lax.psum_scatter(
            table_grad.astype(BF), ("dp", "section"), scatter_dimension=1, tiled=True
        ).astype(F32)
    act, ing, tables, vocab_part, *rest = finished(
        sums, voc, gathered, table_rows, act, ing, side
    )
    if table_part is None:
        table_part = tables
    *layer_sums, gains_sum, shifts_sum, gain_sum, shift_sum = rest
    return (
        act, ing, table_part, vocab_part, gain_sum, shift_sum, *layer_sums, gains_sum, shifts_sum,
    )


def solution(mesh):
    both = ("dp", "section")
    by_section = P("section", None, None)
    return jax.shard_map(
        on_device,
        mesh=mesh,
        in_specs=(
            P(both, None), P(None, "dp"), P("dp", None), P("dp", None), P(both, None), P(),
            P("dp", None), P(), P(), by_section, by_section, by_section, by_section,
            P("section", None), by_section, P(), P(),
        ),
        out_specs=(
            P(both, None), P(both, None), P(None, both, None), P(both, None), P(), P(),
            by_section, by_section, by_section, by_section, P("section", None), by_section,
            P(), P(),
        ),
        check_vma=False,
    )
```
